32 devices in a mesh: replica: 2 (over y), shard: 16 (over z, x, core).
Axes of the slice: x: 2, y: 2, z: 4, core: 2. Of those that a mesh axis runs over, the one named last changes fastest.
Arguments:
- tokens: bfloat16 [32, 288, 2048], P(('replica', 'shard')), may hold values from -6 to 6
- ln1_gain: bfloat16 [2048], P('shard'), may hold values from 0.5 to 1.5
- ln1_bias: bfloat16 [2048], P('shard'), may hold values from -1 to 1
- ln2_gain: bfloat16 [2048], P('shard'), may hold values from 0.5 to 1.5
- ln2_bias: bfloat16 [2048], P('shard'), may hold values from -1 to 1
- qkv_weight: bfloat16 [2048, 6144], P('shard'), may hold values from -0.125 to 0.125
- qkv_bias: bfloat16 [6144], P('shard'), may hold values from -1 to 1
- out_weight: bfloat16 [2048, 2048], P('shard'), may hold values from -0.375 to 0.375
- out_bias: bfloat16 [2048], P('shard'), may hold values from -1 to 1
- fc1_weight: bfloat16 [2048, 8192], P('shard'), may hold values from -0.125 to 0.125
- fc1_bias: bfloat16 [8192], P('shard'), may hold values from -1 to 1
- fc2_weight: bfloat16 [8192, 2048], P('shard'), may hold values from -0.0625 to 0.0625
- fc2_bias: bfloat16 [2048], P('shard'), may hold values from -1 to 1
- cotangent: bfloat16 [32, 288, 2048], P(('replica', 'shard')), may hold values from -6 to 6
Outputs:
- output: bfloat16 [32, 288, 2048], P(('replica', 'shard'))
- input_grad: bfloat16 [32, 288, 2048], P(('replica', 'shard'))
- ln1_gain_grad: float32 [2048], P('shard')
- ln1_bias_grad: float32 [2048], P('shard')
- ln2_gain_grad: float32 [2048], P('shard')
- ln2_bias_grad: float32 [2048], P('shard')
- qkv_weight_grad: float32 [2048, 6144], P('shard')
- qkv_bias_grad: float32 [6144], P('shard')
- out_weight_grad: float32 [2048, 2048], P('shard')
- out_bias_grad: float32 [2048], P('shard')
- fc1_weight_grad: float32 [2048, 8192], P('shard')
- fc1_bias_grad: float32 [8192], P('shard')
- fc2_weight_grad: float32 [8192, 2048], P('shard')
- fc2_bias_grad: float32 [2048], P('shard')
The draws below stay inside these ranges and needn't reach their ends.
All inputs are finite; a program needn't handle non-finite values.
Results may differ from the reference program's by a relative error of at most 0.0086.
Values may be sent and summed in bfloat16 or wider, within the bound.
A program may use at most 704 MiB of HBM per device.

```python
import jax
import jax.numpy as jnp
from jax import lax

D = 2048
HEADS = 8
HEAD_DIM = 256
ROTARY = 64
FF = 8192
SEQ = 288
BATCH = 32


def levels(key, dims, cuts, least, high):
    gain = 1.0
    for axis_at, blocks in cuts:
        steps = jax.random.uniform(jax.random.fold_in(jax.random.fold_in(key, 6), axis_at), (blocks,), jnp.float32, least / len(cuts), high / len(cuts))
        gain = gain * jnp.repeat(jnp.exp(steps), dims[axis_at] // blocks).reshape((-1,) + (1,) * (len(dims) - 1 - axis_at))
    return gain


def gaussian(key, shape, spread, reach, split=(), kind=jnp.bfloat16):
    entries = jax.random.normal(key, shape, jnp.float32) * spread
    if len(split) > 0:
        entries = levels(key, shape, split, -0.22, 0.18) * entries
    return jnp.clip(entries, min=-reach, max=reach).astype(kind)


def setup_inputs(seed: int = 0) -> dict:
    streams_of = jax.random.split(jax.random.key(seed), 15)
    tokens = gaussian(streams_of[0], (BATCH, SEQ, D), 1.0, 6.0, ((0, 32),))
    ln1_gain = jnp.clip(1.0 + 0.1 * jax.random.normal(streams_of[1], (D,), jnp.float32), 0.5, 1.5).astype(jnp.bfloat16)
    ln1_bias = gaussian(streams_of[2], (D,), 0.2, 1.0, ((0, 16),))
    ln2_gain = jnp.clip(1.0 + 0.1 * jax.random.normal(streams_of[3], (D,), jnp.float32), 0.5, 1.5).astype(jnp.bfloat16)
    ln2_bias = gaussian(streams_of[4], (D,), 0.2, 1.0, ((0, 16),))
    qkv_weight = gaussian(streams_of[5], (D, 3 * D), D ** -0.5, 0.125, ((0, 16),))
    qkv_bias = gaussian(streams_of[6], (3 * D,), 0.2, 1.0, ((0, 16),))
    out_weight = gaussian(streams_of[7], (D, D), (D // 8) ** -0.5, 0.375, ((0, 16),))
    out_bias = gaussian(streams_of[8], (D,), 0.2, 1.0, ((0, 16),))
    fc1_weight = gaussian(streams_of[9], (D, FF), D ** -0.5, 0.125, ((0, 16),))
    fc1_bias = gaussian(streams_of[10], (FF,), 0.2, 1.0, ((0, 16),))
    fc2_weight = gaussian(streams_of[11], (FF, D), FF ** -0.5, 0.0625, ((0, 16),))
    fc2_bias = gaussian(streams_of[12], (D,), 0.2, 1.0, ((0, 16),))
    cotangent = gaussian(streams_of[13], (BATCH, SEQ, D), 1.0, 6.0, ((0, 32),))
    return {"tokens": tokens, "ln1_gain": ln1_gain, "ln1_bias": ln1_bias, "ln2_gain": ln2_gain, "ln2_bias": ln2_bias, "qkv_weight": qkv_weight, "qkv_bias": qkv_bias, "out_weight": out_weight, "out_bias": out_bias, "fc1_weight": fc1_weight, "fc1_bias": fc1_bias, "fc2_weight": fc2_weight, "fc2_bias": fc2_bias, "cotangent": cotangent}


EPS = 1e-05
HIGH = lax.Precision.HIGHEST

@jax.custom_vjp
def low(v):
    return lax.optimization_barrier(v.astype(jnp.bfloat16)).astype(jnp.float32)

@jax.custom_vjp
def low_back(v):
    return v

def low_keep(v):
    return (low(v), None)

def low_pass(kept, grad):
    return (grad,)

def back_keep(v):
    return (v, None)

def back_low(kept, grad):
    return (low(grad),)
low.defvjp(low_keep, low_pass)
low_back.defvjp(back_keep, back_low)

def norm_rows(values, scales, shifts):
    row_mean = lax.optimization_barrier(jnp.mean(values, axis=-1, keepdims=True))
    centred = values - row_mean
    row_var = lax.optimization_barrier(jnp.mean(centred * centred, axis=-1, keepdims=True))
    return centred * lax.rsqrt(row_var + EPS) * scales + shifts

def rotary_tables(length, rot_dims):
    places = jnp.arange(length, dtype=jnp.float32)
    frequency = 10000.0 ** (-jnp.arange(0, rot_dims, 2, dtype=jnp.float32) / rot_dims)
    angles = places[:, None] * frequency[None, :]
    angles = jnp.concatenate([angles, angles], axis=-1)
    return (jnp.cos(angles)[:, None, :], jnp.sin(angles)[:, None, :])

def rotate(head_rows, cosine_table, sine_table, rot_dims):
    rotated_part = head_rows[..., :rot_dims]
    half_dims = rot_dims // 2
    turned = jnp.concatenate([-rotated_part[..., half_dims:], rotated_part[..., :half_dims]], axis=-1)
    return jnp.concatenate([rotated_part * cosine_table + turned * sine_table, head_rows[..., rot_dims:]], axis=-1)

def layer_forward(params, inputs):
    ln1_scale, ln1_shift, ln2_scale, ln2_shift, qkv_w, qkv_b, out_w, out_b, fc1_w, fc1_b, fc2_w, fc2_b = params
    groups, length, model_width = inputs.shape
    cosine_table, sine_table = rotary_tables(length, ROTARY)
    normed_one = low(norm_rows(inputs, ln1_scale, ln1_shift))
    packed = low_back(jnp.matmul(normed_one, qkv_w, precision=HIGH) + qkv_b)
    packed = packed.reshape(groups, length, HEADS, 3, HEAD_DIM)
    queries = low(rotate(packed[:, :, :, 0], cosine_table, sine_table, ROTARY))
    keys_all = low(rotate(packed[:, :, :, 1], cosine_table, sine_table, ROTARY))
    values_all = low(packed[:, :, :, 2])
    scores = jnp.einsum('gqhd,gkhd->ghqk', queries, keys_all, precision=HIGH) * HEAD_DIM ** (-0.5)
    scores = low_back(scores)
    causal = jnp.arange(length)[:, None] >= jnp.arange(length)[None, :]
    scores = jnp.where(causal, scores, -1e+30)
    attn_probs = low(jax.nn.softmax(scores, axis=-1))
    mixed_heads = jnp.einsum('ghqk,gkhd->gqhd', attn_probs, values_all, precision=HIGH)
    mixed_heads = low(low_back(mixed_heads)).reshape(groups, length, model_width)
    attended = jnp.matmul(mixed_heads, out_w, precision=HIGH) + out_b
    normed_two = low(norm_rows(inputs, ln2_scale, ln2_shift))
    upward = low_back(jnp.matmul(normed_two, fc1_w, precision=HIGH) + fc1_b)
    hidden = low(jax.nn.gelu(upward, approximate=False))
    return inputs + attended + jnp.matmul(hidden, fc2_w, precision=HIGH) + fc2_b

def reference(tokens, ln1_gain, ln1_bias, ln2_gain, ln2_bias, qkv_weight, qkv_bias, out_weight, out_bias, fc1_weight, fc1_bias, fc2_weight, fc2_bias, cotangent):
    params = tuple((tensor.astype(jnp.float32) for tensor in (ln1_gain, ln1_bias, ln2_gain, ln2_bias, qkv_weight, qkv_bias, out_weight, out_bias, fc1_weight, fc1_bias, fc2_weight, fc2_bias)))
    sequences, length, model_width = tokens.shape
    group_count = sequences // 8
    inputs = tokens.astype(jnp.float32).reshape(group_count, 8, length, model_width)
    cot_groups = cotangent.astype(jnp.float32).reshape(group_count, 8, length, model_width)

    def one_group(totals, inputs_pair):
        outputs_now, pullback = jax.vjp(layer_forward, params, inputs_pair[0])
        grads, input_now = pullback(inputs_pair[1])
        totals = jax.tree.map(lambda earlier, latest: earlier + latest, totals, grads)
        return (totals, (outputs_now.astype(jnp.bfloat16), input_now.astype(jnp.bfloat16)))
    zeros_init = jax.tree.map(jnp.zeros_like, params)
    totals, (outputs, input_grads) = lax.scan(one_group, zeros_init, (inputs, cot_groups))
    output = outputs.reshape(sequences, length, model_width)
    input_grad = input_grads.reshape(sequences, length, model_width)
    return (output, input_grad, totals[0], totals[1], totals[2], totals[3], totals[4], totals[5], totals[6], totals[7], totals[8], totals[9], totals[10], totals[11])
```

```python
import functools

import jax
import jax.numpy as jnp
import numpy as np
from jax import lax
from jax.experimental import pallas as pl
from jax.experimental.pallas import tpu as pltpu
from jax.sharding import Mesh
from jax.sharding import PartitionSpec as P

HEADS = 8
HEAD_DIM = 256
ROTARY = 64
EPS = 1e-05
NEG_FILL = -1e30
SCALE = HEAD_DIM ** (-0.5)
BF16 = jnp.bfloat16
F32 = jnp.float32
NT = (((1,), (1,)), ((), ()))
TN = (((0,), (0,)), ((), ()))
NN = (((1,), (0,)), ((), ()))


def dot(a, b, dims=NN):
    return lax.dot_general(a, b, dims, preferred_element_type=F32)


def exch(a, axis):
    return lax.ppermute(a, axis, [(0, 1), (1, 0)])


def pick(a, bit, axis=0):
    return lax.dynamic_index_in_dim(a, bit, axis, keepdims=False)


def ordered(bit, mine, other, axis=0):
    first = jnp.where(bit == 0, mine, other)
    second = jnp.where(bit == 0, other, mine)
    return jnp.stack([first, second], axis)


def add_bf16(a, b):
    return (a.astype(F32) + b.astype(F32)).astype(BF16)


def gather_tokens(a):
    half = a.shape[0] // 2
    pair = jnp.stack([a, exch(a, "lo")])
    one, two = pair[:, :half], pair[:, half:]
    one = jnp.stack([one, exch(one, "x")])
    two = jnp.stack([two, exch(two, "y")])
    one = jnp.stack([one, exch(one, "y")])
    two = jnp.stack([two, exch(two, "x")], 1)
    full = jnp.concatenate([one, two], axis=3)
    return full.reshape((8,) + a.shape)


def scatter_tokens(parts):
    _, length, width = parts.shape
    half = length // 2
    parts = parts.reshape(2, 2, 2, length, width)
    one, two = parts[..., :half, :], parts[..., half:, :]
    one = add_bf16(one[0], exch(one[1], "y"))
    two = add_bf16(two[:, 0], exch(two[:, 1], "x"))
    one = add_bf16(one[0], exch(one[1], "x"))
    two = add_bf16(two[0], exch(two[1], "y"))
    both = jnp.concatenate([one, two], axis=1)
    return both[0].astype(F32) + exch(both[1], "lo").astype(F32)


def gather_small(rows, bits):
    rows = rows[None]
    for name in ("c", "x", "lo", "hi"):
        other = exch(rows, name)
        rows = ordered(bits[name], rows, other).reshape((-1,) + rows.shape[1:])
    return rows


def scatter_small(rows, bits):
    for name in ("hi", "lo", "x", "c"):
        rows = rows.reshape((2, -1) + rows.shape[1:])
        rows = pick(rows, bits[name]) + exch(pick(rows, 1 - bits[name]), name)
    rows = rows[0]
    return rows + exch(rows, "y")


def columns_in(weight, bits):
    width = weight.shape[1] // 8
    y, lo, x = bits["y"], bits["lo"], bits["x"]

    def block(lo_at, x_at):
        return lax.dynamic_slice_in_dim(weight, ((y * 2 + lo_at) * 2 + x_at) * width, width, axis=1)

    rows = weight.shape[0]
    came = exch(jnp.stack([block(0, 1 - x), block(1, 1 - x)]), "x")
    keep = ordered(x, block(lo, x), pick(came, lo))
    came = exch(ordered(x, block(1 - lo, x), pick(came, 1 - lo)), "lo")
    keep = ordered(lo, keep, came)
    keep = ordered(bits["hi"], keep, exch(keep, "hi"))
    keep = ordered(bits["c"], keep, exch(keep, "c"), axis=3)
    return keep.reshape(16 * rows, width)


def columns_out(grad, bits):
    width = grad.shape[1]
    grad = grad.reshape(2, 2, 2, 2, -1, width)
    c, hi, lo, x = bits["c"], bits["hi"], bits["lo"], bits["x"]
    part = add_bf16(pick(grad, c, 3), exch(pick(grad, 1 - c, 3), "c"))
    part = add_bf16(pick(part, hi), exch(pick(part, 1 - hi), "hi"))
    part = ordered(lo, pick(part, lo), exch(pick(part, 1 - lo), "lo"))
    part = ordered(x, pick(part, x, 1), exch(pick(part, 1 - x, 1), "x"), axis=1)
    part = ordered(bits["y"], part, exch(part, "y"))
    part = part.reshape((8,) + part.shape[3:])
    return jnp.concatenate([part[i] for i in range(8)], axis=1).astype(F32)


def rows_in(fc2, out, bits):
    mine = jnp.concatenate([fc2, out], axis=0)
    half = mine.shape[0] // 2
    holds = bits["hi"] == bits["y"]
    sent = jnp.where(holds, mine[:half], mine[half:])
    came = exch(sent, "hi")
    last = lax.ppermute(came, ("y", "hi"), [(0, 2), (3, 1)])
    rows = jnp.where(holds, mine, jnp.concatenate([came, last], axis=0))
    both = ordered(bits["c"], rows, exch(rows, "c"))
    cut = fc2.shape[0]
    width = mine.shape[1]
    return both[:, :cut].reshape(-1, width), both[:, cut:].reshape(-1, width)


def rows_out(fc2_grad, out_grad, bits):
    width = fc2_grad.shape[1]
    fc2_grad = fc2_grad.reshape(2, -1, width)
    out_grad = out_grad.reshape(2, -1, width)
    c = bits["c"]
    cut = fc2_grad.shape[1]

    def side(at):
        return jnp.concatenate([pick(fc2_grad, at), pick(out_grad, at)], axis=0)

    part = add_bf16(side(c), exch(side(1 - c), "c"))
    half = part.shape[0] // 2
    one, two = part[:half], exch(part[half:], "y")
    holds = bits["hi"] == bits["y"]
    total = add_bf16(jnp.where(holds, one, two), exch(jnp.where(holds, two, one), "hi"))
    other = exch(total, "y")
    first = jnp.where(holds, total, other)
    second = jnp.where(holds, other, total)
    rows = jnp.concatenate([first, second], axis=0).astype(F32)
    return rows[:cut], rows[cut:]


def rotary_tables(length):
    places = np.arange(length, dtype=np.float32)
    frequency = (10000.0 ** (-np.arange(0, ROTARY, 2, dtype=np.float32) / ROTARY)).astype(np.float32)
    angles = places[:, None] * frequency[None, :]
    cosine, sine = np.cos(angles), np.sin(angles)
    half = ROTARY // 2
    tables = np.zeros((3, length, HEAD_DIM), np.float32)
    tables[0] = 1.0
    tables[0, :, :half] = cosine
    tables[0, :, half:ROTARY] = cosine
    tables[1, :, :half] = -sine
    tables[2, :, half:ROTARY] = sine
    return tables


def turn(rows, tables, sign):
    half = ROTARY // 2
    ahead = pltpu.roll(rows, HEAD_DIM - half, 1)
    behind = pltpu.roll(rows, half, 1)
    return rows * tables[0] + sign * (ahead * tables[1] + behind * tables[2])


def causal_scores(queries, keys_all):
    length = queries.shape[0]
    scores = dot(queries, keys_all, NT) * SCALE
    row = lax.broadcasted_iota(jnp.int32, (length, length), 0)
    col = lax.broadcasted_iota(jnp.int32, (length, length), 1)
    return jnp.where(row >= col, scores, NEG_FILL)


def softmax(scores):
    raised = jnp.exp(scores - jnp.max(scores, axis=-1, keepdims=True))
    return raised / jnp.sum(raised, axis=-1, keepdims=True)


def forward_kernel(
    x_ref, norm_ref, qkv_ref, qkv_bias_ref, fc1_ref, fc1_bias_ref, fc2_ref, out_ref, tables_ref,
    a1_ref, a2_ref, heads_ref, mixed_ref, hidden_ref, slope_ref, y_ref,
):
    x = x_ref[0].astype(F32)
    centred = x - jnp.mean(x, axis=-1, keepdims=True)
    var = jnp.mean(centred * centred, axis=-1, keepdims=True)
    normed = centred * lax.rsqrt(var + EPS)
    a1_ref[0] = (normed * norm_ref[0:1] + norm_ref[1:2]).astype(BF16)
    a2_ref[0] = (normed * norm_ref[2:3] + norm_ref[3:4]).astype(BF16)

    packed = dot(a1_ref[0], qkv_ref[...]) + qkv_bias_ref[...]
    queries = turn(packed[:, :HEAD_DIM], tables_ref, 1.0).astype(BF16)
    keys_all = turn(packed[:, HEAD_DIM : 2 * HEAD_DIM], tables_ref, 1.0).astype(BF16)
    values_all = packed[:, 2 * HEAD_DIM :].astype(BF16)
    heads_ref[0, :, :HEAD_DIM] = queries
    heads_ref[0, :, HEAD_DIM : 2 * HEAD_DIM] = keys_all
    heads_ref[0, :, 2 * HEAD_DIM :] = values_all
    probs = softmax(causal_scores(queries, keys_all)).astype(BF16)
    mixed_ref[0] = dot(probs, values_all).astype(BF16)

    upward = dot(a2_ref[0], fc1_ref[...]) + fc1_bias_ref[...]
    below = 0.5 * (1.0 + lax.erf(upward * np.float32(0.5**0.5)))
    hidden_ref[0] = (upward * below).astype(BF16)
    slope_ref[0] = below + upward * (jnp.exp(-0.5 * upward * upward) * np.float32((2 * np.pi) ** -0.5))

    y_ref[0] = (dot(hidden_ref[0], fc2_ref[...]) + dot(mixed_ref[0], out_ref[...])).astype(BF16)


def backward_kernel(
    g_ref, heads_ref, slope_ref, gain_ref, qkv_ref, fc1_ref, fc2_ref, out_ref, tables_ref,
    packed_ref, up_ref, dx_ref, packed_sum_ref, up_sum_ref,
):
    @pl.when(pl.program_id(0) == 0)
    def _():
        packed_sum_ref[...] = jnp.zeros_like(packed_sum_ref)
        up_sum_ref[...] = jnp.zeros_like(up_sum_ref)

    grad_up = dot(g_ref[0], fc2_ref[...], NT) * slope_ref[0]
    grad_up = grad_up.astype(BF16)
    up_ref[0] = grad_up
    up_sum_ref[...] += jnp.sum(grad_up.astype(F32), axis=0, keepdims=True)

    grad_mixed = dot(g_ref[0], out_ref[...], NT).astype(BF16)
    queries = heads_ref[0, :, :HEAD_DIM]
    keys_all = heads_ref[0, :, HEAD_DIM : 2 * HEAD_DIM]
    values_all = heads_ref[0, :, 2 * HEAD_DIM :]
    probs = softmax(causal_scores(queries, keys_all))
    grad_probs = dot(grad_mixed, values_all, NT)
    grad_values = dot(probs.astype(BF16), grad_mixed, TN)
    inner = jnp.sum(grad_probs * probs, axis=-1, keepdims=True)
    grad_scores = (probs * (grad_probs - inner)).astype(BF16)
    grad_queries = turn(dot(grad_scores, keys_all) * SCALE, tables_ref, -1.0)
    grad_keys = turn(dot(grad_scores, queries, TN) * SCALE, tables_ref, -1.0)
    packed_ref[0, :, :HEAD_DIM] = grad_queries.astype(BF16)
    packed_ref[0, :, HEAD_DIM : 2 * HEAD_DIM] = grad_keys.astype(BF16)
    packed_ref[0, :, 2 * HEAD_DIM :] = grad_values.astype(BF16)
    packed_sum_ref[...] += jnp.sum(packed_ref[0].astype(F32), axis=0, keepdims=True)

    dx_ref[0] = (
        dot(packed_ref[0], qkv_ref[...], NT) * gain_ref[0:1] + dot(up_ref[0], fc1_ref[...], NT) * gain_ref[2:3]
    ).astype(BF16)


def whole(array):
    return pl.BlockSpec(array.shape, lambda i: (0,) * array.ndim, pipeline_mode=pl.Buffered(1))


def blocks(array):
    return pl.BlockSpec((1,) + array.shape[1:], lambda i: (i,) + (0,) * (array.ndim - 1))


def run(kernel, inputs, outputs, flops, name):
    count = inputs[0][0].shape[0]
    shapes = [jax.ShapeDtypeStruct(shape, kind) for shape, kind, _ in outputs]
    moved = sum(a.size * a.dtype.itemsize for a, _ in inputs)
    moved += sum(s.size * s.dtype.itemsize for s in shapes)
    return pl.pallas_call(
        kernel,
        grid=(count,),
        in_specs=[blocks(a) if each else whole(a) for a, each in inputs],
        out_specs=[
            blocks(s) if each else pl.BlockSpec(s.shape, lambda i, n=len(s.shape): (0,) * n)
            for s, (_, _, each) in zip(shapes, outputs)
        ],
        out_shape=shapes,
        compiler_params=pltpu.CompilerParams(vmem_limit_bytes=60 * 2**20),
        cost_estimate=pl.CostEstimate(flops=flops, bytes_accessed=moved, transcendentals=0),
        name=name,
    )(*[a for a, _ in inputs])


def body(
    tokens, ln1_gain, ln1_bias, ln2_gain, ln2_bias, qkv_weight, qkv_bias, out_weight, out_bias,
    fc1_weight, fc1_bias, fc2_weight, fc2_bias, cotangent, extra,
):
    bits = {name: lax.axis_index(name) for name in ("y", "hi", "lo", "x", "c")}
    block_at = (bits["y"] * 2 + bits["lo"]) * 2 + bits["x"]
    vectors = [ln1_gain, ln1_bias, ln2_gain, ln2_bias, out_bias, fc2_bias, qkv_bias, fc1_bias]
    if extra > 1:
        gather = functools.partial(lax.all_gather, axis_name="e", axis=0, tiled=True)
        vectors = [gather(v) for v in vectors]
        qkv_weight, out_weight, fc1_weight, fc2_weight = [
            gather(w) for w in (qkv_weight, out_weight, fc1_weight, fc2_weight)
        ]
    length, width = tokens.shape[1:]
    tables = jnp.asarray(rotary_tables(length))

    small = jnp.concatenate([v.reshape(-1, 128) for v in vectors], axis=0)
    small = gather_small(small, bits).astype(F32)
    unit = ln1_gain.shape[0] * extra // 128
    norm = jnp.stack([small[:, i * unit : (i + 1) * unit].reshape(-1) for i in range(6)])
    shift_rest = norm[4] + norm[5]
    norm = norm[:4]
    qkv_rows = vectors[6].shape[0] // 128
    small_qkv = small[:, 6 * unit : 6 * unit + qkv_rows].reshape(8, 1, -1)
    small_fc1 = small[:, 6 * unit + qkv_rows :].reshape(8, 1, -1)
    qkv_shift, fc1_shift = pick(small_qkv, block_at), pick(small_fc1, block_at)

    x_all = gather_tokens(tokens[0])
    qkv_cols = columns_in(qkv_weight, bits)
    fc1_cols = columns_in(fc1_weight, bits)
    fc2_rows, out_rows = rows_in(fc2_weight, out_weight, bits)
    g_all = gather_tokens(cotangent[0])

    count = x_all.shape[0]
    n_qkv, n_fc1, n_mix = qkv_cols.shape[1], fc1_cols.shape[1], out_rows.shape[0]
    flops = 2 * count * length * width * (n_qkv + n_fc1 + n_fc1 + n_mix)
    a1, a2, heads, mixed, hidden, slope, y_part = run(
        forward_kernel,
        [
            (x_all, True), (norm, False), (qkv_cols, False), (qkv_shift, False), (fc1_cols, False),
            (fc1_shift, False), (fc2_rows, False), (out_rows, False), (tables, False),
        ],
        [
            ((count, length, width), BF16, True),
            ((count, length, width), BF16, True),
            ((count, length, n_qkv), BF16, True),
            ((count, length, n_mix), BF16, True),
            ((count, length, n_fc1), BF16, True),
            ((count, length, n_fc1), F32, True),
            ((count, length, width), BF16, True),
        ],
        flops,
        "forward",
    )
    output = tokens[0].astype(F32) + shift_rest[None] + scatter_tokens(y_part)

    grad_packed, grad_up, dx_part, packed_sum, up_sum = run(
        backward_kernel,
        [
            (g_all, True), (heads, True), (slope, True), (norm, False), (qkv_cols, False), (fc1_cols, False),
            (fc2_rows, False), (out_rows, False), (tables, False),
        ],
        [
            ((count, length, n_qkv), BF16, True),
            ((count, length, n_fc1), BF16, True),
            ((count, length, width), BF16, True),
            ((1, n_qkv), F32, False),
            ((1, n_fc1), F32, False),
        ],
        flops,
        "backward",
    )

    def flat(a):
        return a.reshape(-1, a.shape[-1])

    fc1_part = dot(flat(a2), flat(grad_up), TN)
    qkv_part = dot(flat(a1), flat(grad_packed), TN)
    fc2_part = dot(flat(hidden), flat(g_all), TN).astype(BF16)
    out_part = dot(flat(mixed), flat(g_all), TN).astype(BF16)

    fc2_grad, out_grad = rows_out(fc2_part, out_part, bits)
    fc1_grad = columns_out(fc1_part.astype(BF16), bits)
    qkv_grad = columns_out(qkv_part.astype(BF16), bits)

    def norm_grads(weight, part, sums, gain, bias):
        weight = weight.astype(F32)
        bias_grad = jnp.sum(weight * sums, axis=1)
        return (jnp.sum(weight * part, axis=1) - bias * bias_grad) / gain, bias_grad

    gain1_grad, bias1_grad = norm_grads(qkv_cols, qkv_part, packed_sum, norm[0], norm[1])
    gain2_grad, bias2_grad = norm_grads(fc1_cols, fc1_part, up_sum, norm[2], norm[3])
    column_total = jnp.sum(cotangent[0].astype(F32), axis=0)
    rows = [v.reshape(16, -1, 128) for v in (gain1_grad, bias1_grad, gain2_grad, bias2_grad, column_total)]
    place = (jnp.arange(8) == block_at)[:, None, None]
    rows += [jnp.where(place, v[None], 0.0).reshape(16, -1, 128) for v in (packed_sum, up_sum)]
    small_grads = scatter_small(jnp.concatenate(rows, axis=1), bits)
    cuts = np.cumsum([r.shape[1] for r in rows])[:-1]
    small_grads = [v.reshape(-1) for v in jnp.split(small_grads, cuts, axis=0)]

    inputs = tokens[0].astype(F32)
    centred = inputs - jnp.mean(inputs, axis=-1, keepdims=True)
    scale = lax.rsqrt(jnp.mean(centred * centred, axis=-1, keepdims=True) + EPS)
    normed = centred * scale
    dx = scatter_tokens(dx_part)
    dx = scale * (
        dx - jnp.mean(dx, axis=-1, keepdims=True) - normed * jnp.mean(dx * normed, axis=-1, keepdims=True)
    )
    input_grad = cotangent[0].astype(F32) + dx

    weight_grads = [qkv_grad, out_grad, fc1_grad, fc2_grad]
    if extra > 1:
        scatter = functools.partial(lax.psum_scatter, axis_name="e", scatter_dimension=0, tiled=True)
        weight_grads = [scatter(v) for v in weight_grads]
        small_grads = [scatter(v) for v in small_grads]
    qkv_grad, out_grad, fc1_grad, fc2_grad = weight_grads
    gain1, bias1, gain2, bias2, total, packed_bias, up_bias = small_grads
    return (
        output.astype(BF16)[None],
        input_grad.astype(BF16)[None],
        gain1,
        bias1,
        gain2,
        bias2,
        qkv_grad,
        packed_bias,
        out_grad,
        total,
        fc1_grad,
        up_bias,
        fc2_grad,
        total,
    )


def solution(mesh):
    extra = mesh.shape["shard"] // 16
    axes = ("y", "hi", "lo", "x", "c", "e")
    fine = Mesh(mesh.devices.reshape(2, 2, 2, 2, 2, extra), axes)
    split = P(axes, None, None)
    row, flat = P(axes[1:], None), P(axes[1:])
    in_specs = (split, flat, flat, flat, flat, row, flat, row, flat, row, flat, row, flat, split)
    out_specs = (split, split, flat, flat, flat, flat, row, flat, row, flat, row, flat, row, flat)
    return jax.shard_map(
        functools.partial(body, extra=extra), mesh=fine, in_specs=in_specs, out_specs=out_specs, check_vma=False
    )
```

```python
import functools

import jax
import jax.numpy as jnp
import numpy as np
from jax import lax
from jax.experimental import pallas as pl
from jax.experimental.pallas import tpu as pltpu
from jax.sharding import Mesh
from jax.sharding import PartitionSpec as P

HEADS = 8
HEAD_DIM = 256
ROTARY = 64
EPS = 1e-05
NEG_FILL = -1e30
SCALE = HEAD_DIM ** (-0.5)
BF16 = jnp.bfloat16
F32 = jnp.float32
NT = (((1,), (1,)), ((), ()))
TN = (((0,), (0,)), ((), ()))
NN = (((1,), (0,)), ((), ()))


def dot(a, b, dims=NN):
    return lax.dot_general(a, b, dims, preferred_element_type=F32)


def exch(a, axis):
    return lax.ppermute(a, axis, [(0, 1), (1, 0)])


def pick(a, bit, axis=0):
    return lax.dynamic_index_in_dim(a, bit, axis, keepdims=False)


def ordered(bit, mine, other, axis=0):
    first = jnp.where(bit == 0, mine, other)
    second = jnp.where(bit == 0, other, mine)
    return jnp.stack([first, second], axis)


def add_bf16(a, b):
    return (a.astype(F32) + b.astype(F32)).astype(BF16)


def scatter_tokens(parts):
    _, length, width = parts.shape
    half = length // 2
    parts = parts.reshape(2, 2, 2, length, width)
    one, two = parts[..., :half, :], parts[..., half:, :]
    one = add_bf16(one[0], exch(one[1], "y"))
    two = add_bf16(two[:, 0], exch(two[:, 1], "x"))
    one = add_bf16(one[0], exch(one[1], "x"))
    two = add_bf16(two[0], exch(two[1], "y"))
    both = jnp.concatenate([one, two], axis=1)
    return both[0].astype(F32) + exch(both[1], "lo").astype(F32)


def scatter_small(rows, bits):
    for name in ("hi", "lo", "x", "c"):
        rows = rows.reshape((2, -1) + rows.shape[1:])
        rows = pick(rows, bits[name]) + exch(pick(rows, 1 - bits[name]), name)
    rows = rows[0]
    return rows + exch(rows, "y")


def columns_out(grad, bits):
    width = grad.shape[1]
    grad = grad.reshape(2, 2, 2, 2, -1, width)
    c, hi, lo, x = bits["c"], bits["hi"], bits["lo"], bits["x"]
    part = add_bf16(pick(grad, c, 3), exch(pick(grad, 1 - c, 3), "c"))
    part = add_bf16(pick(part, hi), exch(pick(part, 1 - hi), "hi"))
    part = ordered(lo, pick(part, lo), exch(pick(part, 1 - lo), "lo"))
    part = ordered(x, pick(part, x, 1), exch(pick(part, 1 - x, 1), "x"), axis=1)
    part = ordered(bits["y"], part, exch(part, "y"))
    part = part.reshape((8,) + part.shape[3:])
    return jnp.concatenate([part[i] for i in range(8)], axis=1).astype(F32)


def rows_out(fc2_grad, out_grad, bits):
    width = fc2_grad.shape[1]
    fc2_grad = fc2_grad.reshape(2, -1, width)
    out_grad = out_grad.reshape(2, -1, width)
    c = bits["c"]
    cut = fc2_grad.shape[1]

    def side(at):
        return jnp.concatenate([pick(fc2_grad, at), pick(out_grad, at)], axis=0)

    part = add_bf16(side(c), exch(side(1 - c), "c"))
    half = part.shape[0] // 2
    one, two = part[:half], exch(part[half:], "y")
    holds = bits["hi"] == bits["y"]
    total = add_bf16(jnp.where(holds, one, two), exch(jnp.where(holds, two, one), "hi"))
    other = exch(total, "y")
    first = jnp.where(holds, total, other)
    second = jnp.where(holds, other, total)
    rows = jnp.concatenate([first, second], axis=0).astype(F32)
    return rows[:cut], rows[cut:]


NAMES = ("y", "hi", "lo", "x", "c")
ORDERS = (("lo", "x", "y"), ("lo", "y", "x"))
PLACE = {"lo": 1, "x": 2, "y": 4}


class Copies:
    def __init__(self, at, send_sem, recv_sem, local_sem):
        self.at, self.send_sem, self.recv_sem, self.local_sem = at, send_sem, recv_sem, local_sem
        self.sent, self.planned, self.local = [], 0, 0

    def plan(self, src, dst, axis):
        spot = self.planned
        self.planned += 1
        return pltpu.make_async_remote_copy(
            src_ref=src,
            dst_ref=dst,
            send_sem=self.send_sem.at[spot],
            recv_sem=self.recv_sem.at[spot],
            device_id={axis: 1 - self.at[axis]},
            device_id_type=pl.DeviceIdType.MESH,
        )

    def send(self, src, dst, axis):
        copy = self.plan(src, dst, axis)
        self.sent.append(copy)
        copy.start()
        return copy

    def move(self, src, dst):
        copy = pltpu.make_async_copy(src, dst, self.local_sem.at[self.local])
        self.local += 1
        copy.start()
        return copy


def greet(at, names):
    barrier = pltpu.get_barrier_semaphore()
    for name in names:
        pl.semaphore_signal(
            barrier, inc=1, device_id={name: 1 - at[name]}, device_id_type=pl.DeviceIdType.MESH
        )
    pl.semaphore_wait(barrier, len(names))


class TokenGather:
    def __init__(self, copies, own, full):
        self.copies, self.own, self.full = copies, own, full
        rows = own.shape[0] // len(ORDERS)
        self.chunks = [(pl.ds(i * rows, rows), order) for i, order in enumerate(ORDERS)]
        self.came = {}

    def forward(self, chunk, block, axes):
        rows, _ = self.chunks[chunk]
        src = self.own.at[rows] if block == 0 else self.full.at[block, rows]
        for axis in axes:
            there = block + PLACE[axis]
            self.came[chunk, there] = self.copies.send(src, self.full.at[there, rows], axis)

    def start(self):
        for step in range(3):
            for chunk, (_, order) in enumerate(self.chunks):
                self.forward(chunk, 0, order[step : step + 1])

    def arrive(self, chunk, block):
        self.came[chunk, block].wait_recv()

    def relay_one(self):
        for chunk, (_, order) in enumerate(self.chunks):
            first = PLACE[order[0]]
            self.arrive(chunk, first)
            self.forward(chunk, first, order[1:])

    def relay_two(self):
        for has_first in (0, 1):
            for chunk, (_, order) in enumerate(self.chunks):
                block = PLACE[order[1]] + has_first * PLACE[order[0]]
                self.arrive(chunk, block)
                self.forward(chunk, block, order[2:])

    def finish(self):
        for chunk, (_, order) in enumerate(self.chunks):
            for block in range(8):
                if block & PLACE[order[2]]:
                    self.arrive(chunk, block)


class ColumnGather:
    def __init__(self, copies, weight, full, relay):
        self.copies, self.weight, self.full, self.relay = copies, weight, full, relay
        self.rows, self.width = weight.shape[0], full.shape[1]

    def block(self, lo, x):
        at = (self.copies.at["y"] * 2 + lo) * 2 + x
        return self.weight.at[:, pl.ds(pl.multiple_of(at * self.width, 128), self.width)]

    def place(self, hi, lo, x, c):
        at = ((hi * 2 + lo) * 2 + x) * 2 + c
        return self.full.at[pl.ds(pl.multiple_of(at * self.rows, 128), self.rows)]

    def start(self):
        at, copies = self.copies.at, self.copies
        hi, lo, x, c = (at[n] for n in ("hi", "lo", "x", "c"))
        mine = self.place(hi, lo, x, c)
        self.relayed = copies.send(self.block(1 - lo, 1 - x), self.relay, "x")
        self.from_x = copies.send(self.block(lo, 1 - x), mine, "x")
        self.from_lo = copies.send(self.block(1 - lo, x), mine, "lo")
        self.from_hi = [copies.send(self.block(lo, x), mine, "hi")]
        self.from_c = [copies.send(self.block(lo, x), mine, "c")]
        self.kept = copies.move(self.block(lo, x), mine)

    def onward(self, place, axes):
        for axis in axes:
            copy = self.copies.send(place, place, axis)
            (self.from_hi if axis == "hi" else self.from_c).append(copy)

    def relay_x(self):
        at, copies = self.copies.at, self.copies
        hi, lo, x, c = (at[n] for n in ("hi", "lo", "x", "c"))
        self.relayed.wait_recv()
        self.from_far = copies.send(self.relay, self.place(hi, lo, 1 - x, c), "lo")
        self.from_x.wait_recv()
        self.onward(self.place(hi, lo, 1 - x, c), ("hi", "c"))

    def relay_lo(self):
        at = self.copies.at
        hi, lo, x, c = (at[n] for n in ("hi", "lo", "x", "c"))
        self.from_lo.wait_recv()
        self.onward(self.place(hi, 1 - lo, x, c), ("hi", "c"))
        self.from_far.wait_recv()
        self.onward(self.place(hi, 1 - lo, 1 - x, c), ("hi", "c"))

    def relay_hi(self):
        at = self.copies.at
        hi, lo, x, c = (at[n] for n in ("hi", "lo", "x", "c"))
        places = [(lo, x), (lo, 1 - x), (1 - lo, x), (1 - lo, 1 - x)]
        for copy, (lo_at, x_at) in zip(list(self.from_hi), places):
            copy.wait_recv()
            self.onward(self.place(1 - hi, lo_at, x_at, c), ("c",))

    def finish(self):
        for copy in self.from_c:
            copy.wait_recv()
        self.kept.wait()


class RowGather:
    def __init__(self, copies, weight, full):
        self.copies, self.weight, self.full = copies, weight, full
        self.rows = weight.shape[0]

    def at_row(self, start, count):
        return self.full.at[pl.ds(pl.multiple_of(start, 16), count)]

    def start(self):
        at, copies, rows = self.copies.at, self.copies, self.rows
        half = rows // 2
        self.holds = 1 - (at["hi"] + at["y"]) % 2
        there = self.holds * (at["c"] * rows) + (1 - self.holds) * 2 * rows
        source = pl.multiple_of((1 - self.holds) * half, 16)
        self.from_hi = copies.send(self.weight.at[pl.ds(source, half)], self.at_row(there, half), "hi")
        self.kept = pltpu.make_async_copy(
            self.weight, self.at_row(at["c"] * rows, rows), copies.local_sem.at[copies.local]
        )
        copies.local += 1
        pl.when(self.holds == 1)(self.kept.start)

    def relay_hi(self):
        at, copies, rows = self.copies.at, self.copies, self.rows
        half = rows // 2
        self.from_hi.wait_recv()
        first = self.at_row(at["c"] * rows, half)
        second = self.at_row(at["c"] * rows + half, half)
        self.from_y = copies.plan(self.at_row(2 * rows, half), second, "y")

        @pl.when(self.holds == 1)
        def _():
            self.from_y.start()
            self.kept.wait()

        self.from_c = [copies.send(first, first, "c")]

    def relay_y(self):
        at, copies, rows = self.copies.at, self.copies, self.rows
        second = self.at_row(at["c"] * rows + rows // 2, rows // 2)
        pl.when(self.holds == 0)(self.from_y.wait_recv)
        self.from_c.append(copies.send(second, second, "c"))

    def finish(self):
        for copy in self.from_c:
            copy.wait_recv()
        pl.when(self.holds == 1)(self.from_y.wait_send)


def gather_kernel(
    x_ref, g_ref, small_ref, qkv_ref, fc1_ref, fc2_ref, out_ref,
    x_all, g_all, small_all, qkv_all, fc1_all, fc2_all, out_all,
    relay_qkv, relay_fc1, send_sem, recv_sem, local_sem,
):
    at = {name: lax.axis_index(name) for name in NAMES}
    greet(at, NAMES)
    copies = Copies(at, send_sem, recv_sem, local_sem)
    x_own = copies.move(x_ref, x_all.at[0])
    g_own = copies.move(g_ref, g_all.at[0])

    where = ((at["hi"] * 2 + at["lo"]) * 2 + at["x"]) * 2 + at["c"]
    small_all[pl.ds(where, 1)] = small_ref[...][None]
    count = 1
    base = where
    last = copies.send(small_all.at[pl.ds(base, count)], small_all.at[pl.ds(base, count)], "c")

    qkv = ColumnGather(copies, qkv_ref, qkv_all, relay_qkv)
    fc1 = ColumnGather(copies, fc1_ref, fc1_all, relay_fc1)
    fc2 = RowGather(copies, fc2_ref, fc2_all)
    out = RowGather(copies, out_ref, out_all)
    x = TokenGather(copies, x_ref, x_all)
    g = TokenGather(copies, g_ref, g_all)

    qkv.start()
    fc1.start()
    for axis in ("x", "lo", "hi"):
        last.wait_recv()
        base = base - at[{"x": "c", "lo": "x", "hi": "lo"}[axis]] * count
        count *= 2
        last = copies.send(small_all.at[pl.ds(base, count)], small_all.at[pl.ds(base, count)], axis)
    x.start()
    qkv.relay_x()
    fc1.relay_x()
    qkv.relay_lo()
    fc1.relay_lo()
    x.relay_one()
    fc2.start()
    out.start()
    qkv.relay_hi()
    x.relay_two()
    g.start()
    fc1.relay_hi()
    x.finish()
    g.relay_one()
    fc2.relay_hi()
    out.relay_hi()
    g.relay_two()
    fc2.relay_y()
    out.relay_y()
    g.finish()
    last.wait_recv()
    for part in (qkv, fc1, fc2, out):
        part.finish()
    x_own.wait()
    g_own.wait()
    for copy in copies.sent:
        copy.wait_send()


def gather(tokens, cotangent, small, qkv_weight, fc1_weight, fc2_weight, out_weight):
    def far(array):
        return pl.BlockSpec(memory_space=pl.ANY)

    near = pl.BlockSpec(memory_space=pltpu.VMEM)
    width = tokens.shape[-1]
    rows = qkv_weight.shape[0]
    n_qkv, n_fc1 = qkv_weight.shape[1] // 8, fc1_weight.shape[1] // 8
    outputs = [
        ((8,) + tokens.shape, far),
        ((8,) + tokens.shape, far),
        ((16,) + small.shape, None),
        ((16 * rows, n_qkv), far),
        ((16 * rows, n_fc1), far),
        ((fc2_weight.shape[0] * 5 // 2, width), far),
        ((out_weight.shape[0] * 5 // 2, width), far),
    ]
    count = 4 + 2 * 16 + 2 * 4 + 2 * 7 * len(ORDERS)
    return pl.pallas_call(
        gather_kernel,
        in_specs=[far(None), far(None), near, far(None), far(None), far(None), far(None)],
        out_specs=[near if spec is None else spec(None) for _, spec in outputs],
        out_shape=[jax.ShapeDtypeStruct(shape, BF16) for shape, _ in outputs],
        scratch_shapes=[
            pltpu.VMEM((rows, n_qkv), BF16),
            pltpu.VMEM((rows, n_fc1), BF16),
            pltpu.SemaphoreType.DMA((count,)),
            pltpu.SemaphoreType.DMA((count,)),
            pltpu.SemaphoreType.DMA((8,)),
        ],
        compiler_params=pltpu.CompilerParams(
            collective_id=1, has_side_effects=True, vmem_limit_bytes=16 * 2**20
        ),
        name="gather",
    )(tokens, cotangent, small, qkv_weight, fc1_weight, fc2_weight, out_weight)


def rotary_tables(length):
    places = np.arange(length, dtype=np.float32)
    frequency = (10000.0 ** (-np.arange(0, ROTARY, 2, dtype=np.float32) / ROTARY)).astype(np.float32)
    angles = places[:, None] * frequency[None, :]
    cosine, sine = np.cos(angles), np.sin(angles)
    half = ROTARY // 2
    tables = np.zeros((3, length, HEAD_DIM), np.float32)
    tables[0] = 1.0
    tables[0, :, :half] = cosine
    tables[0, :, half:ROTARY] = cosine
    tables[1, :, :half] = -sine
    tables[2, :, half:ROTARY] = sine
    return tables


def turn(rows, tables, sign):
    half = ROTARY // 2
    ahead = pltpu.roll(rows, HEAD_DIM - half, 1)
    behind = pltpu.roll(rows, half, 1)
    return rows * tables[0] + sign * (ahead * tables[1] + behind * tables[2])


def causal_scores(queries, keys_all):
    length = queries.shape[0]
    scores = dot(queries, keys_all, NT) * SCALE
    row = lax.broadcasted_iota(jnp.int32, (length, length), 0)
    col = lax.broadcasted_iota(jnp.int32, (length, length), 1)
    return jnp.where(row >= col, scores, NEG_FILL)


def softmax(scores):
    raised = jnp.exp(scores - jnp.max(scores, axis=-1, keepdims=True))
    return raised / jnp.sum(raised, axis=-1, keepdims=True)


def forward_kernel(
    x_ref, norm_ref, qkv_ref, qkv_bias_ref, fc1_ref, fc1_bias_ref, fc2_ref, out_ref, tables_ref,
    a1_ref, a2_ref, heads_ref, mixed_ref, hidden_ref, slope_ref, y_ref,
):
    x = x_ref[0].astype(F32)
    centred = x - jnp.mean(x, axis=-1, keepdims=True)
    var = jnp.mean(centred * centred, axis=-1, keepdims=True)
    normed = centred * lax.rsqrt(var + EPS)
    a1_ref[0] = (normed * norm_ref[0:1] + norm_ref[1:2]).astype(BF16)
    a2_ref[0] = (normed * norm_ref[2:3] + norm_ref[3:4]).astype(BF16)

    packed = dot(a1_ref[0], qkv_ref[...]) + qkv_bias_ref[...]
    queries = turn(packed[:, :HEAD_DIM], tables_ref, 1.0).astype(BF16)
    keys_all = turn(packed[:, HEAD_DIM : 2 * HEAD_DIM], tables_ref, 1.0).astype(BF16)
    values_all = packed[:, 2 * HEAD_DIM :].astype(BF16)
    heads_ref[0, :, :HEAD_DIM] = queries
    heads_ref[0, :, HEAD_DIM : 2 * HEAD_DIM] = keys_all
    heads_ref[0, :, 2 * HEAD_DIM :] = values_all
    probs = softmax(causal_scores(queries, keys_all)).astype(BF16)
    mixed_ref[0] = dot(probs, values_all).astype(BF16)

    upward = dot(a2_ref[0], fc1_ref[...]) + fc1_bias_ref[...]
    below = 0.5 * (1.0 + lax.erf(upward * np.float32(0.5**0.5)))
    hidden_ref[0] = (upward * below).astype(BF16)
    slope_ref[0] = below + upward * (jnp.exp(-0.5 * upward * upward) * np.float32((2 * np.pi) ** -0.5))

    y_ref[0] = (dot(hidden_ref[0], fc2_ref[...]) + dot(mixed_ref[0], out_ref[...])).astype(BF16)


def backward_kernel(
    g_ref, heads_ref, slope_ref, gain_ref, qkv_ref, fc1_ref, fc2_ref, out_ref, tables_ref,
    packed_ref, up_ref, dx_ref, packed_sum_ref, up_sum_ref,
):
    @pl.when(pl.program_id(0) == 0)
    def _():
        packed_sum_ref[...] = jnp.zeros_like(packed_sum_ref)
        up_sum_ref[...] = jnp.zeros_like(up_sum_ref)

    grad_up = dot(g_ref[0], fc2_ref[...], NT) * slope_ref[0]
    grad_up = grad_up.astype(BF16)
    up_ref[0] = grad_up
    up_sum_ref[...] += jnp.sum(grad_up.astype(F32), axis=0, keepdims=True)

    grad_mixed = dot(g_ref[0], out_ref[...], NT).astype(BF16)
    queries = heads_ref[0, :, :HEAD_DIM]
    keys_all = heads_ref[0, :, HEAD_DIM : 2 * HEAD_DIM]
    values_all = heads_ref[0, :, 2 * HEAD_DIM :]
    probs = softmax(causal_scores(queries, keys_all))
    grad_probs = dot(grad_mixed, values_all, NT)
    grad_values = dot(probs.astype(BF16), grad_mixed, TN)
    inner = jnp.sum(grad_probs * probs, axis=-1, keepdims=True)
    grad_scores = (probs * (grad_probs - inner)).astype(BF16)
    grad_queries = turn(dot(grad_scores, keys_all) * SCALE, tables_ref, -1.0)
    grad_keys = turn(dot(grad_scores, queries, TN) * SCALE, tables_ref, -1.0)
    packed_ref[0, :, :HEAD_DIM] = grad_queries.astype(BF16)
    packed_ref[0, :, HEAD_DIM : 2 * HEAD_DIM] = grad_keys.astype(BF16)
    packed_ref[0, :, 2 * HEAD_DIM :] = grad_values.astype(BF16)
    packed_sum_ref[...] += jnp.sum(packed_ref[0].astype(F32), axis=0, keepdims=True)

    dx_ref[0] = (
        dot(packed_ref[0], qkv_ref[...], NT) * gain_ref[0:1] + dot(up_ref[0], fc1_ref[...], NT) * gain_ref[2:3]
    ).astype(BF16)


def whole(array, rows=None):
    shape = (rows or array.shape[0],) + array.shape[1:]
    return pl.BlockSpec(shape, lambda i: (0,) * array.ndim, pipeline_mode=pl.Buffered(1))


def blocks(array):
    return pl.BlockSpec((1,) + array.shape[1:], lambda i: (i,) + (0,) * (array.ndim - 1))


def run(kernel, inputs, outputs, flops, name):
    count = inputs[0][0].shape[0]
    shapes = [jax.ShapeDtypeStruct(shape, kind) for shape, kind, _ in outputs]
    moved = sum(a.size * a.dtype.itemsize for a, _ in inputs)
    moved += sum(s.size * s.dtype.itemsize for s in shapes)
    return pl.pallas_call(
        kernel,
        grid=(count,),
        in_specs=[blocks(a) if each is True else whole(a, each) for a, each in inputs],
        out_specs=[
            blocks(s) if each else pl.BlockSpec(s.shape, lambda i, n=len(s.shape): (0,) * n)
            for s, (_, _, each) in zip(shapes, outputs)
        ],
        out_shape=shapes,
        compiler_params=pltpu.CompilerParams(vmem_limit_bytes=60 * 2**20),
        cost_estimate=pl.CostEstimate(flops=flops, bytes_accessed=moved, transcendentals=0),
        name=name,
    )(*[a for a, _ in inputs])


def body(
    tokens, ln1_gain, ln1_bias, ln2_gain, ln2_bias, qkv_weight, qkv_bias, out_weight, out_bias,
    fc1_weight, fc1_bias, fc2_weight, fc2_bias, cotangent, extra,
):
    bits = {name: lax.axis_index(name) for name in ("y", "hi", "lo", "x", "c")}
    block_at = (bits["y"] * 2 + bits["lo"]) * 2 + bits["x"]
    vectors = [ln1_gain, ln1_bias, ln2_gain, ln2_bias, out_bias, fc2_bias, qkv_bias, fc1_bias]
    if extra > 1:
        join = functools.partial(lax.all_gather, axis_name="e", axis=0, tiled=True)
        vectors = [join(v) for v in vectors]
        qkv_weight, out_weight, fc1_weight, fc2_weight = [
            join(w) for w in (qkv_weight, out_weight, fc1_weight, fc2_weight)
        ]
    length, width = tokens.shape[1:]
    tables = jnp.asarray(rotary_tables(length))

    small = jnp.concatenate([v.reshape(-1, 128) for v in vectors], axis=0)
    small = jnp.pad(small, ((0, -small.shape[0] % 16), (0, 0)))
    x_all, g_all, small, qkv_cols, fc1_cols, fc2_rows, out_rows = gather(
        tokens[0], cotangent[0], small, qkv_weight, fc1_weight, fc2_weight, out_weight
    )
    small = small.astype(F32)
    unit = ln1_gain.shape[0] * extra // 128
    norm = jnp.stack([small[:, i * unit : (i + 1) * unit].reshape(-1) for i in range(6)])
    shift_rest = norm[4] + norm[5]
    norm = norm[:4]
    qkv_rows = vectors[6].shape[0] // 128
    small_qkv = small[:, 6 * unit : 6 * unit + qkv_rows].reshape(8, 1, -1)
    fc1_rows = vectors[7].shape[0] // 128
    small_fc1 = small[:, 6 * unit + qkv_rows : 6 * unit + qkv_rows + fc1_rows].reshape(8, 1, -1)
    qkv_shift, fc1_shift = pick(small_qkv, block_at), pick(small_fc1, block_at)

    count = x_all.shape[0]
    n_qkv, n_fc1, n_mix = qkv_cols.shape[1], fc1_cols.shape[1], out_weight.shape[0] * 2
    flops = 2 * count * length * width * (n_qkv + n_fc1 + n_fc1 + n_mix)
    a1, a2, heads, mixed, hidden, slope, y_part = run(
        forward_kernel,
        [
            (x_all, True), (norm, None), (qkv_cols, None), (qkv_shift, None), (fc1_cols, None),
            (fc1_shift, None), (fc2_rows, n_fc1), (out_rows, n_mix), (tables, None),
        ],
        [
            ((count, length, width), BF16, True),
            ((count, length, width), BF16, True),
            ((count, length, n_qkv), BF16, True),
            ((count, length, n_mix), BF16, True),
            ((count, length, n_fc1), BF16, True),
            ((count, length, n_fc1), F32, True),
            ((count, length, width), BF16, True),
        ],
        flops,
        "forward",
    )
    output = tokens[0].astype(F32) + shift_rest[None] + scatter_tokens(y_part)

    grad_packed, grad_up, dx_part, packed_sum, up_sum = run(
        backward_kernel,
        [
            (g_all, True), (heads, True), (slope, True), (norm, None), (qkv_cols, None), (fc1_cols, None),
            (fc2_rows, n_fc1), (out_rows, n_mix), (tables, None),
        ],
        [
            ((count, length, n_qkv), BF16, True),
            ((count, length, n_fc1), BF16, True),
            ((count, length, width), BF16, True),
            ((1, n_qkv), F32, False),
            ((1, n_fc1), F32, False),
        ],
        flops,
        "backward",
    )

    def flat(a):
        return a.reshape(-1, a.shape[-1])

    fc1_part = dot(flat(a2), flat(grad_up), TN)
    qkv_part = dot(flat(a1), flat(grad_packed), TN)
    fc2_part = dot(flat(hidden), flat(g_all), TN).astype(BF16)
    out_part = dot(flat(mixed), flat(g_all), TN).astype(BF16)

    fc2_grad, out_grad = rows_out(fc2_part, out_part, bits)
    fc1_grad = columns_out(fc1_part.astype(BF16), bits)
    qkv_grad = columns_out(qkv_part.astype(BF16), bits)

    def norm_grads(weight, part, sums, gain, bias):
        weight = weight.astype(F32)
        bias_grad = jnp.sum(weight * sums, axis=1)
        return (jnp.sum(weight * part, axis=1) - bias * bias_grad) / gain, bias_grad

    gain1_grad, bias1_grad = norm_grads(qkv_cols, qkv_part, packed_sum, norm[0], norm[1])
    gain2_grad, bias2_grad = norm_grads(fc1_cols, fc1_part, up_sum, norm[2], norm[3])
    column_total = jnp.sum(cotangent[0].astype(F32), axis=0)
    rows = [v.reshape(16, -1, 128) for v in (gain1_grad, bias1_grad, gain2_grad, bias2_grad, column_total)]
    place = (jnp.arange(8) == block_at)[:, None, None]
    rows += [jnp.where(place, v[None], 0.0).reshape(16, -1, 128) for v in (packed_sum, up_sum)]
    small_grads = scatter_small(jnp.concatenate(rows, axis=1), bits)
    cuts = np.cumsum([r.shape[1] for r in rows])[:-1]
    small_grads = [v.reshape(-1) for v in jnp.split(small_grads, cuts, axis=0)]

    inputs = tokens[0].astype(F32)
    centred = inputs - jnp.mean(inputs, axis=-1, keepdims=True)
    scale = lax.rsqrt(jnp.mean(centred * centred, axis=-1, keepdims=True) + EPS)
    normed = centred * scale
    dx = scatter_tokens(dx_part)
    dx = scale * (
        dx - jnp.mean(dx, axis=-1, keepdims=True) - normed * jnp.mean(dx * normed, axis=-1, keepdims=True)
    )
    input_grad = cotangent[0].astype(F32) + dx

    weight_grads = [qkv_grad, out_grad, fc1_grad, fc2_grad]
    if extra > 1:
        scatter = functools.partial(lax.psum_scatter, axis_name="e", scatter_dimension=0, tiled=True)
        weight_grads = [scatter(v) for v in weight_grads]
        small_grads = [scatter(v) for v in small_grads]
    qkv_grad, out_grad, fc1_grad, fc2_grad = weight_grads
    gain1, bias1, gain2, bias2, total, packed_bias, up_bias = small_grads
    return (
        output.astype(BF16)[None],
        input_grad.astype(BF16)[None],
        gain1,
        bias1,
        gain2,
        bias2,
        qkv_grad,
        packed_bias,
        out_grad,
        total,
        fc1_grad,
        up_bias,
        fc2_grad,
        total,
    )


def solution(mesh):
    extra = mesh.shape["shard"] // 16
    axes = ("y", "hi", "lo", "x", "c", "e")
    fine = Mesh(mesh.devices.reshape(2, 2, 2, 2, 2, extra), axes)
    split = P(axes, None, None)
    row, flat = P(axes[1:], None), P(axes[1:])
    in_specs = (split, flat, flat, flat, flat, row, flat, row, flat, row, flat, row, flat, split)
    out_specs = (split, split, flat, flat, flat, flat, row, flat, row, flat, row, flat, row, flat)
    return jax.shard_map(
        functools.partial(body, extra=extra), mesh=fine, in_specs=in_specs, out_specs=out_specs, check_vma=False
    )
```

```python
import functools

import jax
import jax.numpy as jnp
import numpy as np
from jax import lax
from jax.experimental import pallas as pl
from jax.experimental.pallas import tpu as pltpu
from jax.sharding import Mesh
from jax.sharding import PartitionSpec as P

HEADS = 8
HEAD_DIM = 256
ROTARY = 64
EPS = 1e-05
NEG_FILL = -1e30
SCALE = HEAD_DIM ** (-0.5)
BF16 = jnp.bfloat16
F32 = jnp.float32
NT = (((1,), (1,)), ((), ()))
TN = (((0,), (0,)), ((), ()))
NN = (((1,), (0,)), ((), ()))


def dot(a, b, dims=NN):
    return lax.dot_general(a, b, dims, preferred_element_type=F32)


def exch(a, axis):
    return lax.ppermute(a, axis, [(0, 1), (1, 0)])


def pick(a, bit, axis=0):
    return lax.dynamic_index_in_dim(a, bit, axis, keepdims=False)


def ordered(bit, mine, other, axis=0):
    first = jnp.where(bit == 0, mine, other)
    second = jnp.where(bit == 0, other, mine)
    return jnp.stack([first, second], axis)


def add_bf16(a, b):
    return (a.astype(F32) + b.astype(F32)).astype(BF16)


def scatter_tokens(parts):
    _, length, width = parts.shape
    half = length // 2
    parts = parts.reshape(2, 2, 2, length, width)
    one, two = parts[..., :half, :], parts[..., half:, :]
    one = add_bf16(one[0], exch(one[1], "y"))
    two = add_bf16(two[:, 0], exch(two[:, 1], "x"))
    one = add_bf16(one[0], exch(one[1], "x"))
    two = add_bf16(two[0], exch(two[1], "y"))
    both = jnp.concatenate([one, two], axis=1)
    return both[0].astype(F32) + exch(both[1], "lo").astype(F32)


def scatter_small(rows, bits):
    for name in ("hi", "lo", "x", "c"):
        rows = rows.reshape((2, -1) + rows.shape[1:])
        rows = pick(rows, bits[name]) + exch(pick(rows, 1 - bits[name]), name)
    rows = rows[0]
    return rows + exch(rows, "y")


def columns_out(grad, bits):
    width = grad.shape[1]
    grad = grad.reshape(2, 2, 2, 2, -1, width)
    c, hi, lo, x = bits["c"], bits["hi"], bits["lo"], bits["x"]
    part = add_bf16(pick(grad, c, 3), exch(pick(grad, 1 - c, 3), "c"))
    part = add_bf16(pick(part, hi), exch(pick(part, 1 - hi), "hi"))
    part = ordered(lo, pick(part, lo), exch(pick(part, 1 - lo), "lo"))
    part = ordered(x, pick(part, x, 1), exch(pick(part, 1 - x, 1), "x"), axis=1)
    part = ordered(bits["y"], part, exch(part, "y"))
    part = part.reshape((8,) + part.shape[3:])
    return jnp.concatenate([part[i] for i in range(8)], axis=1).astype(F32)


def rows_out(fc2_grad, out_grad, bits):
    width = fc2_grad.shape[1]
    fc2_grad = fc2_grad.reshape(2, -1, width)
    out_grad = out_grad.reshape(2, -1, width)
    c = bits["c"]
    cut = fc2_grad.shape[1]

    def side(at):
        return jnp.concatenate([pick(fc2_grad, at), pick(out_grad, at)], axis=0)

    part = add_bf16(side(c), exch(side(1 - c), "c"))
    half = part.shape[0] // 2
    one, two = part[:half], exch(part[half:], "y")
    holds = bits["hi"] == bits["y"]
    total = add_bf16(jnp.where(holds, one, two), exch(jnp.where(holds, two, one), "hi"))
    other = exch(total, "y")
    first = jnp.where(holds, total, other)
    second = jnp.where(holds, other, total)
    rows = jnp.concatenate([first, second], axis=0).astype(F32)
    return rows[:cut], rows[cut:]


NAMES = ("y", "hi", "lo", "x", "c")
ORDERS = (("lo", "x", "y"), ("lo", "y", "x"), ("y", "x", "lo"))
PLACE = {"lo": 1, "x": 2, "y": 4}


def row_chunks(length):
    last = length // 96 * 16
    first = (length - last + 31) // 32 * 16
    return ((0, first), (first, length - last - first), (length - last, last))


class Copies:
    def __init__(self, at, send_sem, recv_sem, local_sem):
        self.at, self.send_sem, self.recv_sem, self.local_sem = at, send_sem, recv_sem, local_sem
        self.remote, self.planned, self.local = [], 0, 0

    def plan(self, src, dst, axis, everywhere=True):
        spot = self.planned
        self.planned += 1
        copy = pltpu.make_async_remote_copy(
            src_ref=src,
            dst_ref=dst,
            send_sem=self.send_sem.at[spot],
            recv_sem=self.recv_sem.at[spot],
            device_id={axis: 1 - self.at[axis]},
            device_id_type=pl.DeviceIdType.MESH,
        )
        if everywhere:
            self.remote.append(copy)
        return copy

    def move(self, src, dst):
        copy = pltpu.make_async_copy(src, dst, self.local_sem.at[self.local])
        self.local += 1
        return copy


def greet(at, names):
    barrier = pltpu.get_barrier_semaphore()
    for name in names:
        pl.semaphore_signal(
            barrier, inc=1, device_id={name: 1 - at[name]}, device_id_type=pl.DeviceIdType.MESH
        )
    pl.semaphore_wait(barrier, len(names))


class TokenGather:
    def __init__(self, copies, own, full):
        rows = row_chunks(own.shape[0])
        self.plans, self.unseen = {}, set()
        self.kept = copies.move(own, full.at[0])
        for chunk, order in enumerate(ORDERS):
            part = pl.ds(*rows[chunk])
            for step, axis in enumerate(order):
                for block in range(8):
                    if all(block & PLACE[later] == 0 for later in order[step:]):
                        src = own.at[part] if block == 0 else full.at[block, part]
                        there = full.at[block + PLACE[axis], part]
                        self.plans[chunk, block + PLACE[axis]] = copies.plan(src, there, axis)
                        self.unseen.add((chunk, block + PLACE[axis]))

    def send(self, chunk, block, axis):
        self.plans[chunk, block + PLACE[axis]].start()

    def arrive(self, chunk, block):
        if (chunk, block) in self.unseen:
            self.unseen.remove((chunk, block))
            self.plans[chunk, block].wait_recv()

    def start(self):
        self.kept.start()
        for step in range(3):
            for chunk, order in enumerate(ORDERS):
                self.send(chunk, 0, order[step])

    def relay_one(self):
        for chunk, order in enumerate(ORDERS):
            self.arrive(chunk, PLACE[order[0]])
            self.send(chunk, PLACE[order[0]], order[1])
            self.send(chunk, PLACE[order[0]], order[2])

    def relay_two(self):
        for has_first in (0, 1):
            for chunk, order in enumerate(ORDERS):
                block = PLACE[order[1]] + has_first * PLACE[order[0]]
                self.arrive(chunk, block)
                self.send(chunk, block, order[2])

    def take(self, block):
        for chunk in range(len(ORDERS)):
            self.arrive(chunk, block)

    def finish(self):
        for block in range(8):
            self.take(block)
        self.kept.wait()


class ColumnGather:
    def __init__(self, copies, weight, full, relay):
        at = copies.at
        hi, lo, x, c = (at[n] for n in ("hi", "lo", "x", "c"))
        rows, width = weight.shape[0], full.shape[1]

        def block(lo_at, x_at):
            spot = (at["y"] * 2 + lo_at) * 2 + x_at
            return weight.at[:, pl.ds(pl.multiple_of(spot * width, 128), width)]

        def place(hi_at, lo_at, x_at):
            spot = ((hi_at * 2 + lo_at) * 2 + x_at) * 2 + c
            return full.at[pl.ds(pl.multiple_of(spot * rows, 128), rows)]

        mine = place(hi, lo, x)
        self.by_x = [copies.plan(block(1 - lo, 1 - x), relay, "x"), copies.plan(block(lo, 1 - x), mine, "x")]
        self.by_lo = [
            copies.plan(block(1 - lo, x), mine, "lo"),
            copies.plan(relay, place(hi, lo, 1 - x), "lo"),
        ]
        near = [place(hi, lo, x), place(hi, lo, 1 - x), place(hi, 1 - lo, x), place(hi, 1 - lo, 1 - x)]
        far = [place(1 - hi, lo, x), place(1 - hi, lo, 1 - x), place(1 - hi, 1 - lo, x), place(1 - hi, 1 - lo, 1 - x)]
        source = [block(lo, x)] + near[1:]
        self.by_hi = [copies.plan(src, dst, "hi") for src, dst in zip(source, near)]
        self.by_c = [copies.plan(src, dst, "c") for src, dst in zip(source + far, near + far)]
        self.kept = copies.move(block(lo, x), mine)

    def start(self):
        for copy in self.by_x + self.by_lo[:1] + self.by_hi[:1] + self.by_c[:1] + [self.kept]:
            copy.start()

    def relay_x(self):
        self.by_x[0].wait_recv()
        self.by_lo[1].start()
        self.by_x[1].wait_recv()
        self.by_hi[1].start()
        self.by_c[1].start()

    def relay_lo(self):
        for i in (0, 1):
            self.by_lo[i].wait_recv()
            self.by_hi[2 + i].start()
            self.by_c[2 + i].start()

    def relay_hi(self):
        for i in range(4):
            self.by_hi[i].wait_recv()
            self.by_c[4 + i].start()

    def finish(self):
        for copy in self.by_c:
            copy.wait_recv()
        self.kept.wait()


class RowGather:
    def __init__(self, copies, weight, full):
        at, rows = copies.at, weight.shape[0]
        half = rows // 2

        def spot(start, count):
            return full.at[pl.ds(pl.multiple_of(start, 16), count)]

        self.copies = copies
        self.holds = 1 - (at["hi"] + at["y"]) % 2
        first, second = spot(at["c"] * rows, half), spot(at["c"] * rows + half, half)
        there = spot(self.holds * (at["c"] * rows) + (1 - self.holds) * 2 * rows, half)
        source = weight.at[pl.ds(pl.multiple_of((1 - self.holds) * half, 16), half)]
        self.by_hi = copies.plan(source, there, "hi")
        self.by_y = copies.plan(spot(2 * rows, half), second, "y", everywhere=False)
        self.by_c = [copies.plan(first, first, "c"), copies.plan(second, second, "c")]
        self.kept = copies.move(weight, spot(at["c"] * rows, rows))

    def start(self):
        self.by_hi.start()
        pl.when(self.holds == 1)(self.kept.start)

    def relay_hi(self):
        self.by_hi.wait_recv()

        @pl.when(self.holds == 1)
        def _():
            self.by_y.start()
            self.kept.wait()

        self.by_c[0].start()

    def relay_y(self):
        pl.when(self.holds == 0)(self.by_y.wait_recv)
        self.by_c[1].start()

    def finish(self):
        for copy in self.by_c:
            copy.wait_recv()

    def sent(self):
        pl.when(self.holds == 1)(self.by_y.wait_send)


class SmallGather:
    def __init__(self, copies, full):
        at = copies.at
        base = ((at["hi"] * 2 + at["lo"]) * 2 + at["x"]) * 2 + at["c"]
        self.own = full.at[pl.ds(base, 1)]
        self.steps, count = [], 1
        for name in ("c", "x", "lo", "hi"):
            part = full.at[pl.ds(base, count)]
            self.steps.append(copies.plan(part, part, name))
            base = base - at[name] * count
            count *= 2

    def start(self):
        self.steps[0].start()

    def step(self, at):
        self.steps[at - 1].wait_recv()
        if at < 4:
            self.steps[at].start()


def rotary_tables(length):
    places = np.arange(length, dtype=np.float32)
    frequency = (10000.0 ** (-np.arange(0, ROTARY, 2, dtype=np.float32) / ROTARY)).astype(np.float32)
    angles = places[:, None] * frequency[None, :]
    cosine, sine = np.cos(angles), np.sin(angles)
    half = ROTARY // 2
    tables = np.zeros((3, length, HEAD_DIM), np.float32)
    tables[0] = 1.0
    tables[0, :, :half] = cosine
    tables[0, :, half:ROTARY] = cosine
    tables[1, :, :half] = -sine
    tables[2, :, half:ROTARY] = sine
    return tables


def turn(rows, tables, sign):
    half = ROTARY // 2
    ahead = pltpu.roll(rows, HEAD_DIM - half, 1)
    behind = pltpu.roll(rows, half, 1)
    return rows * tables[0] + sign * (ahead * tables[1] + behind * tables[2])


def causal_scores(queries, keys_all):
    length = queries.shape[0]
    scores = dot(queries, keys_all, NT) * SCALE
    row = lax.broadcasted_iota(jnp.int32, (length, length), 0)
    col = lax.broadcasted_iota(jnp.int32, (length, length), 1)
    return jnp.where(row >= col, scores, NEG_FILL)


def softmax(scores):
    raised = jnp.exp(scores - jnp.max(scores, axis=-1, keepdims=True))
    return raised / jnp.sum(raised, axis=-1, keepdims=True)


def forward_kernel(
    x_ref, g_ref, small_ref, qkv_ref, fc1_ref, fc2_ref, out_ref, tables_ref,
    g_all, small_out, qkv_out, fc1_out, fc2_out, out_out,
    a1_ref, a2_ref, heads_ref, mixed_ref, hidden_ref, slope_ref, y_ref,
    x_all, small_all, qkv_all, fc1_all, fc2_all, out_all, norm, qkv_bias, fc1_bias, mixed_all, hidden_all,
    relay_qkv, relay_fc1, send_sem, recv_sem, local_sem,
):
    step = pl.program_id(0)
    at = {name: lax.axis_index(name) for name in NAMES}
    copies = Copies(at, send_sem, recv_sem, local_sem)
    small = SmallGather(copies, small_all)
    qkv = ColumnGather(copies, qkv_ref, qkv_all, relay_qkv)
    fc1 = ColumnGather(copies, fc1_ref, fc1_all, relay_fc1)
    fc2 = RowGather(copies, fc2_ref, fc2_all)
    out = RowGather(copies, out_ref, out_all)
    x = TokenGather(copies, x_ref, x_all)
    g = TokenGather(copies, g_ref, g_all)
    kept = [
        copies.move(src.at[pl.ds(0, dst.shape[0])], dst)
        for src, dst in ((qkv_all, qkv_out), (fc1_all, fc1_out), (fc2_all, fc2_out), (out_all, out_out))
    ]

    @pl.when(step == 0)
    def _():
        greet(at, NAMES)
        small.own[...] = small_ref[...][None]
        small.start()
        qkv.start()
        fc1.start()
        x.start()
        small.step(1)
        small.step(2)
        qkv.relay_x()
        small.step(3)
        fc1.relay_x()
        qkv.relay_lo()
        x.relay_one()
        fc1.relay_lo()
        small.step(4)
        for spot in range(16):
            norm[:, spot * 128 : (spot + 1) * 128] = small_all[spot, :8].astype(F32)
        first = (at["y"] * 4 + at["lo"] * 2 + at["x"]) * 2
        for half in range(2):
            own = small_all[first + half].astype(F32)
            for bias, start in ((qkv_bias, 6), (fc1_bias, 6 + qkv_bias.shape[1] // 256)):
                rows = bias.shape[1] // 256
                for i in range(rows):
                    bias[:, (half * rows + i) * 128 : (half * rows + i + 1) * 128] = own[start + i : start + i + 1]
        qkv.relay_hi()
        x.relay_two()
        g.start()
        g.relay_one()
        fc2.start()
        out.start()
        fc1.relay_hi()
        x.kept.wait()
        qkv.finish()
        fc1.finish()
        kept[0].start()
        kept[1].start()

    for block in range(1, 8):
        pl.when(step == block)(functools.partial(x.take, block))

    @pl.when(step == 4)
    def _():
        g.relay_two()
        fc2.relay_hi()
        out.relay_hi()

    @pl.when(step < 8)
    def _():
        value = x_all[step].astype(F32)
        centred = value - jnp.mean(value, axis=-1, keepdims=True)
        var = jnp.mean(centred * centred, axis=-1, keepdims=True)
        normed = centred * lax.rsqrt(var + EPS)
        a1_ref[0] = (normed * norm[0:1] + norm[1:2]).astype(BF16)
        a2_ref[0] = (normed * norm[2:3] + norm[3:4]).astype(BF16)

        packed = dot(a1_ref[0], qkv_all[...]) + qkv_bias[...]
        queries = turn(packed[:, :HEAD_DIM], tables_ref, 1.0).astype(BF16)
        keys_all = turn(packed[:, HEAD_DIM : 2 * HEAD_DIM], tables_ref, 1.0).astype(BF16)
        values_all = packed[:, 2 * HEAD_DIM :].astype(BF16)
        heads_ref[0, :, :HEAD_DIM] = queries
        heads_ref[0, :, HEAD_DIM : 2 * HEAD_DIM] = keys_all
        heads_ref[0, :, 2 * HEAD_DIM :] = values_all
        probs = softmax(causal_scores(queries, keys_all)).astype(BF16)
        mixed_ref[0] = dot(probs, values_all).astype(BF16)
        mixed_all[step] = mixed_ref[0]

        upward = dot(a2_ref[0], fc1_all[...]) + fc1_bias[...]
        below = 0.5 * (1.0 + lax.erf(upward * np.float32(0.5**0.5)))
        hidden_ref[0] = (upward * below).astype(BF16)
        hidden_all[step] = hidden_ref[0]
        slope_ref[0] = below + upward * (jnp.exp(-0.5 * upward * upward) * np.float32((2 * np.pi) ** -0.5))

    @pl.when(step == 8)
    def _():
        fc2.relay_y()
        out.relay_y()
        fc2.finish()
        out.finish()
        kept[2].start()
        kept[3].start()

    @pl.when(step >= 8)
    def _():
        y = dot(hidden_all[step - 8], fc2_all[: hidden_ref.shape[2]])
        y_ref[0] = (y + dot(mixed_all[step - 8], out_all[: mixed_ref.shape[2]])).astype(BF16)

    @pl.when(step == 15)
    def _():
        small_out[...] = small_all[...]
        g.finish()
        for copy in kept:
            copy.wait()
        for copy in copies.remote:
            copy.wait_send()
        fc2.sent()
        out.sent()


def forward(tokens, cotangent, small, qkv_weight, fc1_weight, fc2_weight, out_weight, tables):
    far = pl.BlockSpec(memory_space=pl.ANY)
    length, width = tokens.shape
    rows = qkv_weight.shape[0]
    n_qkv, n_fc1, n_mix = qkv_weight.shape[1] // 8, fc1_weight.shape[1] // 8, out_weight.shape[0] * 2
    each = [(width, BF16), (width, BF16), (n_qkv, BF16), (n_mix, BF16), (n_fc1, BF16), (n_fc1, F32), (width, BF16)]
    count = 4 + 2 * 16 + 2 * 4 + 2 * 7 * len(ORDERS)
    weights = [(16 * rows, n_qkv), (16 * rows, n_fc1), (n_fc1, width), (n_mix, width)]
    flops = 2 * 8 * length * width * (n_qkv + n_fc1 + n_fc1 + n_mix)
    return pl.pallas_call(
        forward_kernel,
        grid=(16,),
        in_specs=[far, far, whole(small), far, far, far, far, whole(tables)],
        out_specs=[far, whole(jax.ShapeDtypeStruct((16,) + small.shape, BF16)), far, far, far, far]
        + [pl.BlockSpec((1, length, n), lambda i: (jnp.minimum(i, 7), 0, 0)) for n, _ in each[:-1]]
        + [pl.BlockSpec((1, length, width), lambda i: (jnp.maximum(i - 8, 0), 0, 0))],
        out_shape=[
            jax.ShapeDtypeStruct((8, length, width), BF16),
            jax.ShapeDtypeStruct((16,) + small.shape, BF16),
        ]
        + [jax.ShapeDtypeStruct(shape, BF16) for shape in weights]
        + [jax.ShapeDtypeStruct((8, length, n), kind) for n, kind in each],
        scratch_shapes=[
            pltpu.VMEM((8, length, width), BF16),
            pltpu.VMEM((16,) + small.shape, BF16),
            pltpu.VMEM(weights[0], BF16),
            pltpu.VMEM(weights[1], BF16),
            pltpu.VMEM((n_fc1 * 5 // 4, width), BF16),
            pltpu.VMEM((n_mix * 5 // 4, width), BF16),
            pltpu.VMEM((8, width), F32),
            pltpu.VMEM((1, n_qkv), F32),
            pltpu.VMEM((1, n_fc1), F32),
            pltpu.VMEM((8, length, n_mix), BF16),
            pltpu.VMEM((8, length, n_fc1), BF16),
            pltpu.VMEM((rows, n_qkv), BF16),
            pltpu.VMEM((rows, n_fc1), BF16),
            pltpu.SemaphoreType.DMA((count,)),
            pltpu.SemaphoreType.DMA((count,)),
            pltpu.SemaphoreType.DMA((10,)),
        ],
        compiler_params=pltpu.CompilerParams(
            collective_id=1, has_side_effects=True, vmem_limit_bytes=60 * 2**20
        ),
        cost_estimate=pl.CostEstimate(flops=flops, bytes_accessed=10**8, transcendentals=0),
        name="forward",
    )(tokens, cotangent, small, qkv_weight, fc1_weight, fc2_weight, out_weight, tables)


def backward_kernel(
    g_ref, heads_ref, slope_ref, gain_ref, qkv_ref, fc1_ref, fc2_ref, out_ref, tables_ref,
    packed_ref, up_ref, dx_ref, packed_sum_ref, up_sum_ref,
):
    @pl.when(pl.program_id(0) == 0)
    def _():
        packed_sum_ref[...] = jnp.zeros_like(packed_sum_ref)
        up_sum_ref[...] = jnp.zeros_like(up_sum_ref)

    grad_up = dot(g_ref[0], fc2_ref[...], NT) * slope_ref[0]
    grad_up = grad_up.astype(BF16)
    up_ref[0] = grad_up
    up_sum_ref[...] += jnp.sum(grad_up.astype(F32), axis=0, keepdims=True)

    grad_mixed = dot(g_ref[0], out_ref[...], NT).astype(BF16)
    queries = heads_ref[0, :, :HEAD_DIM]
    keys_all = heads_ref[0, :, HEAD_DIM : 2 * HEAD_DIM]
    values_all = heads_ref[0, :, 2 * HEAD_DIM :]
    probs = softmax(causal_scores(queries, keys_all))
    grad_probs = dot(grad_mixed, values_all, NT)
    grad_values = dot(probs.astype(BF16), grad_mixed, TN)
    inner = jnp.sum(grad_probs * probs, axis=-1, keepdims=True)
    grad_scores = (probs * (grad_probs - inner)).astype(BF16)
    grad_queries = turn(dot(grad_scores, keys_all) * SCALE, tables_ref, -1.0)
    grad_keys = turn(dot(grad_scores, queries, TN) * SCALE, tables_ref, -1.0)
    packed_ref[0, :, :HEAD_DIM] = grad_queries.astype(BF16)
    packed_ref[0, :, HEAD_DIM : 2 * HEAD_DIM] = grad_keys.astype(BF16)
    packed_ref[0, :, 2 * HEAD_DIM :] = grad_values.astype(BF16)
    packed_sum_ref[...] += jnp.sum(packed_ref[0].astype(F32), axis=0, keepdims=True)

    dx_ref[0] = (
        dot(packed_ref[0], qkv_ref[...], NT) * gain_ref[0:1] + dot(up_ref[0], fc1_ref[...], NT) * gain_ref[2:3]
    ).astype(BF16)


def whole(array, rows=None):
    shape = (rows or array.shape[0],) + array.shape[1:]
    return pl.BlockSpec(shape, lambda i: (0,) * array.ndim, pipeline_mode=pl.Buffered(1))


def blocks(array):
    return pl.BlockSpec((1,) + array.shape[1:], lambda i: (i,) + (0,) * (array.ndim - 1))


def run(kernel, inputs, outputs, flops, name):
    count = inputs[0][0].shape[0]
    shapes = [jax.ShapeDtypeStruct(shape, kind) for shape, kind, _ in outputs]
    moved = sum(a.size * a.dtype.itemsize for a, _ in inputs)
    moved += sum(s.size * s.dtype.itemsize for s in shapes)
    return pl.pallas_call(
        kernel,
        grid=(count,),
        in_specs=[blocks(a) if each is True else whole(a, each) for a, each in inputs],
        out_specs=[
            blocks(s) if each else pl.BlockSpec(s.shape, lambda i, n=len(s.shape): (0,) * n)
            for s, (_, _, each) in zip(shapes, outputs)
        ],
        out_shape=shapes,
        compiler_params=pltpu.CompilerParams(vmem_limit_bytes=60 * 2**20),
        cost_estimate=pl.CostEstimate(flops=flops, bytes_accessed=moved, transcendentals=0),
        name=name,
    )(*[a for a, _ in inputs])


def body(
    tokens, ln1_gain, ln1_bias, ln2_gain, ln2_bias, qkv_weight, qkv_bias, out_weight, out_bias,
    fc1_weight, fc1_bias, fc2_weight, fc2_bias, cotangent, extra,
):
    bits = {name: lax.axis_index(name) for name in ("y", "hi", "lo", "x", "c")}
    block_at = (bits["y"] * 2 + bits["lo"]) * 2 + bits["x"]
    vectors = [ln1_gain, ln1_bias, ln2_gain, ln2_bias, out_bias, fc2_bias, qkv_bias, fc1_bias]
    if extra > 1:
        join = functools.partial(lax.all_gather, axis_name="e", axis=0, tiled=True)
        vectors = [join(v) for v in vectors]
        qkv_weight, out_weight, fc1_weight, fc2_weight = [
            join(w) for w in (qkv_weight, out_weight, fc1_weight, fc2_weight)
        ]
    length, width = tokens.shape[1:]
    tables = jnp.asarray(rotary_tables(length))

    small = jnp.concatenate([v.reshape(-1, 128) for v in vectors], axis=0)
    small = jnp.pad(small, ((0, -small.shape[0] % 16), (0, 0)))
    (
        g_all, small, qkv_cols, fc1_cols, fc2_rows, out_rows, a1, a2, heads, mixed, hidden, slope, y_part
    ) = forward(tokens[0], cotangent[0], small, qkv_weight, fc1_weight, fc2_weight, out_weight, tables)
    small = small.astype(F32)
    norm = jnp.stack([small[:, i].reshape(-1) for i in range(6)])
    shift_rest = norm[4] + norm[5]
    norm = norm[:4]
    count = g_all.shape[0]
    n_qkv, n_fc1, n_mix = qkv_cols.shape[1], fc1_cols.shape[1], out_rows.shape[0]
    flops = 2 * count * length * width * (n_qkv + n_fc1 + n_fc1 + n_mix)
    output = tokens[0].astype(F32) + shift_rest[None] + scatter_tokens(y_part)

    grad_packed, grad_up, dx_part, packed_sum, up_sum = run(
        backward_kernel,
        [
            (g_all, True), (heads, True), (slope, True), (norm, None), (qkv_cols, None), (fc1_cols, None),
            (fc2_rows, None), (out_rows, None), (tables, None),
        ],
        [
            ((count, length, n_qkv), BF16, True),
            ((count, length, n_fc1), BF16, True),
            ((count, length, width), BF16, True),
            ((1, n_qkv), F32, False),
            ((1, n_fc1), F32, False),
        ],
        flops,
        "backward",
    )

    def flat(a):
        return a.reshape(-1, a.shape[-1])

    fc1_part = dot(flat(a2), flat(grad_up), TN)
    qkv_part = dot(flat(a1), flat(grad_packed), TN)
    fc2_part = dot(flat(hidden), flat(g_all), TN).astype(BF16)
    out_part = dot(flat(mixed), flat(g_all), TN).astype(BF16)

    fc2_grad, out_grad = rows_out(fc2_part, out_part, bits)
    fc1_grad = columns_out(fc1_part.astype(BF16), bits)
    qkv_grad = columns_out(qkv_part.astype(BF16), bits)

    def norm_grads(weight, part, sums, gain, bias):
        weight = weight.astype(F32)
        bias_grad = jnp.sum(weight * sums, axis=1)
        return (jnp.sum(weight * part, axis=1) - bias * bias_grad) / gain, bias_grad

    gain1_grad, bias1_grad = norm_grads(qkv_cols, qkv_part, packed_sum, norm[0], norm[1])
    gain2_grad, bias2_grad = norm_grads(fc1_cols, fc1_part, up_sum, norm[2], norm[3])
    column_total = jnp.sum(cotangent[0].astype(F32), axis=0)
    rows = [v.reshape(16, -1, 128) for v in (gain1_grad, bias1_grad, gain2_grad, bias2_grad, column_total)]
    place = (jnp.arange(8) == block_at)[:, None, None]
    rows += [jnp.where(place, v[None], 0.0).reshape(16, -1, 128) for v in (packed_sum, up_sum)]
    small_grads = scatter_small(jnp.concatenate(rows, axis=1), bits)
    cuts = np.cumsum([r.shape[1] for r in rows])[:-1]
    small_grads = [v.reshape(-1) for v in jnp.split(small_grads, cuts, axis=0)]

    inputs = tokens[0].astype(F32)
    centred = inputs - jnp.mean(inputs, axis=-1, keepdims=True)
    scale = lax.rsqrt(jnp.mean(centred * centred, axis=-1, keepdims=True) + EPS)
    normed = centred * scale
    dx = scatter_tokens(dx_part)
    dx = scale * (
        dx - jnp.mean(dx, axis=-1, keepdims=True) - normed * jnp.mean(dx * normed, axis=-1, keepdims=True)
    )
    input_grad = cotangent[0].astype(F32) + dx

    weight_grads = [qkv_grad, out_grad, fc1_grad, fc2_grad]
    if extra > 1:
        scatter = functools.partial(lax.psum_scatter, axis_name="e", scatter_dimension=0, tiled=True)
        weight_grads = [scatter(v) for v in weight_grads]
        small_grads = [scatter(v) for v in small_grads]
    qkv_grad, out_grad, fc1_grad, fc2_grad = weight_grads
    gain1, bias1, gain2, bias2, total, packed_bias, up_bias = small_grads
    return (
        output.astype(BF16)[None],
        input_grad.astype(BF16)[None],
        gain1,
        bias1,
        gain2,
        bias2,
        qkv_grad,
        packed_bias,
        out_grad,
        total,
        fc1_grad,
        up_bias,
        fc2_grad,
        total,
    )


def solution(mesh):
    extra = mesh.shape["shard"] // 16
    axes = ("y", "hi", "lo", "x", "c", "e")
    fine = Mesh(mesh.devices.reshape(2, 2, 2, 2, 2, extra), axes)
    split = P(axes, None, None)
    row, flat = P(axes[1:], None), P(axes[1:])
    in_specs = (split, flat, flat, flat, flat, row, flat, row, flat, row, flat, row, flat, split)
    out_specs = (split, split, flat, flat, flat, flat, row, flat, row, flat, row, flat, row, flat)
    return jax.shard_map(
        functools.partial(body, extra=extra), mesh=fine, in_specs=in_specs, out_specs=out_specs, check_vma=False
    )
```

```python
import functools

import jax
import jax.numpy as jnp
import numpy as np
from jax import lax
from jax.experimental import pallas as pl
from jax.experimental.pallas import tpu as pltpu
from jax.sharding import Mesh
from jax.sharding import PartitionSpec as P

HEADS = 8
HEAD_DIM = 256
ROTARY = 64
EPS = 1e-05
NEG_FILL = -1e30
SCALE = HEAD_DIM ** (-0.5)
BF16 = jnp.bfloat16
F32 = jnp.float32
NT = (((1,), (1,)), ((), ()))
TN = (((0,), (0,)), ((), ()))
NN = (((1,), (0,)), ((), ()))


def dot(a, b, dims=NN):
    return lax.dot_general(a, b, dims, preferred_element_type=F32)


NAMES = ("y", "hi", "lo", "x", "c")
ORDERS = (("lo", "x", "y"), ("lo", "y", "x"), ("y", "x", "lo"))
PLACE = {"lo": 1, "x": 2, "y": 4}


def row_chunks(length):
    last = length // 96 * 16
    first = (length - last + 31) // 32 * 16
    return ((0, first), (first, length - last - first), (length - last, last))


class Copies:
    def __init__(self, at, send_sem, recv_sem, local_sem):
        self.at, self.send_sem, self.recv_sem, self.local_sem = at, send_sem, recv_sem, local_sem
        self.remote, self.planned, self.local = [], 0, 0

    def plan(self, src, dst, axis, everywhere=True):
        spot = self.planned
        self.planned += 1
        copy = pltpu.make_async_remote_copy(
            src_ref=src,
            dst_ref=dst,
            send_sem=self.send_sem.at[spot],
            recv_sem=self.recv_sem.at[spot],
            device_id={axis: 1 - self.at[axis]},
            device_id_type=pl.DeviceIdType.MESH,
        )
        if everywhere:
            self.remote.append(copy)
        return copy

    def move(self, src, dst):
        copy = pltpu.make_async_copy(src, dst, self.local_sem.at[self.local])
        self.local += 1
        return copy


def greet(at, names):
    barrier = pltpu.get_barrier_semaphore()
    for name in names:
        pl.semaphore_signal(
            barrier, inc=1, device_id={name: 1 - at[name]}, device_id_type=pl.DeviceIdType.MESH
        )
    pl.semaphore_wait(barrier, len(names))


class TokenGather:
    def __init__(self, copies, own, full):
        rows = row_chunks(own.shape[0])
        self.plans, self.unseen = {}, set()
        self.kept = copies.move(own, full.at[0])
        for chunk, order in enumerate(ORDERS):
            part = pl.ds(*rows[chunk])
            for step, axis in enumerate(order):
                for block in range(8):
                    if all(block & PLACE[later] == 0 for later in order[step:]):
                        src = own.at[part] if block == 0 else full.at[block, part]
                        there = full.at[block + PLACE[axis], part]
                        self.plans[chunk, block + PLACE[axis]] = copies.plan(src, there, axis)
                        self.unseen.add((chunk, block + PLACE[axis]))

    def send(self, chunk, block, axis):
        self.plans[chunk, block + PLACE[axis]].start()

    def arrive(self, chunk, block):
        if (chunk, block) in self.unseen:
            self.unseen.remove((chunk, block))
            self.plans[chunk, block].wait_recv()

    def start(self):
        self.kept.start()
        for step in range(3):
            for chunk, order in enumerate(ORDERS):
                self.send(chunk, 0, order[step])

    def relay_one(self):
        for chunk, order in enumerate(ORDERS):
            self.arrive(chunk, PLACE[order[0]])
            self.send(chunk, PLACE[order[0]], order[1])
            self.send(chunk, PLACE[order[0]], order[2])

    def relay_two(self):
        for has_first in (0, 1):
            for chunk, order in enumerate(ORDERS):
                block = PLACE[order[1]] + has_first * PLACE[order[0]]
                self.arrive(chunk, block)
                self.send(chunk, block, order[2])

    def take(self, block):
        for chunk in range(len(ORDERS)):
            self.arrive(chunk, block)

    def finish(self):
        for block in range(8):
            self.take(block)
        self.kept.wait()


class TokenScatter:
    def __init__(self, copies, parts, came, stage, total):
        self.came, self.stage, self.total = came, stage, total
        rows = row_chunks(parts.shape[1])
        self.rows, self.first, self.second, self.third, self.loads = rows, {}, {}, {}, []
        steps = []
        for chunk, order in enumerate(ORDERS):
            third, second, first = order
            part = pl.ds(*rows[chunk])
            for slot in (3, 2, 1, 0):
                block = PLACE[second] * (slot // 2) + PLACE[third] * (slot % 2)
                src = parts.at[block + PLACE[first], part]
                self.first[chunk, slot] = copies.plan(src, came.at[slot, part], first)
                steps.append((slot, chunk, block))
            for slot in (3, 2):
                self.second[chunk, slot] = copies.plan(came.at[slot, part], came.at[2 + slot, part], second)
            self.third[chunk] = copies.plan(came.at[1, part], came.at[6, part], third)
        self.at = {}
        for spot, (slot, chunk, block) in enumerate(sorted(steps, key=lambda s: (-s[0], s[1]))):
            part = pl.ds(*rows[chunk])
            self.at[slot, chunk] = spot
            self.loads.append(copies.move(parts.at[block, part], stage.at[spot % 2, pl.ds(0, rows[chunk][1])]))

    def start(self):
        for slot in (3, 2, 1, 0):
            for chunk in range(len(ORDERS)):
                self.first[chunk, slot].start()
        self.loads[0].start()
        self.loads[1].start()

    def own(self, slot, chunk):
        spot = self.at[slot, chunk]
        self.loads[spot].wait()
        return self.stage[spot % 2, : self.rows[chunk][1]].astype(F32)

    def used(self, slot, chunk):
        spot = self.at[slot, chunk]
        if spot + 2 < len(self.loads):
            self.loads[spot + 2].start()

    def add(self, slot, chunk, more=()):
        part = pl.ds(*self.rows[chunk])
        self.first[chunk, slot].wait_recv()
        value = self.own(slot, chunk)
        for other in (slot,) + more:
            value = value + self.came[other, part].astype(F32)
        self.used(slot, chunk)
        return value

    def pass_second(self, slot):
        for chunk in range(len(ORDERS)):
            self.came[slot, pl.ds(*self.rows[chunk])] = self.add(slot, chunk).astype(BF16)
            self.second[chunk, slot].start()

    def pass_third(self):
        for chunk in range(len(ORDERS)):
            self.second[chunk, 3].wait_recv()
            self.came[1, pl.ds(*self.rows[chunk])] = self.add(1, chunk, (5,)).astype(BF16)
            self.third[chunk].start()

    def last(self):
        for chunk in range(len(ORDERS)):
            self.second[chunk, 2].wait_recv()
            self.third[chunk].wait_recv()
            self.total[pl.ds(*self.rows[chunk])] = self.add(0, chunk, (4, 6))


class ColumnGather:
    def __init__(self, copies, weight, full, relay):
        at = copies.at
        hi, lo, x, c = (at[n] for n in ("hi", "lo", "x", "c"))
        rows, width = weight.shape[0], full.shape[1]

        def block(lo_at, x_at):
            spot = (at["y"] * 2 + lo_at) * 2 + x_at
            return weight.at[:, pl.ds(pl.multiple_of(spot * width, 128), width)]

        def place(hi_at, lo_at, x_at):
            spot = ((hi_at * 2 + lo_at) * 2 + x_at) * 2 + c
            return full.at[pl.ds(pl.multiple_of(spot * rows, 128), rows)]

        mine = place(hi, lo, x)
        self.by_x = [copies.plan(block(1 - lo, 1 - x), relay, "x"), copies.plan(block(lo, 1 - x), mine, "x")]
        self.by_lo = [
            copies.plan(block(1 - lo, x), mine, "lo"),
            copies.plan(relay, place(hi, lo, 1 - x), "lo"),
        ]
        near = [place(hi, lo, x), place(hi, lo, 1 - x), place(hi, 1 - lo, x), place(hi, 1 - lo, 1 - x)]
        far = [place(1 - hi, lo, x), place(1 - hi, lo, 1 - x), place(1 - hi, 1 - lo, x), place(1 - hi, 1 - lo, 1 - x)]
        source = [block(lo, x)] + near[1:]
        self.by_hi = [copies.plan(src, dst, "hi") for src, dst in zip(source, near)]
        self.by_c = [copies.plan(src, dst, "c") for src, dst in zip(source + far, near + far)]
        self.kept = copies.move(block(lo, x), mine)

    def start(self):
        for copy in self.by_x + self.by_lo[:1] + self.by_hi[:1] + self.by_c[:1] + [self.kept]:
            copy.start()

    def relay_x(self):
        self.by_x[0].wait_recv()
        self.by_lo[1].start()
        self.by_x[1].wait_recv()
        self.by_hi[1].start()
        self.by_c[1].start()

    def relay_lo(self):
        for i in (0, 1):
            self.by_lo[i].wait_recv()
            self.by_hi[2 + i].start()
            self.by_c[2 + i].start()

    def relay_hi(self):
        for i in range(4):
            self.by_hi[i].wait_recv()
            self.by_c[4 + i].start()

    def finish(self):
        for copy in self.by_c:
            copy.wait_recv()
        self.kept.wait()


class RowGather:
    def __init__(self, copies, weight, full):
        at, rows = copies.at, weight.shape[0]
        half = rows // 2

        def spot(start, count):
            return full.at[pl.ds(pl.multiple_of(start, 16), count)]

        self.copies = copies
        self.holds = 1 - (at["hi"] + at["y"]) % 2
        first, second = spot(at["c"] * rows, half), spot(at["c"] * rows + half, half)
        there = spot(self.holds * (at["c"] * rows) + (1 - self.holds) * 2 * rows, half)
        source = weight.at[pl.ds(pl.multiple_of((1 - self.holds) * half, 16), half)]
        self.by_hi = copies.plan(source, there, "hi")
        self.by_y = copies.plan(spot(2 * rows, half), second, "y", everywhere=False)
        self.by_c = [copies.plan(first, first, "c"), copies.plan(second, second, "c")]
        self.kept = copies.move(weight, spot(at["c"] * rows, rows))

    def start(self):
        self.by_hi.start()
        pl.when(self.holds == 1)(self.kept.start)

    def relay_hi(self):
        self.by_hi.wait_recv()

        @pl.when(self.holds == 1)
        def _():
            self.by_y.start()
            self.kept.wait()

        self.by_c[0].start()

    def relay_y(self):
        pl.when(self.holds == 0)(self.by_y.wait_recv)
        self.by_c[1].start()

    def finish(self):
        for copy in self.by_c:
            copy.wait_recv()

    def sent(self):
        pl.when(self.holds == 1)(self.by_y.wait_send)


class SmallGather:
    def __init__(self, copies, full):
        at = copies.at
        base = ((at["hi"] * 2 + at["lo"]) * 2 + at["x"]) * 2 + at["c"]
        self.own = full.at[pl.ds(base, 1)]
        self.steps, count = [], 1
        for name in ("c", "x", "lo", "hi"):
            part = full.at[pl.ds(base, count)]
            self.steps.append(copies.plan(part, part, name))
            base = base - at[name] * count
            count *= 2

    def start(self):
        self.steps[0].start()

    def step(self, at):
        self.steps[at - 1].wait_recv()
        if at < 4:
            self.steps[at].start()


def rotary_tables(length):
    places = np.arange(length, dtype=np.float32)
    frequency = (10000.0 ** (-np.arange(0, ROTARY, 2, dtype=np.float32) / ROTARY)).astype(np.float32)
    angles = places[:, None] * frequency[None, :]
    cosine, sine = np.cos(angles), np.sin(angles)
    half = ROTARY // 2
    tables = np.zeros((3, length, HEAD_DIM), np.float32)
    tables[0] = 1.0
    tables[0, :, :half] = cosine
    tables[0, :, half:ROTARY] = cosine
    tables[1, :, :half] = -sine
    tables[2, :, half:ROTARY] = sine
    return tables


def turn(rows, tables, sign):
    half = ROTARY // 2
    ahead = pltpu.roll(rows, HEAD_DIM - half, 1)
    behind = pltpu.roll(rows, half, 1)
    return rows * tables[0] + sign * (ahead * tables[1] + behind * tables[2])


def causal_scores(queries, keys_all):
    length = queries.shape[0]
    scores = dot(queries, keys_all, NT) * SCALE
    row = lax.broadcasted_iota(jnp.int32, (length, length), 0)
    col = lax.broadcasted_iota(jnp.int32, (length, length), 1)
    return jnp.where(row >= col, scores, NEG_FILL)


def softmax(scores):
    raised = jnp.exp(scores - jnp.max(scores, axis=-1, keepdims=True))
    return raised / jnp.sum(raised, axis=-1, keepdims=True)


def forward_kernel(
    x_ref, g_ref, small_ref, qkv_ref, fc1_ref, fc2_ref, out_ref, tables_ref,
    g_all, small_out, qkv_out, fc1_out, fc2_out, out_out,
    a1_ref, a2_ref, heads_ref, mixed_ref, hidden_ref, slope_ref, y_ref,
    x_all, small_all, qkv_all, fc1_all, fc2_all, out_all, norm, qkv_bias, fc1_bias, mixed_all, hidden_all,
    relay_qkv, relay_fc1, send_sem, recv_sem, local_sem,
):
    step = pl.program_id(0)
    at = {name: lax.axis_index(name) for name in NAMES}
    copies = Copies(at, send_sem, recv_sem, local_sem)
    small = SmallGather(copies, small_all)
    qkv = ColumnGather(copies, qkv_ref, qkv_all, relay_qkv)
    fc1 = ColumnGather(copies, fc1_ref, fc1_all, relay_fc1)
    fc2 = RowGather(copies, fc2_ref, fc2_all)
    out = RowGather(copies, out_ref, out_all)
    x = TokenGather(copies, x_ref, x_all)
    g = TokenGather(copies, g_ref, g_all)
    kept = [
        copies.move(src.at[pl.ds(0, dst.shape[0])], dst)
        for src, dst in ((qkv_all, qkv_out), (fc1_all, fc1_out), (fc2_all, fc2_out), (out_all, out_out))
    ]

    @pl.when(step == 0)
    def _():
        greet(at, NAMES)
        small.own[...] = small_ref[...][None]
        small.start()
        qkv.start()
        fc1.start()
        x.start()
        small.step(1)
        small.step(2)
        qkv.relay_x()
        small.step(3)
        fc1.relay_x()
        qkv.relay_lo()
        x.relay_one()
        fc1.relay_lo()
        small.step(4)
        for spot in range(16):
            norm[:, spot * 128 : (spot + 1) * 128] = small_all[spot, :8].astype(F32)
        first = (at["y"] * 4 + at["lo"] * 2 + at["x"]) * 2
        for half in range(2):
            own = small_all[first + half].astype(F32)
            for bias, start in ((qkv_bias, 6), (fc1_bias, 6 + qkv_bias.shape[1] // 256)):
                rows = bias.shape[1] // 256
                for i in range(rows):
                    bias[:, (half * rows + i) * 128 : (half * rows + i + 1) * 128] = own[start + i : start + i + 1]
        qkv.relay_hi()
        x.relay_two()
        g.start()
        g.relay_one()
        fc2.start()
        out.start()
        fc1.relay_hi()
        x.kept.wait()
        qkv.finish()
        fc1.finish()
        kept[0].start()
        kept[1].start()

    for block in range(1, 8):
        pl.when(step == block)(functools.partial(x.take, block))

    @pl.when(step == 4)
    def _():
        g.relay_two()
        fc2.relay_hi()
        out.relay_hi()

    @pl.when(step < 8)
    def _():
        value = x_all[step].astype(F32)
        centred = value - jnp.mean(value, axis=-1, keepdims=True)
        var = jnp.mean(centred * centred, axis=-1, keepdims=True)
        normed = centred * lax.rsqrt(var + EPS)
        a1_ref[0] = (normed * norm[0:1] + norm[1:2]).astype(BF16)
        a2_ref[0] = (normed * norm[2:3] + norm[3:4]).astype(BF16)

        packed = dot(a1_ref[0], qkv_all[...]) + qkv_bias[...]
        queries = turn(packed[:, :HEAD_DIM], tables_ref, 1.0).astype(BF16)
        keys_all = turn(packed[:, HEAD_DIM : 2 * HEAD_DIM], tables_ref, 1.0).astype(BF16)
        values_all = packed[:, 2 * HEAD_DIM :].astype(BF16)
        heads_ref[0, :, :HEAD_DIM] = queries
        heads_ref[0, :, HEAD_DIM : 2 * HEAD_DIM] = keys_all
        heads_ref[0, :, 2 * HEAD_DIM :] = values_all
        probs = softmax(causal_scores(queries, keys_all)).astype(BF16)
        mixed_ref[0] = dot(probs, values_all).astype(BF16)
        mixed_all[step] = mixed_ref[0]

        upward = dot(a2_ref[0], fc1_all[...]) + fc1_bias[...]
        below = 0.5 * (1.0 + lax.erf(upward * np.float32(0.5**0.5)))
        hidden_ref[0] = (upward * below).astype(BF16)
        hidden_all[step] = hidden_ref[0]
        slope_ref[0] = below + upward * (jnp.exp(-0.5 * upward * upward) * np.float32((2 * np.pi) ** -0.5))

    @pl.when(step == 8)
    def _():
        fc2.relay_y()
        out.relay_y()
        fc2.finish()
        out.finish()
        kept[2].start()
        kept[3].start()

    @pl.when(step >= 8)
    def _():
        y = dot(hidden_all[step - 8], fc2_all[: hidden_ref.shape[2]])
        y_ref[0] = (y + dot(mixed_all[step - 8], out_all[: mixed_ref.shape[2]])).astype(BF16)

    @pl.when(step == 15)
    def _():
        small_out[...] = small_all[...]
        g.finish()
        for copy in kept:
            copy.wait()
        for copy in copies.remote:
            copy.wait_send()
        fc2.sent()
        out.sent()


def forward(tokens, cotangent, small, qkv_weight, fc1_weight, fc2_weight, out_weight, tables):
    far = pl.BlockSpec(memory_space=pl.ANY)
    length, width = tokens.shape
    rows = qkv_weight.shape[0]
    n_qkv, n_fc1, n_mix = qkv_weight.shape[1] // 8, fc1_weight.shape[1] // 8, out_weight.shape[0] * 2
    each = [(width, BF16), (width, BF16), (n_qkv, BF16), (n_mix, BF16), (n_fc1, BF16), (n_fc1, F32), (width, BF16)]
    count = 4 + 2 * 16 + 2 * 4 + 2 * 7 * len(ORDERS)
    weights = [(16 * rows, n_qkv), (16 * rows, n_fc1), (n_fc1, width), (n_mix, width)]
    flops = 2 * 8 * length * width * (n_qkv + n_fc1 + n_fc1 + n_mix)
    return pl.pallas_call(
        forward_kernel,
        grid=(16,),
        in_specs=[far, far, whole(small), far, far, far, far, whole(tables)],
        out_specs=[far, whole(jax.ShapeDtypeStruct((16,) + small.shape, BF16)), far, far, far, far]
        + [pl.BlockSpec((1, length, n), lambda i: (jnp.minimum(i, 7), 0, 0)) for n, _ in each[:-1]]
        + [pl.BlockSpec((1, length, width), lambda i: (jnp.maximum(i - 8, 0), 0, 0))],
        out_shape=[
            jax.ShapeDtypeStruct((8, length, width), BF16),
            jax.ShapeDtypeStruct((16,) + small.shape, BF16),
        ]
        + [jax.ShapeDtypeStruct(shape, BF16) for shape in weights]
        + [jax.ShapeDtypeStruct((8, length, n), kind) for n, kind in each],
        scratch_shapes=[
            pltpu.VMEM((8, length, width), BF16),
            pltpu.VMEM((16,) + small.shape, BF16),
            pltpu.VMEM(weights[0], BF16),
            pltpu.VMEM(weights[1], BF16),
            pltpu.VMEM((n_fc1 * 5 // 4, width), BF16),
            pltpu.VMEM((n_mix * 5 // 4, width), BF16),
            pltpu.VMEM((8, width), F32),
            pltpu.VMEM((1, n_qkv), F32),
            pltpu.VMEM((1, n_fc1), F32),
            pltpu.VMEM((8, length, n_mix), BF16),
            pltpu.VMEM((8, length, n_fc1), BF16),
            pltpu.VMEM((rows, n_qkv), BF16),
            pltpu.VMEM((rows, n_fc1), BF16),
            pltpu.SemaphoreType.DMA((count,)),
            pltpu.SemaphoreType.DMA((count,)),
            pltpu.SemaphoreType.DMA((10,)),
        ],
        compiler_params=pltpu.CompilerParams(
            collective_id=1, has_side_effects=True, vmem_limit_bytes=60 * 2**20
        ),
        cost_estimate=pl.CostEstimate(flops=flops, bytes_accessed=10**8, transcendentals=0),
        name="forward",
    )(tokens, cotangent, small, qkv_weight, fc1_weight, fc2_weight, out_weight, tables)


def add_rows(dst, dst_row, src, src_row, count):
    for start in range(0, count, 64):
        here = pl.ds(pl.multiple_of(dst_row + start, 16), 64)
        there = pl.ds(pl.multiple_of(src_row + start, 16), 64)
        dst[here] = (dst[here].astype(F32) + src[there].astype(F32)).astype(BF16)


class RowScatter:
    def __init__(self, copies, part, kept, came, n_fc2, n_out):
        at = copies.at
        c = at["c"]
        self.part, self.kept, self.came = part, kept, came
        self.sizes = n_fc2, n_out
        self.holds = 1 - (at["hi"] + at["y"]) % 2
        own, half = n_fc2 + n_out, (n_fc2 // 2, n_out // 2)

        def rows(ref, start, count):
            return ref.at[pl.ds(pl.multiple_of(start, 16), count)]

        self.pieces = [
            [(0, n_fc2, 0, half[0]), (2 * n_fc2, n_out, n_fc2, half[1])],
            [(half[0], n_fc2, half[0], half[0]), (2 * n_fc2 + half[1], n_out, n_fc2 + half[1], half[1])],
        ]
        self.c = c
        self.by_c = [
            [copies.plan(rows(part, base + (1 - c) * size, n), rows(kept, to, n), "c") for base, size, to, n in side]
            for side in self.pieces
        ]
        self.by_y = [
            copies.plan(rows(kept, half[0], half[0]), rows(kept, own, half[0]), "y"),
            copies.plan(rows(kept, n_fc2 + half[1], half[1]), rows(kept, own + half[0], half[1]), "y"),
        ]
        holds = self.holds
        sent = [holds * own, holds * (own + half[0]) + (1 - holds) * n_fc2]
        self.keeps = [(1 - holds) * own, (1 - holds) * (own + half[0]) + holds * n_fc2]
        self.by_hi = [
            copies.plan(rows(kept, sent[0], half[0]), rows(came, 0, half[0]), "hi"),
            copies.plan(rows(kept, sent[1], half[1]), rows(came, half[0], half[1]), "hi"),
        ]
        self.half = half

    def send_c(self, side):
        for copy in self.by_c[side]:
            copy.start()

    def add_c(self, side):
        for copy, (base, size, to, n) in zip(self.by_c[side], self.pieces[side]):
            copy.wait_recv()
            add_rows(self.kept, to, self.part, base + self.c * size, n)

    def send_y(self):
        for copy in self.by_y:
            copy.start()

    def send_hi(self):
        for copy in self.by_y:
            copy.wait_recv()
        for copy in self.by_hi:
            copy.start()

    def add_hi(self):
        for copy in self.by_hi:
            copy.wait_recv()
        add_rows(self.came, 0, self.kept, self.keeps[0], self.half[0])
        add_rows(self.came, self.half[0], self.kept, self.keeps[1], self.half[1])


def backward_kernel(
    y_ref, g_ref, hidden_ref, mixed_ref, heads_ref, slope_ref, norm_ref, qkv_ref, fc1_ref, fc2_ref, out_ref, tables_ref,
    y_out, grads_ref, dx_ref, packed_sum_ref, up_sum_ref, total_ref, rows_out,
    g_all, qkv, fc1, fc2, out, came, stage, part, kept, rows_came, send_sem, recv_sem, local_sem,
):
    step = pl.program_id(0)
    at = {name: lax.axis_index(name) for name in NAMES}
    copies = Copies(at, send_sem, recv_sem, local_sem)
    scatter = TokenScatter(copies, y_ref, came, stage, y_out)
    n_fc1, n_mix, n_qkv = fc2_ref.shape[0], out_ref.shape[0], qkv_ref.shape[1]
    rows = RowScatter(copies, part, kept, rows_came, n_fc1 // 2, n_mix // 2)
    load_g = copies.move(g_ref, g_all)
    loads = [copies.move(src, dst) for src, dst in ((qkv_ref, qkv), (fc1_ref, fc1), (fc2_ref, fc2), (out_ref, out))]
    store = copies.move(rows_came, rows_out)
    width = n_fc1 // 4
    count, length, _ = g_all.shape

    @pl.when(step == 0)
    def _():
        greet(at, NAMES)
        load_g.start()
        scatter.start()
        for copy in loads:
            copy.start()
        packed_sum_ref[...] = jnp.zeros_like(packed_sum_ref)
        up_sum_ref[...] = jnp.zeros_like(up_sum_ref)
        load_g.wait()
        total_ref[...] = jnp.sum(g_all[0].astype(F32), axis=0, keepdims=True)

    for spot, tile in ((0, 1), (1, 3), (3, 0), (4, 2)):

        @pl.when(step == spot)
        def _(tile=tile):
            grads = dot(hidden_ref[...], g_all[...].reshape(count * length, -1), TN)
            part[tile * width : (tile + 1) * width] = grads.astype(BF16)

    @pl.when(step == 2)
    def _():
        part[n_fc1:] = dot(mixed_ref[...], g_all[...].reshape(count * length, -1), TN).astype(BF16)
        rows.send_c(1)

    @pl.when(step == 3)
    def _():
        rows.add_c(1)
        rows.send_y()

    @pl.when(step == 4)
    def _():
        rows.send_c(0)

    @pl.when(step == 5)
    def _():
        for copy in loads:
            copy.wait()
        rows.add_c(0)
        scatter.pass_second(3)

    @pl.when(step == 7)
    def _():
        scatter.pass_second(2)

    @pl.when(step == 9)
    def _():
        rows.send_hi()

    @pl.when(step == 11)
    def _():
        scatter.pass_third()

    @pl.when(step >= 5)
    def _():
        g = g_all[step - 5]
        grad_up = (dot(g, fc2[...], NT) * slope_ref[0]).astype(BF16)
        grads_ref[0, :, n_qkv:] = grad_up
        up_sum_ref[...] += jnp.sum(grad_up.astype(F32), axis=0, keepdims=True)

        grad_mixed = dot(g, out[...], NT).astype(BF16)
        queries = heads_ref[0, :, :HEAD_DIM]
        keys_all = heads_ref[0, :, HEAD_DIM : 2 * HEAD_DIM]
        values_all = heads_ref[0, :, 2 * HEAD_DIM :]
        probs = softmax(causal_scores(queries, keys_all))
        grad_probs = dot(grad_mixed, values_all, NT)
        grad_values = dot(probs.astype(BF16), grad_mixed, TN)
        inner = jnp.sum(grad_probs * probs, axis=-1, keepdims=True)
        grad_scores = (probs * (grad_probs - inner)).astype(BF16)
        grad_queries = turn(dot(grad_scores, keys_all) * SCALE, tables_ref, -1.0)
        grad_keys = turn(dot(grad_scores, queries, TN) * SCALE, tables_ref, -1.0)
        grads_ref[0, :, :HEAD_DIM] = grad_queries.astype(BF16)
        grads_ref[0, :, HEAD_DIM : 2 * HEAD_DIM] = grad_keys.astype(BF16)
        grads_ref[0, :, 2 * HEAD_DIM : n_qkv] = grad_values.astype(BF16)
        packed_sum_ref[...] += jnp.sum(grads_ref[0, :, :n_qkv].astype(F32), axis=0, keepdims=True)

        dx_ref[0] = (
            dot(grads_ref[0, :, :n_qkv], qkv[...], NT) * norm_ref[0:1]
            + dot(grads_ref[0, :, n_qkv:], fc1[...], NT) * norm_ref[2:3]
        ).astype(BF16)

    @pl.when(step == 12)
    def _():
        scatter.last()
        rows.add_hi()
        store.start()
        store.wait()
        for copy in copies.remote:
            copy.wait_send()


def backward(y_part, g_all, hidden, mixed, heads, slope, norm, qkv, fc1, fc2, out, tables):
    far = pl.BlockSpec(memory_space=pl.ANY)
    count, length, width = g_all.shape
    n_qkv, n_fc1, n_mix = qkv.shape[1], fc1.shape[1], out.shape[0]
    tokens = count * length
    hidden, mixed = hidden.reshape(tokens, n_fc1), mixed.reshape(tokens, n_mix)
    own = (n_fc1 + n_mix) // 2
    longest = max(n for _, n in row_chunks(length))

    def tile(i):
        return jnp.where(i == 0, 1, jnp.where(i < 3, 3, jnp.where(i == 3, 0, 2)))

    def each(n):
        return pl.BlockSpec((1, length, n), lambda i: (jnp.maximum(i - 5, 0), 0, 0))

    outputs = [
        ((length, width), F32, None),
        ((count, length, n_qkv + n_fc1), BF16, each(n_qkv + n_fc1)),
        ((count, length, width), BF16, each(width)),
        ((1, n_qkv), F32, None),
        ((1, n_fc1), F32, None),
        ((1, width), F32, None),
        ((own // 2, width), BF16, far),
    ]
    shapes = [jax.ShapeDtypeStruct(shape, kind) for shape, kind, _ in outputs]
    copies = 7 * len(ORDERS) + 8
    flops = 2 * tokens * width * (n_qkv + 3 * n_fc1 + 2 * n_mix)
    return pl.pallas_call(
        backward_kernel,
        grid=(13,),
        in_specs=[
            far, far, pl.BlockSpec((tokens, n_fc1 // 4), lambda i: (0, tile(i))), whole(mixed), each(n_qkv), each(n_fc1),
            whole(norm), far, far, far, far, whole(tables),
        ],
        out_specs=[whole(s) if spec is None else spec for s, (_, _, spec) in zip(shapes, outputs)],
        out_shape=shapes,
        scratch_shapes=[
            pltpu.VMEM(g_all.shape, BF16),
            pltpu.VMEM(qkv.shape, BF16),
            pltpu.VMEM(fc1.shape, BF16),
            pltpu.VMEM(fc2.shape, BF16),
            pltpu.VMEM(out.shape, BF16),
            pltpu.VMEM((7, length, width), BF16),
            pltpu.VMEM((2, longest, width), BF16),
            pltpu.VMEM((n_fc1 + n_mix, width), BF16),
            pltpu.VMEM((own + own // 2, width), BF16),
            pltpu.VMEM((own // 2, width), BF16),
            pltpu.SemaphoreType.DMA((copies,)),
            pltpu.SemaphoreType.DMA((copies,)),
            pltpu.SemaphoreType.DMA((4 * len(ORDERS) + 6,)),
        ],
        compiler_params=pltpu.CompilerParams(
            collective_id=2, has_side_effects=True, vmem_limit_bytes=62 * 2**20
        ),
        cost_estimate=pl.CostEstimate(flops=flops, bytes_accessed=10**8, transcendentals=0),
        name="backward",
    )(y_part, g_all, hidden, mixed, heads, slope, norm, qkv, fc1, fc2, out, tables)


class ColumnScatter:
    def __init__(self, copies, tiles, by_c, by_hi, relay, full):
        at = copies.at
        self.copies, self.tiles, self.came_c, self.came_hi = copies, tiles, by_c, by_hi
        y, hi, lo, x, c = (at[n] for n in NAMES)
        rows = by_c.shape[1]
        self.rows, self.c = rows, c
        hops = ((1 - lo, 1 - x), (1 - lo, x), (lo, 1 - x), (lo, x))
        self.places = [(hi_at * 2 + lo_at) * 2 + x_at for hi_at in (1 - hi, hi) for lo_at, x_at in hops]
        away = pl.ds(pl.multiple_of((1 - c) * rows, 16), rows)
        self.by_c = [copies.plan(tiles.at[i, away], by_c.at[i], "c") for i in range(8)]
        self.by_hi = [copies.plan(by_c.at[i], by_hi.at[i], "hi") for i in range(4)]

        def spot(lo_at, x_at):
            return full.at[(y * 2 + lo_at) * 2 + x_at]

        self.far = copies.plan(by_hi.at[0], relay, "lo")
        self.far_on = copies.plan(relay, spot(1 - lo, x), "x")
        self.by_lo = copies.plan(by_hi.at[1], spot(lo, x), "lo")
        self.by_x = copies.plan(by_hi.at[2], spot(lo, x), "x")
        self.mine = copies.move(by_hi.at[3], spot(lo, x))
        self.by_y = [
            copies.plan(by_hi.at[3], spot(lo, x), "y"),
            copies.plan(spot(1 - lo, x), spot(1 - lo, x), "y"),
            copies.plan(spot(lo, 1 - x), spot(lo, 1 - x), "y"),
            copies.plan(spot(1 - lo, 1 - x), spot(1 - lo, 1 - x), "y"),
        ]

    def send_c(self, i):
        self.by_c[i].start()

    def add_c(self, i):
        self.by_c[i].wait_recv()
        own = self.tiles[i, pl.ds(pl.multiple_of(self.c * self.rows, 16), self.rows)]
        self.came_c[i] = (self.came_c[i].astype(F32) + own.astype(F32)).astype(BF16)
        if i < 4:
            self.by_hi[i].start()

    def add_hi(self, i):
        self.by_hi[i].wait_recv()
        self.came_hi[i] = (self.came_hi[i].astype(F32) + self.came_c[4 + i].astype(F32)).astype(BF16)
        if i < 3:
            (self.far, self.by_lo, self.by_x)[i].start()
        else:
            self.mine.start()
            self.by_y[0].start()

    def relay_far(self):
        self.far.wait_recv()
        self.far_on.start()

    def relay_lo(self):
        self.by_lo.wait_recv()
        self.by_y[1].start()

    def relay_x(self):
        self.by_x.wait_recv()
        self.by_y[2].start()

    def relay_last(self):
        self.far_on.wait_recv()
        self.by_y[3].start()

    def finish(self):
        self.mine.wait()
        for copy in self.by_y:
            copy.wait_recv()


class SmallScatter:
    def __init__(self, copies, parts, came):
        at = copies.at
        self.parts, self.came, self.steps = parts, came, []
        base, count, spot = 0, 8, 0
        for name in ("hi", "lo", "x", "c"):
            away = parts.at[pl.ds(base + (1 - at[name]) * count, count)]
            base = base + at[name] * count
            self.steps.append((copies.plan(away, came.at[pl.ds(spot, count)], name), base, spot, count))
            spot += count
            count //= 2
        own = parts.at[pl.ds(base, 1)]
        self.steps.append((copies.plan(own, came.at[pl.ds(spot, 1)], "y"), base, spot, 1))
        self.base, self.spot = base, spot

    def send(self, step):
        self.steps[step][0].start()

    def add(self, step):
        copy, base, spot, count = self.steps[step]
        copy.wait_recv()
        if step < 4:
            for i in range(count):
                self.parts[base + i] += self.came[spot + i]
            self.send(step + 1)

    def total(self):
        return self.parts[self.base] + self.came[self.spot]


def reduce_kernel(
    dx_ref, a1_ref, a2_ref, grads_ref, qkv_ref, fc1_ref, rows_ref, norm_ref, packed_sum_ref, up_sum_ref, total_ref,
    dx_out, rows_other, full, small_out,
    grads, a1, a2, qkv, fc1, came, stage, tiles, by_c, by_hi, relay, vectors, parts, parts_came,
    send_sem, recv_sem, local_sem,
):
    step = pl.program_id(0)
    at = {name: lax.axis_index(name) for name in NAMES}
    copies = Copies(at, send_sem, recv_sem, local_sem)
    scatter = TokenScatter(copies, dx_ref, came, stage, dx_out)
    columns = ColumnScatter(copies, tiles, by_c, by_hi, relay, full)
    small = SmallScatter(copies, parts, parts_came)
    by_y = copies.plan(rows_ref, rows_other, "y")
    load_grads = copies.move(grads_ref, grads)
    size = 2 * by_c.shape[1]
    n_qkv, n_fc1 = qkv.shape[2], fc1.shape[2]

    def loads(i):
        start = pl.multiple_of(columns.places[i] * size, 128)
        slot = i % 2
        first = copies.local
        made = [
            copies.move(a1_ref.at[:, pl.ds(start, size)], a1.at[slot]),
            copies.move(a2_ref.at[:, pl.ds(start, size)], a2.at[slot]),
            copies.move(qkv_ref.at[pl.ds(start, size)], qkv.at[slot]),
            copies.move(fc1_ref.at[pl.ds(start, size)], fc1.at[slot]),
        ]
        if i >= 2:
            copies.local = first
        return made

    tile_loads = [None] * 8
    base = copies.local
    for i in range(8):
        copies.local = base + 4 * (i % 2)
        tile_loads[i] = loads(i)
    copies.local = base + 8

    @pl.when(step == 0)
    def _():
        greet(at, NAMES)
        for copy in tile_loads[0]:
            copy.start()
        load_grads.start()
        by_y.start()
        scatter.start()
        load_grads.wait()

    for i in range(8):

        @pl.when(step == i)
        def _(i=i):
            if i < 7:
                for copy in tile_loads[i + 1]:
                    copy.start()
            for copy in tile_loads[i]:
                copy.wait()
            if i > 0:
                columns.add_c(i - 1)

    slot = step % 2
    place = columns.places[0]
    for i in range(1, 8):
        place = jnp.where(step == i, columns.places[i], place)
    qkv_part = dot(a1[slot], grads[:, :n_qkv], TN)
    tiles[step, :, :n_qkv] = qkv_part.astype(BF16)
    fc1_part = dot(a2[slot], grads[:, n_qkv:], TN)
    tiles[step, :, n_qkv:] = fc1_part.astype(BF16)
    lane = lax.broadcasted_iota(jnp.int32, (size, 128), 1)
    packed = jnp.zeros((size, 128), F32)
    for at_lane, (weight, part, sums) in enumerate(
        ((qkv, qkv_part, packed_sum_ref), (fc1, fc1_part, up_sum_ref))
    ):
        weight = weight[slot].astype(F32)
        packed = jnp.where(lane == 2 * at_lane, jnp.sum(weight * part, axis=1, keepdims=True), packed)
        packed = jnp.where(lane == 2 * at_lane + 1, jnp.sum(weight * sums[...], axis=1, keepdims=True), packed)
    vectors[:, pl.ds(pl.multiple_of(place * size, 128), size)] = jnp.transpose(packed)[:8]

    for i in range(8):
        pl.when(step == i)(functools.partial(columns.send_c, i))

    @pl.when(step == 3)
    def _():
        scatter.pass_second(3)

    @pl.when(step == 6)
    def _():
        scatter.pass_second(2)

    @pl.when(step == 7)
    def _():
        columns.add_c(7)
        parts[...] = jnp.zeros_like(parts)
        rows = []
        for i in (0, 2):
            gain, bias = norm_ref[i : i + 1], norm_ref[i + 1 : i + 2]
            bias_grad = vectors[i + 1 : i + 2]
            rows += [(vectors[i : i + 1] - bias * bias_grad) / gain, bias_grad]
        rows.append(total_ref[...])
        for spot in range(16):
            for i, row in enumerate(rows):
                parts[spot, i : i + 1] = row[:, spot * 128 : (spot + 1) * 128]
        first = (at["y"] * 4 + at["lo"] * 2 + at["x"]) * 2
        for half in range(2):
            start = len(rows)
            for sums in (packed_sum_ref, up_sum_ref):
                count = sums.shape[1] // 256
                for i in range(count):
                    lanes = slice((half * count + i) * 128, (half * count + i + 1) * 128)
                    parts[first + half, start + i : start + i + 1] = sums[:, lanes]
                start += count
        small.send(0)
        columns.add_hi(0)
        small.add(0)
        scatter.pass_third()
        small.add(1)
        columns.add_hi(1)
        small.add(2)
        columns.relay_far()
        small.add(3)
        columns.relay_lo()
        scatter.last()
        columns.add_hi(2)
        columns.relay_last()
        small.add(4)
        small_out[...] = small.total()
        columns.add_hi(3)
        columns.relay_x()
        by_y.wait_recv()
        columns.finish()
        for copy in copies.remote:
            copy.wait_send()


def reduce(dx_part, a1, a2, grads, qkv, fc1, rows_total, norm, packed_sum, up_sum, column_total):
    far = pl.BlockSpec(memory_space=pl.ANY)
    count, length, width = dx_part.shape
    tokens = count * length
    n_qkv, n_fc1 = qkv.shape[1], fc1.shape[1]
    wide = n_qkv + n_fc1
    a1, a2, grads = a1.reshape(tokens, width), a2.reshape(tokens, width), grads.reshape(tokens, wide)
    size = width // 8
    longest = max(n for _, n in row_chunks(length))
    outputs = [
        ((length, width), F32, None),
        (rows_total.shape, BF16, far),
        ((8, size // 2, wide), BF16, far),
        ((16, 128), F32, None),
    ]
    shapes = [jax.ShapeDtypeStruct(shape, kind) for shape, kind, _ in outputs]
    copies = 7 * len(ORDERS) + 20 + 5 + 1
    return pl.pallas_call(
        reduce_kernel,
        grid=(8,),
        in_specs=[far] * 7 + [whole(norm), whole(packed_sum), whole(up_sum), whole(column_total)],
        out_specs=[whole(s) if spec is None else spec for s, (_, _, spec) in zip(shapes, outputs)],
        out_shape=shapes,
        scratch_shapes=[
            pltpu.VMEM((tokens, wide), BF16),
            pltpu.VMEM((2, tokens, size), BF16),
            pltpu.VMEM((2, tokens, size), BF16),
            pltpu.VMEM((2, size, n_qkv), BF16),
            pltpu.VMEM((2, size, n_fc1), BF16),
            pltpu.VMEM((7, length, width), BF16),
            pltpu.VMEM((2, longest, width), BF16),
            pltpu.VMEM((8, size, wide), BF16),
            pltpu.VMEM((8, size // 2, wide), BF16),
            pltpu.VMEM((4, size // 2, wide), BF16),
            pltpu.VMEM((size // 2, wide), BF16),
            pltpu.VMEM((8, width), F32),
            pltpu.VMEM((16, 16, 128), F32),
            pltpu.VMEM((16, 16, 128), F32),
            pltpu.SemaphoreType.DMA((copies,)),
            pltpu.SemaphoreType.DMA((copies,)),
            pltpu.SemaphoreType.DMA((4 * len(ORDERS) + 10,)),
        ],
        compiler_params=pltpu.CompilerParams(
            collective_id=3, has_side_effects=True, vmem_limit_bytes=60 * 2**20
        ),
        cost_estimate=pl.CostEstimate(
            flops=2 * tokens * width * wide, bytes_accessed=10**8, transcendentals=0
        ),
        name="reduce",
    )(dx_part, a1, a2, grads, qkv, fc1, rows_total, norm, packed_sum, up_sum, column_total)


def whole(array, rows=None):
    shape = (rows or array.shape[0],) + array.shape[1:]
    return pl.BlockSpec(shape, lambda i: (0,) * array.ndim, pipeline_mode=pl.Buffered(1))


def body(
    tokens, ln1_gain, ln1_bias, ln2_gain, ln2_bias, qkv_weight, qkv_bias, out_weight, out_bias,
    fc1_weight, fc1_bias, fc2_weight, fc2_bias, cotangent, extra,
):
    bits = {name: lax.axis_index(name) for name in NAMES}
    vectors = [ln1_gain, ln1_bias, ln2_gain, ln2_bias, out_bias, fc2_bias, qkv_bias, fc1_bias]
    if extra > 1:
        join = functools.partial(lax.all_gather, axis_name="e", axis=0, tiled=True)
        vectors = [join(v) for v in vectors]
        qkv_weight, out_weight, fc1_weight, fc2_weight = [
            join(w) for w in (qkv_weight, out_weight, fc1_weight, fc2_weight)
        ]
    length, width = tokens.shape[1:]
    tables = jnp.asarray(rotary_tables(length))

    small = jnp.concatenate([v.reshape(-1, 128) for v in vectors], axis=0)
    small = jnp.pad(small, ((0, -small.shape[0] % 16), (0, 0)))
    (
        g_all, small, qkv_cols, fc1_cols, fc2_rows, out_rows, a1, a2, heads, mixed, hidden, slope, y_part
    ) = forward(tokens[0], cotangent[0], small, qkv_weight, fc1_weight, fc2_weight, out_weight, tables)
    small = small.astype(F32)
    norm = jnp.stack([small[:, i].reshape(-1) for i in range(8)])
    y_sum, grads, dx_part, packed_sum, up_sum, column_total, rows_total = backward(
        y_part, g_all, hidden, mixed, heads, slope, norm, qkv_cols, fc1_cols, fc2_rows, out_rows, tables
    )
    output = tokens[0].astype(F32) + (norm[4] + norm[5])[None] + y_sum
    dx, rows_other, columns, small_grads = reduce(
        dx_part, a1, a2, grads, qkv_cols, fc1_cols, rows_total, norm, packed_sum, up_sum, column_total
    )

    n_qkv, n_fc2 = qkv_cols.shape[1], fc2_weight.shape[0] // 2
    holds = bits["hi"] == bits["y"]
    first = jnp.where(holds, rows_total, rows_other)
    second = jnp.where(holds, rows_other, rows_total)
    fc2_grad = jnp.concatenate([first[:n_fc2], second[:n_fc2]], axis=0).astype(F32)
    out_grad = jnp.concatenate([first[n_fc2:], second[n_fc2:]], axis=0).astype(F32)
    qkv_grad = jnp.concatenate([columns[i, :, :n_qkv] for i in range(8)], axis=1).astype(F32)
    fc1_grad = jnp.concatenate([columns[i, :, n_qkv:] for i in range(8)], axis=1).astype(F32)
    cuts = np.cumsum([1, 1, 1, 1, 1, qkv_bias.shape[0] * extra // 128, fc1_bias.shape[0] * extra // 128])
    small_grads = [v.reshape(-1) for v in jnp.split(small_grads, cuts, axis=0)[:-1]]

    inputs = tokens[0].astype(F32)
    centred = inputs - jnp.mean(inputs, axis=-1, keepdims=True)
    scale = lax.rsqrt(jnp.mean(centred * centred, axis=-1, keepdims=True) + EPS)
    normed = centred * scale
    dx = scale * (
        dx - jnp.mean(dx, axis=-1, keepdims=True) - normed * jnp.mean(dx * normed, axis=-1, keepdims=True)
    )
    input_grad = cotangent[0].astype(F32) + dx

    weight_grads = [qkv_grad, out_grad, fc1_grad, fc2_grad]
    if extra > 1:
        scatter = functools.partial(lax.psum_scatter, axis_name="e", scatter_dimension=0, tiled=True)
        weight_grads = [scatter(v) for v in weight_grads]
        small_grads = [scatter(v) for v in small_grads]
    qkv_grad, out_grad, fc1_grad, fc2_grad = weight_grads
    gain1, bias1, gain2, bias2, total, packed_bias, up_bias = small_grads
    return (
        output.astype(BF16)[None],
        input_grad.astype(BF16)[None],
        gain1,
        bias1,
        gain2,
        bias2,
        qkv_grad,
        packed_bias,
        out_grad,
        total,
        fc1_grad,
        up_bias,
        fc2_grad,
        total,
    )


def solution(mesh):
    extra = mesh.shape["shard"] // 16
    axes = ("y", "hi", "lo", "x", "c", "e")
    fine = Mesh(mesh.devices.reshape(2, 2, 2, 2, 2, extra), axes)
    split = P(axes, None, None)
    row, flat = P(axes[1:], None), P(axes[1:])
    in_specs = (split, flat, flat, flat, flat, row, flat, row, flat, row, flat, row, flat, split)
    out_specs = (split, split, flat, flat, flat, flat, row, flat, row, flat, row, flat, row, flat)
    return jax.shard_map(
        functools.partial(body, extra=extra), mesh=fine, in_specs=in_specs, out_specs=out_specs, check_vma=False
    )
```

```python
import functools

import jax
import jax.numpy as jnp
import numpy as np
from jax import lax
from jax.experimental import pallas as pl
from jax.experimental.pallas import tpu as pltpu
from jax.sharding import Mesh
from jax.sharding import PartitionSpec as P

HEADS = 8
HEAD_DIM = 256
ROTARY = 64
EPS = 1e-05
NEG_FILL = -1e30
SCALE = HEAD_DIM ** (-0.5)
BF16 = jnp.bfloat16
F32 = jnp.float32
NT = (((1,), (1,)), ((), ()))
TN = (((0,), (0,)), ((), ()))
NN = (((1,), (0,)), ((), ()))


def dot(a, b, dims=NN):
    return lax.dot_general(a, b, dims, preferred_element_type=F32)


NAMES = ("y", "hi", "lo", "x", "c")
PLACE = {"lo": 1, "x": 2, "y": 4}


def gather_chunks(length):
    last = length // 96 * 16
    first = (length - last + 31) // 32 * 16
    return (
        (0, first, ("lo", "x", "y")),
        (first, length - last - first, ("lo", "y", "x")),
        (length - last, last, ("y", "x", "lo")),
    )


def scatter_chunks(length):
    last = length // 96 * 16
    second = length * 5 // 288 * 16
    first = length - 2 * last - second
    return (
        (0, first, ("y", "lo", "x")),
        (first, second, ("lo", "y", "x")),
        (first + second, last, ("y", "x", "lo")),
        (first + second + last, last, ("lo", "x", "y")),
    )


class Copies:
    def __init__(self, at, send_sem, recv_sem, local_sem):
        self.at, self.send_sem, self.recv_sem, self.local_sem = at, send_sem, recv_sem, local_sem
        self.remote, self.planned, self.local = [], 0, 0

    def plan(self, src, dst, axis, everywhere=True):
        spot = self.planned
        self.planned += 1
        copy = pltpu.make_async_remote_copy(
            src_ref=src,
            dst_ref=dst,
            send_sem=self.send_sem.at[spot],
            recv_sem=self.recv_sem.at[spot],
            device_id={axis: 1 - self.at[axis]},
            device_id_type=pl.DeviceIdType.MESH,
        )
        if everywhere:
            self.remote.append(copy)
        return copy

    def move(self, src, dst):
        copy = pltpu.make_async_copy(src, dst, self.local_sem.at[self.local])
        self.local += 1
        return copy


def greet(at, names):
    barrier = pltpu.get_barrier_semaphore()
    for name in names:
        pl.semaphore_signal(
            barrier, inc=1, device_id={name: 1 - at[name]}, device_id_type=pl.DeviceIdType.MESH
        )
    pl.semaphore_wait(barrier, len(names))


class TokenGather:
    def __init__(self, copies, own, full):
        self.plans, self.unseen = {}, set()
        self.kept = copies.move(own, full.at[0])
        chunks = gather_chunks(own.shape[0])
        self.orders = [order for _, _, order in chunks]
        for chunk, (start, rows, order) in enumerate(chunks):
            part = pl.ds(start, rows)
            for step, axis in enumerate(order):
                for block in range(8):
                    if all(block & PLACE[later] == 0 for later in order[step:]):
                        src = own.at[part] if block == 0 else full.at[block, part]
                        there = full.at[block + PLACE[axis], part]
                        self.plans[chunk, block + PLACE[axis]] = copies.plan(src, there, axis)
                        self.unseen.add((chunk, block + PLACE[axis]))

    def send(self, chunk, block, axis):
        self.plans[chunk, block + PLACE[axis]].start()

    def arrive(self, chunk, block):
        if (chunk, block) in self.unseen:
            self.unseen.remove((chunk, block))
            self.plans[chunk, block].wait_recv()

    def start(self):
        self.kept.start()
        for step in range(3):
            for chunk, order in enumerate(self.orders):
                self.send(chunk, 0, order[step])

    def relay_one(self):
        for chunk, order in enumerate(self.orders):
            self.arrive(chunk, PLACE[order[0]])
            self.send(chunk, PLACE[order[0]], order[1])
            self.send(chunk, PLACE[order[0]], order[2])

    def relay_two(self):
        for has_first in (0, 1):
            for chunk, order in enumerate(self.orders):
                block = PLACE[order[1]] + has_first * PLACE[order[0]]
                self.arrive(chunk, block)
                self.send(chunk, block, order[2])

    def take(self, block):
        for chunk in range(len(self.orders)):
            self.arrive(chunk, block)

    def finish(self):
        for block in range(8):
            self.take(block)
        self.kept.wait()


class TokenScatter:
    def __init__(self, copies, parts, came, far_parts, stage, room, total):
        self.parts, self.came, self.far_parts, self.stage, self.room = parts, came, far_parts, stage, room
        self.chunks = scatter_chunks(parts.shape[1])
        self.first, self.second, self.third, self.stores, self.loads, self.near = {}, {}, [], [], {}, {}
        base = copies.local
        for chunk, (start, rows, order) in enumerate(self.chunks):
            third, second, first = order
            part = pl.ds(start, rows)

            def load(src, spot):
                copies.local = base + spot
                return copies.move(src.at[part], stage.at[spot, pl.ds(0, rows)])

            for slot in (3, 2, 1, 0):
                block = PLACE[second] * (slot // 2) + PLACE[third] * (slot % 2)
                src = parts.at[block + PLACE[first], part]
                self.first[chunk, slot] = copies.plan(src, came.at[slot, part], first)
                near = came.at[slot, part] if far_parts else parts.at[block, part]
                if slot > 1:
                    self.second[chunk, slot] = copies.plan(near, came.at[2 + slot, part], second)
                if slot == 1:
                    self.third.append(copies.plan(near, came.at[6, part], third))
                far = [came.at[i] for i in {0: (0, 4, 6), 1: (1, 5)}.get(slot, (slot,))]
                sources = [parts.at[block]] if far_parts else far
                self.loads[chunk, slot] = [load(src, spot) for spot, src in enumerate(sources)]
                self.near[chunk, slot] = near
        copies.local = base + 3
        for chunk, (start, rows, order) in enumerate(self.chunks):
            self.stores.append(copies.move(room.at[pl.ds(0, rows)], total.at[pl.ds(start, rows)]))

    def send(self, slot):
        for chunk in range(len(self.chunks)):
            self.first[chunk, slot].start()

    def add(self, slot, chunk):
        start, rows, order = self.chunks[chunk]
        part = pl.ds(start, rows)
        self.first[chunk, slot].wait_recv()
        loads = self.loads[chunk, slot]
        for copy in loads:
            copy.start()
        if self.far_parts:
            more = {0: (0, 4, 6), 1: (1, 5)}.get(slot, (slot,))
            value = sum(self.came[i, part].astype(F32) for i in more)
        else:
            third, second, _ = order
            block = PLACE[second] * (slot // 2) + PLACE[third] * (slot % 2)
            value = self.parts[block, part].astype(F32)
        for spot, copy in enumerate(loads):
            copy.wait()
            value = value + self.stage[spot, :rows].astype(F32)
        return value

    def pass_second(self, slot):
        for chunk in range(len(self.chunks)):
            self.near[chunk, slot][...] = self.add(slot, chunk).astype(BF16)
            self.second[chunk, slot].start()

    def pass_third(self):
        for chunk in range(len(self.chunks)):
            self.second[chunk, 3].wait_recv()
            self.near[chunk, 1][...] = self.add(1, chunk).astype(BF16)
            self.third[chunk].start()

    def last(self):
        for chunk, (_, rows, _) in enumerate(self.chunks):
            self.second[chunk, 2].wait_recv()
            self.third[chunk].wait_recv()
            self.room[:rows] = self.add(0, chunk)
            self.stores[chunk].start()
            self.stores[chunk].wait()

    def sent(self):
        for copy in list(self.first.values()) + list(self.second.values()) + self.third:
            copy.wait_send()


class ColumnGather:
    def __init__(self, copies, weight, full, relay):
        at = copies.at
        hi, lo, x, c = (at[n] for n in ("hi", "lo", "x", "c"))
        rows, width = weight.shape[0], full.shape[1]

        def block(lo_at, x_at):
            spot = (at["y"] * 2 + lo_at) * 2 + x_at
            return weight.at[:, pl.ds(pl.multiple_of(spot * width, 128), width)]

        def place(hi_at, lo_at, x_at):
            spot = ((hi_at * 2 + lo_at) * 2 + x_at) * 2 + c
            return full.at[pl.ds(pl.multiple_of(spot * rows, 128), rows)]

        mine = place(hi, lo, x)
        self.by_x = [copies.plan(block(1 - lo, 1 - x), relay, "x"), copies.plan(block(lo, 1 - x), mine, "x")]
        self.by_lo = [
            copies.plan(block(1 - lo, x), mine, "lo"),
            copies.plan(relay, place(hi, lo, 1 - x), "lo"),
        ]
        near = [place(hi, lo, x), place(hi, lo, 1 - x), place(hi, 1 - lo, x), place(hi, 1 - lo, 1 - x)]
        far = [place(1 - hi, lo, x), place(1 - hi, lo, 1 - x), place(1 - hi, 1 - lo, x), place(1 - hi, 1 - lo, 1 - x)]
        source = [block(lo, x)] + near[1:]
        self.by_hi = [copies.plan(src, dst, "hi") for src, dst in zip(source, near)]
        self.by_c = [copies.plan(src, dst, "c") for src, dst in zip(source + far, near + far)]
        self.kept = copies.move(block(lo, x), mine)

    def start(self):
        for copy in self.by_x + self.by_lo[:1] + self.by_hi[:1] + self.by_c[:1] + [self.kept]:
            copy.start()

    def relay_x(self):
        self.by_x[0].wait_recv()
        self.by_lo[1].start()
        self.by_x[1].wait_recv()
        self.by_hi[1].start()
        self.by_c[1].start()

    def relay_lo(self):
        for i in (0, 1):
            self.by_lo[i].wait_recv()
            self.by_hi[2 + i].start()
            self.by_c[2 + i].start()

    def relay_hi(self):
        for i in range(4):
            self.by_hi[i].wait_recv()
            self.by_c[4 + i].start()

    def finish(self):
        for copy in self.by_c:
            copy.wait_recv()
        self.kept.wait()


class RowGather:
    def __init__(self, copies, weight, full):
        at, rows = copies.at, weight.shape[0]
        half = rows // 2

        def spot(start, count):
            return full.at[pl.ds(pl.multiple_of(start, 16), count)]

        self.copies = copies
        self.holds = 1 - (at["hi"] + at["y"]) % 2
        first, second = spot(at["c"] * rows, half), spot(at["c"] * rows + half, half)
        there = spot(self.holds * (at["c"] * rows) + (1 - self.holds) * 2 * rows, half)
        source = weight.at[pl.ds(pl.multiple_of((1 - self.holds) * half, 16), half)]
        self.by_hi = copies.plan(source, there, "hi")
        self.by_y = copies.plan(spot(2 * rows, half), second, "y", everywhere=False)
        self.by_c = [copies.plan(first, first, "c"), copies.plan(second, second, "c")]
        self.kept = copies.move(weight, spot(at["c"] * rows, rows))

    def start(self):
        self.by_hi.start()
        pl.when(self.holds == 1)(self.kept.start)

    def relay_hi(self):
        self.by_hi.wait_recv()

        @pl.when(self.holds == 1)
        def _():
            self.by_y.start()
            self.kept.wait()

        self.by_c[0].start()

    def relay_y(self):
        pl.when(self.holds == 0)(self.by_y.wait_recv)
        self.by_c[1].start()

    def finish(self):
        for copy in self.by_c:
            copy.wait_recv()

    def sent(self):
        pl.when(self.holds == 1)(self.by_y.wait_send)


class SmallGather:
    def __init__(self, copies, full):
        at = copies.at
        base = ((at["hi"] * 2 + at["lo"]) * 2 + at["x"]) * 2 + at["c"]
        self.own = full.at[pl.ds(base, 1)]
        self.steps, count = [], 1
        for name in ("c", "x", "lo", "hi"):
            part = full.at[pl.ds(base, count)]
            self.steps.append(copies.plan(part, part, name))
            base = base - at[name] * count
            count *= 2

    def start(self):
        self.steps[0].start()

    def step(self, at):
        self.steps[at - 1].wait_recv()
        if at < 4:
            self.steps[at].start()


def rotary_tables(length):
    places = np.arange(length, dtype=np.float32)
    frequency = (10000.0 ** (-np.arange(0, ROTARY, 2, dtype=np.float32) / ROTARY)).astype(np.float32)
    angles = places[:, None] * frequency[None, :]
    cosine, sine = np.cos(angles), np.sin(angles)
    half = ROTARY // 2
    tables = np.zeros((3, length, HEAD_DIM), np.float32)
    tables[0] = 1.0
    tables[0, :, :half] = cosine
    tables[0, :, half:ROTARY] = cosine
    tables[1, :, :half] = -sine
    tables[2, :, half:ROTARY] = sine
    return tables


def turn(rows, tables, sign):
    half = ROTARY // 2
    ahead = pltpu.roll(rows, HEAD_DIM - half, 1)
    behind = pltpu.roll(rows, half, 1)
    return rows * tables[0] + sign * (ahead * tables[1] + behind * tables[2])


def causal_scores(queries, keys_all):
    length = queries.shape[0]
    scores = dot(queries, keys_all, NT) * SCALE
    row = lax.broadcasted_iota(jnp.int32, (length, length), 0)
    col = lax.broadcasted_iota(jnp.int32, (length, length), 1)
    return jnp.where(row >= col, scores, NEG_FILL)


def softmax(scores):
    raised = jnp.exp(scores - jnp.max(scores, axis=-1, keepdims=True))
    return raised / jnp.sum(raised, axis=-1, keepdims=True)


def forward_kernel(
    x_ref, g_ref, small_ref, qkv_ref, fc1_ref, fc2_ref, out_ref, tables_ref,
    g_all, small_out, qkv_out, fc1_out, fc2_out, out_out,
    a1_ref, a2_ref, heads_ref, mixed_ref, hidden_ref, slope_ref, y_ref,
    x_all, small_all, qkv_all, fc1_all, fc2_all, out_all, norm, qkv_bias, fc1_bias, mixed_all, hidden_all,
    relay_qkv, relay_fc1, send_sem, recv_sem, local_sem,
):
    step = pl.program_id(0)
    at = {name: lax.axis_index(name) for name in NAMES}
    copies = Copies(at, send_sem, recv_sem, local_sem)
    small = SmallGather(copies, small_all)
    qkv = ColumnGather(copies, qkv_ref, qkv_all, relay_qkv)
    fc1 = ColumnGather(copies, fc1_ref, fc1_all, relay_fc1)
    fc2 = RowGather(copies, fc2_ref, fc2_all)
    out = RowGather(copies, out_ref, out_all)
    x = TokenGather(copies, x_ref, x_all)
    g = TokenGather(copies, g_ref, g_all)
    kept = [
        copies.move(src.at[pl.ds(0, dst.shape[0])], dst)
        for src, dst in ((qkv_all, qkv_out), (fc1_all, fc1_out), (fc2_all, fc2_out), (out_all, out_out))
    ]

    @pl.when(step == 0)
    def _():
        greet(at, NAMES)
        small.own[...] = small_ref[...][None]
        small.start()
        qkv.start()
        fc1.start()
        x.start()
        small.step(1)
        small.step(2)
        qkv.relay_x()
        small.step(3)
        fc1.relay_x()
        qkv.relay_lo()
        x.relay_one()
        fc1.relay_lo()
        small.step(4)
        for spot in range(16):
            norm[:, spot * 128 : (spot + 1) * 128] = small_all[spot, :8].astype(F32)
        first = (at["y"] * 4 + at["lo"] * 2 + at["x"]) * 2
        for half in range(2):
            own = small_all[first + half].astype(F32)
            for bias, start in ((qkv_bias, 6), (fc1_bias, 6 + qkv_bias.shape[1] // 256)):
                rows = bias.shape[1] // 256
                for i in range(rows):
                    bias[:, (half * rows + i) * 128 : (half * rows + i + 1) * 128] = own[start + i : start + i + 1]
        qkv.relay_hi()
        x.relay_two()
        g.start()
        g.relay_one()
        fc2.start()
        out.start()
        fc1.relay_hi()
        x.kept.wait()
        qkv.finish()
        fc1.finish()
        kept[0].start()
        kept[1].start()

    for block in range(1, 8):
        pl.when(step == block)(functools.partial(x.take, block))

    @pl.when(step == 4)
    def _():
        g.relay_two()
        fc2.relay_hi()
        out.relay_hi()

    @pl.when(step < 8)
    def _():
        value = x_all[step].astype(F32)
        centred = value - jnp.mean(value, axis=-1, keepdims=True)
        var = jnp.mean(centred * centred, axis=-1, keepdims=True)
        normed = centred * lax.rsqrt(var + EPS)
        a1_ref[0] = (normed * norm[0:1] + norm[1:2]).astype(BF16)
        a2_ref[0] = (normed * norm[2:3] + norm[3:4]).astype(BF16)

        packed = dot(a1_ref[0], qkv_all[...]) + qkv_bias[...]
        queries = turn(packed[:, :HEAD_DIM], tables_ref, 1.0).astype(BF16)
        keys_all = turn(packed[:, HEAD_DIM : 2 * HEAD_DIM], tables_ref, 1.0).astype(BF16)
        values_all = packed[:, 2 * HEAD_DIM :].astype(BF16)
        heads_ref[0, :, :HEAD_DIM] = queries
        heads_ref[0, :, HEAD_DIM : 2 * HEAD_DIM] = keys_all
        heads_ref[0, :, 2 * HEAD_DIM :] = values_all
        probs = softmax(causal_scores(queries, keys_all)).astype(BF16)
        mixed_ref[0] = dot(probs, values_all).astype(BF16)
        mixed_all[step] = mixed_ref[0]

        upward = dot(a2_ref[0], fc1_all[...]) + fc1_bias[...]
        below = 0.5 * (1.0 + lax.erf(upward * np.float32(0.5**0.5)))
        hidden_ref[0] = (upward * below).astype(BF16)
        hidden_all[step] = hidden_ref[0]
        slope_ref[0] = below + upward * (jnp.exp(-0.5 * upward * upward) * np.float32((2 * np.pi) ** -0.5))

    @pl.when(step == 8)
    def _():
        fc2.relay_y()
        out.relay_y()
        fc2.finish()
        out.finish()
        kept[2].start()
        kept[3].start()

    @pl.when(step >= 8)
    def _():
        y = dot(hidden_all[step - 8], fc2_all[: hidden_ref.shape[2]])
        y_ref[0] = (y + dot(mixed_all[step - 8], out_all[: mixed_ref.shape[2]])).astype(BF16)

    @pl.when(step == 15)
    def _():
        small_out[...] = small_all[...]
        g.finish()
        for copy in kept:
            copy.wait()
        for copy in copies.remote:
            copy.wait_send()
        fc2.sent()
        out.sent()


def forward(tokens, cotangent, small, qkv_weight, fc1_weight, fc2_weight, out_weight, tables):
    far = pl.BlockSpec(memory_space=pl.ANY)
    length, width = tokens.shape
    rows = qkv_weight.shape[0]
    n_qkv, n_fc1, n_mix = qkv_weight.shape[1] // 8, fc1_weight.shape[1] // 8, out_weight.shape[0] * 2
    each = [(width, BF16), (width, BF16), (n_qkv, BF16), (n_mix, BF16), (n_fc1, BF16), (n_fc1, F32), (width, BF16)]
    count = 4 + 2 * 16 + 2 * 4 + 2 * 7 * len(gather_chunks(length))
    weights = [(16 * rows, n_qkv), (16 * rows, n_fc1), (n_fc1, width), (n_mix, width)]
    flops = 2 * 8 * length * width * (n_qkv + n_fc1 + n_fc1 + n_mix)
    return pl.pallas_call(
        forward_kernel,
        grid=(16,),
        in_specs=[far, far, whole(small), far, far, far, far, whole(tables)],
        out_specs=[far, whole(jax.ShapeDtypeStruct((16,) + small.shape, BF16)), far, far, far, far]
        + [pl.BlockSpec((1, length, n), lambda i: (jnp.minimum(i, 7), 0, 0)) for n, _ in each[:-1]]
        + [pl.BlockSpec((1, length, width), lambda i: (jnp.maximum(i - 8, 0), 0, 0))],
        out_shape=[
            jax.ShapeDtypeStruct((8, length, width), BF16),
            jax.ShapeDtypeStruct((16,) + small.shape, BF16),
        ]
        + [jax.ShapeDtypeStruct(shape, BF16) for shape in weights]
        + [jax.ShapeDtypeStruct((8, length, n), kind) for n, kind in each],
        scratch_shapes=[
            pltpu.VMEM((8, length, width), BF16),
            pltpu.VMEM((16,) + small.shape, BF16),
            pltpu.VMEM(weights[0], BF16),
            pltpu.VMEM(weights[1], BF16),
            pltpu.VMEM((n_fc1 * 5 // 4, width), BF16),
            pltpu.VMEM((n_mix * 5 // 4, width), BF16),
            pltpu.VMEM((8, width), F32),
            pltpu.VMEM((1, n_qkv), F32),
            pltpu.VMEM((1, n_fc1), F32),
            pltpu.VMEM((8, length, n_mix), BF16),
            pltpu.VMEM((8, length, n_fc1), BF16),
            pltpu.VMEM((rows, n_qkv), BF16),
            pltpu.VMEM((rows, n_fc1), BF16),
            pltpu.SemaphoreType.DMA((count,)),
            pltpu.SemaphoreType.DMA((count,)),
            pltpu.SemaphoreType.DMA((10,)),
        ],
        compiler_params=pltpu.CompilerParams(
            collective_id=1, has_side_effects=True, vmem_limit_bytes=60 * 2**20
        ),
        cost_estimate=pl.CostEstimate(flops=flops, bytes_accessed=10**8, transcendentals=0),
        name="forward",
    )(tokens, cotangent, small, qkv_weight, fc1_weight, fc2_weight, out_weight, tables)


def add_rows(dst, dst_row, src, src_row, count):
    for start in range(0, count, 64):
        here = pl.ds(pl.multiple_of(dst_row + start, 16), 64)
        there = pl.ds(pl.multiple_of(src_row + start, 16), 64)
        dst[here] = (dst[here].astype(F32) + src[there].astype(F32)).astype(BF16)


class RowScatter:
    def __init__(self, copies, part, kept, came, n_fc2, n_out):
        at = copies.at
        c = at["c"]
        self.part, self.kept, self.came = part, kept, came
        self.sizes = n_fc2, n_out
        self.holds = 1 - (at["hi"] + at["y"]) % 2
        own, half = n_fc2 + n_out, (n_fc2 // 2, n_out // 2)

        def rows(ref, start, count):
            return ref.at[pl.ds(pl.multiple_of(start, 16), count)]

        self.pieces = [
            [(0, n_fc2, 0, half[0]), (2 * n_fc2, n_out, n_fc2, half[1])],
            [(half[0], n_fc2, half[0], half[0]), (2 * n_fc2 + half[1], n_out, n_fc2 + half[1], half[1])],
        ]
        self.c = c
        self.by_c = [
            [copies.plan(rows(part, base + (1 - c) * size, n), rows(kept, to, n), "c") for base, size, to, n in side]
            for side in self.pieces
        ]
        self.by_y = [
            copies.plan(rows(kept, half[0], half[0]), rows(kept, own, half[0]), "y"),
            copies.plan(rows(kept, n_fc2 + half[1], half[1]), rows(kept, own + half[0], half[1]), "y"),
        ]
        holds = self.holds
        sent = [holds * own, holds * (own + half[0]) + (1 - holds) * n_fc2]
        self.keeps = [(1 - holds) * own, (1 - holds) * (own + half[0]) + holds * n_fc2]
        self.by_hi = [
            copies.plan(rows(kept, sent[0], half[0]), rows(came, 0, half[0]), "hi"),
            copies.plan(rows(kept, sent[1], half[1]), rows(came, half[0], half[1]), "hi"),
        ]
        self.half = half

    def send_c(self, side):
        for copy in self.by_c[side]:
            copy.start()

    def sent_c(self):
        for copy in self.by_c[0] + self.by_c[1]:
            copy.wait_send()

    def add_c(self, side):
        for copy, (base, size, to, n) in zip(self.by_c[side], self.pieces[side]):
            copy.wait_recv()
            add_rows(self.kept, to, self.part, base + self.c * size, n)

    def send_y(self):
        for copy in self.by_y:
            copy.start()

    def send_hi(self):
        for copy in self.by_y:
            copy.wait_recv()
        for copy in self.by_hi:
            copy.start()

    def add_hi(self):
        for copy in self.by_hi:
            copy.wait_recv()
        add_rows(self.came, 0, self.kept, self.keeps[0], self.half[0])
        add_rows(self.came, self.half[0], self.kept, self.keeps[1], self.half[1])


class ColumnScatter:
    def __init__(self, copies, qkv, fc1, room, by_hi, relay, full):
        at = copies.at
        self.qkv, self.fc1, self.room, self.came_hi = qkv, fc1, room, by_hi
        y, hi, lo, x, c = (at[n] for n in NAMES)
        rows = by_hi.shape[1]
        n_qkv, n_fc1 = qkv.shape[1], fc1.shape[1]
        self.rows, self.n_qkv, self.wide = rows, n_qkv, n_qkv + n_fc1
        hops = ((1 - lo, 1 - x), (1 - lo, x), (lo, 1 - x), (lo, x))
        places = [(hi_at * 2 + lo_at) * 2 + x_at for hi_at in (1 - hi, hi) for lo_at, x_at in hops]
        self.starts = [pl.multiple_of(place * 2 * rows, 128) for place in places]
        self.own = [pl.ds(pl.multiple_of(start + c * rows, 128), rows) for start in self.starts]
        self.by_c, self.by_hi = [], []
        for i, start in enumerate(self.starts):
            away = pl.ds(pl.multiple_of(start + (1 - c) * rows, 128), rows)
            here = pl.ds(i * rows, rows)
            self.by_c.append(
                (
                    copies.plan(qkv.at[away], room.at[here, pl.ds(0, n_qkv)], "c"),
                    copies.plan(fc1.at[away], room.at[here, pl.ds(n_qkv, n_fc1)], "c"),
                )
            )
            if i < 4:
                self.by_hi.append(copies.plan(room.at[here, pl.ds(0, self.wide)], by_hi.at[i], "hi"))

        def spot(lo_at, x_at):
            return full.at[(y * 2 + lo_at) * 2 + x_at]

        self.far = copies.plan(by_hi.at[0], relay, "lo")
        self.far_on = copies.plan(relay, spot(1 - lo, x), "x")
        self.by_lo = copies.plan(by_hi.at[1], spot(lo, x), "lo")
        self.by_x = copies.plan(by_hi.at[2], spot(lo, x), "x")
        self.mine = copies.move(by_hi.at[3], spot(lo, x))
        self.by_y = [
            copies.plan(by_hi.at[3], spot(lo, x), "y"),
            copies.plan(spot(1 - lo, x), spot(1 - lo, x), "y"),
            copies.plan(spot(lo, 1 - x), spot(lo, 1 - x), "y"),
            copies.plan(spot(1 - lo, 1 - x), spot(1 - lo, 1 - x), "y"),
        ]

    def send_c(self, i):
        for copy in self.by_c[i]:
            copy.start()

    def add_c(self, i):
        for copy in self.by_c[i]:
            copy.wait_recv()
        here = pl.ds(i * self.rows, self.rows)
        for ref, lanes in ((self.qkv, slice(0, self.n_qkv)), (self.fc1, slice(self.n_qkv, self.wide))):
            value = self.room[here, lanes].astype(F32) + ref[self.own[i]].astype(F32)
            self.room[here, lanes] = value.astype(BF16)

    def start_hi(self):
        self.by_hi[0].start()

    def add_hi(self, i):
        self.by_hi[i].wait_recv()
        if i < 3:
            self.by_hi[i + 1].start()
        other = self.room[pl.ds((4 + i) * self.rows, self.rows), : self.wide]
        self.came_hi[i] = (self.came_hi[i].astype(F32) + other.astype(F32)).astype(BF16)
        if i < 3:
            (self.far, self.by_lo, self.by_x)[i].start()
        else:
            self.mine.start()
            self.by_y[0].start()

    def relay_far(self):
        self.far.wait_recv()
        self.far_on.start()

    def relay_lo(self):
        self.by_lo.wait_recv()
        self.by_y[1].start()

    def relay_x(self):
        self.by_x.wait_recv()
        self.by_y[2].start()

    def relay_last(self):
        self.far_on.wait_recv()
        self.by_y[3].start()

    def finish(self):
        self.mine.wait()
        for copy in self.by_y:
            copy.wait_recv()


class SmallScatter:
    def __init__(self, copies, parts, came):
        at = copies.at
        self.parts, self.came, self.steps = parts, came, []
        base, count, spot = 0, 8, 0
        for name in ("hi", "lo", "x", "c"):
            away = parts.at[pl.ds(base + (1 - at[name]) * count, count)]
            base = base + at[name] * count
            self.steps.append((copies.plan(away, came.at[pl.ds(spot, count)], name), base, spot, count))
            spot += count
            count //= 2
        own = parts.at[pl.ds(base, 1)]
        self.steps.append((copies.plan(own, came.at[pl.ds(spot, 1)], "y"), base, spot, 1))
        self.base, self.spot = base, spot

    def send(self, step):
        self.steps[step][0].start()

    def add(self, step):
        copy, base, spot, count = self.steps[step]
        copy.wait_recv()
        if step < 4:
            for i in range(count):
                self.parts[base + i] += self.came[spot + i]
            self.send(step + 1)

    def total(self):
        return self.parts[self.base] + self.came[self.spot]


ROW_TILES, SEQUENCES, COLUMN_TILES = 5, 8, 8


def sequence_at(step):
    i = jnp.clip(step - ROW_TILES, 0, SEQUENCES - 1)
    return 2 * (1 - i // 4) + (1 - i % 2) + 4 * (1 - (i % 4) // 2)


def backward_kernel(
    y_ref, g_ref, hidden_ref, mixed_ref, heads_ref, slope_ref, norm_ref, qkv_ref, fc1_ref, fc2_ref, out_ref, tables_ref,
    a1_ref, a2_ref,
    y_out, dx_out, rows_mine, rows_other, full, dx_came, small_out,
    g_all, grads, qkv, fc1, part, came, y_stage, dx_stage, room, kept, rows_came, a1, a2, by_hi, relay,
    packed_sum, up_sum, column_total, vectors, parts, parts_came,
    send_sem, recv_sem, local_sem, free_c_sem,
):
    step = pl.program_id(0)
    at = {name: lax.axis_index(name) for name in NAMES}
    copies = Copies(at, send_sem, recv_sem, local_sem)
    n_fc1, n_mix, n_qkv = fc2_ref.shape[0], out_ref.shape[0], qkv_ref.shape[1]
    count, length, _ = g_all.shape
    tokens = count * length
    tile = n_mix
    y = TokenScatter(copies, y_ref, came, True, y_stage, room, y_out)
    dx = TokenScatter(copies, g_all, dx_came, False, dx_stage, room, dx_out)
    rows = RowScatter(copies, part, kept, rows_came, n_fc1 // 2, n_mix // 2)
    rows_by_y = copies.plan(rows_came, rows_other, "y")
    rows_store = copies.move(rows_came, rows_mine)
    columns = ColumnScatter(copies, qkv, fc1, part, by_hi, relay, full)
    small = SmallScatter(copies, parts, parts_came)
    load_g = copies.move(g_ref, g_all)
    loads = [copies.move(qkv_ref, qkv), copies.move(fc1_ref, fc1)]
    late_loads = [
        copies.move(fc2_ref, part.at[pl.ds(0, n_fc1)]),
        copies.move(out_ref, part.at[pl.ds(n_fc1, n_mix)]),
    ]

    def hidden_tile(i):
        return hidden_ref.at[:, pl.ds(i * tile, tile)]

    row_tiles = [
        (1, a1, 0, copies.move(hidden_tile(1), a1.at[0])),
        (3, a1, 1, copies.move(hidden_tile(3), a1.at[1])),
        (4, a2, 0, copies.move(mixed_ref, a2.at[0])),
        (0, a2, 1, copies.move(hidden_tile(0), a2.at[1])),
        (2, a1, 0, copies.move(hidden_tile(2), a1.at[0])),
    ]
    base = copies.local
    column_tiles = []
    for i, start in enumerate(columns.starts):
        copies.local = base + 2 * (i % 2)
        lanes = pl.ds(start, tile)
        column_tiles.append(
            [copies.move(a1_ref.at[:, lanes], a1.at[i % 2]), copies.move(a2_ref.at[:, lanes], a2.at[i % 2])]
        )

    def at_step(spot):
        return pl.when(step == spot)

    @at_step(0)
    def _():
        greet(at, NAMES)
        load_g.start()
        for _, _, _, copy in row_tiles[:4]:
            copy.start()
        y.send(3)
        for copy in loads:
            copy.start()
        packed_sum[...] = jnp.zeros_like(packed_sum)
        up_sum[...] = jnp.zeros_like(up_sum)
        load_g.wait()
        column_total[...] = jnp.sum(g_all[0].astype(F32), axis=0, keepdims=True)

    for spot, (i, ref, slot, copy) in enumerate(row_tiles):

        @at_step(spot)
        def _(spot=spot, i=i, ref=ref, slot=slot, copy=copy):
            copy.wait()
            value = dot(ref[slot], g_all[...].reshape(tokens, -1), TN)
            part[i * tile : (i + 1) * tile] = value.astype(BF16)
            if spot == 0:
                row_tiles[4][3].start()
            if spot == 2:
                rows.send_c(1)
                y.send(2)
            if spot == 3:
                rows.add_c(1)
                rows.send_y()
            if spot == 4:
                rows.send_c(0)

    first = ROW_TILES

    @at_step(first)
    def _():
        rows.add_c(0)
        rows.sent_c()
        for copy in late_loads:
            copy.start()
        for copy in column_tiles[0]:
            copy.start()
        for copy in loads + late_loads:
            copy.wait()

    @at_step(first + 1)
    def _():
        y.pass_second(3)
        y.send(1)

    @at_step(first + 4)
    def _():
        y.pass_second(2)
        y.send(0)

    @at_step(first + 5)
    def _():
        rows.send_hi()

    @at_step(first + 7)
    def _():
        y.pass_third()

    @pl.when((step >= first) & (step < first + SEQUENCES))
    def _():
        j = sequence_at(step)
        fc2, out = part.at[pl.ds(0, n_fc1)], part.at[pl.ds(n_fc1, n_mix)]
        here = pl.ds(pl.multiple_of(j * length, 16), length)
        grad_up = (dot(g_all[j], fc2[...], NT) * slope_ref[0]).astype(BF16)
        grads[here, n_qkv:] = grad_up
        up_sum[...] += jnp.sum(grad_up.astype(F32), axis=0, keepdims=True)

        grad_mixed = dot(g_all[j], out[...], NT).astype(BF16)
        queries = heads_ref[0, :, :HEAD_DIM]
        keys_all = heads_ref[0, :, HEAD_DIM : 2 * HEAD_DIM]
        values_all = heads_ref[0, :, 2 * HEAD_DIM :]
        probs = softmax(causal_scores(queries, keys_all))
        grad_probs = dot(grad_mixed, values_all, NT)
        grad_values = dot(probs.astype(BF16), grad_mixed, TN)
        inner = jnp.sum(grad_probs * probs, axis=-1, keepdims=True)
        grad_scores = (probs * (grad_probs - inner)).astype(BF16)
        grad_queries = turn(dot(grad_scores, keys_all) * SCALE, tables_ref, -1.0)
        grad_keys = turn(dot(grad_scores, queries, TN) * SCALE, tables_ref, -1.0)
        grads[here, :HEAD_DIM] = grad_queries.astype(BF16)
        grads[here, HEAD_DIM : 2 * HEAD_DIM] = grad_keys.astype(BF16)
        grads[here, 2 * HEAD_DIM : n_qkv] = grad_values.astype(BF16)
        packed_sum[...] += jnp.sum(grads[here, :n_qkv].astype(F32), axis=0, keepdims=True)

        g_all[j] = (
            dot(grads[here, :n_qkv], qkv[...], NT) * norm_ref[0:1]
            + dot(grads[here, n_qkv:], fc1[...], NT) * norm_ref[2:3]
        ).astype(BF16)

    first = ROW_TILES + SEQUENCES

    @at_step(first)
    def _():
        pl.semaphore_signal(
            free_c_sem, inc=1, device_id={"c": 1 - at["c"]}, device_id_type=pl.DeviceIdType.MESH
        )

    for i in range(COLUMN_TILES):

        @at_step(first + i)
        def _(i=i):
            if i < COLUMN_TILES - 1:
                for copy in column_tiles[i + 1]:
                    copy.start()
            for copy in column_tiles[i]:
                copy.wait()
            if i > 0:
                columns.add_c(i - 1)

    @pl.when(step >= first)
    def _():
        slot = lax.rem(step - first, 2)
        start = columns.starts[0]
        for i in range(1, COLUMN_TILES):
            start = jnp.where(step == first + i, columns.starts[i], start)
        here = pl.ds(pl.multiple_of(start, 128), tile)
        lane = lax.broadcasted_iota(jnp.int32, (tile, 128), 1)
        sides = jnp.zeros((tile, 128), F32)
        for at_lane, (ref, values, sums, lanes) in enumerate(
            ((qkv, a1, packed_sum, slice(0, n_qkv)), (fc1, a2, up_sum, slice(n_qkv, n_qkv + n_fc1)))
        ):
            value = dot(values[slot], grads[:, lanes], TN)
            weight = ref[here].astype(F32)
            ref[here] = value.astype(BF16)
            sides = jnp.where(lane == 2 * at_lane, jnp.sum(weight * value, axis=1, keepdims=True), sides)
            sides = jnp.where(lane == 2 * at_lane + 1, jnp.sum(weight * sums[...], axis=1, keepdims=True), sides)
        vectors[:, here] = jnp.transpose(sides)[:8]

    @at_step(first)
    def _():
        pl.semaphore_wait(free_c_sem, 1)

    for i in range(COLUMN_TILES):
        pl.when(step == first + i)(functools.partial(columns.send_c, i))

    @at_step(first)
    def _():
        dx.send(3)

    @at_step(first + 4)
    def _():
        dx.send(2)

    @at_step(first + 6)
    def _():
        y.last()

    @at_step(first + 7)
    def _():
        columns.add_c(7)
        parts[...] = jnp.zeros_like(parts)
        lines = []
        for i in (0, 2):
            gain, bias = norm_ref[i : i + 1], norm_ref[i + 1 : i + 2]
            bias_grad = vectors[i + 1 : i + 2]
            lines += [(vectors[i : i + 1] - bias * bias_grad) / gain, bias_grad]
        lines.append(column_total[...])
        for spot in range(16):
            for i, line in enumerate(lines):
                parts[spot, i : i + 1] = line[:, spot * 128 : (spot + 1) * 128]
        own = (at["y"] * 4 + at["lo"] * 2 + at["x"]) * 2
        for half in range(2):
            start = len(lines)
            for sums in (packed_sum, up_sum):
                units = sums.shape[1] // 256
                for i in range(units):
                    lanes = slice((half * units + i) * 128, (half * units + i + 1) * 128)
                    parts[own + half, start + i : start + i + 1] = sums[:, lanes]
                start += units
        small.send(0)
        dx.pass_second(3)
        dx.send(1)
        small.add(0)
        small.add(1)
        rows.add_hi()
        rows_by_y.start()
        rows_store.start()
        columns.start_hi()
        small.add(2)
        dx.pass_second(2)
        dx.send(0)
        small.add(3)
        columns.add_hi(0)
        small.add(4)
        small_out[...] = small.total()
        dx.pass_third()
        columns.relay_far()
        columns.add_hi(1)
        columns.relay_last()
        columns.relay_lo()
        dx.last()
        columns.add_hi(2)
        columns.relay_x()
        columns.add_hi(3)
        rows_by_y.wait_recv()
        rows_store.wait()
        columns.finish()
        y.sent()
        dx.sent()
        for copy in rows.by_y + rows.by_hi + [rows_by_y]:
            copy.wait_send()
        for pair in columns.by_c:
            for copy in pair:
                copy.wait_send()
        for copy in columns.by_hi + columns.by_y + [columns.far, columns.far_on, columns.by_lo, columns.by_x]:
            copy.wait_send()
        for small_step in small.steps:
            small_step[0].wait_send()


def backward(y_part, g_all, hidden, mixed, heads, slope, norm, qkv, fc1, fc2, out, tables, a1, a2):
    far = pl.BlockSpec(memory_space=pl.ANY)
    count, length, width = g_all.shape
    n_qkv, n_fc1, n_mix = qkv.shape[1], fc1.shape[1], out.shape[0]
    wide = n_qkv + n_fc1
    tokens = count * length
    a1, a2 = a1.reshape(tokens, width), a2.reshape(tokens, width)
    hidden, mixed = hidden.reshape(tokens, n_fc1), mixed.reshape(tokens, n_mix)
    own = (n_fc1 + n_mix) // 2
    size = width // 8
    chunks = scatter_chunks(length)
    longest = max(rows for _, rows, _ in chunks)

    def each(n):
        return pl.BlockSpec((1, length, n), lambda i: (sequence_at(i), 0, 0))

    outputs = [
        ((length, width), F32, far),
        ((length, width), F32, far),
        ((own // 2, width), BF16, far),
        ((own // 2, width), BF16, far),
        ((8, size // 2, wide), BF16, far),
        ((7, length, width), BF16, far),
        ((16, 128), F32, None),
    ]
    shapes = [jax.ShapeDtypeStruct(shape, kind) for shape, kind, _ in outputs]
    copies = 2 * 7 * len(chunks) + 9 + 28 + 5
    flops = 2 * tokens * width * (2 * n_qkv + 3 * n_fc1 + 2 * n_mix)
    return pl.pallas_call(
        backward_kernel,
        grid=(ROW_TILES + SEQUENCES + COLUMN_TILES,),
        in_specs=[far] * 4 + [each(n_qkv), each(n_fc1), whole(norm)] + [far] * 4 + [whole(tables), far, far],
        out_specs=[whole(s) if spec is None else spec for s, (_, _, spec) in zip(shapes, outputs)],
        out_shape=shapes,
        scratch_shapes=[
            pltpu.VMEM(g_all.shape, BF16),
            pltpu.VMEM((tokens, wide), BF16),
            pltpu.VMEM(qkv.shape, BF16),
            pltpu.VMEM(fc1.shape, BF16),
            pltpu.VMEM((n_fc1 + n_mix, width), BF16),
            pltpu.VMEM((7, length, width), BF16),
            pltpu.VMEM((1, longest, width), BF16),
            pltpu.VMEM((3, longest, width), BF16),
            pltpu.VMEM((longest, width), F32),
            pltpu.VMEM((own + own // 2, width), BF16),
            pltpu.VMEM((own // 2, width), BF16),
            pltpu.VMEM((2, tokens, size), BF16),
            pltpu.VMEM((2, tokens, size), BF16),
            pltpu.VMEM((4, size // 2, wide), BF16),
            pltpu.VMEM((size // 2, wide), BF16),
            pltpu.VMEM((1, n_qkv), F32),
            pltpu.VMEM((1, n_fc1), F32),
            pltpu.VMEM((1, width), F32),
            pltpu.VMEM((8, width), F32),
            pltpu.VMEM((16, 16, 128), F32),
            pltpu.VMEM((16, 16, 128), F32),
            pltpu.SemaphoreType.DMA((copies,)),
            pltpu.SemaphoreType.DMA((copies,)),
            pltpu.SemaphoreType.DMA((6 * len(chunks) + 16,)),
            pltpu.SemaphoreType.REGULAR,
        ],
        compiler_params=pltpu.CompilerParams(
            collective_id=2, has_side_effects=True, vmem_limit_bytes=63 * 2**20
        ),
        cost_estimate=pl.CostEstimate(flops=flops, bytes_accessed=10**8, transcendentals=0),
        name="backward",
    )(y_part, g_all, hidden, mixed, heads, slope, norm, qkv, fc1, fc2, out, tables, a1, a2)


def whole(array):
    return pl.BlockSpec(array.shape, lambda i: (0,) * array.ndim, pipeline_mode=pl.Buffered(1))


def body(
    tokens, ln1_gain, ln1_bias, ln2_gain, ln2_bias, qkv_weight, qkv_bias, out_weight, out_bias,
    fc1_weight, fc1_bias, fc2_weight, fc2_bias, cotangent, extra,
):
    bits = {name: lax.axis_index(name) for name in NAMES}
    vectors = [ln1_gain, ln1_bias, ln2_gain, ln2_bias, out_bias, fc2_bias, qkv_bias, fc1_bias]
    if extra > 1:
        join = functools.partial(lax.all_gather, axis_name="e", axis=0, tiled=True)
        vectors = [join(v) for v in vectors]
        qkv_weight, out_weight, fc1_weight, fc2_weight = [
            join(w) for w in (qkv_weight, out_weight, fc1_weight, fc2_weight)
        ]
    length, width = tokens.shape[1:]
    tables = jnp.asarray(rotary_tables(length))

    small = jnp.concatenate([v.reshape(-1, 128) for v in vectors], axis=0)
    small = jnp.pad(small, ((0, -small.shape[0] % 16), (0, 0)))
    (
        g_all, small, qkv_cols, fc1_cols, fc2_rows, out_rows, a1, a2, heads, mixed, hidden, slope, y_part
    ) = forward(tokens[0], cotangent[0], small, qkv_weight, fc1_weight, fc2_weight, out_weight, tables)
    small = small.astype(F32)
    norm = jnp.stack([small[:, i].reshape(-1) for i in range(8)])
    y_sum, dx, rows_total, rows_other, columns, _, small_grads = backward(
        y_part, g_all, hidden, mixed, heads, slope, norm, qkv_cols, fc1_cols, fc2_rows, out_rows, tables, a1, a2
    )
    output = tokens[0].astype(F32) + (norm[4] + norm[5])[None] + y_sum

    n_qkv, n_fc2 = qkv_cols.shape[1], fc2_weight.shape[0] // 2
    holds = bits["hi"] == bits["y"]
    first = jnp.where(holds, rows_total, rows_other)
    second = jnp.where(holds, rows_other, rows_total)
    fc2_grad = jnp.concatenate([first[:n_fc2], second[:n_fc2]], axis=0).astype(F32)
    out_grad = jnp.concatenate([first[n_fc2:], second[n_fc2:]], axis=0).astype(F32)
    qkv_grad = jnp.concatenate([columns[i, :, :n_qkv] for i in range(8)], axis=1).astype(F32)
    fc1_grad = jnp.concatenate([columns[i, :, n_qkv:] for i in range(8)], axis=1).astype(F32)
    cuts = np.cumsum([1, 1, 1, 1, 1, qkv_bias.shape[0] * extra // 128, fc1_bias.shape[0] * extra // 128])
    small_grads = [v.reshape(-1) for v in jnp.split(small_grads, cuts, axis=0)[:-1]]

    inputs = tokens[0].astype(F32)
    centred = inputs - jnp.mean(inputs, axis=-1, keepdims=True)
    scale = lax.rsqrt(jnp.mean(centred * centred, axis=-1, keepdims=True) + EPS)
    normed = centred * scale
    dx = scale * (
        dx - jnp.mean(dx, axis=-1, keepdims=True) - normed * jnp.mean(dx * normed, axis=-1, keepdims=True)
    )
    input_grad = cotangent[0].astype(F32) + dx

    weight_grads = [qkv_grad, out_grad, fc1_grad, fc2_grad]
    if extra > 1:
        scatter = functools.partial(lax.psum_scatter, axis_name="e", scatter_dimension=0, tiled=True)
        weight_grads = [scatter(v) for v in weight_grads]
        small_grads = [scatter(v) for v in small_grads]
    qkv_grad, out_grad, fc1_grad, fc2_grad = weight_grads
    gain1, bias1, gain2, bias2, total, packed_bias, up_bias = small_grads
    return (
        output.astype(BF16)[None],
        input_grad.astype(BF16)[None],
        gain1,
        bias1,
        gain2,
        bias2,
        qkv_grad,
        packed_bias,
        out_grad,
        total,
        fc1_grad,
        up_bias,
        fc2_grad,
        total,
    )


def solution(mesh):
    extra = mesh.shape["shard"] // 16
    axes = ("y", "hi", "lo", "x", "c", "e")
    fine = Mesh(mesh.devices.reshape(2, 2, 2, 2, 2, extra), axes)
    split = P(axes, None, None)
    row, flat = P(axes[1:], None), P(axes[1:])
    in_specs = (split, flat, flat, flat, flat, row, flat, row, flat, row, flat, row, flat, split)
    out_specs = (split, split, flat, flat, flat, flat, row, flat, row, flat, row, flat, row, flat)
    return jax.shard_map(
        functools.partial(body, extra=extra), mesh=fine, in_specs=in_specs, out_specs=out_specs, check_vma=False
    )
```

```python
import functools

import jax
import jax.numpy as jnp
import numpy as np
from jax import lax
from jax.experimental import pallas as pl
from jax.experimental.pallas import tpu as pltpu
from jax.sharding import Mesh
from jax.sharding import PartitionSpec as P

HEADS = 8
HEAD_DIM = 256
ROTARY = 64
EPS = 1e-05
NEG_FILL = -1e30
SCALE = HEAD_DIM ** (-0.5)
BF16 = jnp.bfloat16
F32 = jnp.float32
NT = (((1,), (1,)), ((), ()))
TN = (((0,), (0,)), ((), ()))
NN = (((1,), (0,)), ((), ()))


def dot(a, b, dims=NN):
    return lax.dot_general(a, b, dims, preferred_element_type=F32)


NAMES = ("y", "hi", "lo", "x", "c")
PLACE = {"lo": 1, "x": 2, "y": 4}


def chunks_of(length, plan):
    chunks, start, share = [], 0, 0
    for part, order in plan:
        share += part
        end = length * share // 288 * 16 if share < 18 else length
        chunks.append((start, end - start, order))
        start = end
    return chunks


SCATTER_CHUNKS = ((8, ("lo", "y", "x")), (5, ("x", "lo", "y")), (5, ("y", "lo", "x")))
SCATTER_EVENTS = (
    ("Y.first.0.3", "Y.first.1.3"),
    ("Y.first.1.2",),
    ("Y.second.1.3", "Y.first.2.3"),
    ("Y.second.0.3", "r.c1"),
    ("Y.second.1.2",),
    ("Y.second.2.3", "r.add1", "r.c0", "Y.first.2.2"),
    (),
    ("r.add0",),
    ("Y.second.2.2", "Y.first.0.1"),
    (),
    (),
    (),
    (),
    ("Y.first.2.1",),
    ("f.c0",),
    ("f.c1", "f.a0", "f.hi0"),
    ("Y.first.0.0", "f.c2", "f.a1", "Y.third.2"),
    ("f.c3", "f.a2"),
    ("f.c4", "f.a3"),
    ("Y.first.1.1", "r.hi", "f.c5", "f.a4"),
    ("f.c6", "Y.first.0.2", "f.a5", "f.h0"),
    ("f.c7", "f.a6", "Y.first.1.0"),
    ("Y.third.1", "f.a7", "X.first.1.3"),
    ("f.far", "X.first.1.1"),
    ("Y.second.0.2", "Y.third.0"),
    ("X.first.2.3", "Y.last.1", "f.y3", "X.first.0.3"),
    (),
    (),
    ("X.first.0.2",),
    ("X.first.1.0", "X.second.1.3", "Y.last.0", "X.first.1.2", "X.second.2.3", "X.first.2.2"),
    ("k.c0", "X.second.0.3"),
    ("k.c1", "k.a0"),
    ("k.c2", "k.a1"),
    ("f.hi1", "k.c3", "k.a2"),
    (
        "r.y2", "Y.first.2.0", "k.c4", "k.a3", "X.second.0.2", "k.a4", "X.second.1.2", "X.second.2.2", "X.first.0.1",
        "X.third.1",
    ),
    ("k.c5",),
    ("k.c6", "k.a5"),
    (
        "s.0", "Y.last.2", "f.h1", "k.c7", "k.a6", "k.a7", "f.hi2", "s.1", "X.first.2.1", "s.2", "s.3", "s.4",
        "X.first.0.0", "X.last.1", "X.third.0", "s.fin", "f.y1", "f.hi3", "X.first.2.0", "f.h2", "X.third.2", "k.hi0",
        "f.h3", "f.y2", "k.hi1", "k.h0", "X.last.0", "X.last.2", "k.hi2", "k.h1", "k.far", "r.fin", "k.y3", "f.fin",
        "k.hi3", "k.h2", "k.y1", "k.y2", "k.h3", "k.fin",
    ),
)


GATHER_CHUNKS = ((8, ("lo", "x", "y")), (7, ("lo", "y", "x")), (3, ("y", "x", "lo")))
GATHER_EVENTS = (
    (
        "s.0", "q.x0", "q.x1", "q.l0", "q.hi0", "q.c0", "f.x0", "f.x1", "f.l0", "f.hi0", "f.c0", "x.own.0.0",
        "x.own.2.0", "x.own.1.1", "s.1", "x.own.0.2", "s.2", "s.3", "s.4", "g.own.2.0", "x.r1.2.1", "q.l1", "q.c1",
        "x.own.0.1", "x.own.2.1", "q.hi1", "f.l1", "f.c1", "q.c2", "q.c4", "g.own.1.1", "x.own.1.2", "g.own.0.2",
        "q.hi2", "f.c2", "f.c4", "x.r2.1.0", "x.r2.2.1", "q.c3", "q.hi3", "q.c5", "x.r2.2.0", "f.hi1", "f.c3", "q.c6",
        "g.r1.2.1", "x.r2.0.0", "g.r2.1.0", "x.r1.2.2", "x.r1.0.2", "x.own.1.0", "x.r1.0.1", "f.hi2", "q.c7",
        "g.own.0.1", "x.own.2.2", "f.hi3", "g.r2.2.1", "f.c5", "g.own.2.1", "r.hi", "g.r1.2.2", "f.c6", "g.own.1.2",
        "x.r2.0.1", "g.r2.0.0", "g.r2.2.0", "o.hi", "f.c7", "g.own.0.0", "x.r1.1.1", "x.r1.1.2",
    ),
    ("g.own.1.0",),
    ("g.own.2.2",),
    (),
    ("x.r2.1.1",),
    ("o.y", "o.c0"),
    (),
    ("o.c1",),
    ("g.r1.0.1", "g.r1.1.1", "g.r1.0.2", "g.r1.1.2", "r.y", "r.c0", "g.r2.0.1", "g.r2.1.1", "r.c1"),
    (),
    (),
    (),
    (),
    (),
    (),
    (),
    (),
)


class Copies:
    def __init__(self, at, send_sem, recv_sem, local_sem):
        self.at, self.send_sem, self.recv_sem, self.local_sem = at, send_sem, recv_sem, local_sem
        self.remote, self.planned, self.local, self.seen = [], 0, 0, set()

    def plan(self, src, dst, axis, everywhere=True):
        spot = self.planned
        self.planned += 1
        copy = pltpu.make_async_remote_copy(
            src_ref=src,
            dst_ref=dst,
            send_sem=self.send_sem.at[spot],
            recv_sem=self.recv_sem.at[spot],
            device_id={axis: 1 - self.at[axis]},
            device_id_type=pl.DeviceIdType.MESH,
        )
        if everywhere:
            self.remote.append(copy)
        return copy

    def arrive(self, *copies):
        for copy in copies:
            if id(copy) not in self.seen:
                self.seen.add(id(copy))
                copy.wait_recv()

    def move(self, src, dst):
        copy = pltpu.make_async_copy(src, dst, self.local_sem.at[self.local])
        self.local += 1
        return copy


def greet(at, names):
    barrier = pltpu.get_barrier_semaphore()
    for name in names:
        pl.semaphore_signal(
            barrier, inc=1, device_id={name: 1 - at[name]}, device_id_type=pl.DeviceIdType.MESH
        )
    pl.semaphore_wait(barrier, len(names))


class TokenGather:
    def __init__(self, copies, own, full, name, events):
        self.copies, self.plans = copies, {}
        self.kept = copies.move(own, full.at[0])
        self.chunks = chunks_of(own.shape[0], GATHER_CHUNKS)
        for chunk, (start, rows, order) in enumerate(self.chunks):
            part = pl.ds(start, rows)
            one, two, _ = (PLACE[axis] for axis in order)
            hops = [(f"own.{chunk}.{i}", 0, axis) for i, axis in enumerate(order)]
            hops += [(f"r1.{chunk}.1", one, order[1]), (f"r1.{chunk}.2", one, order[2])]
            hops += [(f"r2.{chunk}.0", two, order[2]), (f"r2.{chunk}.1", one + two, order[2])]
            for label, block, axis in hops:
                src = own.at[part] if block == 0 else full.at[block, part]
                there = block + PLACE[axis]
                self.plans[chunk, there] = copies.plan(src, full.at[there, part], axis)
                events[f"{name}.{label}"] = functools.partial(self.send, chunk, block, there)

    def send(self, chunk, block, there):
        if block:
            self.copies.arrive(self.plans[chunk, block])
        self.plans[chunk, there].start()

    def take(self, block):
        for chunk in range(len(self.chunks)):
            self.copies.arrive(self.plans[chunk, block])

    def finish(self):
        for block in range(1, 8):
            self.take(block)
        self.kept.wait()


class TokenScatter:
    def __init__(self, copies, parts, came, far_parts, stage, room, total, name, events):
        self.copies, self.parts, self.came, self.far_parts = copies, parts, came, far_parts
        self.stage, self.room = stage, room
        self.chunks = chunks_of(parts.shape[1], SCATTER_CHUNKS)
        self.first, self.second, self.third, self.stores, self.loads, self.near = {}, {}, [], [], {}, {}
        base = copies.local
        for chunk, (start, rows, order) in enumerate(self.chunks):
            third, second, first = order
            part = pl.ds(start, rows)
            for slot in (3, 2, 1, 0):
                block = self.block(chunk, slot)
                src = parts.at[block + PLACE[first], part]
                self.first[chunk, slot] = copies.plan(src, came.at[slot, part], first)
                near = came.at[slot, part] if far_parts else parts.at[block, part]
                if slot > 1:
                    self.second[chunk, slot] = copies.plan(near, came.at[2 + slot, part], second)
                if slot == 1:
                    self.third.append(copies.plan(near, came.at[6, part], third))
                self.near[chunk, slot] = near
                if far_parts:
                    copies.local = base + chunk
                    self.loads[chunk, slot] = [copies.move(parts.at[block, part], stage.at[part])]
                else:
                    copies.local = base
                    self.loads[chunk, slot] = [
                        copies.move(came.at[i, part], stage.at[spot, pl.ds(0, rows)])
                        for spot, i in enumerate(self.terms(slot))
                    ]
                events[f"{name}.first.{chunk}.{slot}"] = self.first[chunk, slot].start
            events[f"{name}.second.{chunk}.3"] = functools.partial(self.pass_second, chunk, 3)
            events[f"{name}.second.{chunk}.2"] = functools.partial(self.pass_second, chunk, 2)
            events[f"{name}.third.{chunk}"] = functools.partial(self.pass_third, chunk)
            events[f"{name}.last.{chunk}"] = functools.partial(self.last, chunk)
        copies.local = base + max(3, len(self.chunks))
        for start, rows, _ in self.chunks:
            self.stores.append(copies.move(room.at[pl.ds(0, rows)], total.at[pl.ds(start, rows)]))

    def block(self, chunk, slot):
        third, second, _ = self.chunks[chunk][2]
        return PLACE[second] * (slot // 2) + PLACE[third] * (slot % 2)

    def terms(self, slot):
        return {0: (0, 4, 6), 1: (1, 5)}.get(slot, (slot,))

    def prepare(self):
        if self.far_parts:
            for chunk in range(len(self.chunks)):
                self.loads[chunk, 3][0].start()

    def add(self, chunk, slot):
        start, rows, _ = self.chunks[chunk]
        part = pl.ds(start, rows)
        self.copies.arrive(self.first[chunk, slot])
        loads = self.loads[chunk, slot]
        if self.far_parts:
            loads[0].wait()
            value = self.stage[part].astype(F32)
            for i in self.terms(slot):
                value = value + self.came[i, part].astype(F32)
            if slot > 0:
                self.loads[chunk, slot - 1][0].start()
            return value
        for copy in loads:
            copy.start()
        value = self.parts[self.block(chunk, slot), part].astype(F32)
        for spot, copy in enumerate(loads):
            copy.wait()
            value = value + self.stage[spot, :rows].astype(F32)
        return value

    def pass_second(self, chunk, slot):
        self.near[chunk, slot][...] = self.add(chunk, slot).astype(BF16)
        self.second[chunk, slot].start()

    def pass_third(self, chunk):
        self.copies.arrive(self.second[chunk, 3])
        self.near[chunk, 1][...] = self.add(chunk, 1).astype(BF16)
        self.third[chunk].start()

    def last(self, chunk):
        self.copies.arrive(self.second[chunk, 2], self.third[chunk])
        self.room[: self.chunks[chunk][1]] = self.add(chunk, 0)
        self.stores[chunk].start()
        self.stores[chunk].wait()


class ColumnGather:
    def __init__(self, copies, weight, full, relay, name, events):
        at = copies.at
        hi, lo, x, c = (at[n] for n in ("hi", "lo", "x", "c"))
        rows, width = weight.shape[0], full.shape[1]

        def block(lo_at, x_at):
            spot = (at["y"] * 2 + lo_at) * 2 + x_at
            return weight.at[:, pl.ds(pl.multiple_of(spot * width, 128), width)]

        def place(hi_at, lo_at, x_at):
            spot = ((hi_at * 2 + lo_at) * 2 + x_at) * 2 + c
            return full.at[pl.ds(pl.multiple_of(spot * rows, 128), rows)]

        mine = place(hi, lo, x)
        self.by_x = [copies.plan(block(1 - lo, 1 - x), relay, "x"), copies.plan(block(lo, 1 - x), mine, "x")]
        self.by_lo = [
            copies.plan(block(1 - lo, x), mine, "lo"),
            copies.plan(relay, place(hi, lo, 1 - x), "lo"),
        ]
        near = [place(hi, lo, x), place(hi, lo, 1 - x), place(hi, 1 - lo, x), place(hi, 1 - lo, 1 - x)]
        far = [place(1 - hi, lo, x), place(1 - hi, lo, 1 - x), place(1 - hi, 1 - lo, x), place(1 - hi, 1 - lo, 1 - x)]
        source = [block(lo, x)] + near[1:]
        self.by_hi = [copies.plan(src, dst, "hi") for src, dst in zip(source, near)]
        self.by_c = [copies.plan(src, dst, "c") for src, dst in zip(source + far, near + far)]
        self.kept = copies.move(block(lo, x), mine)
        self.copies = copies
        by_hi, by_c = self.by_hi, self.by_c
        x_then, lo_then = self.by_x, self.by_lo
        hops = [("x0", None, x_then[0]), ("x1", None, x_then[1]), ("l0", None, lo_then[0]), ("l1", x_then[0], lo_then[1])]
        came = [None, x_then[1], lo_then[0], lo_then[1]]
        hops += [(f"hi{i}", came[i], by_hi[i]) for i in range(4)]
        hops += [(f"c{i}", copy, by_c[i]) for i, copy in enumerate(came + by_hi)]
        for label, first, copy in hops:
            events[f"{name}.{label}"] = functools.partial(self.send, first, copy)

    def send(self, first, copy):
        if first is not None:
            self.copies.arrive(first)
        copy.start()

    def finish(self):
        self.copies.arrive(*self.by_c)
        self.kept.wait()


class RowGather:
    def __init__(self, copies, weight, full, name, events):
        at, rows = copies.at, weight.shape[0]
        half = rows // 2

        def spot(start, count):
            return full.at[pl.ds(pl.multiple_of(start, 16), count)]

        self.copies = copies
        self.holds = 1 - (at["hi"] + at["y"]) % 2
        first, second = spot(at["c"] * rows, half), spot(at["c"] * rows + half, half)
        there = spot(self.holds * (at["c"] * rows) + (1 - self.holds) * 2 * rows, half)
        source = weight.at[pl.ds(pl.multiple_of((1 - self.holds) * half, 16), half)]
        self.by_hi = copies.plan(source, there, "hi")
        self.by_y = copies.plan(spot(2 * rows, half), second, "y", everywhere=False)
        self.by_c = [copies.plan(first, first, "c"), copies.plan(second, second, "c")]
        self.kept = copies.move(weight, spot(at["c"] * rows, rows))
        for label, event in (("hi", self.start), ("y", self.relay), ("c0", self.first_to_c), ("c1", self.second_to_c)):
            events[f"{name}.{label}"] = event

    def start(self):
        self.by_hi.start()
        pl.when(self.holds == 1)(self.kept.start)

    def relay(self):
        self.copies.arrive(self.by_hi)

        @pl.when(self.holds == 1)
        def _():
            self.by_y.start()
            self.kept.wait()

    def first_to_c(self):
        self.relayed_before()
        self.by_c[0].start()

    def second_to_c(self):
        self.relayed_before()
        pl.when(self.holds == 0)(self.by_y.wait_recv)
        self.by_c[1].start()

    def relayed_before(self):
        assert id(self.by_hi) in self.copies.seen

    def finish(self):
        for copy in self.by_c:
            copy.wait_recv()

    def sent(self):
        pl.when(self.holds == 1)(self.by_y.wait_send)


class SmallGather:
    def __init__(self, copies, full):
        at = copies.at
        base = ((at["hi"] * 2 + at["lo"]) * 2 + at["x"]) * 2 + at["c"]
        self.own = full.at[pl.ds(base, 1)]
        self.steps, count = [], 1
        for name in ("c", "x", "lo", "hi"):
            part = full.at[pl.ds(base, count)]
            self.steps.append(copies.plan(part, part, name))
            base = base - at[name] * count
            count *= 2

    def step(self, at):
        if at > 0:
            self.steps[at - 1].wait_recv()
        if at < 4:
            self.steps[at].start()


def rotary_tables(length):
    places = np.arange(length, dtype=np.float32)
    frequency = (10000.0 ** (-np.arange(0, ROTARY, 2, dtype=np.float32) / ROTARY)).astype(np.float32)
    angles = places[:, None] * frequency[None, :]
    cosine, sine = np.cos(angles), np.sin(angles)
    half = ROTARY // 2
    tables = np.zeros((3, length, 2 * ROTARY), np.float32)
    tables[0] = 1.0
    tables[0, :, :half] = cosine
    tables[0, :, half:ROTARY] = cosine
    tables[1, :, :half] = -sine
    tables[2, :, half:ROTARY] = sine
    return tables


def turn(rows, tables, sign):
    half, wide = ROTARY // 2, 2 * ROTARY
    near = rows[:, :wide]
    ahead = pltpu.roll(near, wide - half, 1)
    behind = pltpu.roll(near, half, 1)
    near = near * tables[0] + sign * (ahead * tables[1] + behind * tables[2])
    return jnp.concatenate([near, rows[:, wide:]], axis=1)


def causal_scores(queries, keys_all):
    length = queries.shape[0]
    scores = dot(queries, keys_all, NT) * SCALE
    row = lax.broadcasted_iota(jnp.int32, (length, length), 0)
    col = lax.broadcasted_iota(jnp.int32, (length, length), 1)
    return jnp.where(row >= col, scores, NEG_FILL)


def softmax(scores):
    raised = jnp.exp(scores - jnp.max(scores, axis=-1, keepdims=True))
    return raised / jnp.sum(raised, axis=-1, keepdims=True)


def forward_kernel(
    x_ref, g_ref, small_ref, qkv_ref, fc1_ref, fc2_ref, out_ref, tables_ref,
    g_all, small_out, qkv_out, fc1_out, fc2_out, out_out,
    a1_ref, a2_ref, heads_ref, mixed_ref, hidden_ref, slope_ref, y_ref,
    x_all, small_all, qkv_all, fc1_all, fc2_all, out_all, norm, qkv_bias, fc1_bias, mixed_all, hidden_all,
    relay_qkv, relay_fc1, send_sem, recv_sem, local_sem,
):
    step = pl.program_id(0)
    at = {name: lax.axis_index(name) for name in NAMES}
    copies = Copies(at, send_sem, recv_sem, local_sem)
    events = {}
    small = SmallGather(copies, small_all)
    qkv = ColumnGather(copies, qkv_ref, qkv_all, relay_qkv, "q", events)
    fc1 = ColumnGather(copies, fc1_ref, fc1_all, relay_fc1, "f", events)
    fc2 = RowGather(copies, fc2_ref, fc2_all, "r", events)
    out = RowGather(copies, out_ref, out_all, "o", events)
    x = TokenGather(copies, x_ref, x_all, "x", events)
    g = TokenGather(copies, g_ref, g_all, "g", events)
    kept = [
        copies.move(src.at[pl.ds(0, dst.shape[0])], dst)
        for src, dst in ((qkv_all, qkv_out), (fc1_all, fc1_out), (fc2_all, fc2_out), (out_all, out_out))
    ]

    def spread_small():
        small.step(4)
        for spot in range(16):
            norm[:, spot * 128 : (spot + 1) * 128] = small_all[spot, :8].astype(F32)
        first = (at["y"] * 4 + at["lo"] * 2 + at["x"]) * 2
        for half in range(2):
            own = small_all[first + half].astype(F32)
            for bias, start in ((qkv_bias, 6), (fc1_bias, 6 + qkv_bias.shape[1] // 256)):
                rows = bias.shape[1] // 256
                for i in range(rows):
                    bias[:, (half * rows + i) * 128 : (half * rows + i + 1) * 128] = own[start + i : start + i + 1]

    for i in range(4):
        events[f"s.{i}"] = functools.partial(small.step, i)
    events["s.4"] = spread_small

    def before(spot):
        if spot == 0:
            greet(at, NAMES)
            small.own[...] = small_ref[...][None]
            for copy in (x.kept, g.kept, qkv.kept, fc1.kept):
                copy.start()
        for label in GATHER_EVENTS[spot]:
            events[label]()
        if spot == 0:
            x.kept.wait()
            qkv.finish()
            fc1.finish()
            kept[0].start()
            kept[1].start()
        elif spot < 8:
            x.take(spot)
        elif spot == 8:
            fc2.finish()
            out.finish()
            kept[2].start()
            kept[3].start()

    for spot in range(16):
        pl.when(step == spot)(functools.partial(before, spot))

    @pl.when(step < 8)
    def _():
        value = x_all[step].astype(F32)
        centred = value - jnp.mean(value, axis=-1, keepdims=True)
        var = jnp.mean(centred * centred, axis=-1, keepdims=True)
        normed = centred * lax.rsqrt(var + EPS)
        a1_ref[0] = (normed * norm[0:1] + norm[1:2]).astype(BF16)
        a2_ref[0] = (normed * norm[2:3] + norm[3:4]).astype(BF16)

        packed = dot(a1_ref[0], qkv_all[...]) + qkv_bias[...]
        queries = turn(packed[:, :HEAD_DIM], tables_ref, 1.0).astype(BF16)
        keys_all = turn(packed[:, HEAD_DIM : 2 * HEAD_DIM], tables_ref, 1.0).astype(BF16)
        values_all = packed[:, 2 * HEAD_DIM :].astype(BF16)
        heads_ref[0, :, :HEAD_DIM] = queries
        heads_ref[0, :, HEAD_DIM : 2 * HEAD_DIM] = keys_all
        heads_ref[0, :, 2 * HEAD_DIM :] = values_all
        probs = softmax(causal_scores(queries, keys_all)).astype(BF16)
        mixed_ref[0] = dot(probs, values_all).astype(BF16)
        mixed_all[step] = mixed_ref[0]

        upward = dot(a2_ref[0], fc1_all[...]) + fc1_bias[...]
        below = 0.5 * (1.0 + lax.erf(upward * np.float32(0.5**0.5)))
        hidden_ref[0] = (upward * below).astype(BF16)
        hidden_all[step] = hidden_ref[0]
        slope_ref[0] = below + upward * (jnp.exp(-0.5 * upward * upward) * np.float32((2 * np.pi) ** -0.5))

    @pl.when(step >= 8)
    def _():
        y = dot(hidden_all[step - 8], fc2_all[: hidden_ref.shape[2]])
        y_ref[0] = (y + dot(mixed_all[step - 8], out_all[: mixed_ref.shape[2]])).astype(BF16)

    @pl.when(step == 15)
    def _():
        small_out[...] = small_all[...]
        for label in GATHER_EVENTS[16]:
            events[label]()
        g.finish()
        for copy in kept:
            copy.wait()
        for copy in copies.remote:
            copy.wait_send()
        fc2.sent()
        out.sent()


def forward(tokens, cotangent, small, qkv_weight, fc1_weight, fc2_weight, out_weight, tables):
    far = pl.BlockSpec(memory_space=pl.ANY)
    length, width = tokens.shape
    rows = qkv_weight.shape[0]
    n_qkv, n_fc1, n_mix = qkv_weight.shape[1] // 8, fc1_weight.shape[1] // 8, out_weight.shape[0] * 2
    each = [(width, BF16), (width, BF16), (n_qkv, BF16), (n_mix, BF16), (n_fc1, BF16), (n_fc1, F32), (width, BF16)]
    count = 4 + 2 * 16 + 2 * 4 + 2 * 7 * len(GATHER_CHUNKS)
    weights = [(16 * rows, n_qkv), (16 * rows, n_fc1), (n_fc1, width), (n_mix, width)]
    flops = 2 * 8 * length * width * (n_qkv + n_fc1 + n_fc1 + n_mix)
    return pl.pallas_call(
        forward_kernel,
        grid=(16,),
        in_specs=[far, far, whole(small), far, far, far, far, whole(tables)],
        out_specs=[far, whole(jax.ShapeDtypeStruct((16,) + small.shape, BF16)), far, far, far, far]
        + [pl.BlockSpec((1, length, n), lambda i: (jnp.minimum(i, 7), 0, 0)) for n, _ in each[:-1]]
        + [pl.BlockSpec((1, length, width), lambda i: (jnp.maximum(i - 8, 0), 0, 0))],
        out_shape=[
            jax.ShapeDtypeStruct((8, length, width), BF16),
            jax.ShapeDtypeStruct((16,) + small.shape, BF16),
        ]
        + [jax.ShapeDtypeStruct(shape, BF16) for shape in weights]
        + [jax.ShapeDtypeStruct((8, length, n), kind) for n, kind in each],
        scratch_shapes=[
            pltpu.VMEM((8, length, width), BF16),
            pltpu.VMEM((16,) + small.shape, BF16),
            pltpu.VMEM(weights[0], BF16),
            pltpu.VMEM(weights[1], BF16),
            pltpu.VMEM((n_fc1 * 5 // 4, width), BF16),
            pltpu.VMEM((n_mix * 5 // 4, width), BF16),
            pltpu.VMEM((8, width), F32),
            pltpu.VMEM((1, n_qkv), F32),
            pltpu.VMEM((1, n_fc1), F32),
            pltpu.VMEM((8, length, n_mix), BF16),
            pltpu.VMEM((8, length, n_fc1), BF16),
            pltpu.VMEM((rows, n_qkv), BF16),
            pltpu.VMEM((rows, n_fc1), BF16),
            pltpu.SemaphoreType.DMA((count,)),
            pltpu.SemaphoreType.DMA((count,)),
            pltpu.SemaphoreType.DMA((10,)),
        ],
        compiler_params=pltpu.CompilerParams(
            collective_id=1, has_side_effects=True, vmem_limit_bytes=60 * 2**20
        ),
        cost_estimate=pl.CostEstimate(flops=flops, bytes_accessed=10**8, transcendentals=0),
        name="forward",
    )(tokens, cotangent, small, qkv_weight, fc1_weight, fc2_weight, out_weight, tables)


def add_rows(dst, dst_row, src, src_row, count, lanes=None, src_lanes=None):
    lanes = lanes or slice(None)
    src_lanes = src_lanes or lanes
    for start in range(0, count, 64):
        here = pl.ds(pl.multiple_of(dst_row + start, 16), 64)
        there = pl.ds(pl.multiple_of(src_row + start, 16), 64)
        dst[here, lanes] = (dst[here, lanes].astype(F32) + src[there, src_lanes].astype(F32)).astype(BF16)


class RowScatter:
    def __init__(self, copies, wide, slim, kept, came, n_fc2, n_out, other, events):
        at = copies.at
        c = at["c"]
        self.copies, self.kept, self.came, self.wide, self.slim = copies, kept, came, wide, slim
        self.holds = 1 - (at["hi"] + at["y"]) % 2
        own, half = n_fc2 + n_out, (n_fc2 // 2, n_out // 2)
        width, tile = kept.shape[1], 2 * n_out
        self.cuts = [(wide, i, i * 2 * n_fc2, wide.shape[1]) for i in range(width // wide.shape[1])]
        self.slim_cuts = [
            (slim, i, i * tile, min(slim.shape[1], width - i * slim.shape[1]))
            for i in range(-(-width // slim.shape[1]))
        ]

        def rows(ref, start, count):
            return ref.at[pl.ds(pl.multiple_of(start, 16), count)]

        self.pieces = []
        for side in range(2):
            pieces = []
            for cuts, size, n, to in (
                (self.cuts, n_fc2, half[0], side * half[0]),
                (self.slim_cuts, n_out, half[1], n_fc2 + side * half[1]),
            ):
                for ref, i, first, lanes in cuts:
                    step = ref.shape[1]
                    pieces.append((ref, first + side * n, size, n, to, slice(i * step, i * step + lanes), lanes))
            self.pieces.append(pieces)
        self.c = c
        self.by_c = []
        for pieces in self.pieces:
            made = []
            for ref, first, size, n, to, there, lanes in pieces:
                src = ref.at[pl.ds(pl.multiple_of(first + (1 - c) * size, 16), n), pl.ds(0, lanes)]
                dst = kept.at[pl.ds(to, n), pl.ds(there.start, lanes)]
                made.append(copies.plan(src, dst, "c"))
            self.by_c.append(made)
        self.by_y = [
            copies.plan(rows(kept, half[0], half[0]), rows(kept, own, half[0]), "y"),
            copies.plan(rows(kept, n_fc2 + half[1], half[1]), rows(kept, own + half[0], half[1]), "y"),
        ]
        holds = self.holds
        sent = [holds * own, holds * (own + half[0]) + (1 - holds) * n_fc2]
        self.keeps = [(1 - holds) * own, (1 - holds) * (own + half[0]) + holds * n_fc2]
        self.by_hi = [
            copies.plan(rows(kept, sent[0], half[0]), rows(came, 0, half[0]), "hi"),
            copies.plan(rows(kept, sent[1], half[1]), rows(came, half[0], half[1]), "hi"),
        ]
        self.half = half
        self.on_y = copies.plan(came, other, "y")
        events["r.c1"] = functools.partial(self.send, self.by_c[1])
        events["r.c0"] = functools.partial(self.send, self.by_c[0])
        events["r.add1"] = functools.partial(self.add_c, 1)
        events["r.hi"] = self.send_hi
        events["r.fin"] = functools.partial(copies.arrive, self.on_y)

    def store_tile(self, i, value):
        size = value.shape[0]
        cuts = self.slim_cuts if i is None else self.cuts
        for ref, cut, first, lanes in cuts:
            start = first if i is None else first + i * size
            ref[start : start + size, :lanes] = value[:, cut * ref.shape[1] : cut * ref.shape[1] + lanes].astype(BF16)

    def send(self, made):
        for copy in made:
            copy.start()

    def add_c(self, side):
        for copy, (ref, first, size, n, to, there, lanes) in zip(self.by_c[side], self.pieces[side]):
            self.copies.arrive(copy)
            add_rows(self.kept, to, ref, first + self.c * size, n, there, slice(0, lanes))
        if side == 1:
            self.send(self.by_y)

    def sent_c(self):
        for copy in self.by_c[0] + self.by_c[1]:
            copy.wait_send()

    def send_hi(self):
        self.copies.arrive(*self.by_y)
        self.send(self.by_hi)

    def add_hi(self):
        self.copies.arrive(*self.by_hi)
        add_rows(self.came, 0, self.kept, self.keeps[0], self.half[0])
        add_rows(self.came, self.half[0], self.kept, self.keeps[1], self.half[1])
        self.on_y.start()


class ColumnScatter:
    def __init__(self, copies, starts, tile, room, by_hi, relay, full, name, events):
        at = copies.at
        self.copies, self.tile, self.room, self.came_hi = copies, tile, room, by_hi
        y, lo, x, c = (at[n] for n in ("y", "lo", "x", "c"))
        self.c = c
        self.by_c = [copies.plan(tile(i, 1 - c), room(i), "c") for i in range(8)]
        self.by_hi = [copies.plan(room(i), by_hi.at[i], "hi") for i in range(4)]

        def spot(lo_at, x_at):
            return full.at[(y * 2 + lo_at) * 2 + x_at]

        self.far = copies.plan(by_hi.at[0], relay, "lo")
        self.far_on = copies.plan(relay, spot(1 - lo, x), "x")
        self.by_lo = copies.plan(by_hi.at[1], spot(lo, x), "lo")
        self.by_x = copies.plan(by_hi.at[2], spot(lo, x), "x")
        self.mine = copies.move(by_hi.at[3], spot(lo, x))
        self.by_y = [
            copies.plan(by_hi.at[3], spot(lo, x), "y"),
            copies.plan(spot(1 - lo, x), spot(1 - lo, x), "y"),
            copies.plan(spot(lo, 1 - x), spot(lo, 1 - x), "y"),
            copies.plan(spot(1 - lo, 1 - x), spot(1 - lo, 1 - x), "y"),
        ]
        for i in range(8):
            events[f"{name}.c{i}"] = self.by_c[i].start
            events[f"{name}.a{i}"] = functools.partial(self.add_c, i)
        for i in range(4):
            events[f"{name}.hi{i}"] = self.by_hi[i].start
            events[f"{name}.h{i}"] = functools.partial(self.add_hi, i)
        for label, first, then in (
            ("far", self.far, self.far_on),
            ("y1", self.by_lo, self.by_y[1]),
            ("y2", self.by_x, self.by_y[2]),
            ("y3", self.far_on, self.by_y[3]),
        ):
            events[f"{name}.{label}"] = functools.partial(self.relay, first, then)
        events[f"{name}.fin"] = self.finish

    def add_c(self, i):
        self.copies.arrive(self.by_c[i])
        here = self.room(i)
        here[...] = (here[...].astype(F32) + self.tile(i, self.c)[...].astype(F32)).astype(BF16)

    def add_hi(self, i):
        self.copies.arrive(self.by_hi[i])
        self.came_hi[i] = (self.came_hi[i].astype(F32) + self.room(4 + i)[...].astype(F32)).astype(BF16)
        if i < 3:
            (self.far, self.by_lo, self.by_x)[i].start()
        else:
            self.mine.start()
            self.by_y[0].start()

    def relay(self, first, then):
        self.copies.arrive(first)
        then.start()

    def finish(self):
        self.mine.wait()
        self.copies.arrive(*self.by_y)


class SmallScatter:
    def __init__(self, copies, parts, came):
        at = copies.at
        self.copies, self.parts, self.came, self.steps = copies, parts, came, []
        base, count, spot = 0, 8, 0
        for name in ("hi", "lo", "x", "c"):
            away = parts.at[pl.ds(base + (1 - at[name]) * count, count)]
            base = base + at[name] * count
            self.steps.append((copies.plan(away, came.at[pl.ds(spot, count)], name), base, spot, count))
            spot += count
            count //= 2
        own = parts.at[pl.ds(base, 1)]
        self.steps.append((copies.plan(own, came.at[pl.ds(spot, 1)], "y"), base, spot, 1))
        self.base, self.spot = base, spot

    def step(self, step):
        if step > 0:
            copy, base, spot, count = self.steps[step - 1]
            self.copies.arrive(copy)
            for i in range(count):
                self.parts[base + i] += self.came[spot + i]
        self.steps[step][0].start()

    def total(self):
        self.copies.arrive(self.steps[4][0])
        return self.parts[self.base] + self.came[self.spot]


ROW_TILES, SEQUENCES, COLUMN_TILES = 5, 8, 8
UP_AT = ROW_TILES
FC1_AT = UP_AT + SEQUENCES
DX_AT = FC1_AT + COLUMN_TILES
QKV_AT = DX_AT + SEQUENCES
STEPS = QKV_AT + COLUMN_TILES


def sequence_at(step):
    i = jnp.clip(step - DX_AT, 0, SEQUENCES - 1)
    return 2 * (1 - i // 4) + (1 - i % 2) + 4 * (1 - (i % 4) // 2)


def backward_kernel(
    y_ref, g_ref, hidden_ref, mixed_ref, heads_ref, slope_ref, norm_ref, qkv_ref, fc1_ref, fc2_ref, out_ref, tables_ref,
    a1_ref, a2_ref,
    y_out, dx_out, rows_mine, rows_other, full_qkv, full_fc1, dx_came, small_out,
    g_all, grads, qkv, fc1, part, came, y_stage, dx_stage, room, kept, rows_came, a1, a2,
    qkv_hi, fc1_hi, qkv_relay, fc1_relay, packed_sum, up_sum, column_total, vectors, parts, parts_came,
    send_sem, recv_sem, local_sem, free_sem, free_again_sem,
):
    step = pl.program_id(0)
    at = {name: lax.axis_index(name) for name in NAMES}
    copies = Copies(at, send_sem, recv_sem, local_sem)
    events = {}
    n_fc1, n_mix, n_qkv = fc2_ref.shape[0], out_ref.shape[0], qkv_ref.shape[1]
    count, length, _ = g_all.shape
    tokens, tile = count * length, n_mix
    core = tile // 2
    y, hi, lo, x, c = (at[n] for n in NAMES)
    scatter_y = TokenScatter(copies, y_ref, came, True, y_stage, room, y_out, "Y", events)
    TokenScatter(copies, g_all, dx_came, False, dx_stage, room, dx_out, "X", events)
    rows = RowScatter(copies, fc1, qkv, kept, rows_came, n_fc1 // 2, n_mix // 2, rows_other, events)
    rows_store = copies.move(rows_came, rows_mine)

    hops = ((1 - lo, 1 - x), (1 - lo, x), (lo, 1 - x), (lo, x))
    places = [(hi_at * 2 + lo_at) * 2 + x_at for hi_at in (1 - hi, hi) for lo_at, x_at in hops]
    starts = [pl.multiple_of(place * tile, 128) for place in places]

    def fc1_tile(i, of):
        start = 4 * core + i % 4 // 2 * tile
        return part.at[pl.ds(pl.multiple_of(start + of * core, 16), core), pl.ds(i % 2 * n_fc1, n_fc1)]

    def fc1_room(i):
        return part.at[pl.ds(i % 4 * core, core), pl.ds(i // 4 * n_fc1, n_fc1)]

    def qkv_tile(i, of):
        return qkv.at[pl.ds(pl.multiple_of(starts[i] + of * core, 128), core)]

    def qkv_room(i):
        return part.at[pl.ds((4 + i % 4) * core, core), pl.ds(i // 4 * n_qkv, n_qkv)]

    fc1_out = ColumnScatter(copies, starts, fc1_tile, fc1_room, fc1_hi, fc1_relay, full_fc1, "f", events)
    ColumnScatter(copies, starts, qkv_tile, qkv_room, qkv_hi, qkv_relay, full_qkv, "k", events)
    small = SmallScatter(copies, parts, parts_came)
    load_g = copies.move(g_ref, g_all)
    early_loads = [
        copies.move(fc2_ref, part.at[pl.ds(0, n_fc1)]),
        copies.move(out_ref, part.at[pl.ds(n_fc1, n_mix)]),
    ]
    loads = [copies.move(qkv_ref, qkv), copies.move(fc1_ref, fc1)]

    def hidden_tile(i):
        return hidden_ref.at[:, pl.ds(i * tile, tile)]

    row_tiles = [
        (1, a1, 0, copies.move(hidden_tile(1), a1.at[0])),
        (3, a1, 1, copies.move(hidden_tile(3), a1.at[1])),
        (None, a2, 0, copies.move(mixed_ref, a2.at[0])),
        (0, a2, 1, copies.move(hidden_tile(0), a2.at[1])),
        (2, a1, 0, copies.move(hidden_tile(2), a1.at[0])),
    ]

    def column_loads(src, dst):
        base, made = copies.local, []
        for i, start in enumerate(starts):
            copies.local = base + i % 2
            made.append(copies.move(src.at[:, pl.ds(start, tile)], dst.at[i % 2]))
        copies.local = base + 2
        return made

    a1_loads, a2_loads = column_loads(a1_ref, a1), column_loads(a2_ref, a2)

    def start_small():
        parts[...] = jnp.zeros_like(parts)
        lines = []
        for i in (0, 2):
            gain, bias = norm_ref[i : i + 1], norm_ref[i + 1 : i + 2]
            bias_grad = vectors[i + 1 : i + 2]
            lines += [(vectors[i : i + 1] - bias * bias_grad) / gain, bias_grad]
        lines.append(column_total[...])
        for spot in range(16):
            for i, line in enumerate(lines):
                parts[spot, i : i + 1] = line[:, spot * 128 : (spot + 1) * 128]
        own = (y * 4 + lo * 2 + x) * 2
        for half in range(2):
            start = len(lines)
            for sums in (packed_sum, up_sum):
                units = sums.shape[1] // 256
                for i in range(units):
                    lanes = slice((half * units + i) * 128, (half * units + i + 1) * 128)
                    parts[own + half, start + i : start + i + 1] = sums[:, lanes]
                start += units
        small.step(0)

    def end_rows():
        rows.add_hi()
        rows_store.start()

    def end_small():
        small_out[...] = small.total()

    def load_weights():
        rows.add_c(0)
        rows.sent_c()
        for copy in loads:
            copy.start()

    events["r.add0"], events["r.y2"] = load_weights, end_rows
    events["s.0"], events["s.fin"] = start_small, end_small
    for i in range(1, 5):
        events[f"s.{i}"] = functools.partial(small.step, i)

    def tell(sem):
        pl.semaphore_signal(sem, inc=1, device_id={"c": 1 - c}, device_id_type=pl.DeviceIdType.MESH)

    def before(spot):
        if spot == 0:
            greet(at, NAMES)
            load_g.start()
            for _, _, _, copy in row_tiles[:4]:
                copy.start()
            scatter_y.prepare()
        if spot == FC1_AT + 1:
            pl.semaphore_wait(free_sem, 1)
        if spot == QKV_AT + 1:
            pl.semaphore_wait(free_again_sem, 1)
        for label in SCATTER_EVENTS[spot]:
            events[label]()
        if spot == 0:
            for copy in early_loads:
                copy.start()
            packed_sum[...] = jnp.zeros_like(packed_sum)
            up_sum[...] = jnp.zeros_like(up_sum)
            load_g.wait()
            column_total[...] = jnp.sum(g_all[0].astype(F32), axis=0, keepdims=True)
        if spot == UP_AT:
            for copy in early_loads:
                copy.wait()
            for copy in a1_loads[:2] + a2_loads[:2]:
                copy.start()
        if FC1_AT <= spot < DX_AT:
            i = spot - FC1_AT
            if i == 0:
                tell(free_sem)
                for copy in loads:
                    copy.wait()
            if 0 < i < COLUMN_TILES - 1:
                a2_loads[i + 1].start()
            a2_loads[i].wait()
            if i >= 4:
                fc1_out.by_c[i - 4].wait_send()
        if spot == QKV_AT:
            for copy in fc1_out.by_c[4:]:
                copy.wait_send()
            tell(free_again_sem)
        if spot >= QKV_AT:
            i = spot - QKV_AT
            if 0 < i < COLUMN_TILES - 1:
                a1_loads[i + 1].start()
            a1_loads[i].wait()

    for spot in range(STEPS):
        pl.when(step == spot)(functools.partial(before, spot))

    for spot, (i, ref, slot, copy) in enumerate(row_tiles):

        @pl.when(step == spot)
        def _(spot=spot, i=i, ref=ref, slot=slot, copy=copy):
            copy.wait()
            rows.store_tile(i, dot(ref[slot], g_all[...].reshape(tokens, -1), TN))
            if spot == 0:
                row_tiles[4][3].start()

    @pl.when((step >= UP_AT) & (step < FC1_AT))
    def _():
        j = step - UP_AT
        here = pl.ds(pl.multiple_of(j * length, 16), length)
        grad_up = (dot(g_all[j], part[:n_fc1], NT) * slope_ref[0]).astype(BF16)
        grads[here, n_qkv:] = grad_up
        up_sum[...] += jnp.sum(grad_up.astype(F32), axis=0, keepdims=True)

    @pl.when((step >= DX_AT) & (step < QKV_AT))
    def _():
        j = sequence_at(step)
        here = pl.ds(pl.multiple_of(j * length, 16), length)
        grad_mixed = dot(g_all[j], part[n_fc1:], NT).astype(BF16)
        queries = heads_ref[0, :, :HEAD_DIM]
        keys_all = heads_ref[0, :, HEAD_DIM : 2 * HEAD_DIM]
        values_all = heads_ref[0, :, 2 * HEAD_DIM :]
        probs = softmax(causal_scores(queries, keys_all))
        grad_probs = dot(grad_mixed, values_all, NT)
        grad_values = dot(probs.astype(BF16), grad_mixed, TN)
        inner = jnp.sum(grad_probs * probs, axis=-1, keepdims=True)
        grad_scores = (probs * (grad_probs - inner)).astype(BF16)
        grad_queries = turn(dot(grad_scores, keys_all) * SCALE, tables_ref, -1.0)
        grad_keys = turn(dot(grad_scores, queries, TN) * SCALE, tables_ref, -1.0)
        grads[here, :HEAD_DIM] = grad_queries.astype(BF16)
        grads[here, HEAD_DIM : 2 * HEAD_DIM] = grad_keys.astype(BF16)
        grads[here, 2 * HEAD_DIM : n_qkv] = grad_values.astype(BF16)
        packed_sum[...] += jnp.sum(grads[here, :n_qkv].astype(F32), axis=0, keepdims=True)

        g_all[j] = (
            dot(grads[here, :n_qkv], qkv[...], NT) * norm_ref[0:1]
            + dot(grads[here, n_qkv:], fc1[...], NT) * norm_ref[2:3]
        ).astype(BF16)

    def column_tile(first, values, ref, lanes, sums, line, store):
        i = step - first
        start = starts[0]
        for spot in range(1, COLUMN_TILES):
            start = jnp.where(i == spot, starts[spot], start)
        here = pl.ds(pl.multiple_of(start, 128), tile)
        value = dot(values[lax.rem(i, 2)], grads[:, lanes], TN)
        weight = ref[here].astype(F32)
        store(i, here, value.astype(BF16))
        lane = lax.broadcasted_iota(jnp.int32, (tile, 128), 1)
        sides = jnp.where(
            lane == 0, jnp.sum(weight * value, axis=1, keepdims=True), jnp.sum(weight * sums[...], axis=1, keepdims=True)
        )
        vectors[line : line + 2, here] = jnp.transpose(sides)[:2]

    @pl.when((step >= FC1_AT) & (step < DX_AT))
    def _():
        def store(i, here, value):
            start = pl.multiple_of(4 * core + lax.rem(i, 4) // 2 * tile, 16)
            for side in range(2):

                @pl.when(lax.rem(i, 2) == side)
                def _():
                    part[pl.ds(start, tile), side * n_fc1 : (side + 1) * n_fc1] = value

        column_tile(FC1_AT, a2, fc1, slice(n_qkv, n_qkv + n_fc1), up_sum, 2, store)

    @pl.when(step >= QKV_AT)
    def _():
        def store(i, here, value):
            qkv[here] = value

        column_tile(QKV_AT, a1, qkv, slice(0, n_qkv), packed_sum, 0, store)

    @pl.when(step == STEPS - 1)
    def _():
        for label in SCATTER_EVENTS[STEPS]:
            events[label]()
        rows_store.wait()
        done = rows.by_c[0] + rows.by_c[1] + fc1_out.by_c
        for copy in copies.remote:
            if not any(copy is other for other in done):
                copy.wait_send()


def backward(y_part, g_all, hidden, mixed, heads, slope, norm, qkv, fc1, fc2, out, tables, a1, a2):
    far = pl.BlockSpec(memory_space=pl.ANY)
    count, length, width = g_all.shape
    n_qkv, n_fc1, n_mix = qkv.shape[1], fc1.shape[1], out.shape[0]
    wide = n_qkv + n_fc1
    tokens = count * length
    a1, a2 = a1.reshape(tokens, width), a2.reshape(tokens, width)
    hidden, mixed = hidden.reshape(tokens, n_fc1), mixed.reshape(tokens, n_mix)
    own = (n_fc1 + n_mix) // 2
    size = width // 8
    chunks = chunks_of(length, SCATTER_CHUNKS)
    longest = max(rows for _, rows, _ in chunks)

    outputs = [
        ((length, width), F32, far),
        ((length, width), F32, far),
        ((own // 2, width), BF16, far),
        ((own // 2, width), BF16, far),
        ((8, size // 2, n_qkv), BF16, far),
        ((8, size // 2, n_fc1), BF16, far),
        ((7, length, width), BF16, far),
        ((16, 128), F32, None),
    ]
    shapes = [jax.ShapeDtypeStruct(shape, kind) for shape, kind, _ in outputs]
    copies = 2 * 7 * len(chunks) + 15 + 40 + 5
    flops = 2 * tokens * width * (2 * n_qkv + 3 * n_fc1 + 2 * n_mix)
    return pl.pallas_call(
        backward_kernel,
        grid=(STEPS,),
        in_specs=[far] * 4
        + [
            pl.BlockSpec((1, length, n_qkv), lambda i: (sequence_at(i), 0, 0)),
            pl.BlockSpec((1, length, n_fc1), lambda i: (jnp.clip(i - UP_AT, 0, SEQUENCES - 1), 0, 0)),
            whole(norm),
        ]
        + [far] * 4
        + [whole(tables), far, far],
        out_specs=[whole(s) if spec is None else spec for s, (_, _, spec) in zip(shapes, outputs)],
        out_shape=shapes,
        scratch_shapes=[
            pltpu.VMEM(g_all.shape, BF16),
            pltpu.VMEM((tokens, wide), BF16),
            pltpu.VMEM(qkv.shape, BF16),
            pltpu.VMEM(fc1.shape, BF16),
            pltpu.VMEM((n_fc1 + n_mix, width), BF16),
            pltpu.VMEM((7, length, width), BF16),
            pltpu.VMEM((length, width), BF16),
            pltpu.VMEM((3, longest, width), BF16),
            pltpu.VMEM((longest, width), F32),
            pltpu.VMEM((own + own // 2, width), BF16),
            pltpu.VMEM((own // 2, width), BF16),
            pltpu.VMEM((2, tokens, size), BF16),
            pltpu.VMEM((2, tokens, size), BF16),
            pltpu.VMEM((4, size // 2, n_qkv), BF16),
            pltpu.VMEM((4, size // 2, n_fc1), BF16),
            pltpu.VMEM((size // 2, n_qkv), BF16),
            pltpu.VMEM((size // 2, n_fc1), BF16),
            pltpu.VMEM((1, n_qkv), F32),
            pltpu.VMEM((1, n_fc1), F32),
            pltpu.VMEM((1, width), F32),
            pltpu.VMEM((8, width), F32),
            pltpu.VMEM((16, 16, 128), F32),
            pltpu.VMEM((16, 16, 128), F32),
            pltpu.SemaphoreType.DMA((copies,)),
            pltpu.SemaphoreType.DMA((copies,)),
            pltpu.SemaphoreType.DMA((4 * max(3, len(chunks)) + 20,)),
            pltpu.SemaphoreType.REGULAR,
            pltpu.SemaphoreType.REGULAR,
        ],
        compiler_params=pltpu.CompilerParams(
            collective_id=2, has_side_effects=True, vmem_limit_bytes=63 * 2**20
        ),
        cost_estimate=pl.CostEstimate(flops=flops, bytes_accessed=10**8, transcendentals=0),
        name="backward",
    )(y_part, g_all, hidden, mixed, heads, slope, norm, qkv, fc1, fc2, out, tables, a1, a2)


def whole(array):
    return pl.BlockSpec(array.shape, lambda i: (0,) * array.ndim, pipeline_mode=pl.Buffered(1))


def body(
    tokens, ln1_gain, ln1_bias, ln2_gain, ln2_bias, qkv_weight, qkv_bias, out_weight, out_bias,
    fc1_weight, fc1_bias, fc2_weight, fc2_bias, cotangent, extra,
):
    bits = {name: lax.axis_index(name) for name in NAMES}
    vectors = [ln1_gain, ln1_bias, ln2_gain, ln2_bias, out_bias, fc2_bias, qkv_bias, fc1_bias]
    if extra > 1:
        join = functools.partial(lax.all_gather, axis_name="e", axis=0, tiled=True)
        vectors = [join(v) for v in vectors]
        qkv_weight, out_weight, fc1_weight, fc2_weight = [
            join(w) for w in (qkv_weight, out_weight, fc1_weight, fc2_weight)
        ]
    length, width = tokens.shape[1:]
    tables = jnp.asarray(rotary_tables(length))

    small = jnp.concatenate([v.reshape(-1, 128) for v in vectors], axis=0)
    small = jnp.pad(small, ((0, -small.shape[0] % 16), (0, 0)))
    (
        g_all, small, qkv_cols, fc1_cols, fc2_rows, out_rows, a1, a2, heads, mixed, hidden, slope, y_part
    ) = forward(tokens[0], cotangent[0], small, qkv_weight, fc1_weight, fc2_weight, out_weight, tables)
    small = small.astype(F32)
    norm = jnp.stack([small[:, i].reshape(-1) for i in range(8)])
    y_sum, dx, rows_total, rows_other, qkv_grad, fc1_grad, _, small_grads = backward(
        y_part, g_all, hidden, mixed, heads, slope, norm, qkv_cols, fc1_cols, fc2_rows, out_rows, tables, a1, a2
    )
    output = tokens[0].astype(F32) + (norm[4] + norm[5])[None] + y_sum

    n_fc2 = fc2_weight.shape[0] // 2
    holds = bits["hi"] == bits["y"]
    first = jnp.where(holds, rows_total, rows_other)
    second = jnp.where(holds, rows_other, rows_total)
    fc2_grad = jnp.concatenate([first[:n_fc2], second[:n_fc2]], axis=0).astype(F32)
    out_grad = jnp.concatenate([first[n_fc2:], second[n_fc2:]], axis=0).astype(F32)
    qkv_grad = jnp.concatenate([qkv_grad[i] for i in range(8)], axis=1).astype(F32)
    fc1_grad = jnp.concatenate([fc1_grad[i] for i in range(8)], axis=1).astype(F32)
    cuts = np.cumsum([1, 1, 1, 1, 1, qkv_bias.shape[0] * extra // 128, fc1_bias.shape[0] * extra // 128])
    small_grads = [v.reshape(-1) for v in jnp.split(small_grads, cuts, axis=0)[:-1]]

    inputs = tokens[0].astype(F32)
    centred = inputs - jnp.mean(inputs, axis=-1, keepdims=True)
    scale = lax.rsqrt(jnp.mean(centred * centred, axis=-1, keepdims=True) + EPS)
    normed = centred * scale
    dx = scale * (
        dx - jnp.mean(dx, axis=-1, keepdims=True) - normed * jnp.mean(dx * normed, axis=-1, keepdims=True)
    )
    input_grad = cotangent[0].astype(F32) + dx

    weight_grads = [qkv_grad, out_grad, fc1_grad, fc2_grad]
    if extra > 1:
        scatter = functools.partial(lax.psum_scatter, axis_name="e", scatter_dimension=0, tiled=True)
        weight_grads = [scatter(v) for v in weight_grads]
        small_grads = [scatter(v) for v in small_grads]
    qkv_grad, out_grad, fc1_grad, fc2_grad = weight_grads
    gain1, bias1, gain2, bias2, total, packed_bias, up_bias = small_grads
    return (
        output.astype(BF16)[None],
        input_grad.astype(BF16)[None],
        gain1,
        bias1,
        gain2,
        bias2,
        qkv_grad,
        packed_bias,
        out_grad,
        total,
        fc1_grad,
        up_bias,
        fc2_grad,
        total,
    )


def solution(mesh):
    extra = mesh.shape["shard"] // 16
    axes = ("y", "hi", "lo", "x", "c", "e")
    fine = Mesh(mesh.devices.reshape(2, 2, 2, 2, 2, extra), axes)
    split = P(axes, None, None)
    row, flat = P(axes[1:], None), P(axes[1:])
    in_specs = (split, flat, flat, flat, flat, row, flat, row, flat, row, flat, row, flat, split)
    out_specs = (split, split, flat, flat, flat, flat, row, flat, row, flat, row, flat, row, flat)
    return jax.shard_map(
        functools.partial(body, extra=extra), mesh=fine, in_specs=in_specs, out_specs=out_specs, check_vma=False
    )
```

```python
import functools

import jax
import jax.numpy as jnp
import numpy as np
from jax import lax
from jax.experimental import pallas as pl
from jax.experimental.pallas import tpu as pltpu
from jax.sharding import Mesh
from jax.sharding import PartitionSpec as P

HEADS = 8
HEAD_DIM = 256
ROTARY = 64
EPS = 1e-05
NEG_FILL = -1e30
SCALE = HEAD_DIM ** (-0.5)
BF16 = jnp.bfloat16
F32 = jnp.float32
NT = (((1,), (1,)), ((), ()))
TN = (((0,), (0,)), ((), ()))
NN = (((1,), (0,)), ((), ()))


def dot(a, b, dims=NN):
    return lax.dot_general(a, b, dims, preferred_element_type=F32)


NAMES = ("y", "hi", "lo", "x", "c")

X, G, QKV, FC1, FC2, OUT, Y, DX, ROWS, SMALL = range(10)
OWN, NEXT, ONWARD, BY_X, BY_LO, HI, CORE, ALONG_Y, FIRST, SECOND, THIRD, LAST, ADD, PASS, FAR, RELAY, STEP, END = range(18)
PLACE = {"lo": 1, "x": 2, "y": 4}


def chunks_of(length, plan):
    chunks, start, share = [], 0, 0
    for part, order in plan:
        share += part
        end = length * share // 288 * 16 if share < 18 else length
        chunks.append((start, end - start, order))
        start = end
    return chunks


SCATTER_CHUNKS = ((8, ("lo", "y", "x")), (5, ("x", "lo", "y")), (5, ("y", "lo", "x")))
SCATTER_EVENTS = (
    (
        (Y, FIRST, 0, 3), (Y, FIRST, 1, 3),
    ),
    (
        (Y, FIRST, 1, 2),
    ),
    (
        (Y, SECOND, 1, 3), (Y, FIRST, 2, 3),
    ),
    (
        (Y, SECOND, 0, 3), (ROWS, CORE, 1),
    ),
    (
        (Y, SECOND, 1, 2),
    ),
    (
        (Y, SECOND, 2, 3), (ROWS, ADD, 1), (ROWS, CORE, 0), (Y, FIRST, 2, 2),
    ),
    (),
    (
        (ROWS, ADD, 0),
    ),
    (
        (Y, SECOND, 2, 2), (Y, FIRST, 0, 1),
    ),
    (),
    (),
    (),
    (),
    (
        (Y, FIRST, 2, 1),
    ),
    (
        (FC1, CORE, 0),
    ),
    (
        (FC1, CORE, 1), (FC1, ADD, 0), (FC1, HI, 0),
    ),
    (
        (Y, FIRST, 0, 0), (FC1, CORE, 2), (FC1, ADD, 1), (Y, THIRD, 2),
    ),
    (
        (FC1, CORE, 3), (FC1, ADD, 2),
    ),
    (
        (FC1, CORE, 4), (FC1, ADD, 3),
    ),
    (
        (Y, FIRST, 1, 1), (ROWS, HI, 0), (FC1, CORE, 5), (FC1, ADD, 4),
    ),
    (
        (FC1, CORE, 6), (Y, FIRST, 0, 2), (FC1, ADD, 5), (FC1, PASS, 0),
    ),
    (
        (FC1, CORE, 7), (FC1, ADD, 6), (Y, FIRST, 1, 0),
    ),
    (
        (Y, THIRD, 1), (FC1, ADD, 7), (DX, FIRST, 1, 3),
    ),
    (
        (FC1, FAR, 0), (DX, FIRST, 1, 1),
    ),
    (
        (Y, SECOND, 0, 2), (Y, THIRD, 0),
    ),
    (
        (DX, FIRST, 2, 3), (Y, LAST, 1), (FC1, RELAY, 3), (DX, FIRST, 0, 3),
    ),
    (),
    (),
    (
        (DX, FIRST, 0, 2),
    ),
    (
        (DX, FIRST, 1, 0), (DX, SECOND, 1, 3), (Y, LAST, 0), (DX, FIRST, 1, 2), (DX, SECOND, 2, 3), (DX, FIRST, 2, 2),
    ),
    (
        (QKV, CORE, 0), (DX, SECOND, 0, 3),
    ),
    (
        (QKV, CORE, 1), (QKV, ADD, 0),
    ),
    (
        (QKV, CORE, 2), (QKV, ADD, 1),
    ),
    (
        (FC1, HI, 1), (QKV, CORE, 3), (QKV, ADD, 2),
    ),
    (
        (ROWS, ALONG_Y, 0), (Y, FIRST, 2, 0), (QKV, CORE, 4), (QKV, ADD, 3), (DX, SECOND, 0, 2), (QKV, ADD, 4),
        (DX, SECOND, 1, 2), (DX, SECOND, 2, 2), (DX, FIRST, 0, 1), (DX, THIRD, 1),
    ),
    (
        (QKV, CORE, 5),
    ),
    (
        (QKV, CORE, 6), (QKV, ADD, 5),
    ),
    (
        (SMALL, STEP, 0), (Y, LAST, 2), (FC1, PASS, 1), (QKV, CORE, 7), (QKV, ADD, 6), (QKV, ADD, 7), (FC1, HI, 2),
        (SMALL, STEP, 1), (DX, FIRST, 2, 1), (SMALL, STEP, 2), (SMALL, STEP, 3), (SMALL, STEP, 4), (DX, FIRST, 0, 0),
        (DX, LAST, 1), (DX, THIRD, 0), (SMALL, END, 0), (FC1, RELAY, 1), (FC1, HI, 3), (DX, FIRST, 2, 0),
        (FC1, PASS, 2), (DX, THIRD, 2), (QKV, HI, 0), (FC1, PASS, 3), (FC1, RELAY, 2), (QKV, HI, 1), (QKV, PASS, 0),
        (DX, LAST, 0), (DX, LAST, 2), (QKV, HI, 2), (QKV, PASS, 1), (QKV, FAR, 0), (ROWS, END, 0), (QKV, RELAY, 3),
        (FC1, END, 0), (QKV, HI, 3), (QKV, PASS, 2), (QKV, RELAY, 1), (QKV, RELAY, 2), (QKV, PASS, 3), (QKV, END, 0),
    ),
)


GATHER_CHUNKS = ((9, ("lo", "y", "x")), (9, ("lo", "x", "y")))
GATHER_EVENTS = (
    (
        (SMALL, STEP, 0), (QKV, BY_X, 0), (QKV, BY_LO, 0), (QKV, HI, 0), (X, OWN, 0, 1), (X, OWN, 1, 2),
        (X, OWN, 0, 0), (X, OWN, 1, 0), (X, OWN, 1, 1), (FC2, HI, 0), (QKV, CORE, 0), (FC1, HI, 0), (X, OWN, 0, 2),
        (FC1, CORE, 0), (SMALL, STEP, 1), (SMALL, STEP, 2), (SMALL, STEP, 3), (SMALL, STEP, 4), (G, OWN, 1, 2),
        (QKV, CORE, 2), (QKV, HI, 2), (X, ONWARD, 0, 0), (QKV, CORE, 4), (X, ONWARD, 1, 0), (OUT, HI, 0),
        (FC1, CORE, 4), (QKV, BY_X, 1), (FC1, BY_X, 0), (QKV, CORE, 1), (G, OWN, 0, 1), (QKV, HI, 1), (FC1, BY_X, 1),
        (QKV, CORE, 6), (G, OWN, 1, 1), (QKV, BY_LO, 1), (FC1, CORE, 1), (X, NEXT, 0, 2), (X, NEXT, 1, 1),
        (X, NEXT, 1, 2), (X, NEXT, 0, 1), (FC1, BY_LO, 0), (QKV, CORE, 3), (QKV, HI, 3), (OUT, CORE, 0),
        (OUT, ALONG_Y, 0), (FC1, HI, 1), (QKV, CORE, 5), (FC1, BY_LO, 1), (FC1, CORE, 2), (OUT, CORE, 1),
        (G, OWN, 1, 0), (FC1, CORE, 3), (G, ONWARD, 1, 0), (FC1, HI, 3), (X, ONWARD, 0, 1), (QKV, CORE, 7),
        (X, ONWARD, 1, 1),
    ),
    (),
    (),
    (
        (G, OWN, 0, 2),
    ),
    (
        (FC1, CORE, 5), (FC1, HI, 2),
    ),
    (
        (G, OWN, 0, 0),
    ),
    (
        (G, NEXT, 1, 2),
    ),
    (
        (G, NEXT, 1, 1),
    ),
    (
        (FC1, CORE, 7), (FC2, CORE, 0), (FC2, ALONG_Y, 0), (G, ONWARD, 0, 0), (FC1, CORE, 6),
    ),
    (),
    (),
    (
        (G, NEXT, 0, 2),
    ),
    (),
    (
        (G, NEXT, 0, 1), (FC2, CORE, 1),
    ),
    (),
    (),
    (),
    (
        (G, ONWARD, 1, 1), (G, ONWARD, 0, 1),
    ),
    (),
    (),
    (),
    (),
    (),
    (),
    (),
)


class Copies:
    def __init__(self, at, send_sem, recv_sem, local_sem):
        self.at, self.send_sem, self.recv_sem, self.local_sem = at, send_sem, recv_sem, local_sem
        self.remote, self.planned, self.local, self.seen = [], 0, 0, set()

    def plan(self, src, dst, axis, everywhere=True):
        spot = self.planned
        self.planned += 1
        copy = pltpu.make_async_remote_copy(
            src_ref=src,
            dst_ref=dst,
            send_sem=self.send_sem.at[spot],
            recv_sem=self.recv_sem.at[spot],
            device_id={axis: 1 - self.at[axis]},
            device_id_type=pl.DeviceIdType.MESH,
        )
        if everywhere:
            self.remote.append(copy)
        return copy

    def arrive(self, *copies):
        for copy in copies:
            if id(copy) not in self.seen:
                self.seen.add(id(copy))
                copy.wait_recv()

    def move(self, src, dst):
        copy = pltpu.make_async_copy(src, dst, self.local_sem.at[self.local])
        self.local += 1
        return copy


def greet(at, names):
    barrier = pltpu.get_barrier_semaphore()
    for name in names:
        pl.semaphore_signal(
            barrier, inc=1, device_id={name: 1 - at[name]}, device_id_type=pl.DeviceIdType.MESH
        )
    pl.semaphore_wait(barrier, len(names))


class TokenGather:
    def __init__(self, copies, own, full, name, events):
        self.copies, self.plans = copies, {}
        self.kept = copies.move(own, full.at[0])
        self.chunks = chunks_of(own.shape[0], GATHER_CHUNKS)
        for chunk, (start, rows, order) in enumerate(self.chunks):
            part = pl.ds(start, rows)
            one, two, _ = (PLACE[axis] for axis in order)
            hops = [((OWN, chunk, i), 0, axis) for i, axis in enumerate(order)]
            hops += [((NEXT, chunk, 1), one, order[1]), ((NEXT, chunk, 2), one, order[2])]
            hops += [((ONWARD, chunk, 0), two, order[2]), ((ONWARD, chunk, 1), one + two, order[2])]
            for label, block, axis in hops:
                src = own.at[part] if block == 0 else full.at[block, part]
                there = block + PLACE[axis]
                self.plans[chunk, there] = copies.plan(src, full.at[there, part], axis)
                events[(name,) + label] = functools.partial(self.send, chunk, block, there)

    def send(self, chunk, block, there):
        if block:
            self.copies.arrive(self.plans[chunk, block])
        self.plans[chunk, there].start()

    def take(self, block):
        for chunk in range(len(self.chunks)):
            self.copies.arrive(self.plans[chunk, block])

    def finish(self):
        for block in range(1, 8):
            self.take(block)
        self.kept.wait()


class TokenScatter:
    def __init__(self, copies, parts, came, far_parts, stage, room, total, name, events):
        self.copies, self.parts, self.came, self.far_parts = copies, parts, came, far_parts
        self.stage, self.room = stage, room
        self.chunks = chunks_of(parts.shape[1], SCATTER_CHUNKS)
        self.first, self.second, self.third, self.stores, self.loads, self.near = {}, {}, [], [], {}, {}
        base = copies.local
        for chunk, (start, rows, order) in enumerate(self.chunks):
            third, second, first = order
            part = pl.ds(start, rows)
            for slot in (3, 2, 1, 0):
                block = self.block(chunk, slot)
                src = parts.at[block + PLACE[first], part]
                self.first[chunk, slot] = copies.plan(src, came.at[slot, part], first)
                near = came.at[slot, part] if far_parts else parts.at[block, part]
                if slot > 1:
                    self.second[chunk, slot] = copies.plan(near, came.at[2 + slot, part], second)
                if slot == 1:
                    self.third.append(copies.plan(near, came.at[6, part], third))
                self.near[chunk, slot] = near
                if far_parts:
                    copies.local = base + chunk
                    self.loads[chunk, slot] = [copies.move(parts.at[block, part], stage.at[part])]
                else:
                    copies.local = base
                    self.loads[chunk, slot] = [
                        copies.move(came.at[i, part], stage.at[spot, pl.ds(0, rows)])
                        for spot, i in enumerate(self.terms(slot))
                    ]
                events[name, FIRST, chunk, slot] = self.first[chunk, slot].start
            events[name, SECOND, chunk, 3] = functools.partial(self.pass_second, chunk, 3)
            events[name, SECOND, chunk, 2] = functools.partial(self.pass_second, chunk, 2)
            events[name, THIRD, chunk] = functools.partial(self.pass_third, chunk)
            events[name, LAST, chunk] = functools.partial(self.last, chunk)
        copies.local = base + max(3, len(self.chunks))
        for start, rows, _ in self.chunks:
            self.stores.append(copies.move(room.at[pl.ds(0, rows)], total.at[pl.ds(start, rows)]))

    def block(self, chunk, slot):
        third, second, _ = self.chunks[chunk][2]
        return PLACE[second] * (slot // 2) + PLACE[third] * (slot % 2)

    def terms(self, slot):
        return {0: (0, 4, 6), 1: (1, 5)}.get(slot, (slot,))

    def prepare(self):
        if self.far_parts:
            for chunk in range(len(self.chunks)):
                self.loads[chunk, 3][0].start()

    def add(self, chunk, slot):
        start, rows, _ = self.chunks[chunk]
        part = pl.ds(start, rows)
        self.copies.arrive(self.first[chunk, slot])
        loads = self.loads[chunk, slot]
        if self.far_parts:
            loads[0].wait()
            value = self.stage[part].astype(F32)
            for i in self.terms(slot):
                value = value + self.came[i, part].astype(F32)
            if slot > 0:
                self.loads[chunk, slot - 1][0].start()
            return value
        for copy in loads:
            copy.start()
        value = self.parts[self.block(chunk, slot), part].astype(F32)
        for spot, copy in enumerate(loads):
            copy.wait()
            value = value + self.stage[spot, :rows].astype(F32)
        return value

    def pass_second(self, chunk, slot):
        self.near[chunk, slot][...] = self.add(chunk, slot).astype(BF16)
        self.second[chunk, slot].start()

    def pass_third(self, chunk):
        self.copies.arrive(self.second[chunk, 3])
        self.near[chunk, 1][...] = self.add(chunk, 1).astype(BF16)
        self.third[chunk].start()

    def last(self, chunk):
        self.copies.arrive(self.second[chunk, 2], self.third[chunk])
        self.room[: self.chunks[chunk][1]] = self.add(chunk, 0)
        self.stores[chunk].start()
        self.stores[chunk].wait()


class ColumnGather:
    def __init__(self, copies, weight, full, relay, name, events):
        at = copies.at
        hi, lo, x, c = (at[n] for n in ("hi", "lo", "x", "c"))
        rows, width = weight.shape[0], full.shape[1]

        def block(lo_at, x_at):
            spot = (at["y"] * 2 + lo_at) * 2 + x_at
            return weight.at[:, pl.ds(pl.multiple_of(spot * width, 128), width)]

        def place(hi_at, lo_at, x_at):
            spot = ((hi_at * 2 + lo_at) * 2 + x_at) * 2 + c
            return full.at[pl.ds(pl.multiple_of(spot * rows, 128), rows)]

        mine = place(hi, lo, x)
        self.by_x = [copies.plan(block(1 - lo, 1 - x), relay, "x"), copies.plan(block(lo, 1 - x), mine, "x")]
        self.by_lo = [
            copies.plan(block(1 - lo, x), mine, "lo"),
            copies.plan(relay, place(hi, lo, 1 - x), "lo"),
        ]
        near = [place(hi, lo, x), place(hi, lo, 1 - x), place(hi, 1 - lo, x), place(hi, 1 - lo, 1 - x)]
        far = [place(1 - hi, lo, x), place(1 - hi, lo, 1 - x), place(1 - hi, 1 - lo, x), place(1 - hi, 1 - lo, 1 - x)]
        source = [block(lo, x)] + near[1:]
        self.by_hi = [copies.plan(src, dst, "hi") for src, dst in zip(source, near)]
        self.by_c = [copies.plan(src, dst, "c") for src, dst in zip(source + far, near + far)]
        self.kept = copies.move(block(lo, x), mine)
        self.copies = copies
        by_hi, by_c = self.by_hi, self.by_c
        x_then, lo_then = self.by_x, self.by_lo
        hops = [((BY_X, i), None, x_then[i]) for i in range(2)]
        hops += [((BY_LO, 0), None, lo_then[0]), ((BY_LO, 1), x_then[0], lo_then[1])]
        came = [None, x_then[1], lo_then[0], lo_then[1]]
        hops += [((HI, i), came[i], by_hi[i]) for i in range(4)]
        hops += [((CORE, i), copy, by_c[i]) for i, copy in enumerate(came + by_hi)]
        for label, first, copy in hops:
            events[(name,) + label] = functools.partial(self.send, first, copy)

    def send(self, first, copy):
        if first is not None:
            self.copies.arrive(first)
        copy.start()

    def finish(self):
        self.copies.arrive(*self.by_c)
        self.kept.wait()


class RowGather:
    def __init__(self, copies, weight, full, name, events):
        at, rows = copies.at, weight.shape[0]
        half = rows // 2

        def spot(start, count):
            return full.at[pl.ds(pl.multiple_of(start, 16), count)]

        self.copies = copies
        self.holds = 1 - (at["hi"] + at["y"]) % 2
        first, second = spot(at["c"] * rows, half), spot(at["c"] * rows + half, half)
        there = spot(self.holds * (at["c"] * rows) + (1 - self.holds) * 2 * rows, half)
        source = weight.at[pl.ds(pl.multiple_of((1 - self.holds) * half, 16), half)]
        self.by_hi = copies.plan(source, there, "hi")
        self.by_y = copies.plan(spot(2 * rows, half), second, "y", everywhere=False)
        self.by_c = [copies.plan(first, first, "c"), copies.plan(second, second, "c")]
        self.kept = copies.move(weight, spot(at["c"] * rows, rows))
        events[name, HI, 0], events[name, ALONG_Y, 0] = self.start, self.relay
        events[name, CORE, 0], events[name, CORE, 1] = self.first_to_c, self.second_to_c

    def start(self):
        self.by_hi.start()
        pl.when(self.holds == 1)(self.kept.start)

    def ready(self):
        if id(self.by_hi) not in self.copies.seen:
            self.copies.arrive(self.by_hi)
            pl.when(self.holds == 1)(self.kept.wait)

    def relay(self):
        self.ready()
        pl.when(self.holds == 1)(self.by_y.start)

    def first_to_c(self):
        self.ready()
        self.by_c[0].start()

    def second_to_c(self):
        self.ready()
        pl.when(self.holds == 0)(self.by_y.wait_recv)
        self.by_c[1].start()

    def finish(self):
        for copy in self.by_c:
            copy.wait_recv()

    def sent(self):
        pl.when(self.holds == 1)(self.by_y.wait_send)


class SmallGather:
    def __init__(self, copies, full):
        at = copies.at
        base = ((at["hi"] * 2 + at["lo"]) * 2 + at["x"]) * 2 + at["c"]
        self.own = full.at[pl.ds(base, 1)]
        self.steps, count = [], 1
        for name in ("c", "x", "lo", "hi"):
            part = full.at[pl.ds(base, count)]
            self.steps.append(copies.plan(part, part, name))
            base = base - at[name] * count
            count *= 2

    def step(self, at):
        if at > 0:
            self.steps[at - 1].wait_recv()
        if at < 4:
            self.steps[at].start()


def rotary_tables(length):
    places = np.arange(length, dtype=np.float32)
    frequency = (10000.0 ** (-np.arange(0, ROTARY, 2, dtype=np.float32) / ROTARY)).astype(np.float32)
    angles = places[:, None] * frequency[None, :]
    cosine, sine = np.cos(angles), np.sin(angles)
    half = ROTARY // 2
    tables = np.zeros((3, length, 2 * ROTARY), np.float32)
    tables[0] = 1.0
    tables[0, :, :half] = cosine
    tables[0, :, half:ROTARY] = cosine
    tables[1, :, :half] = -sine
    tables[2, :, half:ROTARY] = sine
    return tables


def turn(rows, tables, sign):
    half, wide = ROTARY // 2, 2 * ROTARY
    near = rows[:, :wide]
    ahead = pltpu.roll(near, wide - half, 1)
    behind = pltpu.roll(near, half, 1)
    near = near * tables[0] + sign * (ahead * tables[1] + behind * tables[2])
    return jnp.concatenate([near, rows[:, wide:]], axis=1)


def causal_scores(queries, keys_all):
    length = queries.shape[0]
    scores = dot(queries, keys_all, NT) * SCALE
    row = lax.broadcasted_iota(jnp.int32, (length, length), 0)
    col = lax.broadcasted_iota(jnp.int32, (length, length), 1)
    return jnp.where(row >= col, scores, NEG_FILL)


def softmax(scores):
    raised = jnp.exp(scores - jnp.max(scores, axis=-1, keepdims=True))
    return raised / jnp.sum(raised, axis=-1, keepdims=True)


MLP_AT, OUTPUT_AT, FORWARD_STEPS = 8, 16, 24


def forward_kernel(
    x_ref, g_ref, small_ref, qkv_ref, fc1_ref, fc2_ref, out_ref, tables_ref,
    g_all, small_out, qkv_out, fc1_out, fc2_out, out_out,
    a1_ref, a2_ref, heads_ref, mixed_ref, hidden_ref, slope_ref, y_ref,
    x_all, small_all, qkv_all, fc1_all, fc2_all, out_all, norm, qkv_bias, fc1_bias, mixed_all, hidden_all,
    relay_qkv, relay_fc1, send_sem, recv_sem, local_sem,
):
    step = pl.program_id(0)
    at = {name: lax.axis_index(name) for name in NAMES}
    copies = Copies(at, send_sem, recv_sem, local_sem)
    events = {}
    small = SmallGather(copies, small_all)
    qkv = ColumnGather(copies, qkv_ref, qkv_all, relay_qkv, QKV, events)
    fc1 = ColumnGather(copies, fc1_ref, fc1_all, relay_fc1, FC1, events)
    fc2 = RowGather(copies, fc2_ref, fc2_all, FC2, events)
    out = RowGather(copies, out_ref, out_all, OUT, events)
    x = TokenGather(copies, x_ref, x_all, X, events)
    g = TokenGather(copies, g_ref, g_all, G, events)
    kept = [
        copies.move(src.at[pl.ds(0, dst.shape[0])], dst)
        for src, dst in ((qkv_all, qkv_out), (fc1_all, fc1_out), (fc2_all, fc2_out), (out_all, out_out))
    ]

    def spread_small():
        small.step(4)
        for spot in range(16):
            norm[:, spot * 128 : (spot + 1) * 128] = small_all[spot, :8].astype(F32)
        first = (at["y"] * 4 + at["lo"] * 2 + at["x"]) * 2
        for half in range(2):
            own = small_all[first + half].astype(F32)
            for bias, start in ((qkv_bias, 6), (fc1_bias, 6 + qkv_bias.shape[1] // 256)):
                rows = bias.shape[1] // 256
                for i in range(rows):
                    bias[:, (half * rows + i) * 128 : (half * rows + i + 1) * 128] = own[start + i : start + i + 1]

    for i in range(4):
        events[SMALL, STEP, i] = functools.partial(small.step, i)
    events[SMALL, STEP, 4] = spread_small

    def before(spot):
        if spot == 0:
            greet(at, NAMES)
            small.own[...] = small_ref[...][None]
            for copy in (x.kept, g.kept, qkv.kept, fc1.kept):
                copy.start()
        for label in GATHER_EVENTS[spot]:
            events[label]()
        if spot == 0:
            x.kept.wait()
            qkv.finish()
            kept[0].start()
        elif spot < MLP_AT:
            x.take(spot)
        elif spot == MLP_AT:
            fc1.finish()
            kept[1].start()
        elif spot == OUTPUT_AT:
            fc2.finish()
            out.finish()
            kept[2].start()
            kept[3].start()

    for spot in range(FORWARD_STEPS):
        pl.when(step == spot)(functools.partial(before, spot))

    def normed(j, line):
        value = x_all[j].astype(F32)
        centred = value - jnp.mean(value, axis=-1, keepdims=True)
        var = jnp.mean(centred * centred, axis=-1, keepdims=True)
        return (centred * lax.rsqrt(var + EPS) * norm[line : line + 1] + norm[line + 1 : line + 2]).astype(BF16)

    @pl.when(step < MLP_AT)
    def _():
        a1_ref[0] = normed(step, 0)
        packed = dot(a1_ref[0], qkv_all[...]) + qkv_bias[...]
        queries = turn(packed[:, :HEAD_DIM], tables_ref, 1.0).astype(BF16)
        keys_all = turn(packed[:, HEAD_DIM : 2 * HEAD_DIM], tables_ref, 1.0).astype(BF16)
        values_all = packed[:, 2 * HEAD_DIM :].astype(BF16)
        heads_ref[0, :, :HEAD_DIM] = queries
        heads_ref[0, :, HEAD_DIM : 2 * HEAD_DIM] = keys_all
        heads_ref[0, :, 2 * HEAD_DIM :] = values_all
        probs = softmax(causal_scores(queries, keys_all)).astype(BF16)
        mixed_ref[0] = dot(probs, values_all).astype(BF16)
        mixed_all[step] = mixed_ref[0]

    @pl.when((step >= MLP_AT) & (step < OUTPUT_AT))
    def _():
        j = step - MLP_AT
        a2_ref[0] = normed(j, 2)
        upward = dot(a2_ref[0], fc1_all[...]) + fc1_bias[...]
        below = 0.5 * (1.0 + lax.erf(upward * np.float32(0.5**0.5)))
        hidden_ref[0] = (upward * below).astype(BF16)
        hidden_all[j] = hidden_ref[0]
        slope_ref[0] = below + upward * (jnp.exp(-0.5 * upward * upward) * np.float32((2 * np.pi) ** -0.5))

    @pl.when(step >= OUTPUT_AT)
    def _():
        j = step - OUTPUT_AT
        y = dot(hidden_all[j], fc2_all[: hidden_ref.shape[2]])
        y_ref[0] = (y + dot(mixed_all[j], out_all[: mixed_ref.shape[2]])).astype(BF16)

    @pl.when(step == FORWARD_STEPS - 1)
    def _():
        small_out[...] = small_all[...]
        for label in GATHER_EVENTS[FORWARD_STEPS]:
            events[label]()
        g.finish()
        for copy in kept:
            copy.wait()
        for copy in copies.remote:
            copy.wait_send()
        fc2.sent()
        out.sent()


def forward(tokens, cotangent, small, qkv_weight, fc1_weight, fc2_weight, out_weight, tables):
    far = pl.BlockSpec(memory_space=pl.ANY)
    length, width = tokens.shape
    rows = qkv_weight.shape[0]
    n_qkv, n_fc1, n_mix = qkv_weight.shape[1] // 8, fc1_weight.shape[1] // 8, out_weight.shape[0] * 2
    each = [(width, BF16), (width, BF16), (n_qkv, BF16), (n_mix, BF16), (n_fc1, BF16), (n_fc1, F32), (width, BF16)]
    count = 4 + 2 * 16 + 2 * 4 + 2 * 7 * len(GATHER_CHUNKS)
    weights = [(16 * rows, n_qkv), (16 * rows, n_fc1), (n_fc1, width), (n_mix, width)]
    flops = 2 * 8 * length * width * (n_qkv + n_fc1 + n_fc1 + n_mix)
    return pl.pallas_call(
        forward_kernel,
        grid=(FORWARD_STEPS,),
        in_specs=[far, far, whole(small), far, far, far, far, whole(tables)],
        out_specs=[far, whole(jax.ShapeDtypeStruct((16,) + small.shape, BF16)), far, far, far, far]
        + [
            pl.BlockSpec((1, length, n), lambda i, start=start: (jnp.clip(i - start, 0, 7), 0, 0))
            for (n, _), start in zip(each, (0, MLP_AT, 0, 0, MLP_AT, MLP_AT, OUTPUT_AT))
        ],
        out_shape=[
            jax.ShapeDtypeStruct((8, length, width), BF16),
            jax.ShapeDtypeStruct((16,) + small.shape, BF16),
        ]
        + [jax.ShapeDtypeStruct(shape, BF16) for shape in weights]
        + [jax.ShapeDtypeStruct((8, length, n), kind) for n, kind in each],
        scratch_shapes=[
            pltpu.VMEM((8, length, width), BF16),
            pltpu.VMEM((16,) + small.shape, BF16),
            pltpu.VMEM(weights[0], BF16),
            pltpu.VMEM(weights[1], BF16),
            pltpu.VMEM((n_fc1 * 5 // 4, width), BF16),
            pltpu.VMEM((n_mix * 5 // 4, width), BF16),
            pltpu.VMEM((8, width), F32),
            pltpu.VMEM((1, n_qkv), F32),
            pltpu.VMEM((1, n_fc1), F32),
            pltpu.VMEM((8, length, n_mix), BF16),
            pltpu.VMEM((8, length, n_fc1), BF16),
            pltpu.VMEM((rows, n_qkv), BF16),
            pltpu.VMEM((rows, n_fc1), BF16),
            pltpu.SemaphoreType.DMA((count,)),
            pltpu.SemaphoreType.DMA((count,)),
            pltpu.SemaphoreType.DMA((10,)),
        ],
        compiler_params=pltpu.CompilerParams(
            collective_id=1, has_side_effects=True, vmem_limit_bytes=60 * 2**20
        ),
        cost_estimate=pl.CostEstimate(flops=flops, bytes_accessed=10**8, transcendentals=0),
        name="forward",
    )(tokens, cotangent, small, qkv_weight, fc1_weight, fc2_weight, out_weight, tables)


def add_rows(dst, dst_row, src, src_row, count, lanes=None, src_lanes=None):
    lanes = lanes or slice(None)
    src_lanes = src_lanes or lanes
    for start in range(0, count, 64):
        here = pl.ds(pl.multiple_of(dst_row + start, 16), 64)
        there = pl.ds(pl.multiple_of(src_row + start, 16), 64)
        dst[here, lanes] = (dst[here, lanes].astype(F32) + src[there, src_lanes].astype(F32)).astype(BF16)


class RowScatter:
    def __init__(self, copies, wide, slim, kept, came, n_fc2, n_out, other, events):
        at = copies.at
        c = at["c"]
        self.copies, self.kept, self.came, self.wide, self.slim = copies, kept, came, wide, slim
        self.holds = 1 - (at["hi"] + at["y"]) % 2
        own, half = n_fc2 + n_out, (n_fc2 // 2, n_out // 2)
        width, tile = kept.shape[1], 2 * n_out
        self.cuts = [(wide, i, i * 2 * n_fc2, wide.shape[1]) for i in range(width // wide.shape[1])]
        self.slim_cuts = [
            (slim, i, i * tile, min(slim.shape[1], width - i * slim.shape[1]))
            for i in range(-(-width // slim.shape[1]))
        ]

        def rows(ref, start, count):
            return ref.at[pl.ds(pl.multiple_of(start, 16), count)]

        self.pieces = []
        for side in range(2):
            pieces = []
            for cuts, size, n, to in (
                (self.cuts, n_fc2, half[0], side * half[0]),
                (self.slim_cuts, n_out, half[1], n_fc2 + side * half[1]),
            ):
                for ref, i, first, lanes in cuts:
                    step = ref.shape[1]
                    pieces.append((ref, first + side * n, size, n, to, slice(i * step, i * step + lanes), lanes))
            self.pieces.append(pieces)
        self.c = c
        self.by_c = []
        for pieces in self.pieces:
            made = []
            for ref, first, size, n, to, there, lanes in pieces:
                src = ref.at[pl.ds(pl.multiple_of(first + (1 - c) * size, 16), n), pl.ds(0, lanes)]
                dst = kept.at[pl.ds(to, n), pl.ds(there.start, lanes)]
                made.append(copies.plan(src, dst, "c"))
            self.by_c.append(made)
        self.by_y = [
            copies.plan(rows(kept, half[0], half[0]), rows(kept, own, half[0]), "y"),
            copies.plan(rows(kept, n_fc2 + half[1], half[1]), rows(kept, own + half[0], half[1]), "y"),
        ]
        holds = self.holds
        sent = [holds * own, holds * (own + half[0]) + (1 - holds) * n_fc2]
        self.keeps = [(1 - holds) * own, (1 - holds) * (own + half[0]) + holds * n_fc2]
        self.by_hi = [
            copies.plan(rows(kept, sent[0], half[0]), rows(came, 0, half[0]), "hi"),
            copies.plan(rows(kept, sent[1], half[1]), rows(came, half[0], half[1]), "hi"),
        ]
        self.half = half
        self.on_y = copies.plan(came, other, "y")
        events[ROWS, CORE, 1] = functools.partial(self.send, self.by_c[1])
        events[ROWS, CORE, 0] = functools.partial(self.send, self.by_c[0])
        events[ROWS, ADD, 1] = functools.partial(self.add_c, 1)
        events[ROWS, HI, 0] = self.send_hi
        events[ROWS, END, 0] = functools.partial(copies.arrive, self.on_y)

    def store_tile(self, i, value):
        size = value.shape[0]
        cuts = self.slim_cuts if i is None else self.cuts
        for ref, cut, first, lanes in cuts:
            start = first if i is None else first + i * size
            ref[start : start + size, :lanes] = value[:, cut * ref.shape[1] : cut * ref.shape[1] + lanes].astype(BF16)

    def send(self, made):
        for copy in made:
            copy.start()

    def add_c(self, side):
        for copy, (ref, first, size, n, to, there, lanes) in zip(self.by_c[side], self.pieces[side]):
            self.copies.arrive(copy)
            add_rows(self.kept, to, ref, first + self.c * size, n, there, slice(0, lanes))
        if side == 1:
            self.send(self.by_y)

    def sent_c(self):
        for copy in self.by_c[0] + self.by_c[1]:
            copy.wait_send()

    def send_hi(self):
        self.copies.arrive(*self.by_y)
        self.send(self.by_hi)

    def add_hi(self):
        self.copies.arrive(*self.by_hi)
        add_rows(self.came, 0, self.kept, self.keeps[0], self.half[0])
        add_rows(self.came, self.half[0], self.kept, self.keeps[1], self.half[1])
        self.on_y.start()


class ColumnScatter:
    def __init__(self, copies, starts, tile, room, by_hi, relay, full, name, events):
        at = copies.at
        self.copies, self.tile, self.room, self.came_hi = copies, tile, room, by_hi
        y, lo, x, c = (at[n] for n in ("y", "lo", "x", "c"))
        self.c = c
        self.by_c = [copies.plan(tile(i, 1 - c), room(i), "c") for i in range(8)]
        self.by_hi = [copies.plan(room(i), by_hi.at[i], "hi") for i in range(4)]

        def spot(lo_at, x_at):
            return full.at[(y * 2 + lo_at) * 2 + x_at]

        self.far = copies.plan(by_hi.at[0], relay, "lo")
        self.far_on = copies.plan(relay, spot(1 - lo, x), "x")
        self.by_lo = copies.plan(by_hi.at[1], spot(lo, x), "lo")
        self.by_x = copies.plan(by_hi.at[2], spot(lo, x), "x")
        self.mine = copies.move(by_hi.at[3], spot(lo, x))
        self.by_y = [
            copies.plan(by_hi.at[3], spot(lo, x), "y"),
            copies.plan(spot(1 - lo, x), spot(1 - lo, x), "y"),
            copies.plan(spot(lo, 1 - x), spot(lo, 1 - x), "y"),
            copies.plan(spot(1 - lo, 1 - x), spot(1 - lo, 1 - x), "y"),
        ]
        for i in range(8):
            events[name, CORE, i] = self.by_c[i].start
            events[name, ADD, i] = functools.partial(self.add_c, i)
        for i in range(4):
            events[name, HI, i] = self.by_hi[i].start
            events[name, PASS, i] = functools.partial(self.add_hi, i)
        for label, first, then in (
            ((FAR, 0), self.far, self.far_on),
            ((RELAY, 1), self.by_lo, self.by_y[1]),
            ((RELAY, 2), self.by_x, self.by_y[2]),
            ((RELAY, 3), self.far_on, self.by_y[3]),
        ):
            events[(name,) + label] = functools.partial(self.relay, first, then)
        events[name, END, 0] = self.finish

    def add_c(self, i):
        self.copies.arrive(self.by_c[i])
        here = self.room(i)
        here[...] = (here[...].astype(F32) + self.tile(i, self.c)[...].astype(F32)).astype(BF16)

    def add_hi(self, i):
        self.copies.arrive(self.by_hi[i])
        self.came_hi[i] = (self.came_hi[i].astype(F32) + self.room(4 + i)[...].astype(F32)).astype(BF16)
        if i < 3:
            (self.far, self.by_lo, self.by_x)[i].start()
        else:
            self.mine.start()
            self.by_y[0].start()

    def relay(self, first, then):
        self.copies.arrive(first)
        then.start()

    def finish(self):
        self.mine.wait()
        self.copies.arrive(*self.by_y)


class SmallScatter:
    def __init__(self, copies, parts, came):
        at = copies.at
        self.copies, self.parts, self.came, self.steps = copies, parts, came, []
        base, count, spot = 0, 8, 0
        for name in ("hi", "lo", "x", "c"):
            away = parts.at[pl.ds(base + (1 - at[name]) * count, count)]
            base = base + at[name] * count
            self.steps.append((copies.plan(away, came.at[pl.ds(spot, count)], name), base, spot, count))
            spot += count
            count //= 2
        own = parts.at[pl.ds(base, 1)]
        self.steps.append((copies.plan(own, came.at[pl.ds(spot, 1)], "y"), base, spot, 1))
        self.base, self.spot = base, spot

    def step(self, step):
        if step > 0:
            copy, base, spot, count = self.steps[step - 1]
            self.copies.arrive(copy)
            for i in range(count):
                self.parts[base + i] += self.came[spot + i]
        self.steps[step][0].start()

    def total(self):
        self.copies.arrive(self.steps[4][0])
        return self.parts[self.base] + self.came[self.spot]


ROW_TILES, SEQUENCES, COLUMN_TILES = 5, 8, 8
UP_AT = ROW_TILES
FC1_AT = UP_AT + SEQUENCES
DX_AT = FC1_AT + COLUMN_TILES
QKV_AT = DX_AT + SEQUENCES
STEPS = QKV_AT + COLUMN_TILES


def sequence_at(step):
    i = jnp.clip(step - DX_AT, 0, SEQUENCES - 1)
    return 2 * (1 - i // 4) + (1 - i % 2) + 4 * (1 - (i % 4) // 2)


def backward_kernel(
    y_ref, g_ref, hidden_ref, mixed_ref, heads_ref, slope_ref, norm_ref, qkv_ref, fc1_ref, fc2_ref, out_ref, tables_ref,
    a1_ref, a2_ref,
    y_out, dx_out, rows_mine, rows_other, full_qkv, full_fc1, dx_came, small_out,
    g_all, grads, qkv, fc1, part, came, y_stage, dx_stage, room, kept, rows_came, a1, a2,
    qkv_hi, fc1_hi, qkv_relay, fc1_relay, packed_sum, up_sum, column_total, vectors, parts, parts_came,
    send_sem, recv_sem, local_sem, free_sem, free_again_sem,
):
    step = pl.program_id(0)
    at = {name: lax.axis_index(name) for name in NAMES}
    copies = Copies(at, send_sem, recv_sem, local_sem)
    events = {}
    n_fc1, n_mix, n_qkv = fc2_ref.shape[0], out_ref.shape[0], qkv_ref.shape[1]
    count, length, _ = g_all.shape
    tokens, tile = count * length, n_mix
    core = tile // 2
    y, hi, lo, x, c = (at[n] for n in NAMES)
    scatter_y = TokenScatter(copies, y_ref, came, True, y_stage, room, y_out, Y, events)
    TokenScatter(copies, g_all, dx_came, False, dx_stage, room, dx_out, DX, events)
    rows = RowScatter(copies, fc1, qkv, kept, rows_came, n_fc1 // 2, n_mix // 2, rows_other, events)
    rows_store = copies.move(rows_came, rows_mine)

    hops = ((1 - lo, 1 - x), (1 - lo, x), (lo, 1 - x), (lo, x))
    places = [(hi_at * 2 + lo_at) * 2 + x_at for hi_at in (1 - hi, hi) for lo_at, x_at in hops]
    starts = [pl.multiple_of(place * tile, 128) for place in places]

    def fc1_tile(i, of):
        start = 4 * core + i % 4 // 2 * tile
        return part.at[pl.ds(pl.multiple_of(start + of * core, 16), core), pl.ds(i % 2 * n_fc1, n_fc1)]

    def fc1_room(i):
        return part.at[pl.ds(i % 4 * core, core), pl.ds(i // 4 * n_fc1, n_fc1)]

    def qkv_tile(i, of):
        return qkv.at[pl.ds(pl.multiple_of(starts[i] + of * core, 128), core)]

    def qkv_room(i):
        return part.at[pl.ds((4 + i % 4) * core, core), pl.ds(i // 4 * n_qkv, n_qkv)]

    fc1_out = ColumnScatter(copies, starts, fc1_tile, fc1_room, fc1_hi, fc1_relay, full_fc1, FC1, events)
    ColumnScatter(copies, starts, qkv_tile, qkv_room, qkv_hi, qkv_relay, full_qkv, QKV, events)
    small = SmallScatter(copies, parts, parts_came)
    load_g = copies.move(g_ref, g_all)
    early_loads = [
        copies.move(fc2_ref, part.at[pl.ds(0, n_fc1)]),
        copies.move(out_ref, part.at[pl.ds(n_fc1, n_mix)]),
    ]
    loads = [copies.move(qkv_ref, qkv), copies.move(fc1_ref, fc1)]

    def hidden_tile(i):
        return hidden_ref.at[:, pl.ds(i * tile, tile)]

    row_tiles = [
        (1, a1, 0, copies.move(hidden_tile(1), a1.at[0])),
        (3, a1, 1, copies.move(hidden_tile(3), a1.at[1])),
        (None, a2, 0, copies.move(mixed_ref, a2.at[0])),
        (0, a2, 1, copies.move(hidden_tile(0), a2.at[1])),
        (2, a1, 0, copies.move(hidden_tile(2), a1.at[0])),
    ]

    def column_loads(src, dst):
        base, made = copies.local, []
        for i, start in enumerate(starts):
            copies.local = base + i % 2
            made.append(copies.move(src.at[:, pl.ds(start, tile)], dst.at[i % 2]))
        copies.local = base + 2
        return made

    a1_loads, a2_loads = column_loads(a1_ref, a1), column_loads(a2_ref, a2)

    def start_small():
        parts[...] = jnp.zeros_like(parts)
        lines = []
        for i in (0, 2):
            gain, bias = norm_ref[i : i + 1], norm_ref[i + 1 : i + 2]
            bias_grad = vectors[i + 1 : i + 2]
            lines += [(vectors[i : i + 1] - bias * bias_grad) / gain, bias_grad]
        lines.append(column_total[...])
        for spot in range(16):
            for i, line in enumerate(lines):
                parts[spot, i : i + 1] = line[:, spot * 128 : (spot + 1) * 128]
        own = (y * 4 + lo * 2 + x) * 2
        for half in range(2):
            start = len(lines)
            for sums in (packed_sum, up_sum):
                units = sums.shape[1] // 256
                for i in range(units):
                    lanes = slice((half * units + i) * 128, (half * units + i + 1) * 128)
                    parts[own + half, start + i : start + i + 1] = sums[:, lanes]
                start += units
        small.step(0)

    def end_rows():
        rows.add_hi()
        rows_store.start()

    def end_small():
        small_out[...] = small.total()

    def load_weights():
        rows.add_c(0)
        rows.sent_c()
        for copy in loads:
            copy.start()

    events[ROWS, ADD, 0], events[ROWS, ALONG_Y, 0] = load_weights, end_rows
    events[SMALL, STEP, 0], events[SMALL, END, 0] = start_small, end_small
    for i in range(1, 5):
        events[SMALL, STEP, i] = functools.partial(small.step, i)

    def tell(sem):
        pl.semaphore_signal(sem, inc=1, device_id={"c": 1 - c}, device_id_type=pl.DeviceIdType.MESH)

    def before(spot):
        if spot == 0:
            greet(at, NAMES)
            load_g.start()
            for _, _, _, copy in row_tiles[:4]:
                copy.start()
            scatter_y.prepare()
        if spot == FC1_AT + 1:
            pl.semaphore_wait(free_sem, 1)
        if spot == QKV_AT + 1:
            pl.semaphore_wait(free_again_sem, 1)
        for label in SCATTER_EVENTS[spot]:
            events[label]()
        if spot == 0:
            for copy in early_loads:
                copy.start()
            packed_sum[...] = jnp.zeros_like(packed_sum)
            up_sum[...] = jnp.zeros_like(up_sum)
            load_g.wait()
            column_total[...] = jnp.sum(g_all[0].astype(F32), axis=0, keepdims=True)
        if spot == UP_AT:
            for copy in early_loads:
                copy.wait()
            for copy in a1_loads[:2] + a2_loads[:2]:
                copy.start()
        if FC1_AT <= spot < DX_AT:
            i = spot - FC1_AT
            if i == 0:
                tell(free_sem)
                for copy in loads:
                    copy.wait()
            if 0 < i < COLUMN_TILES - 1:
                a2_loads[i + 1].start()
            a2_loads[i].wait()
            if i >= 4:
                fc1_out.by_c[i - 4].wait_send()
        if spot == QKV_AT:
            for copy in fc1_out.by_c[4:]:
                copy.wait_send()
            tell(free_again_sem)
        if spot >= QKV_AT:
            i = spot - QKV_AT
            if 0 < i < COLUMN_TILES - 1:
                a1_loads[i + 1].start()
            a1_loads[i].wait()

    for spot in range(STEPS):
        pl.when(step == spot)(functools.partial(before, spot))

    for spot, (i, ref, slot, copy) in enumerate(row_tiles):

        @pl.when(step == spot)
        def _(spot=spot, i=i, ref=ref, slot=slot, copy=copy):
            copy.wait()
            rows.store_tile(i, dot(ref[slot], g_all[...].reshape(tokens, -1), TN))
            if spot == 0:
                row_tiles[4][3].start()

    @pl.when((step >= UP_AT) & (step < FC1_AT))
    def _():
        j = step - UP_AT
        here = pl.ds(pl.multiple_of(j * length, 16), length)
        grad_up = (dot(g_all[j], part[:n_fc1], NT) * slope_ref[0]).astype(BF16)
        grads[here, n_qkv:] = grad_up
        up_sum[...] += jnp.sum(grad_up.astype(F32), axis=0, keepdims=True)

    @pl.when((step >= DX_AT) & (step < QKV_AT))
    def _():
        j = sequence_at(step)
        here = pl.ds(pl.multiple_of(j * length, 16), length)
        grad_mixed = dot(g_all[j], part[n_fc1:], NT).astype(BF16)
        queries = heads_ref[0, :, :HEAD_DIM]
        keys_all = heads_ref[0, :, HEAD_DIM : 2 * HEAD_DIM]
        values_all = heads_ref[0, :, 2 * HEAD_DIM :]
        probs = softmax(causal_scores(queries, keys_all))
        grad_probs = dot(grad_mixed, values_all, NT)
        grad_values = dot(probs.astype(BF16), grad_mixed, TN)
        inner = jnp.sum(grad_probs * probs, axis=-1, keepdims=True)
        grad_scores = (probs * (grad_probs - inner)).astype(BF16)
        grad_queries = turn(dot(grad_scores, keys_all) * SCALE, tables_ref, -1.0)
        grad_keys = turn(dot(grad_scores, queries, TN) * SCALE, tables_ref, -1.0)
        grads[here, :HEAD_DIM] = grad_queries.astype(BF16)
        grads[here, HEAD_DIM : 2 * HEAD_DIM] = grad_keys.astype(BF16)
        grads[here, 2 * HEAD_DIM : n_qkv] = grad_values.astype(BF16)
        packed_sum[...] += jnp.sum(grads[here, :n_qkv].astype(F32), axis=0, keepdims=True)

        g_all[j] = (
            dot(grads[here, :n_qkv], qkv[...], NT) * norm_ref[0:1]
            + dot(grads[here, n_qkv:], fc1[...], NT) * norm_ref[2:3]
        ).astype(BF16)

    def column_tile(first, values, ref, lanes, sums, line, store):
        i = step - first
        start = starts[0]
        for spot in range(1, COLUMN_TILES):
            start = jnp.where(i == spot, starts[spot], start)
        here = pl.ds(pl.multiple_of(start, 128), tile)
        value = dot(values[lax.rem(i, 2)], grads[:, lanes], TN)
        weight = ref[here].astype(F32)
        store(i, here, value.astype(BF16))
        lane = lax.broadcasted_iota(jnp.int32, (tile, 128), 1)
        sides = jnp.where(
            lane == 0, jnp.sum(weight * value, axis=1, keepdims=True), jnp.sum(weight * sums[...], axis=1, keepdims=True)
        )
        vectors[line : line + 2, here] = jnp.transpose(sides)[:2]

    @pl.when((step >= FC1_AT) & (step < DX_AT))
    def _():
        def store(i, here, value):
            start = pl.multiple_of(4 * core + lax.rem(i, 4) // 2 * tile, 16)
            for side in range(2):

                @pl.when(lax.rem(i, 2) == side)
                def _():
                    part[pl.ds(start, tile), side * n_fc1 : (side + 1) * n_fc1] = value

        column_tile(FC1_AT, a2, fc1, slice(n_qkv, n_qkv + n_fc1), up_sum, 2, store)

    @pl.when(step >= QKV_AT)
    def _():
        def store(i, here, value):
            qkv[here] = value

        column_tile(QKV_AT, a1, qkv, slice(0, n_qkv), packed_sum, 0, store)

    @pl.when(step == STEPS - 1)
    def _():
        for label in SCATTER_EVENTS[STEPS]:
            events[label]()
        rows_store.wait()
        done = rows.by_c[0] + rows.by_c[1] + fc1_out.by_c
        for copy in copies.remote:
            if not any(copy is other for other in done):
                copy.wait_send()


def backward(y_part, g_all, hidden, mixed, heads, slope, norm, qkv, fc1, fc2, out, tables, a1, a2):
    far = pl.BlockSpec(memory_space=pl.ANY)
    count, length, width = g_all.shape
    n_qkv, n_fc1, n_mix = qkv.shape[1], fc1.shape[1], out.shape[0]
    wide = n_qkv + n_fc1
    tokens = count * length
    a1, a2 = a1.reshape(tokens, width), a2.reshape(tokens, width)
    hidden, mixed = hidden.reshape(tokens, n_fc1), mixed.reshape(tokens, n_mix)
    own = (n_fc1 + n_mix) // 2
    size = width // 8
    chunks = chunks_of(length, SCATTER_CHUNKS)
    longest = max(rows for _, rows, _ in chunks)

    outputs = [
        ((length, width), F32, far),
        ((length, width), F32, far),
        ((own // 2, width), BF16, far),
        ((own // 2, width), BF16, far),
        ((8, size // 2, n_qkv), BF16, far),
        ((8, size // 2, n_fc1), BF16, far),
        ((7, length, width), BF16, far),
        ((16, 128), F32, None),
    ]
    shapes = [jax.ShapeDtypeStruct(shape, kind) for shape, kind, _ in outputs]
    copies = 2 * 7 * len(chunks) + 15 + 40 + 5
    flops = 2 * tokens * width * (2 * n_qkv + 3 * n_fc1 + 2 * n_mix)
    return pl.pallas_call(
        backward_kernel,
        grid=(STEPS,),
        in_specs=[far] * 4
        + [
            pl.BlockSpec((1, length, n_qkv), lambda i: (sequence_at(i), 0, 0)),
            pl.BlockSpec((1, length, n_fc1), lambda i: (jnp.clip(i - UP_AT, 0, SEQUENCES - 1), 0, 0)),
            whole(norm),
        ]
        + [far] * 4
        + [whole(tables), far, far],
        out_specs=[whole(s) if spec is None else spec for s, (_, _, spec) in zip(shapes, outputs)],
        out_shape=shapes,
        scratch_shapes=[
            pltpu.VMEM(g_all.shape, BF16),
            pltpu.VMEM((tokens, wide), BF16),
            pltpu.VMEM(qkv.shape, BF16),
            pltpu.VMEM(fc1.shape, BF16),
            pltpu.VMEM((n_fc1 + n_mix, width), BF16),
            pltpu.VMEM((7, length, width), BF16),
            pltpu.VMEM((length, width), BF16),
            pltpu.VMEM((3, longest, width), BF16),
            pltpu.VMEM((longest, width), F32),
            pltpu.VMEM((own + own // 2, width), BF16),
            pltpu.VMEM((own // 2, width), BF16),
            pltpu.VMEM((2, tokens, size), BF16),
            pltpu.VMEM((2, tokens, size), BF16),
            pltpu.VMEM((4, size // 2, n_qkv), BF16),
            pltpu.VMEM((4, size // 2, n_fc1), BF16),
            pltpu.VMEM((size // 2, n_qkv), BF16),
            pltpu.VMEM((size // 2, n_fc1), BF16),
            pltpu.VMEM((1, n_qkv), F32),
            pltpu.VMEM((1, n_fc1), F32),
            pltpu.VMEM((1, width), F32),
            pltpu.VMEM((8, width), F32),
            pltpu.VMEM((16, 16, 128), F32),
            pltpu.VMEM((16, 16, 128), F32),
            pltpu.SemaphoreType.DMA((copies,)),
            pltpu.SemaphoreType.DMA((copies,)),
            pltpu.SemaphoreType.DMA((4 * max(3, len(chunks)) + 20,)),
            pltpu.SemaphoreType.REGULAR,
            pltpu.SemaphoreType.REGULAR,
        ],
        compiler_params=pltpu.CompilerParams(
            collective_id=2, has_side_effects=True, vmem_limit_bytes=63 * 2**20
        ),
        cost_estimate=pl.CostEstimate(flops=flops, bytes_accessed=10**8, transcendentals=0),
        name="backward",
    )(y_part, g_all, hidden, mixed, heads, slope, norm, qkv, fc1, fc2, out, tables, a1, a2)


def whole(array):
    return pl.BlockSpec(array.shape, lambda i: (0,) * array.ndim, pipeline_mode=pl.Buffered(1))


def finish_kernel(
    x_ref, g_ref, y_ref, dx_ref, shift_ref, qkv_ref, fc1_ref, fc2_mine, fc2_other, out_mine, out_other,
    output_ref, input_grad_ref, qkv_out, fc1_out, fc2_out, out_out,
):
    x = x_ref[...].astype(F32)
    output_ref[...] = (x + shift_ref[4:5] + shift_ref[5:6] + y_ref[...]).astype(BF16)
    centred = x - jnp.mean(x, axis=-1, keepdims=True)
    scale = lax.rsqrt(jnp.mean(centred * centred, axis=-1, keepdims=True) + EPS)
    normed = centred * scale
    dx = dx_ref[...]
    inner = jnp.mean(dx * normed, axis=-1, keepdims=True)
    dx = scale * (dx - jnp.mean(dx, axis=-1, keepdims=True) - normed * inner)
    input_grad_ref[...] = (g_ref[...].astype(F32) + dx).astype(BF16)

    qkv_out[...] = qkv_ref[0].astype(F32)
    fc1_out[...] = fc1_ref[0].astype(F32)
    holds = 1 - (lax.axis_index("hi") + lax.axis_index("y")) % 2
    mine = holds == (jnp.minimum(pl.program_id(0), 7) < 4).astype(jnp.int32)
    for ref, here, there in ((fc2_out, fc2_mine, fc2_other), (out_out, out_mine, out_other)):
        ref[...] = jnp.where(mine, here[...].astype(F32), there[...].astype(F32))


def finish(tokens, cotangent, y_sum, dx, norm, qkv_grad, fc1_grad, rows_mine, rows_other):
    length, width = tokens.shape
    rows = length // 9
    n_qkv, n_fc1, size = qkv_grad.shape[2], fc1_grad.shape[2], qkv_grad.shape[1]
    n_fc2, n_out = rows_mine.shape[0] // 5 // 4 * 4, rows_mine.shape[0] // 5 // 4

    def some(i):
        return jnp.minimum(i, 7)

    token = pl.BlockSpec((rows, width), lambda i: (i, 0))
    fc2 = pl.BlockSpec((n_fc2, width), lambda i: (some(i) % 4, 0))
    out = pl.BlockSpec((n_out, width), lambda i: (16 + some(i) % 4, 0))
    return pl.pallas_call(
        finish_kernel,
        grid=(9,),
        in_specs=[token] * 4
        + [
            whole(norm),
            pl.BlockSpec((1, size, n_qkv), lambda i: (some(i), 0, 0)),
            pl.BlockSpec((1, size, n_fc1), lambda i: (some(i), 0, 0)),
            fc2,
            fc2,
            out,
            out,
        ],
        out_specs=[
            token,
            token,
            pl.BlockSpec((size, n_qkv), lambda i: (0, some(i))),
            pl.BlockSpec((size, n_fc1), lambda i: (0, some(i))),
            pl.BlockSpec((n_fc2, width), lambda i: (some(i), 0)),
            pl.BlockSpec((n_out, width), lambda i: (some(i), 0)),
        ],
        out_shape=[
            jax.ShapeDtypeStruct((length, width), BF16),
            jax.ShapeDtypeStruct((length, width), BF16),
            jax.ShapeDtypeStruct((size, 8 * n_qkv), F32),
            jax.ShapeDtypeStruct((size, 8 * n_fc1), F32),
            jax.ShapeDtypeStruct((8 * n_fc2, width), F32),
            jax.ShapeDtypeStruct((8 * n_out, width), F32),
        ],
        compiler_params=pltpu.CompilerParams(vmem_limit_bytes=60 * 2**20),
        cost_estimate=pl.CostEstimate(flops=10**7, bytes_accessed=3 * 10**7, transcendentals=0),
        name="finish",
    )(tokens, cotangent, y_sum, dx, norm, qkv_grad, fc1_grad, rows_mine, rows_other, rows_mine, rows_other)


def body(
    tokens, ln1_gain, ln1_bias, ln2_gain, ln2_bias, qkv_weight, qkv_bias, out_weight, out_bias,
    fc1_weight, fc1_bias, fc2_weight, fc2_bias, cotangent, extra,
):
    vectors = [ln1_gain, ln1_bias, ln2_gain, ln2_bias, out_bias, fc2_bias, qkv_bias, fc1_bias]
    if extra > 1:
        join = functools.partial(lax.all_gather, axis_name="e", axis=0, tiled=True)
        vectors = [join(v) for v in vectors]
        qkv_weight, out_weight, fc1_weight, fc2_weight = [
            join(w) for w in (qkv_weight, out_weight, fc1_weight, fc2_weight)
        ]
    length, width = tokens.shape[1:]
    tables = jnp.asarray(rotary_tables(length))

    small = jnp.concatenate([v.reshape(-1, 128) for v in vectors], axis=0)
    small = jnp.pad(small, ((0, -small.shape[0] % 16), (0, 0)))
    (
        g_all, small, qkv_cols, fc1_cols, fc2_rows, out_rows, a1, a2, heads, mixed, hidden, slope, y_part
    ) = forward(tokens[0], cotangent[0], small, qkv_weight, fc1_weight, fc2_weight, out_weight, tables)
    small = small.astype(F32)
    norm = jnp.stack([small[:, i].reshape(-1) for i in range(8)])
    y_sum, dx, rows_total, rows_other, qkv_grad, fc1_grad, _, small_grads = backward(
        y_part, g_all, hidden, mixed, heads, slope, norm, qkv_cols, fc1_cols, fc2_rows, out_rows, tables, a1, a2
    )
    output, input_grad, qkv_grad, fc1_grad, fc2_grad, out_grad = finish(
        tokens[0], cotangent[0], y_sum, dx, norm, qkv_grad, fc1_grad, rows_total, rows_other
    )
    cuts = np.cumsum([1, 1, 1, 1, 1, qkv_bias.shape[0] * extra // 128, fc1_bias.shape[0] * extra // 128])
    small_grads = [v.reshape(-1) for v in jnp.split(small_grads, cuts, axis=0)[:-1]]

    weight_grads = [qkv_grad, out_grad, fc1_grad, fc2_grad]
    if extra > 1:
        scatter = functools.partial(lax.psum_scatter, axis_name="e", scatter_dimension=0, tiled=True)
        weight_grads = [scatter(v) for v in weight_grads]
        small_grads = [scatter(v) for v in small_grads]
    qkv_grad, out_grad, fc1_grad, fc2_grad = weight_grads
    gain1, bias1, gain2, bias2, total, packed_bias, up_bias = small_grads
    return (
        output[None],
        input_grad[None],
        gain1,
        bias1,
        gain2,
        bias2,
        qkv_grad,
        packed_bias,
        out_grad,
        total,
        fc1_grad,
        up_bias,
        fc2_grad,
        total,
    )


def solution(mesh):
    extra = mesh.shape["shard"] // 16
    axes = ("y", "hi", "lo", "x", "c", "e")
    fine = Mesh(mesh.devices.reshape(2, 2, 2, 2, 2, extra), axes)
    split = P(axes, None, None)
    row, flat = P(axes[1:], None), P(axes[1:])
    in_specs = (split, flat, flat, flat, flat, row, flat, row, flat, row, flat, row, flat, split)
    out_specs = (split, split, flat, flat, flat, flat, row, flat, row, flat, row, flat, row, flat)
    return jax.shard_map(
        functools.partial(body, extra=extra), mesh=fine, in_specs=in_specs, out_specs=out_specs, check_vma=False
    )
```

```python
import functools

import jax
import jax.numpy as jnp
import numpy as np
from jax import lax
from jax.experimental import pallas as pl
from jax.experimental.pallas import tpu as pltpu
from jax.sharding import Mesh
from jax.sharding import PartitionSpec as P

HEADS = 8
HEAD_DIM = 256
ROTARY = 64
EPS = 1e-05
NEG_FILL = -1e30
SCALE = HEAD_DIM ** (-0.5)
BF16 = jnp.bfloat16
F32 = jnp.float32
NT = (((1,), (1,)), ((), ()))
TN = (((0,), (0,)), ((), ()))
NN = (((1,), (0,)), ((), ()))


def dot(a, b, dims=NN):
    return lax.dot_general(a, b, dims, preferred_element_type=F32)


NAMES = ("y", "hi", "lo", "x", "c")

X, G, QKV, FC1, FC2, OUT, Y, DX, ROWS, SMALL = range(10)
OWN, NEXT, ONWARD, BY_X, BY_LO, HI, CORE, ALONG_Y, FIRST, SECOND, THIRD, LAST, ADD, PASS, FAR, RELAY, STEP, END = range(18)
PLACE = {"lo": 1, "x": 2, "y": 4}


def chunks_of(length, plan):
    chunks, start, share = [], 0, 0
    for part, order in plan:
        share += part
        end = length * share // 288 * 16 if share < 18 else length
        chunks.append((start, end - start, order))
        start = end
    return chunks


SCATTER_CHUNKS = ((9, ("lo", "y", "x")), (4, ("x", "lo", "y")), (5, ("y", "lo", "x")))
SCATTER_EVENTS = (
    (
        (Y, FIRST, 1, 0), (Y, FIRST, 1, 3), (Y, FIRST, 0, 3), (Y, FIRST, 2, 3), (Y, FIRST, 0, 2), (Y, FIRST, 1, 2),
    ),
    (),
    (),
    (
        (ROWS, CORE, 1),
    ),
    (
        (Y, FIRST, 1, 1),
    ),
    (
        (Y, SECOND, 1, 3), (Y, SECOND, 1, 2), (ROWS, ADD, 1), (Y, FIRST, 2, 2),
    ),
    (
        (Y, SECOND, 2, 3),
    ),
    (),
    (),
    (),
    (),
    (
        (Y, THIRD, 1),
    ),
    (
        (Y, SECOND, 0, 3), (Y, SECOND, 0, 2), (Y, FIRST, 0, 1), (FC1, CORE, 0),
    ),
    (
        (FC1, CORE, 1), (Y, SECOND, 2, 2), (Y, FIRST, 2, 1), (FC1, ADD, 0), (FC1, HI, 0),
    ),
    (
        (FC1, CORE, 2), (FC1, ADD, 1),
    ),
    (
        (FC1, CORE, 3), (FC1, ADD, 2),
    ),
    (
        (Y, FIRST, 0, 0), (FC1, CORE, 4), (FC1, ADD, 3),
    ),
    (
        (Y, LAST, 1), (FC1, ADD, 4), (FC1, PASS, 0), (FC1, CORE, 5), (FC1, HI, 1),
    ),
    (
        (FC1, CORE, 6), (FC1, ADD, 5),
    ),
    (
        (FC1, CORE, 7), (FC1, ADD, 6), (Y, FIRST, 2, 0), (FC1, ADD, 7),
    ),
    (
        (Y, THIRD, 2),
    ),
    (
        (ROWS, CORE, 0), (FC1, HI, 2), (FC1, PASS, 1), (FC1, FAR, 0),
    ),
    (
        (ROWS, ADD, 0),
    ),
    (
        (Y, THIRD, 0), (DX, FIRST, 1, 3), (ROWS, HI, 0), (DX, FIRST, 1, 1),
    ),
    (
        (FC1, RELAY, 1), (FC1, PASS, 2), (Y, LAST, 2),
    ),
    (
        (DX, FIRST, 0, 2), (FC1, RELAY, 3),
    ),
    (
        (DX, FIRST, 0, 3), (FC1, RELAY, 2),
    ),
    (),
    (),
    (
        (Y, LAST, 0), (DX, SECOND, 1, 3), (DX, FIRST, 1, 0), (DX, FIRST, 1, 2),
    ),
    (
        (QKV, CORE, 0),
    ),
    (
        (QKV, CORE, 1), (QKV, ADD, 0), (DX, FIRST, 2, 3),
    ),
    (
        (QKV, CORE, 2), (QKV, ADD, 1),
    ),
    (
        (QKV, CORE, 3), (QKV, ADD, 2), (DX, SECOND, 0, 3), (DX, SECOND, 0, 2), (QKV, ADD, 3), (DX, SECOND, 1, 2),
        (DX, THIRD, 1), (DX, SECOND, 2, 3), (DX, FIRST, 2, 2),
    ),
    (
        (QKV, CORE, 4),
    ),
    (
        (QKV, CORE, 5), (QKV, ADD, 4),
    ),
    (
        (QKV, CORE, 6), (QKV, ADD, 5),
    ),
    (
        (SMALL, STEP, 0), (QKV, ADD, 6), (DX, FIRST, 0, 1), (QKV, CORE, 7), (QKV, ADD, 7), (DX, FIRST, 2, 1),
        (DX, SECOND, 2, 2), (QKV, HI, 0), (DX, LAST, 1), (ROWS, ALONG_Y, 0), (SMALL, STEP, 1), (SMALL, STEP, 2),
        (QKV, HI, 1), (SMALL, STEP, 3), (DX, FIRST, 2, 0), (QKV, PASS, 0), (DX, THIRD, 2), (SMALL, STEP, 4),
        (SMALL, END, 0), (DX, FIRST, 0, 0), (DX, THIRD, 0), (QKV, HI, 2), (QKV, PASS, 1), (QKV, FAR, 0),
        (DX, LAST, 2), (QKV, RELAY, 3), (FC1, HI, 3), (QKV, PASS, 2), (QKV, RELAY, 1), (QKV, RELAY, 2), (QKV, HI, 3),
        (FC1, PASS, 3), (ROWS, END, 0), (DX, LAST, 0), (QKV, PASS, 3), (FC1, END, 0), (QKV, END, 0),
    ),
)


GATHER_CHUNKS = ((9, ("y", "lo", "x")), (9, ("lo", "x", "y")))
GATHER_EVENTS = (
    (
        (FC2, HI, 0), (OUT, HI, 0), (SMALL, STEP, 0), (X, OWN, 1, 0), (QKV, CORE, 0), (X, OWN, 0, 1), (X, OWN, 1, 1),
        (QKV, BY_X, 0), (X, OWN, 0, 2), (QKV, BY_LO, 0), (X, OWN, 1, 2), (QKV, HI, 0), (X, OWN, 0, 0), (FC1, CORE, 0),
        (SMALL, STEP, 1), (SMALL, STEP, 2), (SMALL, STEP, 3), (QKV, BY_X, 1), (SMALL, STEP, 4), (FC1, BY_X, 0),
        (G, OWN, 0, 0), (QKV, BY_LO, 1), (QKV, CORE, 1), (X, NEXT, 0, 1), (X, NEXT, 0, 2), (QKV, CORE, 2),
        (QKV, HI, 2), (QKV, CORE, 4), (QKV, HI, 1), (OUT, CORE, 0), (OUT, ALONG_Y, 0), (FC1, BY_X, 1),
        (X, ONWARD, 1, 0), (OUT, CORE, 1), (FC1, CORE, 1), (QKV, CORE, 3), (G, OWN, 1, 2), (QKV, HI, 3),
        (G, OWN, 1, 1), (QKV, CORE, 6), (FC1, HI, 1), (QKV, CORE, 5), (G, NEXT, 0, 2), (G, ONWARD, 1, 0),
        (FC1, BY_LO, 1), (FC1, BY_LO, 0), (X, NEXT, 1, 1), (X, NEXT, 1, 2), (X, ONWARD, 0, 0), (FC1, HI, 0),
        (QKV, CORE, 7),
    ),
    (),
    (),
    (
        (FC1, CORE, 5), (X, ONWARD, 0, 1), (G, OWN, 1, 0), (X, ONWARD, 1, 1), (FC1, HI, 3), (FC1, CORE, 3),
        (FC1, CORE, 2),
    ),
    (
        (FC1, HI, 2), (FC1, CORE, 4),
    ),
    (),
    (
        (G, OWN, 0, 2),
    ),
    (),
    (
        (G, NEXT, 0, 1), (FC2, CORE, 0), (FC2, ALONG_Y, 0), (G, NEXT, 1, 1), (FC1, CORE, 7), (FC1, CORE, 6),
    ),
    (),
    (
        (G, OWN, 0, 1), (G, ONWARD, 0, 1),
    ),
    (),
    (
        (FC2, CORE, 1), (G, ONWARD, 1, 1),
    ),
    (),
    (
        (G, ONWARD, 0, 0),
    ),
    (),
    (
        (G, NEXT, 1, 2),
    ),
    (),
    (),
    (),
    (),
    (),
    (),
    (),
    (),
)


class Copies:
    def __init__(self, at, send_sem, recv_sem, local_sem):
        self.at, self.send_sem, self.recv_sem, self.local_sem = at, send_sem, recv_sem, local_sem
        self.remote, self.planned, self.local, self.seen = [], 0, 0, set()

    def plan(self, src, dst, axis, everywhere=True):
        spot = self.planned
        self.planned += 1
        copy = pltpu.make_async_remote_copy(
            src_ref=src,
            dst_ref=dst,
            send_sem=self.send_sem.at[spot],
            recv_sem=self.recv_sem.at[spot],
            device_id={axis: 1 - self.at[axis]},
            device_id_type=pl.DeviceIdType.MESH,
        )
        if everywhere:
            self.remote.append(copy)
        return copy

    def arrive(self, *copies):
        for copy in copies:
            if id(copy) not in self.seen:
                self.seen.add(id(copy))
                copy.wait_recv()

    def move(self, src, dst):
        copy = pltpu.make_async_copy(src, dst, self.local_sem.at[self.local])
        self.local += 1
        return copy


def greet(at, names):
    barrier = pltpu.get_barrier_semaphore()
    for name in names:
        pl.semaphore_signal(
            barrier, inc=1, device_id={name: 1 - at[name]}, device_id_type=pl.DeviceIdType.MESH
        )
    pl.semaphore_wait(barrier, len(names))


class TokenGather:
    def __init__(self, copies, own, full, name, events):
        self.copies, self.plans = copies, {}
        self.kept = copies.move(own, full.at[0])
        self.chunks = chunks_of(own.shape[0], GATHER_CHUNKS)
        for chunk, (start, rows, order) in enumerate(self.chunks):
            part = pl.ds(start, rows)
            one, two, _ = (PLACE[axis] for axis in order)
            hops = [((OWN, chunk, i), 0, axis) for i, axis in enumerate(order)]
            hops += [((NEXT, chunk, 1), one, order[1]), ((NEXT, chunk, 2), one, order[2])]
            hops += [((ONWARD, chunk, 0), two, order[2]), ((ONWARD, chunk, 1), one + two, order[2])]
            for label, block, axis in hops:
                src = own.at[part] if block == 0 else full.at[block, part]
                there = block + PLACE[axis]
                self.plans[chunk, there] = copies.plan(src, full.at[there, part], axis)
                events[(name,) + label] = functools.partial(self.send, chunk, block, there)

    def send(self, chunk, block, there):
        if block:
            self.copies.arrive(self.plans[chunk, block])
        self.plans[chunk, there].start()

    def take(self, block):
        for chunk in range(len(self.chunks)):
            self.copies.arrive(self.plans[chunk, block])

    def finish(self):
        for block in range(1, 8):
            self.take(block)
        self.kept.wait()


class TokenScatter:
    def __init__(self, copies, parts, came, far_parts, stage, room, total, name, events):
        self.copies, self.parts, self.came, self.far_parts = copies, parts, came, far_parts
        self.stage, self.room = stage, room
        self.chunks = chunks_of(parts.shape[1], SCATTER_CHUNKS)
        self.first, self.second, self.third, self.stores, self.loads, self.near = {}, {}, [], [], {}, {}
        base = copies.local
        for chunk, (start, rows, order) in enumerate(self.chunks):
            third, second, first = order
            part = pl.ds(start, rows)
            for slot in (3, 2, 1, 0):
                block = self.block(chunk, slot)
                src = parts.at[block + PLACE[first], part]
                self.first[chunk, slot] = copies.plan(src, came.at[slot, part], first)
                near = came.at[slot, part] if far_parts else parts.at[block, part]
                if slot > 1:
                    self.second[chunk, slot] = copies.plan(near, came.at[2 + slot, part], second)
                if slot == 1:
                    self.third.append(copies.plan(near, came.at[6, part], third))
                self.near[chunk, slot] = near
                if far_parts:
                    copies.local = base + chunk
                    self.loads[chunk, slot] = [copies.move(parts.at[block, part], stage.at[part])]
                else:
                    copies.local = base
                    self.loads[chunk, slot] = [
                        copies.move(came.at[i, part], stage.at[spot, pl.ds(0, rows)])
                        for spot, i in enumerate(self.terms(slot))
                    ]
                events[name, FIRST, chunk, slot] = self.first[chunk, slot].start
            events[name, SECOND, chunk, 3] = functools.partial(self.pass_second, chunk, 3)
            events[name, SECOND, chunk, 2] = functools.partial(self.pass_second, chunk, 2)
            events[name, THIRD, chunk] = functools.partial(self.pass_third, chunk)
            events[name, LAST, chunk] = functools.partial(self.last, chunk)
        copies.local = base + max(3, len(self.chunks))
        for start, rows, _ in self.chunks:
            self.stores.append(copies.move(room.at[pl.ds(0, rows)], total.at[pl.ds(start, rows)]))

    def block(self, chunk, slot):
        third, second, _ = self.chunks[chunk][2]
        return PLACE[second] * (slot // 2) + PLACE[third] * (slot % 2)

    def terms(self, slot):
        return {0: (0, 4, 6), 1: (1, 5)}.get(slot, (slot,))

    def prepare(self):
        if self.far_parts:
            for chunk in range(len(self.chunks)):
                self.loads[chunk, 3][0].start()

    def add(self, chunk, slot):
        start, rows, _ = self.chunks[chunk]
        part = pl.ds(start, rows)
        self.copies.arrive(self.first[chunk, slot])
        loads = self.loads[chunk, slot]
        if self.far_parts:
            loads[0].wait()
            value = self.stage[part].astype(F32)
            for i in self.terms(slot):
                value = value + self.came[i, part].astype(F32)
            if slot > 0:
                self.loads[chunk, slot - 1][0].start()
            return value
        for copy in loads:
            copy.start()
        value = self.parts[self.block(chunk, slot), part].astype(F32)
        for spot, copy in enumerate(loads):
            copy.wait()
            value = value + self.stage[spot, :rows].astype(F32)
        return value

    def pass_second(self, chunk, slot):
        self.near[chunk, slot][...] = self.add(chunk, slot).astype(BF16)
        self.second[chunk, slot].start()

    def pass_third(self, chunk):
        self.copies.arrive(self.second[chunk, 3])
        self.near[chunk, 1][...] = self.add(chunk, 1).astype(BF16)
        self.third[chunk].start()

    def last(self, chunk):
        self.copies.arrive(self.second[chunk, 2], self.third[chunk])
        self.room[: self.chunks[chunk][1]] = self.add(chunk, 0)
        self.stores[chunk].start()
        self.stores[chunk].wait()


class ColumnGather:
    def __init__(self, copies, weight, full, relay, name, events):
        at = copies.at
        hi, lo, x, c = (at[n] for n in ("hi", "lo", "x", "c"))
        rows, width = weight.shape[0], full.shape[1]

        def block(lo_at, x_at):
            spot = (at["y"] * 2 + lo_at) * 2 + x_at
            return weight.at[:, pl.ds(pl.multiple_of(spot * width, 128), width)]

        def place(hi_at, lo_at, x_at):
            spot = ((hi_at * 2 + lo_at) * 2 + x_at) * 2 + c
            return full.at[pl.ds(pl.multiple_of(spot * rows, 128), rows)]

        mine = place(hi, lo, x)
        self.by_x = [copies.plan(block(1 - lo, 1 - x), relay, "x"), copies.plan(block(lo, 1 - x), mine, "x")]
        self.by_lo = [
            copies.plan(block(1 - lo, x), mine, "lo"),
            copies.plan(relay, place(hi, lo, 1 - x), "lo"),
        ]
        near = [place(hi, lo, x), place(hi, lo, 1 - x), place(hi, 1 - lo, x), place(hi, 1 - lo, 1 - x)]
        far = [place(1 - hi, lo, x), place(1 - hi, lo, 1 - x), place(1 - hi, 1 - lo, x), place(1 - hi, 1 - lo, 1 - x)]
        source = [block(lo, x)] + near[1:]
        self.by_hi = [copies.plan(src, dst, "hi") for src, dst in zip(source, near)]
        self.by_c = [copies.plan(src, dst, "c") for src, dst in zip(source + far, near + far)]
        self.kept = copies.move(block(lo, x), mine)
        self.copies = copies
        by_hi, by_c = self.by_hi, self.by_c
        x_then, lo_then = self.by_x, self.by_lo
        hops = [((BY_X, i), None, x_then[i]) for i in range(2)]
        hops += [((BY_LO, 0), None, lo_then[0]), ((BY_LO, 1), x_then[0], lo_then[1])]
        came = [None, x_then[1], lo_then[0], lo_then[1]]
        hops += [((HI, i), came[i], by_hi[i]) for i in range(4)]
        hops += [((CORE, i), copy, by_c[i]) for i, copy in enumerate(came + by_hi)]
        for label, first, copy in hops:
            events[(name,) + label] = functools.partial(self.send, first, copy)

    def send(self, first, copy):
        if first is not None:
            self.copies.arrive(first)
        copy.start()

    def finish(self):
        self.copies.arrive(*self.by_c)
        self.kept.wait()


class RowGather:
    def __init__(self, copies, weight, full, name, events):
        at, rows = copies.at, weight.shape[0]
        half = rows // 2

        def spot(start, count):
            return full.at[pl.ds(pl.multiple_of(start, 16), count)]

        self.copies = copies
        self.holds = 1 - (at["hi"] + at["y"]) % 2
        first, second = spot(at["c"] * rows, half), spot(at["c"] * rows + half, half)
        there = spot(self.holds * (at["c"] * rows) + (1 - self.holds) * 2 * rows, half)
        source = weight.at[pl.ds(pl.multiple_of((1 - self.holds) * half, 16), half)]
        self.by_hi = copies.plan(source, there, "hi")
        self.by_y = copies.plan(spot(2 * rows, half), second, "y", everywhere=False)
        self.by_c = [copies.plan(first, first, "c"), copies.plan(second, second, "c")]
        self.kept = copies.move(weight, spot(at["c"] * rows, rows))
        events[name, HI, 0], events[name, ALONG_Y, 0] = self.start, self.relay
        events[name, CORE, 0], events[name, CORE, 1] = self.first_to_c, self.second_to_c

    def start(self):
        self.by_hi.start()
        pl.when(self.holds == 1)(self.kept.start)

    def ready(self):
        if id(self.by_hi) not in self.copies.seen:
            self.copies.arrive(self.by_hi)
            pl.when(self.holds == 1)(self.kept.wait)

    def relay(self):
        self.ready()
        pl.when(self.holds == 1)(self.by_y.start)

    def first_to_c(self):
        self.ready()
        self.by_c[0].start()

    def second_to_c(self):
        self.ready()
        pl.when(self.holds == 0)(self.by_y.wait_recv)
        self.by_c[1].start()

    def finish(self):
        for copy in self.by_c:
            copy.wait_recv()

    def sent(self):
        pl.when(self.holds == 1)(self.by_y.wait_send)


class SmallGather:
    def __init__(self, copies, full):
        at = copies.at
        base = ((at["hi"] * 2 + at["lo"]) * 2 + at["x"]) * 2 + at["c"]
        self.own = full.at[pl.ds(base, 1)]
        self.steps, count = [], 1
        for name in ("c", "x", "lo", "hi"):
            part = full.at[pl.ds(base, count)]
            self.steps.append(copies.plan(part, part, name))
            base = base - at[name] * count
            count *= 2

    def step(self, at):
        if at > 0:
            self.steps[at - 1].wait_recv()
        if at < 4:
            self.steps[at].start()


def rotary_tables(length):
    places = np.arange(length, dtype=np.float32)
    frequency = (10000.0 ** (-np.arange(0, ROTARY, 2, dtype=np.float32) / ROTARY)).astype(np.float32)
    angles = places[:, None] * frequency[None, :]
    cosine, sine = np.cos(angles), np.sin(angles)
    half = ROTARY // 2
    tables = np.zeros((3, length, 2 * ROTARY), np.float32)
    tables[0] = 1.0
    tables[0, :, :half] = cosine
    tables[0, :, half:ROTARY] = cosine
    tables[1, :, :half] = -sine
    tables[2, :, half:ROTARY] = sine
    return tables


def turn(rows, tables, sign):
    half, wide = ROTARY // 2, 2 * ROTARY
    near = rows[:, :wide]
    ahead = pltpu.roll(near, wide - half, 1)
    behind = pltpu.roll(near, half, 1)
    near = near * tables[0] + sign * (ahead * tables[1] + behind * tables[2])
    return jnp.concatenate([near, rows[:, wide:]], axis=1)


def causal_scores(queries, keys_all):
    length = queries.shape[0]
    scores = dot(queries, keys_all, NT) * SCALE
    row = lax.broadcasted_iota(jnp.int32, (length, length), 0)
    col = lax.broadcasted_iota(jnp.int32, (length, length), 1)
    return jnp.where(row >= col, scores, NEG_FILL)


def softmax(scores):
    raised = jnp.exp(scores - jnp.max(scores, axis=-1, keepdims=True))
    return raised / jnp.sum(raised, axis=-1, keepdims=True)


MLP_AT, OUTPUT_AT, FORWARD_STEPS = 8, 16, 24


def forward_kernel(
    x_ref, g_ref, small_ref, qkv_ref, fc1_ref, fc2_ref, out_ref, tables_ref,
    g_all, norm_out, qkv_out, fc1_out, fc2_out, out_out,
    a1_ref, a2_ref, heads_ref, mixed_ref, hidden_ref, slope_ref, y_ref,
    x_all, small_all, qkv_all, fc1_all, fc2_all, out_all, norm, qkv_bias, fc1_bias, mixed_all, hidden_all,
    relay_qkv, relay_fc1, send_sem, recv_sem, local_sem,
):
    step = pl.program_id(0)
    at = {name: lax.axis_index(name) for name in NAMES}
    copies = Copies(at, send_sem, recv_sem, local_sem)
    events = {}
    small = SmallGather(copies, small_all)
    qkv = ColumnGather(copies, qkv_ref, qkv_all, relay_qkv, QKV, events)
    fc1 = ColumnGather(copies, fc1_ref, fc1_all, relay_fc1, FC1, events)
    fc2 = RowGather(copies, fc2_ref, fc2_all, FC2, events)
    out = RowGather(copies, out_ref, out_all, OUT, events)
    x = TokenGather(copies, x_ref, x_all, X, events)
    g = TokenGather(copies, g_ref, g_all, G, events)
    kept = [
        copies.move(src.at[pl.ds(0, dst.shape[0])], dst)
        for src, dst in ((qkv_all, qkv_out), (fc1_all, fc1_out), (fc2_all, fc2_out), (out_all, out_out))
    ]

    def spread_small():
        small.step(4)
        for spot in range(16):
            norm[:, spot * 128 : (spot + 1) * 128] = small_all[spot, :8].astype(F32)
        first = (at["y"] * 4 + at["lo"] * 2 + at["x"]) * 2
        for half in range(2):
            own = small_all[first + half].astype(F32)
            for bias, start in ((qkv_bias, 6), (fc1_bias, 6 + qkv_bias.shape[1] // 256)):
                rows = bias.shape[1] // 256
                for i in range(rows):
                    bias[:, (half * rows + i) * 128 : (half * rows + i + 1) * 128] = own[start + i : start + i + 1]

    for i in range(4):
        events[SMALL, STEP, i] = functools.partial(small.step, i)
    events[SMALL, STEP, 4] = spread_small

    def before(spot):
        if spot == 0:
            greet(at, NAMES)
            small.own[...] = small_ref[...][None]
            for copy in (x.kept, g.kept, qkv.kept, fc1.kept):
                copy.start()
        for label in GATHER_EVENTS[spot]:
            events[label]()
        if spot == 0:
            x.kept.wait()
            qkv.finish()
            kept[0].start()
        elif spot < MLP_AT:
            x.take(spot)
        elif spot == MLP_AT:
            fc1.finish()
            kept[1].start()
        elif spot == OUTPUT_AT:
            fc2.finish()
            out.finish()
            kept[2].start()
            kept[3].start()

    for spot in range(FORWARD_STEPS):
        pl.when(step == spot)(functools.partial(before, spot))

    def normed(j, line):
        value = x_all[j].astype(F32)
        centred = value - jnp.mean(value, axis=-1, keepdims=True)
        var = jnp.mean(centred * centred, axis=-1, keepdims=True)
        return (centred * lax.rsqrt(var + EPS) * norm[line : line + 1] + norm[line + 1 : line + 2]).astype(BF16)

    @pl.when(step < MLP_AT)
    def _():
        a1_ref[0] = normed(step, 0)
        packed = dot(a1_ref[0], qkv_all[...]) + qkv_bias[...]
        queries = turn(packed[:, :HEAD_DIM], tables_ref, 1.0).astype(BF16)
        keys_all = turn(packed[:, HEAD_DIM : 2 * HEAD_DIM], tables_ref, 1.0).astype(BF16)
        values_all = packed[:, 2 * HEAD_DIM :].astype(BF16)
        heads_ref[0, :, :HEAD_DIM] = queries
        heads_ref[0, :, HEAD_DIM : 2 * HEAD_DIM] = keys_all
        heads_ref[0, :, 2 * HEAD_DIM :] = values_all
        probs = softmax(causal_scores(queries, keys_all)).astype(BF16)
        mixed_ref[0] = dot(probs, values_all).astype(BF16)
        mixed_all[step] = mixed_ref[0]

    @pl.when((step >= MLP_AT) & (step < OUTPUT_AT))
    def _():
        j = step - MLP_AT
        a2_ref[0] = normed(j, 2)
        upward = dot(a2_ref[0], fc1_all[...]) + fc1_bias[...]
        below = 0.5 * (1.0 + lax.erf(upward * np.float32(0.5**0.5)))
        hidden_ref[0] = (upward * below).astype(BF16)
        hidden_all[j] = hidden_ref[0]
        slope_ref[0] = below + upward * (jnp.exp(-0.5 * upward * upward) * np.float32((2 * np.pi) ** -0.5))

    @pl.when(step >= OUTPUT_AT)
    def _():
        j = step - OUTPUT_AT
        y = dot(hidden_all[j], fc2_all[: hidden_ref.shape[2]])
        y_ref[0] = (y + dot(mixed_all[j], out_all[: mixed_ref.shape[2]])).astype(BF16)

    @pl.when(step == FORWARD_STEPS - 1)
    def _():
        norm_out[...] = norm[...]
        for label in GATHER_EVENTS[FORWARD_STEPS]:
            events[label]()
        g.finish()
        for copy in kept:
            copy.wait()
        for copy in copies.remote:
            copy.wait_send()
        fc2.sent()
        out.sent()


def forward(tokens, cotangent, small, qkv_weight, fc1_weight, fc2_weight, out_weight, tables):
    far = pl.BlockSpec(memory_space=pl.ANY)
    length, width = tokens.shape
    rows = qkv_weight.shape[0]
    n_qkv, n_fc1, n_mix = qkv_weight.shape[1] // 8, fc1_weight.shape[1] // 8, out_weight.shape[0] * 2
    each = [(width, BF16), (width, BF16), (n_qkv, BF16), (n_mix, BF16), (n_fc1, BF16), (n_fc1, F32), (width, BF16)]
    count = 4 + 2 * 16 + 2 * 4 + 2 * 7 * len(GATHER_CHUNKS)
    weights = [(16 * rows, n_qkv), (16 * rows, n_fc1), (n_fc1, width), (n_mix, width)]
    flops = 2 * 8 * length * width * (n_qkv + n_fc1 + n_fc1 + n_mix)
    return pl.pallas_call(
        forward_kernel,
        grid=(FORWARD_STEPS,),
        in_specs=[far, far, whole(small), far, far, far, far, whole(tables)],
        out_specs=[far, whole(jax.ShapeDtypeStruct((8, width), F32)), far, far, far, far]
        + [
            pl.BlockSpec((1, length, n), lambda i, start=start: (jnp.clip(i - start, 0, 7), 0, 0))
            for (n, _), start in zip(each, (0, MLP_AT, 0, 0, MLP_AT, MLP_AT, OUTPUT_AT))
        ],
        out_shape=[
            jax.ShapeDtypeStruct((8, length, width), BF16),
            jax.ShapeDtypeStruct((8, width), F32),
        ]
        + [jax.ShapeDtypeStruct(shape, BF16) for shape in weights]
        + [jax.ShapeDtypeStruct((8, length, n), kind) for n, kind in each],
        scratch_shapes=[
            pltpu.VMEM((8, length, width), BF16),
            pltpu.VMEM((16,) + small.shape, BF16),
            pltpu.VMEM(weights[0], BF16),
            pltpu.VMEM(weights[1], BF16),
            pltpu.VMEM((n_fc1 * 5 // 4, width), BF16),
            pltpu.VMEM((n_mix * 5 // 4, width), BF16),
            pltpu.VMEM((8, width), F32),
            pltpu.VMEM((1, n_qkv), F32),
            pltpu.VMEM((1, n_fc1), F32),
            pltpu.VMEM((8, length, n_mix), BF16),
            pltpu.VMEM((8, length, n_fc1), BF16),
            pltpu.VMEM((rows, n_qkv), BF16),
            pltpu.VMEM((rows, n_fc1), BF16),
            pltpu.SemaphoreType.DMA((count,)),
            pltpu.SemaphoreType.DMA((count,)),
            pltpu.SemaphoreType.DMA((10,)),
        ],
        compiler_params=pltpu.CompilerParams(
            collective_id=1, has_side_effects=True, vmem_limit_bytes=60 * 2**20
        ),
        cost_estimate=pl.CostEstimate(flops=flops, bytes_accessed=10**8, transcendentals=0),
        name="forward",
    )(tokens, cotangent, small, qkv_weight, fc1_weight, fc2_weight, out_weight, tables)


def add_rows(dst, dst_row, src, src_row, count, lanes=None, src_lanes=None):
    lanes = lanes or slice(None)
    src_lanes = src_lanes or lanes
    for start in range(0, count, 64):
        here = pl.ds(pl.multiple_of(dst_row + start, 16), 64)
        there = pl.ds(pl.multiple_of(src_row + start, 16), 64)
        dst[here, lanes] = (dst[here, lanes].astype(F32) + src[there, src_lanes].astype(F32)).astype(BF16)


class RowScatter:
    def __init__(self, copies, wide, slim, late, kept, came, n_fc2, n_out, other, events):
        at = copies.at
        c = at["c"]
        self.copies, self.kept, self.came, self.late = copies, kept, came, late
        self.holds = 1 - (at["hi"] + at["y"]) % 2
        own, half = n_fc2 + n_out, (n_fc2 // 2, n_out // 2)
        width, tile = kept.shape[1], 2 * n_out
        self.cuts = [(wide, i, i * 2 * n_fc2, wide.shape[1]) for i in range(width // wide.shape[1])]
        self.slim_cuts = [
            (slim, i, i * tile, min(slim.shape[1], width - i * slim.shape[1]))
            for i in range(-(-width // slim.shape[1]))
        ]

        def rows(ref, start, count):
            return ref.at[pl.ds(pl.multiple_of(start, 16), count)]

        self.pieces = [[(late, 0, half[0], half[0], 0, slice(0, width), width)], []]
        for ref, i, first, lanes in self.cuts:
            there = slice(i * lanes, (i + 1) * lanes)
            self.pieces[1].append((ref, first + half[0], n_fc2, half[0], half[0], there, lanes))
        for ref, i, first, lanes in self.slim_cuts:
            there = slice(i * ref.shape[1], i * ref.shape[1] + lanes)
            self.pieces[1].append((ref, first, n_out, n_out, n_fc2, there, lanes))
        self.c = c
        self.by_c = []
        for pieces in self.pieces:
            made = []
            for ref, first, size, n, to, there, lanes in pieces:
                src = ref.at[pl.ds(pl.multiple_of(first + (1 - c) * size, 16), n), pl.ds(0, lanes)]
                dst = kept.at[pl.ds(to, n), pl.ds(there.start, lanes)]
                made.append(copies.plan(src, dst, "c"))
            self.by_c.append(made)
        self.by_y = [
            copies.plan(rows(kept, half[0], half[0]), rows(kept, own, half[0]), "y"),
            copies.plan(rows(kept, n_fc2 + half[1], half[1]), rows(kept, own + half[0], half[1]), "y"),
        ]
        holds = self.holds
        sent = [holds * own, holds * (own + half[0]) + (1 - holds) * n_fc2]
        self.keeps = [(1 - holds) * own, (1 - holds) * (own + half[0]) + holds * n_fc2]
        self.by_hi = [
            copies.plan(rows(kept, sent[0], half[0]), rows(came, 0, half[0]), "hi"),
            copies.plan(rows(kept, sent[1], half[1]), rows(came, half[0], half[1]), "hi"),
        ]
        self.half = half
        self.on_y = copies.plan(came, other, "y")
        events[ROWS, CORE, 1] = functools.partial(self.send, self.by_c[1])
        events[ROWS, CORE, 0] = functools.partial(self.send, self.by_c[0])
        events[ROWS, HI, 0] = self.send_hi
        events[ROWS, END, 0] = functools.partial(copies.arrive, self.on_y)

    def store_tile(self, i, value):
        size = value.shape[0]
        if i in (0, 2):
            self.late[i // 2 * size : (i // 2 + 1) * size] = value.astype(BF16)
            return
        cuts = self.slim_cuts if i is None else self.cuts
        for ref, cut, first, lanes in cuts:
            start = first if i is None else first + i * size
            ref[start : start + size, :lanes] = value[:, cut * ref.shape[1] : cut * ref.shape[1] + lanes].astype(BF16)

    def send(self, made):
        for copy in made:
            copy.start()

    def add_c(self, side):
        for copy, (ref, first, size, n, to, there, lanes) in zip(self.by_c[side], self.pieces[side]):
            self.copies.arrive(copy)
            add_rows(self.kept, to, ref, first + self.c * size, n, there, slice(0, lanes))
        if side == 1:
            self.send(self.by_y)

    def send_hi(self):
        self.copies.arrive(*self.by_y)
        self.send(self.by_hi)

    def add_hi(self):
        self.copies.arrive(*self.by_hi)
        add_rows(self.came, 0, self.kept, self.keeps[0], self.half[0])
        add_rows(self.came, self.half[0], self.kept, self.keeps[1], self.half[1])
        self.on_y.start()


class ColumnScatter:
    def __init__(self, copies, starts, tile, room, by_hi, relay, full, name, events):
        at = copies.at
        self.copies, self.tile, self.room, self.came_hi = copies, tile, room, by_hi
        y, lo, x, c = (at[n] for n in ("y", "lo", "x", "c"))
        self.c = c
        self.by_c = [copies.plan(tile(i, 1 - c), room(i), "c") for i in range(8)]
        self.by_hi = [copies.plan(room(i), by_hi.at[i], "hi") for i in range(4)]

        def spot(lo_at, x_at):
            return full.at[(y * 2 + lo_at) * 2 + x_at]

        self.far = copies.plan(by_hi.at[0], relay, "lo")
        self.far_on = copies.plan(relay, spot(1 - lo, x), "x")
        self.by_lo = copies.plan(by_hi.at[1], spot(lo, x), "lo")
        self.by_x = copies.plan(by_hi.at[2], spot(lo, x), "x")
        self.mine = copies.move(by_hi.at[3], spot(lo, x))
        self.by_y = [
            copies.plan(by_hi.at[3], spot(lo, x), "y"),
            copies.plan(spot(1 - lo, x), spot(1 - lo, x), "y"),
            copies.plan(spot(lo, 1 - x), spot(lo, 1 - x), "y"),
            copies.plan(spot(1 - lo, 1 - x), spot(1 - lo, 1 - x), "y"),
        ]
        for i in range(8):
            events[name, CORE, i] = self.by_c[i].start
            events[name, ADD, i] = functools.partial(self.add_c, i)
        for i in range(4):
            events[name, HI, i] = self.by_hi[i].start
            events[name, PASS, i] = functools.partial(self.add_hi, i)
        for label, first, then in (
            ((FAR, 0), self.far, self.far_on),
            ((RELAY, 1), self.by_lo, self.by_y[1]),
            ((RELAY, 2), self.by_x, self.by_y[2]),
            ((RELAY, 3), self.far_on, self.by_y[3]),
        ):
            events[(name,) + label] = functools.partial(self.relay, first, then)
        events[name, END, 0] = self.finish

    def add_c(self, i):
        self.copies.arrive(self.by_c[i])
        here = self.room(i)
        here[...] = (here[...].astype(F32) + self.tile(i, self.c)[...].astype(F32)).astype(BF16)

    def add_hi(self, i):
        self.copies.arrive(self.by_hi[i])
        self.came_hi[i] = (self.came_hi[i].astype(F32) + self.room(4 + i)[...].astype(F32)).astype(BF16)
        if i < 3:
            (self.far, self.by_lo, self.by_x)[i].start()
        else:
            self.mine.start()
            self.by_y[0].start()

    def relay(self, first, then):
        self.copies.arrive(first)
        then.start()

    def finish(self):
        self.mine.wait()
        self.copies.arrive(*self.by_y)


class SmallScatter:
    def __init__(self, copies, parts, came):
        at = copies.at
        self.copies, self.parts, self.came, self.steps = copies, parts, came, []
        base, count, spot = 0, 8, 0
        for name in ("hi", "lo", "x", "c"):
            away = parts.at[pl.ds(base + (1 - at[name]) * count, count)]
            base = base + at[name] * count
            self.steps.append((copies.plan(away, came.at[pl.ds(spot, count)], name), base, spot, count))
            spot += count
            count //= 2
        own = parts.at[pl.ds(base, 1)]
        self.steps.append((copies.plan(own, came.at[pl.ds(spot, 1)], "y"), base, spot, 1))
        self.base, self.spot = base, spot

    def step(self, step):
        if step > 0:
            copy, base, spot, count = self.steps[step - 1]
            self.copies.arrive(copy)
            for i in range(count):
                self.parts[base + i] += self.came[spot + i]
        self.steps[step][0].start()

    def total(self):
        self.copies.arrive(self.steps[4][0])
        return self.parts[self.base] + self.came[self.spot]


SEQUENCES, COLUMN_TILES = 8, 8
UP_AT = 3
FC1_AT = UP_AT + SEQUENCES
LATE_ROWS_AT = FC1_AT + COLUMN_TILES
DX_AT = LATE_ROWS_AT + 2
QKV_AT = DX_AT + SEQUENCES
STEPS = QKV_AT + COLUMN_TILES


def sequence_at(step):
    i = jnp.clip(step - DX_AT, 0, SEQUENCES - 1)
    return 2 * (1 - i // 4) + (1 - i % 2) + 4 * (1 - (i % 4) // 2)


def backward_kernel(
    y_ref, g_ref, hidden_ref, mixed_ref, heads_ref, slope_ref, norm_ref, qkv_ref, fc1_ref, fc2_ref, out_ref, tables_ref,
    a1_ref, a2_ref,
    y_out, dx_out, rows_mine, rows_other, full_qkv, full_fc1, dx_came, small_out,
    g_all, grads, qkv, fc1, part, came, y_stage, dx_stage, room, kept, rows_came, a1, a2,
    qkv_hi, fc1_hi, qkv_relay, fc1_relay, packed_sum, up_sum, column_total, vectors, parts, parts_came,
    send_sem, recv_sem, local_sem, free_sem, free_again_sem,
):
    step = pl.program_id(0)
    at = {name: lax.axis_index(name) for name in NAMES}
    copies = Copies(at, send_sem, recv_sem, local_sem)
    events = {}
    n_fc1, n_mix, n_qkv = fc2_ref.shape[0], out_ref.shape[0], qkv_ref.shape[1]
    count, length, _ = g_all.shape
    tokens, tile = count * length, n_mix
    core = tile // 2
    y, hi, lo, x, c = (at[n] for n in NAMES)
    scatter_y = TokenScatter(copies, y_ref, came, True, y_stage, room, y_out, Y, events)
    TokenScatter(copies, g_all, dx_came, False, dx_stage, room, dx_out, DX, events)
    late = part.at[pl.ds(4 * core, 2 * tile)]
    rows = RowScatter(copies, fc1, qkv, late, kept, rows_came, n_fc1 // 2, n_mix // 2, rows_other, events)
    rows_store = copies.move(rows_came, rows_mine)

    hops = ((1 - lo, 1 - x), (1 - lo, x), (lo, 1 - x), (lo, x))
    places = [(hi_at * 2 + lo_at) * 2 + x_at for hi_at in (1 - hi, hi) for lo_at, x_at in hops]
    starts = [pl.multiple_of(place * tile, 128) for place in places]

    def fc1_tile(i, of):
        start = 4 * core + i % 4 // 2 * tile
        return part.at[pl.ds(pl.multiple_of(start + of * core, 16), core), pl.ds(i % 2 * n_fc1, n_fc1)]

    def fc1_room(i):
        return part.at[pl.ds(i % 4 * core, core), pl.ds(i // 4 * n_fc1, n_fc1)]

    def qkv_tile(i, of):
        return qkv.at[pl.ds(pl.multiple_of(starts[i] + of * core, 128), core)]

    def qkv_room(i):
        return part.at[pl.ds((4 + i % 4) * core, core), pl.ds(i // 4 * n_qkv, n_qkv)]

    fc1_out = ColumnScatter(copies, starts, fc1_tile, fc1_room, fc1_hi, fc1_relay, full_fc1, FC1, events)
    ColumnScatter(copies, starts, qkv_tile, qkv_room, qkv_hi, qkv_relay, full_qkv, QKV, events)
    small = SmallScatter(copies, parts, parts_came)
    load_g = copies.move(g_ref, g_all)
    early_loads = [
        copies.move(fc2_ref, part.at[pl.ds(0, n_fc1)]),
        copies.move(out_ref, part.at[pl.ds(n_fc1, n_mix)]),
    ]
    loads = [copies.move(qkv_ref, qkv), copies.move(fc1_ref, fc1)]

    def hidden_tile(i):
        return hidden_ref.at[:, pl.ds(i * tile, tile)]

    row_tiles = [
        (0, 1, a1, 0, copies.move(hidden_tile(1), a1.at[0])),
        (1, 3, a1, 1, copies.move(hidden_tile(3), a1.at[1])),
        (2, None, a2, 0, copies.move(mixed_ref, a2.at[0])),
        (LATE_ROWS_AT, 0, a1, 0, copies.move(hidden_tile(0), a1.at[0])),
        (LATE_ROWS_AT + 1, 2, a1, 1, copies.move(hidden_tile(2), a1.at[1])),
    ]

    def column_loads(src, dst):
        base, made = copies.local, []
        for i, start in enumerate(starts):
            copies.local = base + i % 2
            made.append(copies.move(src.at[:, pl.ds(start, tile)], dst.at[i % 2]))
        copies.local = base + 2
        return made

    a1_loads, a2_loads = column_loads(a1_ref, a1), column_loads(a2_ref, a2)

    def start_small():
        parts[...] = jnp.zeros_like(parts)
        lines = []
        for i in (0, 2):
            gain, bias = norm_ref[i : i + 1], norm_ref[i + 1 : i + 2]
            bias_grad = vectors[i + 1 : i + 2]
            lines += [(vectors[i : i + 1] - bias * bias_grad) / gain, bias_grad]
        lines.append(column_total[...])
        for spot in range(16):
            for i, line in enumerate(lines):
                parts[spot, i : i + 1] = line[:, spot * 128 : (spot + 1) * 128]
        own = (y * 4 + lo * 2 + x) * 2
        for half in range(2):
            start = len(lines)
            for sums in (packed_sum, up_sum):
                units = sums.shape[1] // 256
                for i in range(units):
                    lanes = slice((half * units + i) * 128, (half * units + i + 1) * 128)
                    parts[own + half, start + i : start + i + 1] = sums[:, lanes]
                start += units
        small.step(0)

    def end_rows():
        rows.add_hi()
        rows_store.start()

    def end_small():
        small_out[...] = small.total()

    def load_weights():
        rows.add_c(1)
        for copy in rows.by_c[1]:
            copy.wait_send()
        for copy in loads:
            copy.start()

    def late_rows():
        rows.add_c(0)
        for copy in rows.by_c[0]:
            copy.wait_send()

    events[ROWS, ADD, 1], events[ROWS, ADD, 0], events[ROWS, ALONG_Y, 0] = load_weights, late_rows, end_rows
    events[SMALL, STEP, 0], events[SMALL, END, 0] = start_small, end_small
    for i in range(1, 5):
        events[SMALL, STEP, i] = functools.partial(small.step, i)

    def tell(sem):
        pl.semaphore_signal(sem, inc=1, device_id={"c": 1 - c}, device_id_type=pl.DeviceIdType.MESH)

    def before(spot):
        if spot == 0:
            greet(at, NAMES)
            load_g.start()
            for tile_loads in row_tiles[:3]:
                tile_loads[-1].start()
            scatter_y.prepare()
        if spot == FC1_AT + 1:
            pl.semaphore_wait(free_sem, 1)
        if spot == QKV_AT + 1:
            pl.semaphore_wait(free_again_sem, 1)
        for label in SCATTER_EVENTS[spot]:
            events[label]()
        if spot == 0:
            for copy in early_loads:
                copy.start()
            packed_sum[...] = jnp.zeros_like(packed_sum)
            up_sum[...] = jnp.zeros_like(up_sum)
            load_g.wait()
            column_total[...] = jnp.sum(g_all[0].astype(F32), axis=0, keepdims=True)
        if spot == UP_AT:
            for copy in early_loads:
                copy.wait()
            for copy in a2_loads[:2] + [row_tiles[3][-1], row_tiles[4][-1]]:
                copy.start()
        if FC1_AT <= spot < LATE_ROWS_AT:
            i = spot - FC1_AT
            if i == 0:
                tell(free_sem)
                for copy in loads:
                    copy.wait()
            if 0 < i < COLUMN_TILES - 1:
                a2_loads[i + 1].start()
            a2_loads[i].wait()
            if i >= 4:
                fc1_out.by_c[i - 4].wait_send()
        if spot == LATE_ROWS_AT:
            for copy in fc1_out.by_c[4:]:
                copy.wait_send()
        if spot == DX_AT:
            a1_loads[0].start()
            a1_loads[1].start()
        if spot == QKV_AT:
            tell(free_again_sem)
        if spot >= QKV_AT:
            i = spot - QKV_AT
            if 0 < i < COLUMN_TILES - 1:
                a1_loads[i + 1].start()
            a1_loads[i].wait()

    for spot in range(STEPS):
        pl.when(step == spot)(functools.partial(before, spot))

    for spot, i, ref, slot, copy in row_tiles:

        @pl.when(step == spot)
        def _(i=i, ref=ref, slot=slot, copy=copy):
            copy.wait()
            rows.store_tile(i, dot(ref[slot], g_all[...].reshape(tokens, -1), TN))

    @pl.when((step >= UP_AT) & (step < FC1_AT))
    def _():
        j = step - UP_AT
        here = pl.ds(pl.multiple_of(j * length, 16), length)
        grad_up = (dot(g_all[j], part[:n_fc1], NT) * slope_ref[0]).astype(BF16)
        grads[here, n_qkv:] = grad_up
        up_sum[...] += jnp.sum(grad_up.astype(F32), axis=0, keepdims=True)

    @pl.when((step >= DX_AT) & (step < QKV_AT))
    def _():
        j = sequence_at(step)
        here = pl.ds(pl.multiple_of(j * length, 16), length)
        grad_mixed = dot(g_all[j], part[n_fc1:], NT).astype(BF16)
        queries = heads_ref[0, :, :HEAD_DIM]
        keys_all = heads_ref[0, :, HEAD_DIM : 2 * HEAD_DIM]
        values_all = heads_ref[0, :, 2 * HEAD_DIM :]
        probs = softmax(causal_scores(queries, keys_all))
        grad_probs = dot(grad_mixed, values_all, NT)
        grad_values = dot(probs.astype(BF16), grad_mixed, TN)
        inner = jnp.sum(grad_probs * probs, axis=-1, keepdims=True)
        grad_scores = (probs * (grad_probs - inner)).astype(BF16)
        grad_queries = turn(dot(grad_scores, keys_all) * SCALE, tables_ref, -1.0)
        grad_keys = turn(dot(grad_scores, queries, TN) * SCALE, tables_ref, -1.0)
        grads[here, :HEAD_DIM] = grad_queries.astype(BF16)
        grads[here, HEAD_DIM : 2 * HEAD_DIM] = grad_keys.astype(BF16)
        grads[here, 2 * HEAD_DIM : n_qkv] = grad_values.astype(BF16)
        packed_sum[...] += jnp.sum(grads[here, :n_qkv].astype(F32), axis=0, keepdims=True)

        g_all[j] = (
            dot(grads[here, :n_qkv], qkv[...], NT) * norm_ref[0:1]
            + dot(grads[here, n_qkv:], fc1[...], NT) * norm_ref[2:3]
        ).astype(BF16)

    def column_tile(first, values, ref, lanes, sums, line, store):
        i = step - first
        start = starts[0]
        for spot in range(1, COLUMN_TILES):
            start = jnp.where(i == spot, starts[spot], start)
        here = pl.ds(pl.multiple_of(start, 128), tile)
        value = dot(values[lax.rem(i, 2)], grads[:, lanes], TN)
        weight = ref[here].astype(F32)
        store(i, here, value.astype(BF16))
        lane = lax.broadcasted_iota(jnp.int32, (tile, 128), 1)
        sides = jnp.where(
            lane == 0, jnp.sum(weight * value, axis=1, keepdims=True), jnp.sum(weight * sums[...], axis=1, keepdims=True)
        )
        vectors[line : line + 2, here] = jnp.transpose(sides)[:2]

    @pl.when((step >= FC1_AT) & (step < LATE_ROWS_AT))
    def _():
        def store(i, here, value):
            start = pl.multiple_of(4 * core + lax.rem(i, 4) // 2 * tile, 16)
            for side in range(2):

                @pl.when(lax.rem(i, 2) == side)
                def _():
                    part[pl.ds(start, tile), side * n_fc1 : (side + 1) * n_fc1] = value

        column_tile(FC1_AT, a2, fc1, slice(n_qkv, n_qkv + n_fc1), up_sum, 2, store)

    @pl.when(step >= QKV_AT)
    def _():
        def store(i, here, value):
            qkv[here] = value

        column_tile(QKV_AT, a1, qkv, slice(0, n_qkv), packed_sum, 0, store)

    @pl.when(step == STEPS - 1)
    def _():
        for label in SCATTER_EVENTS[STEPS]:
            events[label]()
        rows_store.wait()
        done = rows.by_c[0] + rows.by_c[1] + fc1_out.by_c
        for copy in copies.remote:
            if not any(copy is other for other in done):
                copy.wait_send()


def backward(y_part, g_all, hidden, mixed, heads, slope, norm, qkv, fc1, fc2, out, tables, a1, a2):
    far = pl.BlockSpec(memory_space=pl.ANY)
    count, length, width = g_all.shape
    n_qkv, n_fc1, n_mix = qkv.shape[1], fc1.shape[1], out.shape[0]
    wide = n_qkv + n_fc1
    tokens = count * length
    a1, a2 = a1.reshape(tokens, width), a2.reshape(tokens, width)
    hidden, mixed = hidden.reshape(tokens, n_fc1), mixed.reshape(tokens, n_mix)
    own = (n_fc1 + n_mix) // 2
    size = width // 8
    chunks = chunks_of(length, SCATTER_CHUNKS)
    longest = max(rows for _, rows, _ in chunks)

    outputs = [
        ((length, width), F32, far),
        ((length, width), F32, far),
        ((own // 2, width), BF16, far),
        ((own // 2, width), BF16, far),
        ((8, size // 2, n_qkv), BF16, far),
        ((8, size // 2, n_fc1), BF16, far),
        ((7, length, width), BF16, far),
        ((16, 128), F32, None),
    ]
    shapes = [jax.ShapeDtypeStruct(shape, kind) for shape, kind, _ in outputs]
    copies = 2 * 7 * len(chunks) + 15 + 40 + 5
    flops = 2 * tokens * width * (2 * n_qkv + 3 * n_fc1 + 2 * n_mix)
    return pl.pallas_call(
        backward_kernel,
        grid=(STEPS,),
        in_specs=[far] * 4
        + [
            pl.BlockSpec((1, length, n_qkv), lambda i: (sequence_at(i), 0, 0)),
            pl.BlockSpec((1, length, n_fc1), lambda i: (jnp.clip(i - UP_AT, 0, SEQUENCES - 1), 0, 0)),
            whole(norm),
        ]
        + [far] * 4
        + [whole(tables), far, far],
        out_specs=[whole(s) if spec is None else spec for s, (_, _, spec) in zip(shapes, outputs)],
        out_shape=shapes,
        scratch_shapes=[
            pltpu.VMEM(g_all.shape, BF16),
            pltpu.VMEM((tokens, wide), BF16),
            pltpu.VMEM(qkv.shape, BF16),
            pltpu.VMEM(fc1.shape, BF16),
            pltpu.VMEM((n_fc1 + n_mix, width), BF16),
            pltpu.VMEM((7, length, width), BF16),
            pltpu.VMEM((length, width), BF16),
            pltpu.VMEM((3, longest, width), BF16),
            pltpu.VMEM((longest, width), F32),
            pltpu.VMEM((own + own // 2, width), BF16),
            pltpu.VMEM((own // 2, width), BF16),
            pltpu.VMEM((2, tokens, size), BF16),
            pltpu.VMEM((2, tokens, size), BF16),
            pltpu.VMEM((4, size // 2, n_qkv), BF16),
            pltpu.VMEM((4, size // 2, n_fc1), BF16),
            pltpu.VMEM((size // 2, n_qkv), BF16),
            pltpu.VMEM((size // 2, n_fc1), BF16),
            pltpu.VMEM((1, n_qkv), F32),
            pltpu.VMEM((1, n_fc1), F32),
            pltpu.VMEM((1, width), F32),
            pltpu.VMEM((8, width), F32),
            pltpu.VMEM((16, 16, 128), F32),
            pltpu.VMEM((16, 16, 128), F32),
            pltpu.SemaphoreType.DMA((copies,)),
            pltpu.SemaphoreType.DMA((copies,)),
            pltpu.SemaphoreType.DMA((4 * max(3, len(chunks)) + 20,)),
            pltpu.SemaphoreType.REGULAR,
            pltpu.SemaphoreType.REGULAR,
        ],
        compiler_params=pltpu.CompilerParams(
            collective_id=2, has_side_effects=True, vmem_limit_bytes=63 * 2**20
        ),
        cost_estimate=pl.CostEstimate(flops=flops, bytes_accessed=10**8, transcendentals=0),
        name="backward",
    )(y_part, g_all, hidden, mixed, heads, slope, norm, qkv, fc1, fc2, out, tables, a1, a2)


def whole(array):
    return pl.BlockSpec(array.shape, lambda i: (0,) * array.ndim, pipeline_mode=pl.Buffered(1))


def finish_kernel(
    x_ref, g_ref, y_ref, dx_ref, shift_ref, small_ref, qkv_ref, fc1_ref, fc2_mine, fc2_other, out_mine, out_other,
    output_ref, input_grad_ref, qkv_out, fc1_out, fc2_out, out_out, *small_outs,
):
    @pl.when(pl.program_id(0) == 0)
    def _():
        row = 0
        for ref in small_outs:
            for start in range(0, ref.shape[0], 128):
                ref[start : start + 128] = small_ref[row]
                row += 1

    x = x_ref[...].astype(F32)
    output_ref[...] = (x + shift_ref[4:5] + shift_ref[5:6] + y_ref[...]).astype(BF16)
    centred = x - jnp.mean(x, axis=-1, keepdims=True)
    scale = lax.rsqrt(jnp.mean(centred * centred, axis=-1, keepdims=True) + EPS)
    normed = centred * scale
    dx = dx_ref[...]
    inner = jnp.mean(dx * normed, axis=-1, keepdims=True)
    dx = scale * (dx - jnp.mean(dx, axis=-1, keepdims=True) - normed * inner)
    input_grad_ref[...] = (g_ref[...].astype(F32) + dx).astype(BF16)

    qkv_out[...] = qkv_ref[0].astype(F32)
    fc1_out[...] = fc1_ref[0].astype(F32)
    holds = 1 - (lax.axis_index("hi") + lax.axis_index("y")) % 2
    mine = holds == (jnp.minimum(pl.program_id(0), 7) < 4).astype(jnp.int32)
    for ref, here, there in ((fc2_out, fc2_mine, fc2_other), (out_out, out_mine, out_other)):
        ref[...] = jnp.where(mine, here[...].astype(F32), there[...].astype(F32))


def finish(tokens, cotangent, y_sum, dx, norm, small, sizes, qkv_grad, fc1_grad, rows_mine, rows_other):
    length, width = tokens.shape
    rows = length // 9
    n_qkv, n_fc1, size = qkv_grad.shape[2], fc1_grad.shape[2], qkv_grad.shape[1]
    n_fc2, n_out = rows_mine.shape[0] // 5 // 4 * 4, rows_mine.shape[0] // 5 // 4

    def some(i):
        return jnp.minimum(i, 7)

    token = pl.BlockSpec((rows, width), lambda i: (i, 0))
    fc2 = pl.BlockSpec((n_fc2, width), lambda i: (some(i) % 4, 0))
    out = pl.BlockSpec((n_out, width), lambda i: (16 + some(i) % 4, 0))
    return pl.pallas_call(
        finish_kernel,
        grid=(9,),
        in_specs=[token] * 4
        + [
            whole(norm),
            whole(small),
            pl.BlockSpec((1, size, n_qkv), lambda i: (some(i), 0, 0)),
            pl.BlockSpec((1, size, n_fc1), lambda i: (some(i), 0, 0)),
            fc2,
            fc2,
            out,
            out,
        ],
        out_specs=[
            token,
            token,
            pl.BlockSpec((size, n_qkv), lambda i: (0, some(i))),
            pl.BlockSpec((size, n_fc1), lambda i: (0, some(i))),
            pl.BlockSpec((n_fc2, width), lambda i: (some(i), 0)),
            pl.BlockSpec((n_out, width), lambda i: (some(i), 0)),
        ]
        + [pl.BlockSpec((n,), lambda i: (0,)) for n in sizes],
        out_shape=[
            jax.ShapeDtypeStruct((length, width), BF16),
            jax.ShapeDtypeStruct((length, width), BF16),
            jax.ShapeDtypeStruct((size, 8 * n_qkv), F32),
            jax.ShapeDtypeStruct((size, 8 * n_fc1), F32),
            jax.ShapeDtypeStruct((8 * n_fc2, width), F32),
            jax.ShapeDtypeStruct((8 * n_out, width), F32),
        ]
        + [jax.ShapeDtypeStruct((n,), F32) for n in sizes],
        compiler_params=pltpu.CompilerParams(vmem_limit_bytes=60 * 2**20),
        cost_estimate=pl.CostEstimate(flops=10**7, bytes_accessed=3 * 10**7, transcendentals=0),
        name="finish",
    )(tokens, cotangent, y_sum, dx, norm, small, qkv_grad, fc1_grad, rows_mine, rows_other, rows_mine, rows_other)


def body(
    tokens, ln1_gain, ln1_bias, ln2_gain, ln2_bias, qkv_weight, qkv_bias, out_weight, out_bias,
    fc1_weight, fc1_bias, fc2_weight, fc2_bias, cotangent, extra,
):
    vectors = [ln1_gain, ln1_bias, ln2_gain, ln2_bias, out_bias, fc2_bias, qkv_bias, fc1_bias]
    if extra > 1:
        join = functools.partial(lax.all_gather, axis_name="e", axis=0, tiled=True)
        vectors = [join(v) for v in vectors]
        qkv_weight, out_weight, fc1_weight, fc2_weight = [
            join(w) for w in (qkv_weight, out_weight, fc1_weight, fc2_weight)
        ]
    length, width = tokens.shape[1:]
    tables = jnp.asarray(rotary_tables(length))

    small = jnp.concatenate([v.reshape(-1, 128) for v in vectors], axis=0)
    small = jnp.pad(small, ((0, -small.shape[0] % 16), (0, 0)))
    g_all, norm, qkv_cols, fc1_cols, fc2_rows, out_rows, a1, a2, heads, mixed, hidden, slope, y_part = forward(
        tokens[0], cotangent[0], small, qkv_weight, fc1_weight, fc2_weight, out_weight, tables
    )
    y_sum, dx, rows_total, rows_other, qkv_grad, fc1_grad, _, small_grads = backward(
        y_part, g_all, hidden, mixed, heads, slope, norm, qkv_cols, fc1_cols, fc2_rows, out_rows, tables, a1, a2
    )
    sizes = [ln1_gain.shape[0] * extra] * 5 + [qkv_bias.shape[0] * extra, fc1_bias.shape[0] * extra]
    output, input_grad, qkv_grad, fc1_grad, fc2_grad, out_grad, *small_grads = finish(
        tokens[0], cotangent[0], y_sum, dx, norm, small_grads, sizes, qkv_grad, fc1_grad, rows_total, rows_other
    )

    weight_grads = [qkv_grad, out_grad, fc1_grad, fc2_grad]
    if extra > 1:
        scatter = functools.partial(lax.psum_scatter, axis_name="e", scatter_dimension=0, tiled=True)
        weight_grads = [scatter(v) for v in weight_grads]
        small_grads = [scatter(v) for v in small_grads]
    qkv_grad, out_grad, fc1_grad, fc2_grad = weight_grads
    gain1, bias1, gain2, bias2, total, packed_bias, up_bias = small_grads
    return (
        output[None],
        input_grad[None],
        gain1,
        bias1,
        gain2,
        bias2,
        qkv_grad,
        packed_bias,
        out_grad,
        total,
        fc1_grad,
        up_bias,
        fc2_grad,
        total,
    )


def solution(mesh):
    extra = mesh.shape["shard"] // 16
    axes = ("y", "hi", "lo", "x", "c", "e")
    fine = Mesh(mesh.devices.reshape(2, 2, 2, 2, 2, extra), axes)
    split = P(axes, None, None)
    row, flat = P(axes[1:], None), P(axes[1:])
    in_specs = (split, flat, flat, flat, flat, row, flat, row, flat, row, flat, row, flat, split)
    out_specs = (split, split, flat, flat, flat, flat, row, flat, row, flat, row, flat, row, flat)
    return jax.shard_map(
        functools.partial(body, extra=extra), mesh=fine, in_specs=in_specs, out_specs=out_specs, check_vma=False
    )
```

```python
import functools

import jax
import jax.numpy as jnp
import numpy as np
from jax import lax
from jax.experimental import pallas as pl
from jax.experimental.pallas import tpu as pltpu
from jax.sharding import Mesh
from jax.sharding import PartitionSpec as P

HEADS = 8
HEAD_DIM = 256
ROTARY = 64
EPS = 1e-05
NEG_FILL = -1e30
SCALE = HEAD_DIM ** (-0.5)
BF16 = jnp.bfloat16
F32 = jnp.float32
NT = (((1,), (1,)), ((), ()))
TN = (((0,), (0,)), ((), ()))
NN = (((1,), (0,)), ((), ()))


def dot(a, b, dims=NN):
    return lax.dot_general(a, b, dims, preferred_element_type=F32)


NAMES = ("y", "hi", "lo", "x", "c")

X, G, QKV, FC1, FC2, OUT, Y, DX, ROWS, SMALL = range(10)
OWN, NEXT, ONWARD, BY_X, BY_LO, HI, CORE, ALONG_Y, FIRST, SECOND, THIRD, LAST, ADD, PASS, FAR, RELAY, STEP, END = range(18)
PLACE = {"lo": 1, "x": 2, "y": 4}


def chunks_of(length, plan):
    chunks, start, share = [], 0, 0
    for part, order in plan:
        share += part
        end = length * share // 288 * 16 if share < 18 else length
        chunks.append((start, end - start, order))
        start = end
    return chunks


SCATTER_CHUNKS = ((9, ("lo", "y", "x")), (4, ("x", "lo", "y")), (5, ("y", "lo", "x")))
SCATTER_EVENTS = (
    (
        (Y, FIRST, 1, 0), (Y, FIRST, 1, 3), (Y, FIRST, 0, 3), (Y, FIRST, 2, 3), (Y, FIRST, 0, 2), (Y, FIRST, 1, 2),
    ),
    (),
    (),
    (
        (ROWS, CORE, 1),
    ),
    (
        (Y, FIRST, 1, 1),
    ),
    (
        (Y, SECOND, 1, 3), (Y, SECOND, 1, 2), (ROWS, ADD, 1), (Y, FIRST, 2, 2),
    ),
    (
        (Y, SECOND, 2, 3),
    ),
    (),
    (),
    (),
    (),
    (
        (Y, THIRD, 1),
    ),
    (
        (Y, SECOND, 0, 3), (Y, SECOND, 0, 2), (Y, FIRST, 0, 1), (FC1, CORE, 0),
    ),
    (
        (FC1, CORE, 1), (Y, SECOND, 2, 2), (Y, FIRST, 2, 1), (FC1, ADD, 0), (FC1, HI, 0),
    ),
    (
        (FC1, CORE, 2), (FC1, ADD, 1),
    ),
    (
        (FC1, CORE, 3), (FC1, ADD, 2),
    ),
    (
        (Y, FIRST, 0, 0), (FC1, CORE, 4), (FC1, ADD, 3),
    ),
    (
        (Y, LAST, 1), (FC1, ADD, 4), (FC1, PASS, 0), (FC1, CORE, 5), (FC1, HI, 1),
    ),
    (
        (FC1, CORE, 6), (FC1, ADD, 5),
    ),
    (
        (FC1, CORE, 7), (FC1, ADD, 6), (Y, FIRST, 2, 0), (FC1, ADD, 7),
    ),
    (
        (Y, THIRD, 2),
    ),
    (
        (ROWS, CORE, 0), (FC1, HI, 2), (FC1, PASS, 1), (FC1, FAR, 0),
    ),
    (
        (ROWS, ADD, 0),
    ),
    (
        (Y, THIRD, 0), (ROWS, HI, 0), (DX, FIRST, 1, 3), (DX, FIRST, 1, 1),
    ),
    (
        (DX, FIRST, 0, 2), (FC1, RELAY, 1), (FC1, PASS, 2), (Y, LAST, 2),
    ),
    (
        (FC1, RELAY, 3), (DX, FIRST, 0, 3),
    ),
    (),
    (
        (DX, FIRST, 1, 0),
    ),
    (
        (FC1, RELAY, 2), (DX, FIRST, 2, 3),
    ),
    (
        (Y, LAST, 0), (DX, SECOND, 1, 3), (DX, FIRST, 1, 2),
    ),
    (
        (QKV, CORE, 0),
    ),
    (
        (QKV, CORE, 1), (QKV, ADD, 0),
    ),
    (
        (QKV, CORE, 2), (QKV, ADD, 1),
    ),
    (
        (QKV, CORE, 3), (QKV, ADD, 2), (DX, SECOND, 1, 2), (QKV, ADD, 3), (DX, FIRST, 2, 2),
    ),
    (
        (QKV, CORE, 4), (DX, THIRD, 1),
    ),
    (
        (QKV, CORE, 5), (DX, SECOND, 2, 3), (DX, SECOND, 0, 3), (DX, SECOND, 0, 2), (QKV, ADD, 5), (QKV, ADD, 4),
        (DX, FIRST, 0, 1),
    ),
    (
        (QKV, CORE, 6),
    ),
    (
        (SMALL, STEP, 0), (QKV, ADD, 6), (QKV, CORE, 7), (QKV, ADD, 7), (DX, FIRST, 2, 1), (DX, FIRST, 2, 0),
        (DX, LAST, 1), (QKV, HI, 0), (DX, SECOND, 2, 2), (ROWS, ALONG_Y, 0), (SMALL, STEP, 1), (SMALL, STEP, 2),
        (QKV, HI, 1), (SMALL, STEP, 3), (QKV, PASS, 0), (SMALL, STEP, 4), (SMALL, END, 0), (DX, FIRST, 0, 0),
        (DX, THIRD, 2), (QKV, HI, 2), (QKV, PASS, 1), (QKV, FAR, 0), (DX, THIRD, 0), (FC1, HI, 3), (QKV, PASS, 2),
        (QKV, RELAY, 1), (QKV, RELAY, 3), (DX, LAST, 2), (QKV, RELAY, 2), (QKV, HI, 3), (FC1, PASS, 3),
        (QKV, PASS, 3), (DX, LAST, 0), (FC1, END, 0), (QKV, END, 0), (ROWS, END, 0),
    ),
)


GATHER_CHUNKS = ((9, ("y", "lo", "x")), (9, ("lo", "x", "y")))
GATHER_EVENTS = (
    (
        (FC2, HI, 0), (OUT, HI, 0), (SMALL, STEP, 0), (X, OWN, 1, 0), (QKV, CORE, 0), (X, OWN, 0, 1), (X, OWN, 1, 1),
        (QKV, BY_X, 0), (X, OWN, 0, 2), (QKV, BY_LO, 0), (X, OWN, 1, 2), (QKV, HI, 0), (X, OWN, 0, 0), (FC1, CORE, 0),
        (SMALL, STEP, 1), (SMALL, STEP, 2), (SMALL, STEP, 3), (QKV, BY_X, 1), (SMALL, STEP, 4), (FC1, BY_X, 0),
        (G, OWN, 0, 0), (QKV, BY_LO, 1), (QKV, CORE, 1), (X, NEXT, 0, 1), (X, NEXT, 0, 2), (QKV, CORE, 2),
        (QKV, HI, 2), (QKV, CORE, 4), (QKV, HI, 1), (OUT, CORE, 0), (OUT, ALONG_Y, 0), (FC1, BY_X, 1),
        (X, ONWARD, 1, 0), (OUT, CORE, 1), (FC1, CORE, 1), (QKV, CORE, 3), (G, OWN, 1, 2), (QKV, HI, 3),
        (G, OWN, 1, 1), (QKV, CORE, 6), (FC1, HI, 1), (QKV, CORE, 5), (G, NEXT, 0, 2), (G, ONWARD, 1, 0),
        (FC1, BY_LO, 1), (FC1, BY_LO, 0), (X, NEXT, 1, 1), (X, NEXT, 1, 2), (X, ONWARD, 0, 0), (FC1, HI, 0),
        (QKV, CORE, 7),
    ),
    (),
    (),
    (
        (FC1, CORE, 5), (X, ONWARD, 0, 1), (G, OWN, 1, 0), (X, ONWARD, 1, 1), (FC1, HI, 3), (FC1, CORE, 3),
        (FC1, CORE, 2),
    ),
    (
        (FC1, HI, 2), (FC1, CORE, 4),
    ),
    (),
    (
        (G, OWN, 0, 2),
    ),
    (),
    (
        (G, NEXT, 0, 1), (FC2, CORE, 0), (FC2, ALONG_Y, 0), (G, NEXT, 1, 1), (FC1, CORE, 7), (FC1, CORE, 6),
    ),
    (),
    (
        (G, OWN, 0, 1), (G, ONWARD, 0, 1),
    ),
    (),
    (
        (FC2, CORE, 1), (G, ONWARD, 1, 1),
    ),
    (),
    (
        (G, ONWARD, 0, 0),
    ),
    (),
    (
        (G, NEXT, 1, 2),
    ),
    (),
    (),
    (),
    (),
    (),
    (),
    (),
    (),
)


class Copies:
    def __init__(self, at, send_sem, recv_sem, local_sem):
        self.at, self.send_sem, self.recv_sem, self.local_sem = at, send_sem, recv_sem, local_sem
        self.remote, self.planned, self.local, self.seen = [], 0, 0, set()

    def plan(self, src, dst, axis, everywhere=True):
        spot = self.planned
        self.planned += 1
        copy = pltpu.make_async_remote_copy(
            src_ref=src,
            dst_ref=dst,
            send_sem=self.send_sem.at[spot],
            recv_sem=self.recv_sem.at[spot],
            device_id={axis: 1 - self.at[axis]},
            device_id_type=pl.DeviceIdType.MESH,
        )
        if everywhere:
            self.remote.append(copy)
        return copy

    def arrive(self, *copies):
        for copy in copies:
            if id(copy) not in self.seen:
                self.seen.add(id(copy))
                copy.wait_recv()

    def move(self, src, dst):
        copy = pltpu.make_async_copy(src, dst, self.local_sem.at[self.local])
        self.local += 1
        return copy


def greet(at, names):
    barrier = pltpu.get_barrier_semaphore()
    for name in names:
        pl.semaphore_signal(
            barrier, inc=1, device_id={name: 1 - at[name]}, device_id_type=pl.DeviceIdType.MESH
        )
    pl.semaphore_wait(barrier, len(names))


class TokenGather:
    def __init__(self, copies, own, full, name, events):
        self.copies, self.plans = copies, {}
        self.kept = copies.move(own, full.at[0])
        self.chunks = chunks_of(own.shape[0], GATHER_CHUNKS)
        for chunk, (start, rows, order) in enumerate(self.chunks):
            part = pl.ds(start, rows)
            one, two, _ = (PLACE[axis] for axis in order)
            hops = [((OWN, chunk, i), 0, axis) for i, axis in enumerate(order)]
            hops += [((NEXT, chunk, 1), one, order[1]), ((NEXT, chunk, 2), one, order[2])]
            hops += [((ONWARD, chunk, 0), two, order[2]), ((ONWARD, chunk, 1), one + two, order[2])]
            for label, block, axis in hops:
                src = own.at[part] if block == 0 else full.at[block, part]
                there = block + PLACE[axis]
                self.plans[chunk, there] = copies.plan(src, full.at[there, part], axis)
                events[(name,) + label] = functools.partial(self.send, chunk, block, there)

    def send(self, chunk, block, there):
        if block:
            self.copies.arrive(self.plans[chunk, block])
        self.plans[chunk, there].start()

    def take(self, block):
        for chunk in range(len(self.chunks)):
            self.copies.arrive(self.plans[chunk, block])

    def finish(self):
        for block in range(1, 8):
            self.take(block)
        self.kept.wait()


class TokenScatter:
    def __init__(self, copies, parts, came, far_parts, stage, room, total, name, events):
        self.copies, self.parts, self.came, self.far_parts = copies, parts, came, far_parts
        self.stage, self.room = stage, room
        self.chunks = chunks_of(parts.shape[1], SCATTER_CHUNKS)
        self.first, self.second, self.third, self.stores, self.loads, self.near = {}, {}, [], [], {}, {}
        base = copies.local
        for chunk, (start, rows, order) in enumerate(self.chunks):
            third, second, first = order
            part = pl.ds(start, rows)
            for slot in (3, 2, 1, 0):
                block = self.block(chunk, slot)
                src = parts.at[block + PLACE[first], part]
                self.first[chunk, slot] = copies.plan(src, came.at[slot, part], first)
                near = came.at[slot, part] if far_parts else parts.at[block, part]
                if slot > 1:
                    self.second[chunk, slot] = copies.plan(near, came.at[2 + slot, part], second)
                if slot == 1:
                    self.third.append(copies.plan(near, came.at[6, part], third))
                self.near[chunk, slot] = near
                if far_parts:
                    copies.local = base + chunk
                    self.loads[chunk, slot] = [copies.move(parts.at[block, part], stage.at[part])]
                else:
                    copies.local = base
                    self.loads[chunk, slot] = [
                        copies.move(came.at[i, part], stage.at[spot, pl.ds(0, rows)])
                        for spot, i in enumerate(self.terms(slot))
                    ]
                events[name, FIRST, chunk, slot] = self.first[chunk, slot].start
            events[name, SECOND, chunk, 3] = functools.partial(self.pass_second, chunk, 3)
            events[name, SECOND, chunk, 2] = functools.partial(self.pass_second, chunk, 2)
            events[name, THIRD, chunk] = functools.partial(self.pass_third, chunk)
            events[name, LAST, chunk] = functools.partial(self.last, chunk)
        copies.local = base + max(3, len(self.chunks))
        for start, rows, _ in self.chunks:
            self.stores.append(copies.move(room.at[pl.ds(0, rows)], total.at[pl.ds(start, rows)]))

    def block(self, chunk, slot):
        third, second, _ = self.chunks[chunk][2]
        return PLACE[second] * (slot // 2) + PLACE[third] * (slot % 2)

    def terms(self, slot):
        return {0: (0, 4, 6), 1: (1, 5)}.get(slot, (slot,))

    def prepare(self):
        if self.far_parts:
            for chunk in range(len(self.chunks)):
                self.loads[chunk, 3][0].start()

    def add(self, chunk, slot):
        start, rows, _ = self.chunks[chunk]
        part = pl.ds(start, rows)
        self.copies.arrive(self.first[chunk, slot])
        loads = self.loads[chunk, slot]
        if self.far_parts:
            loads[0].wait()
            value = self.stage[part].astype(F32)
            for i in self.terms(slot):
                value = value + self.came[i, part].astype(F32)
            if slot > 0:
                self.loads[chunk, slot - 1][0].start()
            return value
        for copy in loads:
            copy.start()
        value = self.parts[self.block(chunk, slot), part].astype(F32)
        for spot, copy in enumerate(loads):
            copy.wait()
            value = value + self.stage[spot, :rows].astype(F32)
        return value

    def pass_second(self, chunk, slot):
        self.near[chunk, slot][...] = self.add(chunk, slot).astype(BF16)
        self.second[chunk, slot].start()

    def pass_third(self, chunk):
        self.copies.arrive(self.second[chunk, 3])
        self.near[chunk, 1][...] = self.add(chunk, 1).astype(BF16)
        self.third[chunk].start()

    def last(self, chunk):
        self.copies.arrive(self.second[chunk, 2], self.third[chunk])
        self.room[: self.chunks[chunk][1]] = self.add(chunk, 0)
        self.stores[chunk].start()
        self.stores[chunk].wait()


class ColumnGather:
    def __init__(self, copies, weight, full, relay, name, events):
        at = copies.at
        hi, lo, x, c = (at[n] for n in ("hi", "lo", "x", "c"))
        rows, width = weight.shape[0], full.shape[1]

        def block(lo_at, x_at):
            spot = (at["y"] * 2 + lo_at) * 2 + x_at
            return weight.at[:, pl.ds(pl.multiple_of(spot * width, 128), width)]

        def place(hi_at, lo_at, x_at):
            spot = ((hi_at * 2 + lo_at) * 2 + x_at) * 2 + c
            return full.at[pl.ds(pl.multiple_of(spot * rows, 128), rows)]

        mine = place(hi, lo, x)
        self.by_x = [copies.plan(block(1 - lo, 1 - x), relay, "x"), copies.plan(block(lo, 1 - x), mine, "x")]
        self.by_lo = [
            copies.plan(block(1 - lo, x), mine, "lo"),
            copies.plan(relay, place(hi, lo, 1 - x), "lo"),
        ]
        near = [place(hi, lo, x), place(hi, lo, 1 - x), place(hi, 1 - lo, x), place(hi, 1 - lo, 1 - x)]
        far = [place(1 - hi, lo, x), place(1 - hi, lo, 1 - x), place(1 - hi, 1 - lo, x), place(1 - hi, 1 - lo, 1 - x)]
        source = [block(lo, x)] + near[1:]
        self.by_hi = [copies.plan(src, dst, "hi") for src, dst in zip(source, near)]
        self.by_c = [copies.plan(src, dst, "c") for src, dst in zip(source + far, near + far)]
        self.kept = copies.move(block(lo, x), mine)
        self.copies = copies
        by_hi, by_c = self.by_hi, self.by_c
        x_then, lo_then = self.by_x, self.by_lo
        hops = [((BY_X, i), None, x_then[i]) for i in range(2)]
        hops += [((BY_LO, 0), None, lo_then[0]), ((BY_LO, 1), x_then[0], lo_then[1])]
        came = [None, x_then[1], lo_then[0], lo_then[1]]
        hops += [((HI, i), came[i], by_hi[i]) for i in range(4)]
        hops += [((CORE, i), copy, by_c[i]) for i, copy in enumerate(came + by_hi)]
        for label, first, copy in hops:
            events[(name,) + label] = functools.partial(self.send, first, copy)

    def send(self, first, copy):
        if first is not None:
            self.copies.arrive(first)
        copy.start()

    def finish(self):
        self.copies.arrive(*self.by_c)
        self.kept.wait()


class RowGather:
    def __init__(self, copies, weight, full, name, events):
        at, rows = copies.at, weight.shape[0]
        half = rows // 2

        def spot(start, count):
            return full.at[pl.ds(pl.multiple_of(start, 16), count)]

        self.copies = copies
        self.holds = 1 - (at["hi"] + at["y"]) % 2
        first, second = spot(at["c"] * rows, half), spot(at["c"] * rows + half, half)
        there = spot(self.holds * (at["c"] * rows) + (1 - self.holds) * 2 * rows, half)
        source = weight.at[pl.ds(pl.multiple_of((1 - self.holds) * half, 16), half)]
        self.by_hi = copies.plan(source, there, "hi")
        self.by_y = copies.plan(spot(2 * rows, half), second, "y", everywhere=False)
        self.by_c = [copies.plan(first, first, "c"), copies.plan(second, second, "c")]
        self.kept = copies.move(weight, spot(at["c"] * rows, rows))
        events[name, HI, 0], events[name, ALONG_Y, 0] = self.start, self.relay
        events[name, CORE, 0], events[name, CORE, 1] = self.first_to_c, self.second_to_c

    def start(self):
        self.by_hi.start()
        pl.when(self.holds == 1)(self.kept.start)

    def ready(self):
        if id(self.by_hi) not in self.copies.seen:
            self.copies.arrive(self.by_hi)
            pl.when(self.holds == 1)(self.kept.wait)

    def relay(self):
        self.ready()
        pl.when(self.holds == 1)(self.by_y.start)

    def first_to_c(self):
        self.ready()
        self.by_c[0].start()

    def second_to_c(self):
        self.ready()
        pl.when(self.holds == 0)(self.by_y.wait_recv)
        self.by_c[1].start()

    def finish(self):
        for copy in self.by_c:
            copy.wait_recv()

    def sent(self):
        pl.when(self.holds == 1)(self.by_y.wait_send)


class SmallGather:
    def __init__(self, copies, full):
        at = copies.at
        base = ((at["hi"] * 2 + at["lo"]) * 2 + at["x"]) * 2 + at["c"]
        self.own = full.at[pl.ds(base, 1)]
        self.steps, count = [], 1
        for name in ("c", "x", "lo", "hi"):
            part = full.at[pl.ds(base, count)]
            self.steps.append(copies.plan(part, part, name))
            base = base - at[name] * count
            count *= 2

    def step(self, at):
        if at > 0:
            self.steps[at - 1].wait_recv()
        if at < 4:
            self.steps[at].start()


def rotary_tables(length):
    places = np.arange(length, dtype=np.float32)
    frequency = (10000.0 ** (-np.arange(0, ROTARY, 2, dtype=np.float32) / ROTARY)).astype(np.float32)
    angles = places[:, None] * frequency[None, :]
    cosine, sine = np.cos(angles), np.sin(angles)
    half = ROTARY // 2
    tables = np.zeros((3, length, 2 * ROTARY), np.float32)
    tables[0] = 1.0
    tables[0, :, :half] = cosine
    tables[0, :, half:ROTARY] = cosine
    tables[1, :, :half] = -sine
    tables[2, :, half:ROTARY] = sine
    return tables


def turn(rows, tables, sign):
    half, wide = ROTARY // 2, 2 * ROTARY
    near = rows[:, :wide]
    ahead = pltpu.roll(near, wide - half, 1)
    behind = pltpu.roll(near, half, 1)
    near = near * tables[0] + sign * (ahead * tables[1] + behind * tables[2])
    return jnp.concatenate([near, rows[:, wide:]], axis=1)


def causal_scores(queries, keys_all):
    length = queries.shape[0]
    scores = dot(queries, keys_all, NT) * SCALE
    row = lax.broadcasted_iota(jnp.int32, (length, length), 0)
    col = lax.broadcasted_iota(jnp.int32, (length, length), 1)
    return jnp.where(row >= col, scores, NEG_FILL)


def softmax(scores):
    raised = jnp.exp(scores - jnp.max(scores, axis=-1, keepdims=True))
    return raised / jnp.sum(raised, axis=-1, keepdims=True)


MLP_AT, OUTPUT_AT, FORWARD_STEPS = 8, 16, 24


def forward_kernel(
    x_ref, g_ref, small_ref, qkv_ref, fc1_ref, fc2_ref, out_ref, tables_ref,
    g_all, norm_out, qkv_out, fc1_out, fc2_out, out_out,
    a1_ref, a2_ref, heads_ref, mixed_ref, hidden_ref, slope_ref, y_ref,
    x_all, small_all, qkv_all, fc1_all, fc2_all, out_all, norm, qkv_bias, fc1_bias, mixed_all, hidden_all,
    relay_qkv, relay_fc1, send_sem, recv_sem, local_sem,
):
    step = pl.program_id(0)
    at = {name: lax.axis_index(name) for name in NAMES}
    copies = Copies(at, send_sem, recv_sem, local_sem)
    events = {}
    small = SmallGather(copies, small_all)
    qkv = ColumnGather(copies, qkv_ref, qkv_all, relay_qkv, QKV, events)
    fc1 = ColumnGather(copies, fc1_ref, fc1_all, relay_fc1, FC1, events)
    fc2 = RowGather(copies, fc2_ref, fc2_all, FC2, events)
    out = RowGather(copies, out_ref, out_all, OUT, events)
    x = TokenGather(copies, x_ref, x_all, X, events)
    g = TokenGather(copies, g_ref, g_all, G, events)
    kept = [
        copies.move(src.at[pl.ds(0, dst.shape[0])], dst)
        for src, dst in ((qkv_all, qkv_out), (fc1_all, fc1_out), (fc2_all, fc2_out), (out_all, out_out))
    ]

    def spread_small():
        small.step(4)
        for spot in range(16):
            norm[:, spot * 128 : (spot + 1) * 128] = small_all[spot, :8].astype(F32)
        first = (at["y"] * 4 + at["lo"] * 2 + at["x"]) * 2
        for half in range(2):
            own = small_all[first + half].astype(F32)
            for bias, start in ((qkv_bias, 6), (fc1_bias, 6 + qkv_bias.shape[1] // 256)):
                rows = bias.shape[1] // 256
                for i in range(rows):
                    bias[:, (half * rows + i) * 128 : (half * rows + i + 1) * 128] = own[start + i : start + i + 1]

    for i in range(4):
        events[SMALL, STEP, i] = functools.partial(small.step, i)
    events[SMALL, STEP, 4] = spread_small

    def before(spot):
        if spot == 0:
            greet(at, NAMES)
            small.own[...] = small_ref[...][None]
            for copy in (x.kept, g.kept, qkv.kept, fc1.kept):
                copy.start()
        for label in GATHER_EVENTS[spot]:
            events[label]()
        if spot == 0:
            x.kept.wait()
            qkv.finish()
            kept[0].start()
        elif spot < MLP_AT:
            x.take(spot)
        elif spot == MLP_AT:
            fc1.finish()
            kept[1].start()
        elif spot == OUTPUT_AT:
            fc2.finish()
            out.finish()
            kept[2].start()
            kept[3].start()

    for spot in range(FORWARD_STEPS):
        pl.when(step == spot)(functools.partial(before, spot))

    def normed(j, line):
        value = x_all[j].astype(F32)
        centred = value - jnp.mean(value, axis=-1, keepdims=True)
        var = jnp.mean(centred * centred, axis=-1, keepdims=True)
        return (centred * lax.rsqrt(var + EPS) * norm[line : line + 1] + norm[line + 1 : line + 2]).astype(BF16)

    @pl.when(step < MLP_AT)
    def _():
        a1_ref[0] = normed(step, 0)
        packed = dot(a1_ref[0], qkv_all[...]) + qkv_bias[...]
        queries = turn(packed[:, :HEAD_DIM], tables_ref, 1.0).astype(BF16)
        keys_all = turn(packed[:, HEAD_DIM : 2 * HEAD_DIM], tables_ref, 1.0).astype(BF16)
        values_all = packed[:, 2 * HEAD_DIM :].astype(BF16)
        heads_ref[0, :, :HEAD_DIM] = queries
        heads_ref[0, :, HEAD_DIM : 2 * HEAD_DIM] = keys_all
        heads_ref[0, :, 2 * HEAD_DIM :] = values_all
        probs = softmax(causal_scores(queries, keys_all)).astype(BF16)
        mixed_ref[0] = dot(probs, values_all).astype(BF16)
        mixed_all[step] = mixed_ref[0]

    @pl.when((step >= MLP_AT) & (step < OUTPUT_AT))
    def _():
        j = step - MLP_AT
        a2_ref[0] = normed(j, 2)
        upward = dot(a2_ref[0], fc1_all[...]) + fc1_bias[...]
        below = 0.5 * (1.0 + lax.erf(upward * np.float32(0.5**0.5)))
        hidden_ref[0] = (upward * below).astype(BF16)
        hidden_all[j] = hidden_ref[0]
        slope_ref[0] = below + upward * (jnp.exp(-0.5 * upward * upward) * np.float32((2 * np.pi) ** -0.5))

    @pl.when(step >= OUTPUT_AT)
    def _():
        j = step - OUTPUT_AT
        y = dot(hidden_all[j], fc2_all[: hidden_ref.shape[2]])
        y_ref[0] = (y + dot(mixed_all[j], out_all[: mixed_ref.shape[2]])).astype(BF16)

    @pl.when(step == FORWARD_STEPS - 1)
    def _():
        norm_out[...] = norm[...]
        for label in GATHER_EVENTS[FORWARD_STEPS]:
            events[label]()
        g.finish()
        for copy in kept:
            copy.wait()
        for copy in copies.remote:
            copy.wait_send()
        fc2.sent()
        out.sent()


def forward(tokens, cotangent, small, qkv_weight, fc1_weight, fc2_weight, out_weight, tables):
    far = pl.BlockSpec(memory_space=pl.ANY)
    length, width = tokens.shape
    rows = qkv_weight.shape[0]
    n_qkv, n_fc1, n_mix = qkv_weight.shape[1] // 8, fc1_weight.shape[1] // 8, out_weight.shape[0] * 2
    each = [(width, BF16), (width, BF16), (n_qkv, BF16), (n_mix, BF16), (n_fc1, BF16), (n_fc1, F32), (width, BF16)]
    count = 4 + 2 * 16 + 2 * 4 + 2 * 7 * len(GATHER_CHUNKS)
    weights = [(16 * rows, n_qkv), (16 * rows, n_fc1), (n_fc1, width), (n_mix, width)]
    flops = 2 * 8 * length * width * (n_qkv + n_fc1 + n_fc1 + n_mix)
    return pl.pallas_call(
        forward_kernel,
        grid=(FORWARD_STEPS,),
        in_specs=[far, far, whole(small), far, far, far, far, whole(tables)],
        out_specs=[far, whole(jax.ShapeDtypeStruct((8, width), F32)), far, far, far, far]
        + [
            pl.BlockSpec((1, length, n), lambda i, start=start: (jnp.clip(i - start, 0, 7), 0, 0))
            for (n, _), start in zip(each, (0, MLP_AT, 0, 0, MLP_AT, MLP_AT, OUTPUT_AT))
        ],
        out_shape=[
            jax.ShapeDtypeStruct((8, length, width), BF16),
            jax.ShapeDtypeStruct((8, width), F32),
        ]
        + [jax.ShapeDtypeStruct(shape, BF16) for shape in weights]
        + [jax.ShapeDtypeStruct((8, length, n), kind) for n, kind in each],
        scratch_shapes=[
            pltpu.VMEM((8, length, width), BF16),
            pltpu.VMEM((16,) + small.shape, BF16),
            pltpu.VMEM(weights[0], BF16),
            pltpu.VMEM(weights[1], BF16),
            pltpu.VMEM((n_fc1 * 5 // 4, width), BF16),
            pltpu.VMEM((n_mix * 5 // 4, width), BF16),
            pltpu.VMEM((8, width), F32),
            pltpu.VMEM((1, n_qkv), F32),
            pltpu.VMEM((1, n_fc1), F32),
            pltpu.VMEM((8, length, n_mix), BF16),
            pltpu.VMEM((8, length, n_fc1), BF16),
            pltpu.VMEM((rows, n_qkv), BF16),
            pltpu.VMEM((rows, n_fc1), BF16),
            pltpu.SemaphoreType.DMA((count,)),
            pltpu.SemaphoreType.DMA((count,)),
            pltpu.SemaphoreType.DMA((10,)),
        ],
        compiler_params=pltpu.CompilerParams(
            collective_id=1, has_side_effects=True, vmem_limit_bytes=60 * 2**20
        ),
        cost_estimate=pl.CostEstimate(flops=flops, bytes_accessed=10**8, transcendentals=0),
        name="forward",
    )(tokens, cotangent, small, qkv_weight, fc1_weight, fc2_weight, out_weight, tables)


def add_rows(dst, dst_row, src, src_row, count, lanes=None, src_lanes=None):
    lanes = lanes or slice(None)
    src_lanes = src_lanes or lanes
    for start in range(0, count, 64):
        here = pl.ds(pl.multiple_of(dst_row + start, 16), 64)
        there = pl.ds(pl.multiple_of(src_row + start, 16), 64)
        dst[here, lanes] = (dst[here, lanes].astype(F32) + src[there, src_lanes].astype(F32)).astype(BF16)


class RowScatter:
    def __init__(self, copies, wide, slim, late, kept, came, n_fc2, n_out, other, events):
        at = copies.at
        c = at["c"]
        self.copies, self.kept, self.came, self.late = copies, kept, came, late
        self.holds = 1 - (at["hi"] + at["y"]) % 2
        own, half = n_fc2 + n_out, (n_fc2 // 2, n_out // 2)
        width, tile = kept.shape[1], 2 * n_out
        self.cuts = [(wide, i, i * 2 * n_fc2, wide.shape[1]) for i in range(width // wide.shape[1])]
        self.slim_cuts = [
            (slim, i, i * tile, min(slim.shape[1], width - i * slim.shape[1]))
            for i in range(-(-width // slim.shape[1]))
        ]

        def rows(ref, start, count):
            return ref.at[pl.ds(pl.multiple_of(start, 16), count)]

        self.pieces = [[(late, 0, half[0], half[0], 0, slice(0, width), width)], []]
        for ref, i, first, lanes in self.cuts:
            there = slice(i * lanes, (i + 1) * lanes)
            self.pieces[1].append((ref, first + half[0], n_fc2, half[0], half[0], there, lanes))
        for ref, i, first, lanes in self.slim_cuts:
            there = slice(i * ref.shape[1], i * ref.shape[1] + lanes)
            self.pieces[1].append((ref, first, n_out, n_out, n_fc2, there, lanes))
        self.c = c
        self.by_c = []
        for pieces in self.pieces:
            made = []
            for ref, first, size, n, to, there, lanes in pieces:
                src = ref.at[pl.ds(pl.multiple_of(first + (1 - c) * size, 16), n), pl.ds(0, lanes)]
                dst = kept.at[pl.ds(to, n), pl.ds(there.start, lanes)]
                made.append(copies.plan(src, dst, "c"))
            self.by_c.append(made)
        self.by_y = [
            copies.plan(rows(kept, half[0], half[0]), rows(kept, own, half[0]), "y"),
            copies.plan(rows(kept, n_fc2 + half[1], half[1]), rows(kept, own + half[0], half[1]), "y"),
        ]
        holds = self.holds
        sent = [holds * own, holds * (own + half[0]) + (1 - holds) * n_fc2]
        self.keeps = [(1 - holds) * own, (1 - holds) * (own + half[0]) + holds * n_fc2]
        self.by_hi = [
            copies.plan(rows(kept, sent[0], half[0]), rows(came, 0, half[0]), "hi"),
            copies.plan(rows(kept, sent[1], half[1]), rows(came, half[0], half[1]), "hi"),
        ]
        self.half = half
        self.on_y = copies.plan(came, other, "y")
        events[ROWS, CORE, 1] = functools.partial(self.send, self.by_c[1])
        events[ROWS, CORE, 0] = functools.partial(self.send, self.by_c[0])
        events[ROWS, HI, 0] = self.send_hi
        events[ROWS, END, 0] = functools.partial(copies.arrive, self.on_y)

    def store_tile(self, i, value):
        size = value.shape[0]
        if i in (0, 2):
            self.late[i // 2 * size : (i // 2 + 1) * size] = value.astype(BF16)
            return
        cuts = self.slim_cuts if i is None else self.cuts
        for ref, cut, first, lanes in cuts:
            start = first if i is None else first + i * size
            ref[start : start + size, :lanes] = value[:, cut * ref.shape[1] : cut * ref.shape[1] + lanes].astype(BF16)

    def send(self, made):
        for copy in made:
            copy.start()

    def add_c(self, side):
        for copy, (ref, first, size, n, to, there, lanes) in zip(self.by_c[side], self.pieces[side]):
            self.copies.arrive(copy)
            add_rows(self.kept, to, ref, first + self.c * size, n, there, slice(0, lanes))
        if side == 1:
            self.send(self.by_y)

    def send_hi(self):
        self.copies.arrive(*self.by_y)
        self.send(self.by_hi)

    def add_hi(self):
        self.copies.arrive(*self.by_hi)
        add_rows(self.came, 0, self.kept, self.keeps[0], self.half[0])
        add_rows(self.came, self.half[0], self.kept, self.keeps[1], self.half[1])
        self.on_y.start()


class ColumnScatter:
    def __init__(self, copies, starts, tile, room, by_hi, relay, full, name, events):
        at = copies.at
        self.copies, self.tile, self.room, self.came_hi = copies, tile, room, by_hi
        y, lo, x, c = (at[n] for n in ("y", "lo", "x", "c"))
        self.c = c
        self.by_c = [copies.plan(tile(i, 1 - c), room(i), "c") for i in range(8)]
        self.by_hi = [copies.plan(room(i), by_hi.at[i], "hi") for i in range(4)]

        def spot(lo_at, x_at):
            return full.at[(y * 2 + lo_at) * 2 + x_at]

        self.far = copies.plan(by_hi.at[0], relay, "lo")
        self.far_on = copies.plan(relay, spot(1 - lo, x), "x")
        self.by_lo = copies.plan(by_hi.at[1], spot(lo, x), "lo")
        self.by_x = copies.plan(by_hi.at[2], spot(lo, x), "x")
        self.mine = copies.move(by_hi.at[3], spot(lo, x))
        self.by_y = [
            copies.plan(by_hi.at[3], spot(lo, x), "y"),
            copies.plan(spot(1 - lo, x), spot(1 - lo, x), "y"),
            copies.plan(spot(lo, 1 - x), spot(lo, 1 - x), "y"),
            copies.plan(spot(1 - lo, 1 - x), spot(1 - lo, 1 - x), "y"),
        ]
        for i in range(8):
            events[name, CORE, i] = self.by_c[i].start
            events[name, ADD, i] = functools.partial(self.add_c, i)
        for i in range(4):
            events[name, HI, i] = self.by_hi[i].start
            events[name, PASS, i] = functools.partial(self.add_hi, i)
        for label, first, then in (
            ((FAR, 0), self.far, self.far_on),
            ((RELAY, 1), self.by_lo, self.by_y[1]),
            ((RELAY, 2), self.by_x, self.by_y[2]),
            ((RELAY, 3), self.far_on, self.by_y[3]),
        ):
            events[(name,) + label] = functools.partial(self.relay, first, then)
        events[name, END, 0] = self.finish

    def add_c(self, i):
        self.copies.arrive(self.by_c[i])
        here = self.room(i)
        here[...] = (here[...].astype(F32) + self.tile(i, self.c)[...].astype(F32)).astype(BF16)

    def add_hi(self, i):
        self.copies.arrive(self.by_hi[i])
        self.came_hi[i] = (self.came_hi[i].astype(F32) + self.room(4 + i)[...].astype(F32)).astype(BF16)
        if i < 3:
            (self.far, self.by_lo, self.by_x)[i].start()
        else:
            self.mine.start()
            self.by_y[0].start()

    def relay(self, first, then):
        self.copies.arrive(first)
        then.start()

    def finish(self):
        self.mine.wait()
        self.copies.arrive(*self.by_y)


class SmallScatter:
    def __init__(self, copies, parts, came):
        at = copies.at
        self.copies, self.parts, self.came, self.steps = copies, parts, came, []
        base, count, spot = 0, 8, 0
        for name in ("hi", "lo", "x", "c"):
            away = parts.at[pl.ds(base + (1 - at[name]) * count, count)]
            base = base + at[name] * count
            self.steps.append((copies.plan(away, came.at[pl.ds(spot, count)], name), base, spot, count))
            spot += count
            count //= 2
        own = parts.at[pl.ds(base, 1)]
        self.steps.append((copies.plan(own, came.at[pl.ds(spot, 1)], "y"), base, spot, 1))
        self.base, self.spot = base, spot

    def step(self, step):
        if step > 0:
            copy, base, spot, count = self.steps[step - 1]
            self.copies.arrive(copy)
            for i in range(count):
                self.parts[base + i] += self.came[spot + i]
        self.steps[step][0].start()

    def total(self):
        self.copies.arrive(self.steps[4][0])
        return self.parts[self.base] + self.came[self.spot]


SEQUENCES, COLUMN_TILES = 8, 8
UP_AT = 3
FC1_AT = UP_AT + SEQUENCES
LATE_ROWS_AT = FC1_AT + COLUMN_TILES
DX_AT = LATE_ROWS_AT + 2
QKV_AT = DX_AT + SEQUENCES
STEPS = QKV_AT + COLUMN_TILES


def sequence_at(step):
    i = jnp.clip(step - DX_AT, 0, SEQUENCES - 1)
    return 2 * (1 - i // 4) + (1 - i % 2) + 4 * (1 - (i % 4) // 2)


def backward_kernel(
    y_ref, g_ref, hidden_ref, mixed_ref, heads_ref, slope_ref, norm_ref, qkv_ref, fc1_ref, fc2_ref, out_ref, tables_ref,
    a1_ref, a2_ref,
    y_out, dx_out, rows_mine, rows_other, full_qkv, full_fc1, dx_came, small_out,
    g_all, grads, qkv, fc1, part, came, y_stage, dx_stage, room, kept, rows_came, a1, a2,
    qkv_hi, fc1_hi, qkv_relay, fc1_relay, packed_sum, up_sum, column_total, vectors, parts, parts_came,
    send_sem, recv_sem, local_sem, free_sem, free_again_sem,
):
    step = pl.program_id(0)
    at = {name: lax.axis_index(name) for name in NAMES}
    copies = Copies(at, send_sem, recv_sem, local_sem)
    events = {}
    n_fc1, n_mix, n_qkv = fc2_ref.shape[0], out_ref.shape[0], qkv_ref.shape[1]
    count, length, _ = g_all.shape
    tokens, tile = count * length, n_mix
    core = tile // 2
    y, hi, lo, x, c = (at[n] for n in NAMES)
    scatter_y = TokenScatter(copies, y_ref, came, True, y_stage, room, y_out, Y, events)
    TokenScatter(copies, g_all, dx_came, False, dx_stage, room, dx_out, DX, events)
    late = part.at[pl.ds(4 * core, 2 * tile)]
    rows = RowScatter(copies, fc1, qkv, late, kept, rows_came, n_fc1 // 2, n_mix // 2, rows_other, events)
    rows_store = copies.move(rows_came, rows_mine)

    hops = ((1 - lo, 1 - x), (1 - lo, x), (lo, 1 - x), (lo, x))
    places = [(hi_at * 2 + lo_at) * 2 + x_at for hi_at in (1 - hi, hi) for lo_at, x_at in hops]
    starts = [pl.multiple_of(place * tile, 128) for place in places]

    def fc1_tile(i, of):
        start = 4 * core + i % 4 // 2 * tile
        return part.at[pl.ds(pl.multiple_of(start + of * core, 16), core), pl.ds(i % 2 * n_fc1, n_fc1)]

    def fc1_room(i):
        return part.at[pl.ds(i % 4 * core, core), pl.ds(i // 4 * n_fc1, n_fc1)]

    def qkv_tile(i, of):
        return qkv.at[pl.ds(pl.multiple_of(starts[i] + of * core, 128), core)]

    def qkv_room(i):
        return part.at[pl.ds((4 + i % 4) * core, core), pl.ds(i // 4 * n_qkv, n_qkv)]

    fc1_out = ColumnScatter(copies, starts, fc1_tile, fc1_room, fc1_hi, fc1_relay, full_fc1, FC1, events)
    ColumnScatter(copies, starts, qkv_tile, qkv_room, qkv_hi, qkv_relay, full_qkv, QKV, events)
    small = SmallScatter(copies, parts, parts_came)
    load_g = copies.move(g_ref, g_all)
    early_loads = [
        copies.move(fc2_ref, part.at[pl.ds(0, n_fc1)]),
        copies.move(out_ref, part.at[pl.ds(n_fc1, n_mix)]),
    ]
    loads = [copies.move(qkv_ref, qkv), copies.move(fc1_ref, fc1)]

    def hidden_tile(i):
        return hidden_ref.at[:, pl.ds(i * tile, tile)]

    row_tiles = [
        (0, 1, a1, 0, copies.move(hidden_tile(1), a1.at[0])),
        (1, 3, a1, 1, copies.move(hidden_tile(3), a1.at[1])),
        (2, None, a2, 0, copies.move(mixed_ref, a2.at[0])),
        (LATE_ROWS_AT, 0, a1, 0, copies.move(hidden_tile(0), a1.at[0])),
        (LATE_ROWS_AT + 1, 2, a1, 1, copies.move(hidden_tile(2), a1.at[1])),
    ]

    def column_loads(src, dst):
        base, made = copies.local, []
        for i, start in enumerate(starts):
            copies.local = base + i % 2
            made.append(copies.move(src.at[:, pl.ds(start, tile)], dst.at[i % 2]))
        copies.local = base + 2
        return made

    a1_loads, a2_loads = column_loads(a1_ref, a1), column_loads(a2_ref, a2)

    def start_small():
        parts[...] = jnp.zeros_like(parts)
        lines = []
        for i in (0, 2):
            gain, bias = norm_ref[i : i + 1], norm_ref[i + 1 : i + 2]
            bias_grad = vectors[i + 1 : i + 2]
            lines += [(vectors[i : i + 1] - bias * bias_grad) / gain, bias_grad]
        lines.append(column_total[...])
        for spot in range(16):
            for i, line in enumerate(lines):
                parts[spot, i : i + 1] = line[:, spot * 128 : (spot + 1) * 128]
        own = (y * 4 + lo * 2 + x) * 2
        for half in range(2):
            start = len(lines)
            for sums in (packed_sum, up_sum):
                units = sums.shape[1] // 256
                for i in range(units):
                    lanes = slice((half * units + i) * 128, (half * units + i + 1) * 128)
                    parts[own + half, start + i : start + i + 1] = sums[:, lanes]
                start += units
        small.step(0)

    def end_rows():
        rows.add_hi()
        rows_store.start()

    def end_small():
        small_out[...] = small.total()

    def load_weights():
        rows.add_c(1)
        for copy in rows.by_c[1]:
            copy.wait_send()
        for copy in loads:
            copy.start()

    def late_rows():
        rows.add_c(0)
        for copy in rows.by_c[0]:
            copy.wait_send()

    events[ROWS, ADD, 1], events[ROWS, ADD, 0], events[ROWS, ALONG_Y, 0] = load_weights, late_rows, end_rows
    events[SMALL, STEP, 0], events[SMALL, END, 0] = start_small, end_small
    for i in range(1, 5):
        events[SMALL, STEP, i] = functools.partial(small.step, i)

    def tell(sem):
        pl.semaphore_signal(sem, inc=1, device_id={"c": 1 - c}, device_id_type=pl.DeviceIdType.MESH)

    def before(spot):
        if spot == 0:
            greet(at, NAMES)
            load_g.start()
            for tile_loads in row_tiles[:3]:
                tile_loads[-1].start()
            scatter_y.prepare()
        if spot == FC1_AT + 1:
            pl.semaphore_wait(free_sem, 1)
        if spot == QKV_AT + 1:
            pl.semaphore_wait(free_again_sem, 1)
        for label in SCATTER_EVENTS[spot]:
            events[label]()
        if spot == 0:
            for copy in early_loads:
                copy.start()
            packed_sum[...] = jnp.zeros_like(packed_sum)
            up_sum[...] = jnp.zeros_like(up_sum)
            load_g.wait()
            column_total[...] = jnp.sum(g_all[0].astype(F32), axis=0, keepdims=True)
        if spot == UP_AT:
            for copy in early_loads:
                copy.wait()
            for copy in a2_loads[:2] + [row_tiles[3][-1], row_tiles[4][-1]]:
                copy.start()
        if FC1_AT <= spot < LATE_ROWS_AT:
            i = spot - FC1_AT
            if i == 0:
                tell(free_sem)
                for copy in loads:
                    copy.wait()
            if 0 < i < COLUMN_TILES - 1:
                a2_loads[i + 1].start()
            a2_loads[i].wait()
            if i >= 4:
                fc1_out.by_c[i - 4].wait_send()
        if spot == LATE_ROWS_AT:
            for copy in fc1_out.by_c[4:]:
                copy.wait_send()
        if spot == DX_AT:
            a1_loads[0].start()
            a1_loads[1].start()
        if spot == QKV_AT:
            tell(free_again_sem)
        if spot >= QKV_AT:
            i = spot - QKV_AT
            if 0 < i < COLUMN_TILES - 1:
                a1_loads[i + 1].start()
            a1_loads[i].wait()

    for spot in range(STEPS):
        pl.when(step == spot)(functools.partial(before, spot))

    for spot, i, ref, slot, copy in row_tiles:

        @pl.when(step == spot)
        def _(i=i, ref=ref, slot=slot, copy=copy):
            copy.wait()
            rows.store_tile(i, dot(ref[slot], g_all[...].reshape(tokens, -1), TN))

    @pl.when((step >= UP_AT) & (step < FC1_AT))
    def _():
        j = step - UP_AT
        here = pl.ds(pl.multiple_of(j * length, 16), length)
        grad_up = (dot(g_all[j], part[:n_fc1], NT) * slope_ref[0]).astype(BF16)
        grads[here, n_qkv:] = grad_up
        up_sum[...] += jnp.sum(grad_up.astype(F32), axis=0, keepdims=True)

    @pl.when((step >= DX_AT) & (step < QKV_AT))
    def _():
        j = sequence_at(step)
        here = pl.ds(pl.multiple_of(j * length, 16), length)
        grad_mixed = dot(g_all[j], part[n_fc1:], NT).astype(BF16)
        queries = heads_ref[0, :, :HEAD_DIM]
        keys_all = heads_ref[0, :, HEAD_DIM : 2 * HEAD_DIM]
        values_all = heads_ref[0, :, 2 * HEAD_DIM :]
        probs = softmax(causal_scores(queries, keys_all))
        grad_probs = dot(grad_mixed, values_all, NT)
        grad_values = dot(probs.astype(BF16), grad_mixed, TN)
        inner = jnp.sum(grad_probs * probs, axis=-1, keepdims=True)
        grad_scores = (probs * (grad_probs - inner)).astype(BF16)
        grad_queries = turn(dot(grad_scores, keys_all) * SCALE, tables_ref, -1.0)
        grad_keys = turn(dot(grad_scores, queries, TN) * SCALE, tables_ref, -1.0)
        grads[here, :HEAD_DIM] = grad_queries.astype(BF16)
        grads[here, HEAD_DIM : 2 * HEAD_DIM] = grad_keys.astype(BF16)
        grads[here, 2 * HEAD_DIM : n_qkv] = grad_values.astype(BF16)
        packed_sum[...] += jnp.sum(grads[here, :n_qkv].astype(F32), axis=0, keepdims=True)

        g_all[j] = (
            dot(grads[here, :n_qkv], qkv[...], NT) * norm_ref[0:1]
            + dot(grads[here, n_qkv:], fc1[...], NT) * norm_ref[2:3]
        ).astype(BF16)

    def column_tile(first, values, ref, lanes, sums, line, store):
        i = step - first
        start = starts[0]
        for spot in range(1, COLUMN_TILES):
            start = jnp.where(i == spot, starts[spot], start)
        here = pl.ds(pl.multiple_of(start, 128), tile)
        value = dot(values[lax.rem(i, 2)], grads[:, lanes], TN)
        weight = ref[here].astype(F32)
        store(i, here, value.astype(BF16))
        lane = lax.broadcasted_iota(jnp.int32, (tile, 128), 1)
        sides = jnp.where(
            lane == 0, jnp.sum(weight * value, axis=1, keepdims=True), jnp.sum(weight * sums[...], axis=1, keepdims=True)
        )
        vectors[line : line + 2, here] = jnp.transpose(sides)[:2]

    @pl.when((step >= FC1_AT) & (step < LATE_ROWS_AT))
    def _():
        def store(i, here, value):
            start = pl.multiple_of(4 * core + lax.rem(i, 4) // 2 * tile, 16)
            for side in range(2):

                @pl.when(lax.rem(i, 2) == side)
                def _():
                    part[pl.ds(start, tile), side * n_fc1 : (side + 1) * n_fc1] = value

        column_tile(FC1_AT, a2, fc1, slice(n_qkv, n_qkv + n_fc1), up_sum, 2, store)

    @pl.when(step >= QKV_AT)
    def _():
        def store(i, here, value):
            qkv[here] = value

        column_tile(QKV_AT, a1, qkv, slice(0, n_qkv), packed_sum, 0, store)

    @pl.when(step == STEPS - 1)
    def _():
        for label in SCATTER_EVENTS[STEPS]:
            events[label]()
        rows_store.wait()
        done = rows.by_c[0] + rows.by_c[1] + fc1_out.by_c
        for copy in copies.remote:
            if not any(copy is other for other in done):
                copy.wait_send()


def backward(y_part, g_all, hidden, mixed, heads, slope, norm, qkv, fc1, fc2, out, tables, a1, a2):
    far = pl.BlockSpec(memory_space=pl.ANY)
    count, length, width = g_all.shape
    n_qkv, n_fc1, n_mix = qkv.shape[1], fc1.shape[1], out.shape[0]
    wide = n_qkv + n_fc1
    tokens = count * length
    a1, a2 = a1.reshape(tokens, width), a2.reshape(tokens, width)
    hidden, mixed = hidden.reshape(tokens, n_fc1), mixed.reshape(tokens, n_mix)
    own = (n_fc1 + n_mix) // 2
    size = width // 8
    chunks = chunks_of(length, SCATTER_CHUNKS)
    longest = max(rows for _, rows, _ in chunks)

    outputs = [
        ((length, width), F32, far),
        ((length, width), F32, far),
        ((own // 2, width), BF16, far),
        ((own // 2, width), BF16, far),
        ((8, size // 2, n_qkv), BF16, far),
        ((8, size // 2, n_fc1), BF16, far),
        ((7, length, width), BF16, far),
        ((16, 128), F32, None),
    ]
    shapes = [jax.ShapeDtypeStruct(shape, kind) for shape, kind, _ in outputs]
    copies = 2 * 7 * len(chunks) + 15 + 40 + 5
    flops = 2 * tokens * width * (2 * n_qkv + 3 * n_fc1 + 2 * n_mix)
    return pl.pallas_call(
        backward_kernel,
        grid=(STEPS,),
        in_specs=[far] * 4
        + [
            pl.BlockSpec((1, length, n_qkv), lambda i: (sequence_at(i), 0, 0)),
            pl.BlockSpec((1, length, n_fc1), lambda i: (jnp.clip(i - UP_AT, 0, SEQUENCES - 1), 0, 0)),
            whole(norm),
        ]
        + [far] * 4
        + [whole(tables), far, far],
        out_specs=[whole(s) if spec is None else spec for s, (_, _, spec) in zip(shapes, outputs)],
        out_shape=shapes,
        scratch_shapes=[
            pltpu.VMEM(g_all.shape, BF16),
            pltpu.VMEM((tokens, wide), BF16),
            pltpu.VMEM(qkv.shape, BF16),
            pltpu.VMEM(fc1.shape, BF16),
            pltpu.VMEM((n_fc1 + n_mix, width), BF16),
            pltpu.VMEM((7, length, width), BF16),
            pltpu.VMEM((length, width), BF16),
            pltpu.VMEM((3, longest, width), BF16),
            pltpu.VMEM((longest, width), F32),
            pltpu.VMEM((own + own // 2, width), BF16),
            pltpu.VMEM((own // 2, width), BF16),
            pltpu.VMEM((2, tokens, size), BF16),
            pltpu.VMEM((2, tokens, size), BF16),
            pltpu.VMEM((4, size // 2, n_qkv), BF16),
            pltpu.VMEM((4, size // 2, n_fc1), BF16),
            pltpu.VMEM((size // 2, n_qkv), BF16),
            pltpu.VMEM((size // 2, n_fc1), BF16),
            pltpu.VMEM((1, n_qkv), F32),
            pltpu.VMEM((1, n_fc1), F32),
            pltpu.VMEM((1, width), F32),
            pltpu.VMEM((8, width), F32),
            pltpu.VMEM((16, 16, 128), F32),
            pltpu.VMEM((16, 16, 128), F32),
            pltpu.SemaphoreType.DMA((copies,)),
            pltpu.SemaphoreType.DMA((copies,)),
            pltpu.SemaphoreType.DMA((4 * max(3, len(chunks)) + 20,)),
            pltpu.SemaphoreType.REGULAR,
            pltpu.SemaphoreType.REGULAR,
        ],
        compiler_params=pltpu.CompilerParams(
            collective_id=2, has_side_effects=True, vmem_limit_bytes=63 * 2**20
        ),
        cost_estimate=pl.CostEstimate(flops=flops, bytes_accessed=10**8, transcendentals=0),
        name="backward",
    )(y_part, g_all, hidden, mixed, heads, slope, norm, qkv, fc1, fc2, out, tables, a1, a2)


def whole(array):
    return pl.BlockSpec(array.shape, lambda i: (0,) * array.ndim, pipeline_mode=pl.Buffered(1))


def finish_kernel(
    x_ref, g_ref, y_ref, dx_ref, shift_ref, small_ref, qkv_ref, fc1_ref, fc2_mine, fc2_other, out_mine, out_other,
    output_ref, input_grad_ref, qkv_out, fc1_out, fc2_out, out_out, *small_outs,
):
    @pl.when(pl.program_id(0) == 0)
    def _():
        row = 0
        for i, ref in enumerate(small_outs):
            row -= i == 5
            for start in range(0, ref.shape[0], 128):
                ref[start : start + 128] = small_ref[row]
                row += 1

    x = x_ref[...].astype(F32)
    output_ref[...] = (x + shift_ref[4:5] + shift_ref[5:6] + y_ref[...]).astype(BF16)
    centred = x - jnp.mean(x, axis=-1, keepdims=True)
    scale = lax.rsqrt(jnp.mean(centred * centred, axis=-1, keepdims=True) + EPS)
    normed = centred * scale
    dx = dx_ref[...]
    inner = jnp.mean(dx * normed, axis=-1, keepdims=True)
    dx = scale * (dx - jnp.mean(dx, axis=-1, keepdims=True) - normed * inner)
    input_grad_ref[...] = (g_ref[...].astype(F32) + dx).astype(BF16)

    qkv_out[...] = qkv_ref[0].astype(F32)
    fc1_out[...] = fc1_ref[0].astype(F32)
    holds = 1 - (lax.axis_index("hi") + lax.axis_index("y")) % 2
    mine = holds == (jnp.minimum(pl.program_id(0), 7) < 4).astype(jnp.int32)
    for ref, here, there in ((fc2_out, fc2_mine, fc2_other), (out_out, out_mine, out_other)):
        ref[...] = jnp.where(mine, here[...].astype(F32), there[...].astype(F32))


def finish(tokens, cotangent, y_sum, dx, norm, small, sizes, qkv_grad, fc1_grad, rows_mine, rows_other):
    length, width = tokens.shape
    rows = length // 9
    n_qkv, n_fc1, size = qkv_grad.shape[2], fc1_grad.shape[2], qkv_grad.shape[1]
    n_fc2, n_out = rows_mine.shape[0] // 5 // 4 * 4, rows_mine.shape[0] // 5 // 4

    def some(i):
        return jnp.minimum(i, 7)

    token = pl.BlockSpec((rows, width), lambda i: (i, 0))
    fc2 = pl.BlockSpec((n_fc2, width), lambda i: (some(i) % 4, 0))
    out = pl.BlockSpec((n_out, width), lambda i: (16 + some(i) % 4, 0))
    return pl.pallas_call(
        finish_kernel,
        grid=(9,),
        in_specs=[token] * 4
        + [
            whole(norm),
            whole(small),
            pl.BlockSpec((1, size, n_qkv), lambda i: (some(i), 0, 0)),
            pl.BlockSpec((1, size, n_fc1), lambda i: (some(i), 0, 0)),
            fc2,
            fc2,
            out,
            out,
        ],
        out_specs=[
            token,
            token,
            pl.BlockSpec((size, n_qkv), lambda i: (0, some(i))),
            pl.BlockSpec((size, n_fc1), lambda i: (0, some(i))),
            pl.BlockSpec((n_fc2, width), lambda i: (some(i), 0)),
            pl.BlockSpec((n_out, width), lambda i: (some(i), 0)),
        ]
        + [pl.BlockSpec((n,), lambda i: (0,)) for n in sizes],
        out_shape=[
            jax.ShapeDtypeStruct((length, width), BF16),
            jax.ShapeDtypeStruct((length, width), BF16),
            jax.ShapeDtypeStruct((size, 8 * n_qkv), F32),
            jax.ShapeDtypeStruct((size, 8 * n_fc1), F32),
            jax.ShapeDtypeStruct((8 * n_fc2, width), F32),
            jax.ShapeDtypeStruct((8 * n_out, width), F32),
        ]
        + [jax.ShapeDtypeStruct((n,), F32) for n in sizes],
        compiler_params=pltpu.CompilerParams(vmem_limit_bytes=60 * 2**20),
        cost_estimate=pl.CostEstimate(flops=10**7, bytes_accessed=3 * 10**7, transcendentals=0),
        name="finish",
    )(tokens, cotangent, y_sum, dx, norm, small, qkv_grad, fc1_grad, rows_mine, rows_other, rows_mine, rows_other)


def body(
    tokens, ln1_gain, ln1_bias, ln2_gain, ln2_bias, qkv_weight, qkv_bias, out_weight, out_bias,
    fc1_weight, fc1_bias, fc2_weight, fc2_bias, cotangent, extra,
):
    vectors = [ln1_gain, ln1_bias, ln2_gain, ln2_bias, out_bias, fc2_bias, qkv_bias, fc1_bias]
    if extra > 1:
        join = functools.partial(lax.all_gather, axis_name="e", axis=0, tiled=True)
        vectors = [join(v) for v in vectors]
        qkv_weight, out_weight, fc1_weight, fc2_weight = [
            join(w) for w in (qkv_weight, out_weight, fc1_weight, fc2_weight)
        ]
    length, width = tokens.shape[1:]
    tables = jnp.asarray(rotary_tables(length))

    small = jnp.concatenate([v.reshape(-1, 128) for v in vectors], axis=0)
    small = jnp.pad(small, ((0, -small.shape[0] % 16), (0, 0)))
    g_all, norm, qkv_cols, fc1_cols, fc2_rows, out_rows, a1, a2, heads, mixed, hidden, slope, y_part = forward(
        tokens[0], cotangent[0], small, qkv_weight, fc1_weight, fc2_weight, out_weight, tables
    )
    y_sum, dx, rows_total, rows_other, qkv_grad, fc1_grad, _, small_grads = backward(
        y_part, g_all, hidden, mixed, heads, slope, norm, qkv_cols, fc1_cols, fc2_rows, out_rows, tables, a1, a2
    )
    sizes = [ln1_gain.shape[0] * extra] * 6 + [qkv_bias.shape[0] * extra, fc1_bias.shape[0] * extra]
    output, input_grad, qkv_grad, fc1_grad, fc2_grad, out_grad, *small_grads = finish(
        tokens[0], cotangent[0], y_sum, dx, norm, small_grads, sizes, qkv_grad, fc1_grad, rows_total, rows_other
    )

    weight_grads = [qkv_grad, out_grad, fc1_grad, fc2_grad]
    if extra > 1:
        scatter = functools.partial(lax.psum_scatter, axis_name="e", scatter_dimension=0, tiled=True)
        weight_grads = [scatter(v) for v in weight_grads]
        small_grads = [scatter(v) for v in small_grads]
    qkv_grad, out_grad, fc1_grad, fc2_grad = weight_grads
    gain1, bias1, gain2, bias2, out_total, fc2_total, packed_bias, up_bias = small_grads
    return (
        output[None],
        input_grad[None],
        gain1,
        bias1,
        gain2,
        bias2,
        qkv_grad,
        packed_bias,
        out_grad,
        out_total,
        fc1_grad,
        up_bias,
        fc2_grad,
        fc2_total,
    )


def solution(mesh):
    extra = mesh.shape["shard"] // 16
    axes = ("y", "hi", "lo", "x", "c", "e")
    fine = Mesh(mesh.devices.reshape(2, 2, 2, 2, 2, extra), axes)
    split = P(axes, None, None)
    row, flat = P(axes[1:], None), P(axes[1:])
    in_specs = (split, flat, flat, flat, flat, row, flat, row, flat, row, flat, row, flat, split)
    out_specs = (split, split, flat, flat, flat, flat, row, flat, row, flat, row, flat, row, flat)
    return jax.shard_map(
        functools.partial(body, extra=extra), mesh=fine, in_specs=in_specs, out_specs=out_specs, check_vma=False
    )
```
